32 devices in a mesh: shard: 4 (over x, core), ctx: 2 (over y), tensor: 4 (over z).
Axes of the slice: x: 2, y: 2, z: 4, core: 2. Of those that a mesh axis runs over, the one named last changes fastest.
Arguments:
- tokens: bfloat16 [16, 2048, 768], P('shard', 'ctx'), may hold values from -6 to 6
- cotangent: bfloat16 [16, 2048, 768], P('shard', 'ctx'), may hold values from -6 to 6
- segments: int32 [16, 2048], P('shard'), may hold values from 0 to 5, never falling along the last dimension, each value on 1 to 800 neighbouring positions
- rand_blocks: int32 [16, 32, 3], P('shard'), may hold values from 0 to 31
- attn_w: float32 [4, 768, 768], P(None, ('shard', 'ctx'), 'tensor'), may hold values from -3.4641016 to 3.4641016, as said below
- attn_m: float32 [4, 768, 768], P(None, ('shard', 'ctx'), 'tensor'), may hold values from -119.47276 to 119.47276, as said below
- attn_v: float32 [4, 768, 768], P(None, ('shard', 'ctx'), 'tensor'), may hold values from 0.1605632 to 131.072, as said below
- ffn_w: float32 [2, 768, 3072], P(None, ('shard', 'ctx'), 'tensor'), may hold values from -0.21650635 to 0.21650635, as said below
- ffn_m: float32 [2, 768, 3072], P(None, ('shard', 'ctx'), 'tensor'), may hold values from -64 to 64
- ffn_v: float32 [2, 768, 3072], P(None, ('shard', 'ctx'), 'tensor'), may hold values from 8.192 to 32.768
- qv_bias: float32 [2, 768], P(None, 'tensor'), may hold values from -3 to 3
- qv_m: float32 [2, 768], P(None, 'tensor'), may hold values from -128 to 128
- qv_v: float32 [2, 768], P(None, 'tensor'), may hold values from 32.768 to 131.072
- hid_bias: float32 [3072], P('tensor'), may hold values from -3 to 3
- hid_m: float32 [3072], P('tensor'), may hold values from -64 to 64
- hid_v: float32 [3072], P('tensor'), may hold values from 8.192 to 32.768
- vec_par: float32 [6, 768], replicated, may hold values from -3 to 3, as said below
- vec_m: float32 [6, 768], replicated, may hold values from -128 to 128
- vec_v: float32 [6, 768], replicated, may hold values from 32.768 to 131.072
Outputs:
- output: bfloat16 [16, 2048, 768], P('shard', 'ctx')
- grad_tokens: float32 [16, 2048, 768], P('shard', 'ctx')
- attn_moment: float32 [3, 768, 768], P(None, ('shard', 'ctx'), 'tensor')
- attn_square: float32 [3, 768, 768], P(None, ('shard', 'ctx'), 'tensor')
- out_states: float32 [2, 768, 768], P(None, ('shard', 'ctx'), 'tensor')
- attn_new: float32 [4, 768, 768], P(None, ('shard', 'ctx'), 'tensor')
- attn_copy: bfloat16 [4, 768, 768], P(None, ('shard', 'ctx'), 'tensor')
- ffn_moment: float32 [2, 768, 3072], P(None, ('shard', 'ctx'), 'tensor')
- ffn_square: float32 [2, 768, 3072], P(None, ('shard', 'ctx'), 'tensor')
- ffn_new: float32 [2, 768, 3072], P(None, ('shard', 'ctx'), 'tensor')
- ffn_copy: bfloat16 [2, 768, 3072], P(None, ('shard', 'ctx'), 'tensor')
- qv_moment: float32 [2, 768], P(None, 'tensor')
- qv_square: float32 [2, 768], P(None, 'tensor')
- qv_new: float32 [2, 768], P(None, 'tensor')
- hid_moment: float32 [3072], P('tensor')
- hid_square: float32 [3072], P('tensor')
- hid_new: float32 [3072], P('tensor')
- vec_moment: float32 [6, 768], replicated
- vec_square: float32 [6, 768], replicated
- vec_new: float32 [6, 768], replicated
The draws below stay inside these ranges and needn't reach their ends.
Inputs may be any that keep to these rules, and one draw needn't show every extreme that they name: `segments`: within a sequence the document numbers never fall; a document holds at most 800 tokens. `attn_w`: independent entries, spread 1 / sqrt(768) in the first three matrices and 1 / sqrt(3) in the fourth. `attn_m`: independent entries of both signs. `attn_v`: positive entries. `ffn_w`: independent entries, spread 1 / sqrt(768) in the first matrix and 1 / sqrt(3072) in the second. `vec_par`: gains near 1, shifts and biases of both signs.
All inputs are finite; a program needn't handle non-finite values.
Results may differ from the reference program's by a relative error of at most 0.02.
Values may be sent and summed in bfloat16 or wider, within the bound.
A program may use at most 384 MiB of HBM per device.

```python
import math
from functools import partial
import jax
import jax.numpy as jnp
import numpy as np
from jax import lax

D = 768
HEADS = 12
HEAD_DIM = 64
FF = 3072
BLOCK = 64
RAND = 3
LENGTH = 2048
STEP = 5
SEQ_ALL = 16
NBLK = 32
DOC_MOST = 800


def scaled_normal(key, shape, row_scales):
    sampled = jax.random.truncated_normal(key, -6.0, 6.0, shape, jnp.float32)
    return sampled * jnp.array(row_scales, jnp.float32).reshape((-1,) + (1,) * (len(shape) - 1))


def draw_attn_w(key, part):
    key = jax.random.fold_in(key, 11)
    return scaled_normal(key, (4, D, D), [D ** (-0.5), D ** (-0.5), D ** (-0.5), (D // (4 * BLOCK)) ** (-0.5)])


def draw_attn_m(key, part):
    key = jax.random.fold_in(key, 12)
    grad_scale = 0.11 * (SEQ_ALL * LENGTH) ** 0.5
    return scaled_normal(key, (4, D, D), [grad_scale, grad_scale, grad_scale, 0.07 * grad_scale])


def draw_attn_v(key, part):
    key = jax.random.fold_in(key, 13)
    grad_sq = 0.001 * SEQ_ALL * LENGTH
    factors = jnp.exp(jax.random.uniform(key, (4, D, D), jnp.float32, 0.0, 1.3862944))
    row_scales = jnp.array([grad_sq, grad_sq, grad_sq, 0.0049 * grad_sq], jnp.float32)
    return factors * row_scales[:, None, None]


def draw_ffn_w(key, part):
    key = jax.random.fold_in(key, 14)
    return scaled_normal(key, (2, D, FF), [D ** (-0.5), FF ** (-0.5)])


def draw_vec_par(key, part):
    key = jax.random.fold_in(key, 15)
    sampled = jax.random.truncated_normal(key, -5.0, 5.0, (6, D), jnp.float32)
    gain_rows = jnp.array([1.0, 0.0, 1.0, 0.0, 0.0, 0.0], jnp.float32)[:, None]
    spreads = jnp.array([0.1, 0.5, 0.1, 0.5, 0.5, 0.5], jnp.float32)[:, None]
    return gain_rows + spreads * sampled


def place_ends(values, stream_key, low, largest):
    longest = values.shape.index(max(values.shape))
    spots = []
    for shift in (0, 1):
        where = [jax.random.randint(jax.random.fold_in(stream_key, axis), (), 0, length) for axis, length in enumerate(values.shape)]
        where[longest] = (where[longest] + shift) % values.shape[longest]
        spots.append(tuple(where))
    return values.at[spots[0]].set(low).at[spots[1]].set(largest)


def block_levels(rng, shape, shards, least, top_value):
    loudness, own = 1.0, jax.random.fold_in(rng, 6)
    for position, blocks in shards:
        steps = jnp.exp(jax.random.uniform(jax.random.fold_in(own, position), (blocks,), jnp.float32, least / len(shards), top_value / len(shards)))
        loudness = loudness * jnp.repeat(steps, shape[position] // blocks).reshape([-1 if axis == position else 1 for axis in range(len(shape))])
    return loudness


def length_profile(number_of, total, reach, skew):
    weights = [(1 << 20) // math.isqrt(grade ** skew) + 1 for grade in range(2, number_of + 1)]
    spare, holding = total - reach - (number_of - 1), [1] * (number_of - 1)
    while spare > 0:
        movable = [i for i in range(number_of - 1) if holding[i] < reach]
        mass, left = sum([weights[i] for i in movable]), spare
        for i in movable:
            more = min(reach - holding[i], max(1, left * weights[i] // mass), spare)
            holding[i] = holding[i] + more
            spare = spare - more
    return np.array([reach] + holding)


def uneven_parts(own_key, amount, total, reach, skew):
    if amount == 2:
        one = jax.random.randint(own_key, (), max(1, total - reach), min(reach, total - 1) + 1)
        return jnp.stack([one, total - one])
    sizes = jnp.asarray(length_profile(amount, total, reach, skew), jnp.int32)
    pairs = (amount - 1) // 2
    giver, sink = sizes[1:1 + 2 * pairs:2], sizes[2:2 + 2 * pairs:2]
    slack = jnp.minimum(giver - 1, reach - sink)
    moved = jax.random.randint(jax.random.fold_in(own_key, 1), (pairs,), 0, 1 << 20) % (slack + 1)
    sizes = sizes.at[1:1 + 2 * pairs:2].set(giver - moved).at[2:2 + 2 * pairs:2].set(sink + moved)
    return sizes[jax.random.permutation(jax.random.fold_in(own_key, 2), amount)]


def bell_draw(own_key, extent, scale, limit, cuts=(), kind=jnp.bfloat16):
    values = scale * jax.random.normal(own_key, extent, jnp.float32)
    if cuts:
        values = values * block_levels(own_key, extent, cuts, -0.22, 0.18)
    return jnp.clip(values, -limit, limit).astype(kind)


def setup_inputs(seed: int = 0) -> dict:
    key_of = jax.random.split(jax.random.key(seed), 20)
    return {
        "tokens": bell_draw(key_of[0], (SEQ_ALL, LENGTH, D), 1.0, 6.0, ((0, 4), (1, 2))),
        "cotangent": bell_draw(key_of[1], (SEQ_ALL, LENGTH, D), 1.0, 6.0, ((0, 4), (1, 2))),
        "segments": jax.vmap(lambda own: jnp.searchsorted(jnp.cumsum(uneven_parts(own, 6, LENGTH, DOC_MOST, 1)), jnp.arange(LENGTH), side="right"))(jax.random.split(key_of[2], SEQ_ALL)).reshape((SEQ_ALL, LENGTH)).astype(jnp.int32),
        "rand_blocks": place_ends(jax.random.randint(key_of[3], (SEQ_ALL, NBLK, RAND), 0, NBLK), jax.random.fold_in(key_of[3], 1), 0, NBLK - 1).astype(jnp.int32),
        "attn_w": draw_attn_w(jax.random.fold_in(key_of[19], 71), 0),
        "attn_m": draw_attn_m(jax.random.fold_in(key_of[19], 71), 0),
        "attn_v": draw_attn_v(jax.random.fold_in(key_of[19], 71), 0),
        "ffn_w": draw_ffn_w(jax.random.fold_in(key_of[19], 71), 0),
        "ffn_m": bell_draw(key_of[8], (2, D, FF), (0.055 * (SEQ_ALL * LENGTH) ** 0.5), 64.0, ((1, 8), (2, 4)), jnp.float32),
        "ffn_v": jnp.clip(jnp.exp(math.log(32.768) - 1.3862944 * jax.random.uniform(key_of[9], (2, D, FF), jnp.float32) ** block_levels(key_of[9], (2, D, FF), ((1, 8), (2, 4)), -0.2, 0.2)), 8.192, 32.768),
        "qv_bias": bell_draw(key_of[10], (2, D), 0.5, 3.0, ((1, 4),), jnp.float32),
        "qv_m": bell_draw(key_of[11], (2, D), (0.11 * (SEQ_ALL * LENGTH) ** 0.5), 128.0, ((1, 4),), jnp.float32),
        "qv_v": jnp.clip(jnp.exp(math.log(131.072) - 1.3862944 * jax.random.uniform(key_of[12], (2, D), jnp.float32) ** block_levels(key_of[12], (2, D), ((1, 4),), -0.2, 0.2)), 32.768, 131.072),
        "hid_bias": bell_draw(key_of[13], (FF,), 0.5, 3.0, ((0, 4),), jnp.float32),
        "hid_m": bell_draw(key_of[14], (FF,), (0.055 * (SEQ_ALL * LENGTH) ** 0.5), 64.0, ((0, 4),), jnp.float32),
        "hid_v": jnp.clip(jnp.exp(math.log(32.768) - 1.3862944 * jax.random.uniform(key_of[15], (FF,), jnp.float32) ** block_levels(key_of[15], (FF,), ((0, 4),), -0.2, 0.2)), 8.192, 32.768),
        "vec_par": draw_vec_par(jax.random.fold_in(key_of[19], 71), 0),
        "vec_m": bell_draw(key_of[17], (6, D), (0.11 * (SEQ_ALL * LENGTH) ** 0.5), 128.0, (), jnp.float32),
        "vec_v": jnp.clip(jnp.exp(jax.random.uniform(key_of[18], (6, D), jnp.float32, math.log(32.768), math.log(131.072))), 32.768, 131.072),
    }


@jax.custom_vjp
def low(v):
    return lax.optimization_barrier(v.astype(jnp.bfloat16)).astype(jnp.float32)

@jax.custom_vjp
def low_back(v):
    return v

def low_keep(v):
    return (low(v), None)

def low_pass(kept, grad):
    return (grad,)

def back_keep(v):
    return (v, None)

def back_low(kept, grad):
    return (low(grad),)
low.defvjp(low_keep, low_pass)
low_back.defvjp(back_keep, back_low)
beta_first = 0.9
beta_second = 0.999
adam_eps = 1e-08
decay_rate = 0.01
norm_eps = 1e-06
neg_large = -1e+30

def product(left, right):
    return jnp.dot(left, right, precision=lax.Precision.HIGHEST, preferred_element_type=jnp.float32)

def product_nt(left, right):
    return lax.dot_general(left, right, (((1,), (1,)), ((), ())), precision=lax.Precision.HIGHEST, preferred_element_type=jnp.float32)

def layer_norm(hidden, norm_gain, norm_shift):
    centred = hidden - lax.optimization_barrier(jnp.mean(hidden, axis=-1, keepdims=True))
    spread = lax.optimization_barrier(jnp.mean(centred * centred, axis=-1, keepdims=True))
    return centred * lax.rsqrt(spread + norm_eps) * norm_gain + norm_shift

def allowed_keys(segment_row, random_row):
    block_of = jnp.arange(LENGTH, dtype=jnp.int32) // BLOCK
    block_ids = jnp.arange(LENGTH // BLOCK, dtype=jnp.int32)
    near = jnp.abs(block_ids[:, None] - block_ids[None, :]) <= 1
    chosen = jnp.any(random_row[:, :, None] == block_ids[None, None, :], axis=1)
    block_table = near | chosen | (block_ids[None, :] < 2)
    token_table = block_table[block_of][:, block_of]
    same_doc = (segment_row[:, None] == segment_row[None, :]) | (block_of[None, :] < 2)
    return token_table & same_doc | (block_of[:, None] < 2)

def split_heads(matrix):
    return matrix.reshape(LENGTH, HEADS, HEAD_DIM).transpose(1, 0, 2)

def sequence_layer(params, tokens_seq, segment_row, random_row):
    attn_par, ffn_par, qv_par, hid_par, vec_values = params
    queries = low(low_back(product(tokens_seq, attn_par[0]) + qv_par[0]))
    keys_all = low(low_back(product(tokens_seq, attn_par[1])))
    values_all = low(low_back(product(tokens_seq, attn_par[2]) + qv_par[1]))
    scores = low_back(jnp.einsum('hqd,hkd->hqk', split_heads(queries), split_heads(keys_all), precision=lax.Precision.HIGHEST) * 0.125)
    allowed = allowed_keys(segment_row, random_row)
    scores = jnp.where(allowed[None], scores, neg_large)
    probs = low(jax.nn.softmax(scores, axis=-1))
    mixed = jnp.einsum('hqk,hkd->qhd', probs, split_heads(values_all), precision=lax.Precision.HIGHEST).reshape(LENGTH, D)
    mixed = low(low_back(mixed))
    branch = low_back(product_nt(mixed, attn_par[3]) + vec_values[4])
    first_out = layer_norm(tokens_seq + branch, vec_values[0], vec_values[1])
    hidden_pre = low_back(product(low(first_out), ffn_par[0]) + hid_par)
    hidden_act = low(low_back(jax.nn.gelu(hidden_pre, approximate=False)))
    down_out = low_back(product_nt(hidden_act, ffn_par[1]) + vec_values[5])
    return layer_norm(first_out + down_out, vec_values[2], vec_values[3])

def adam_update(weight, moment, square, gradient, step_rates, decay_on):
    moment_new = beta_first * moment + (1.0 - beta_first) * gradient
    square_new = beta_second * square + (1.0 - beta_second) * gradient * gradient
    step_ratio = moment_new / (1.0 - beta_first ** STEP) / (jnp.sqrt(square_new / (1.0 - beta_second ** STEP)) + adam_eps)
    weight_new = weight - step_rates * (step_ratio + decay_on * weight)
    return (moment_new, square_new, weight_new)

def reference(tokens, cotangent, segments, rand_blocks, attn_w, attn_m, attn_v, ffn_w, ffn_m, ffn_v, qv_bias, qv_m, qv_v, hid_bias, hid_m, hid_v, vec_par, vec_m, vec_v):
    attn_cast = attn_w.astype(jnp.bfloat16).astype(jnp.float32)
    ffn_cast = ffn_w.astype(jnp.bfloat16).astype(jnp.float32)
    params = (attn_cast, ffn_cast, qv_bias, hid_bias, vec_par)

    def forward(params_in, tokens_in):
        layer_fn = jax.checkpoint(partial(sequence_layer, params_in))
        return lax.map(lambda item: layer_fn(item[0], item[1], item[2]), (tokens_in, segments, rand_blocks))
    result, pull_back = jax.vjp(forward, params, tokens.astype(jnp.float32))
    param_grads, grad_tokens = pull_back(cotangent.astype(jnp.float32))
    attn_grad, ffn_grad, qv_grad, hid_grad, vec_grad = param_grads
    attn_rates = jnp.array([2.0 / D ** 0.5] * 3 + [2.0 / (D // (4 * BLOCK)) ** 0.5], jnp.float32)[:, None, None]
    ffn_rates = jnp.array([2.0 / D ** 0.5, 2.0 / FF ** 0.5], jnp.float32)[:, None, None]
    attn_moment, attn_square, attn_new = adam_update(attn_w, attn_m, attn_v, attn_grad, attn_rates, decay_rate)
    ffn_moment, ffn_square, ffn_new = adam_update(ffn_w, ffn_m, ffn_v, ffn_grad, ffn_rates, decay_rate)
    qv_moment, qv_square, qv_new = adam_update(qv_bias, qv_m, qv_v, qv_grad, 0.5, 0.0)
    hid_moment, hid_square, hid_new = adam_update(hid_bias, hid_m, hid_v, hid_grad, 0.5, 0.0)
    vec_moment, vec_square, vec_new = adam_update(vec_par, vec_m, vec_v, vec_grad, 0.5, 0.0)
    out_states = jnp.stack([attn_moment[3], attn_square[3]])
    return (result.astype(jnp.bfloat16), grad_tokens, attn_moment[:3], attn_square[:3], out_states, attn_new, attn_new.astype(jnp.bfloat16), ffn_moment, ffn_square, ffn_new, ffn_new.astype(jnp.bfloat16), qv_moment, qv_square, qv_new, hid_moment, hid_square, hid_new, vec_moment, vec_square, vec_new)
```

```python
from functools import partial

import jax
import jax.numpy as jnp
from jax import lax
from jax.experimental import pallas as pl
from jax.experimental.pallas import tpu as pltpu
from jax.sharding import PartitionSpec as P

D = 768
HEAD_DIM = 64
FF = 3072
BLOCK = 64
STEP = 5
GROUP = 4 * HEAD_DIM
GROUPS = D // GROUP
ROWS = 4 * BLOCK
LISTED = 8
KEYS = LISTED * BLOCK
VMEM_LIMIT = 60 * 2**20

beta_first = 0.9
beta_second = 0.999
adam_eps = 1e-08
decay_rate = 0.01
norm_eps = 1e-06
neg_large = -1e30

f32 = jnp.float32
bf16 = jnp.bfloat16


def matmul(left, right):
    return jnp.dot(left, right, preferred_element_type=f32)


def matmul_tn(left, right):
    return lax.dot_general(left, right, (((0,), (0,)), ((), ())), preferred_element_type=f32)


def matmul_nt(left, right):
    return lax.dot_general(left, right, (((1,), (1,)), ((), ())), preferred_element_type=f32)


def column_sum(array_in):
    return jnp.sum(array_in.astype(f32), axis=0)


def adam_update(weight, moment, square, gradient, step_rates, decay_on):
    moment_new = beta_first * moment + (1.0 - beta_first) * gradient
    square_new = beta_second * square + (1.0 - beta_second) * gradient * gradient
    step_ratio = (
        moment_new
        / (1.0 - beta_first**STEP)
        / (jnp.sqrt(square_new / (1.0 - beta_second**STEP)) + adam_eps)
    )
    weight_new = weight - step_rates * (step_ratio + decay_on * weight)
    return (moment_new, square_new, weight_new)


def same_head():
    row_head = lax.broadcasted_iota(jnp.int32, (ROWS, GROUP), 0) // BLOCK
    col_head = lax.broadcasted_iota(jnp.int32, (ROWS, GROUP), 1) // HEAD_DIM
    return row_head == col_head


def spread_heads(block, keep):
    stacked = jnp.concatenate([block] * 4, axis=0)
    return jnp.where(keep, stacked, jnp.zeros_like(stacked))


def fold_heads(full, keep):
    kept = jnp.where(keep, full, 0.0)
    return sum(kept[h * BLOCK : (h + 1) * BLOCK] for h in range(4))


def load_keys(k_all, v_all, seq, k_buf, v_buf, sems):
    return [
        pltpu.make_async_copy(k_all.at[seq], k_buf, sems.at[0]),
        pltpu.make_async_copy(v_all.at[seq], v_buf, sems.at[1]),
    ]


def picked_rows(buf, spots, cols):
    return jnp.concatenate([buf[at, :, cols] for at in spots], axis=0)


def chunk_rows(buf, i, cols):
    blocks = buf[pl.ds(i * LISTED, LISTED), :, cols]
    return blocks.reshape(KEYS, GROUP)


def listed_blocks(rand, base, blk, first, own, total):
    one = lambda condition: condition.astype(jnp.int32)
    me = first + blk
    ids = [me - 1, me, me + 1, me * 0, me * 0 + 1] + [rand[base + n] for n in range(LISTED - 5)]
    spots, unused, common = [], [], []
    for n, block in enumerate(ids):
        out = one(block < 0) + one(block >= total)
        for earlier in ids[:n]:
            out = out + one(block == earlier)
        out = lax.min(out, jnp.int32(1))
        at = lax.max(jnp.int32(0), lax.min(block, jnp.int32(total - 1))) - first + own
        spots.append(at + total * one(at < 0))
        unused.append(out)
        common.append(one(block < 2) * (1 - out))
    return spots, unused, common


def code_rows(tab_ref, spots, unused, common):
    low_half = lax.broadcasted_iota(jnp.int32, (1, 2 * BLOCK), 1) < BLOCK

    def one(n):
        plain = (1 - unused[n] - common[n]).astype(f32)
        return tab_ref[spots[n]] * plain - (unused[n] + 2 * common[n]).astype(f32)

    return [jnp.where(low_half, one(n), one(n + 1)) for n in range(0, LISTED, 2)]


def column_of(row):
    return jnp.broadcast_to(row, (2 * BLOCK, 2 * BLOCK)).T


def mask_bias(document, code):
    return jnp.where((document == code) | (code == -2.0), 0.0, neg_large)


def row_of(column):
    return jnp.broadcast_to(column, (ROWS, 2 * BLOCK)).T[0:1, :]


def forward_block(q_ref, out_ref, lse_ref, k_buf, v_buf, s_buf, tab_ref, rand, base, blk, first, own):
    keep = same_head()
    total_blocks = k_buf.shape[0]
    chunks = total_blocks // LISTED
    is_global = first + blk < 2

    @pl.when(jnp.logical_not(is_global))
    def _():
        spots, unused, common = listed_blocks(rand, base, blk, first, own, total_blocks)
        mine = column_of(tab_ref[own + blk])[:BLOCK]
        mine = jnp.concatenate([mine] * 4, axis=0)
        codes = code_rows(tab_ref, spots, unused, common)
        bias = jnp.concatenate([mask_bias(mine, code) for code in codes], axis=1)
        for g in range(GROUPS):
            cols = slice(g * GROUP, (g + 1) * GROUP)
            q_full = spread_heads(q_ref[:, cols], keep)
            scores = matmul_nt(q_full, picked_rows(k_buf, spots, cols)) + bias
            largest = jnp.max(scores, axis=-1, keepdims=True)
            weights = jnp.exp(scores - largest)
            total = jnp.sum(weights, axis=-1, keepdims=True)
            full = matmul(weights.astype(bf16), picked_rows(v_buf, spots, cols))
            out_ref[:, cols] = fold_heads(full * (1.0 / total), keep).astype(bf16)
            lse_ref[g : g + 1, :] = row_of(largest + jnp.log(total))

    @pl.when(is_global)
    def _():
        for g in range(GROUPS):
            cols = slice(g * GROUP, (g + 1) * GROUP)
            q_full = spread_heads(q_ref[:, cols], keep)

            def score_chunk(i, largest):
                scores = matmul_nt(q_full, chunk_rows(k_buf, i, cols))
                s_buf[i] = scores
                return jnp.maximum(largest, jnp.max(scores, axis=-1, keepdims=True))

            largest = lax.fori_loop(0, chunks, score_chunk, jnp.full((ROWS, 1), neg_large, f32))

            def mix_chunk(i, carry):
                total, full = carry
                weights = jnp.exp(s_buf[i] - largest)
                total = total + jnp.sum(weights, axis=-1, keepdims=True)
                return total, full + matmul(weights.astype(bf16), chunk_rows(v_buf, i, cols))

            total, full = lax.fori_loop(
                0, chunks, mix_chunk, (jnp.zeros((ROWS, 1), f32), jnp.zeros((ROWS, GROUP), f32))
            )
            out_ref[:, cols] = fold_heads(full * (1.0 / total), keep).astype(bf16)
            lse_ref[g : g + 1, :] = row_of(largest + jnp.log(total))


def forward_kernel(
    rand, meta, q_ref, tab_ref, k_all, v_all, out_ref, lse_ref, k_buf, v_buf, s_buf, sems
):
    seq, blk = pl.program_id(0), pl.program_id(1)
    nb = pl.num_programs(1)

    @pl.when(blk == 0)
    def _():
        copies = load_keys(k_all, v_all, seq, k_buf, v_buf, sems)
        for c in copies:
            c.start()
        for c in copies:
            c.wait()

    base = (seq * nb + blk) * (LISTED - 5)
    forward_block(
        q_ref, out_ref, lse_ref, k_buf, v_buf, s_buf, tab_ref, rand, base, blk, meta[0], meta[1]
    )


def back_tile(k_rows, v_rows, q_full, go_full, bias, lse, centre):
    scores = matmul_nt(k_rows, q_full)
    if bias is not None:
        scores = scores + bias
    probs = jnp.exp(scores - lse)
    grad_probs = matmul_nt(v_rows, go_full)
    grad_scores = (probs * (grad_probs - centre)).astype(bf16)
    dv_rows = matmul(probs.astype(bf16), go_full)
    dk_rows = matmul(grad_scores, q_full)
    return matmul_tn(grad_scores, k_rows), dk_rows, dv_rows


def backward_kernel(
    n_out, rand, meta, q_ref, go_ref, mixed_ref, lse_ref, tab_ref, k_all, v_all, dq_ref, *rest
):
    dk_refs, dv_refs = rest[:n_out], rest[n_out : 2 * n_out]
    k_buf, v_buf, dk_acc, dv_acc, sems = rest[2 * n_out :]
    seq, blk = pl.program_id(0), pl.program_id(1)
    nb = pl.num_programs(1)
    total_blocks = k_buf.shape[0]
    chunks = total_blocks // LISTED

    @pl.when(blk == 0)
    def _():
        copies = load_keys(k_all, v_all, seq, k_buf, v_buf, sems)
        for c in copies:
            c.start()
        dk_acc[...] = jnp.zeros_like(dk_acc)
        dv_acc[...] = jnp.zeros_like(dv_acc)
        for c in copies:
            c.wait()

    keep = same_head()
    is_global = meta[0] + blk < 2
    base = (seq * nb + blk) * (LISTED - 5)

    def operands(g):
        cols = slice(g * GROUP, (g + 1) * GROUP)
        q_full = spread_heads(q_ref[:, cols], keep)
        go_full = spread_heads(go_ref[:, cols], keep)
        mixed = jnp.concatenate([mixed_ref[:, cols]] * 4, axis=0)
        product = go_full.astype(f32) * mixed.astype(f32)
        centre = row_of(jnp.sum(product, axis=-1, keepdims=True))
        return cols, q_full, go_full, lse_ref[g : g + 1, :], centre

    @pl.when(jnp.logical_not(is_global))
    def _():
        spots, unused, common = listed_blocks(rand, base, blk, meta[0], meta[1], total_blocks)
        stores = [at + (total_blocks - at) * out for at, out in zip(spots, unused)]
        own = tab_ref[meta[1] + blk]
        codes = code_rows(tab_ref, spots, unused, common)
        bias = jnp.concatenate([mask_bias(own, column_of(code)) for code in codes], axis=0)
        bias = jnp.concatenate([bias, bias], axis=1)
        for g in range(GROUPS):
            cols, q_full, go_full, lse, centre = operands(g)
            k_rows, v_rows = picked_rows(k_buf, spots, cols), picked_rows(v_buf, spots, cols)
            dq_full, dk_rows, dv_rows = back_tile(
                k_rows, v_rows, q_full, go_full, bias, lse, centre
            )
            dq_ref[:, cols] = (fold_heads(dq_full, keep) * 0.125).astype(bf16)
            places = [pl.ds(pl.multiple_of(at * BLOCK, BLOCK), BLOCK) for at in stores]
            dk_old = [dk_acc[at, cols] for at in places]
            dv_old = [dv_acc[at, cols] for at in places]
            for n, at in enumerate(places):
                own_rows = slice(n * BLOCK, (n + 1) * BLOCK)
                dk_acc[at, cols] = dk_old[n] + dk_rows[own_rows]
                dv_acc[at, cols] = dv_old[n] + dv_rows[own_rows]

    @pl.when(is_global)
    def _():
        for g in range(GROUPS):
            cols, q_full, go_full, lse, centre = operands(g)

            def chunk_back(i, dq_full):
                rows = pl.ds(pl.multiple_of(i * KEYS, KEYS), KEYS)
                dq_now, dk_rows, dv_rows = back_tile(
                    chunk_rows(k_buf, i, cols),
                    chunk_rows(v_buf, i, cols),
                    q_full,
                    go_full,
                    None,
                    lse,
                    centre,
                )
                dk_acc[rows, cols] += dk_rows
                dv_acc[rows, cols] += dv_rows
                return dq_full + dq_now

            dq_full = lax.fori_loop(0, chunks, chunk_back, jnp.zeros((ROWS, GROUP), f32))
            dq_ref[:, cols] = (fold_heads(dq_full, keep) * 0.125).astype(bf16)

    @pl.when(blk == nb - 1)
    def _():
        row = 0
        for dk_ref, dv_ref in zip(dk_refs, dv_refs):
            rows = dk_ref.shape[0]
            dk_ref[...] = dk_acc[row : row + rows].astype(bf16)
            dv_ref[...] = dv_acc[row : row + rows].astype(bf16)
            row += rows


def attention_tables(segments, random, piece, nb, own_first):
    seq_count, length = segments.shape
    total = length // BLOCK
    first = piece * nb
    rand = lax.dynamic_slice_in_dim(random, first, nb, 1).reshape(-1)
    table = segments.reshape(seq_count, total, BLOCK).astype(f32)
    table = jnp.concatenate([table, table], axis=2)[:, :, None, :]
    if own_first:
        table = lax.dynamic_slice_in_dim(jnp.concatenate([table, table], axis=1), first, total, 1)
    meta = jnp.stack([first, jnp.zeros_like(first) if own_first else first]).astype(jnp.int32)
    return rand, meta, table


def as_blocks(rows):
    return rows.reshape(rows.shape[0], -1, BLOCK, D)


def attend(tables, q, keys, values):
    rand, meta, table = tables
    seq_count, piece_len, _ = q.shape
    nb = piece_len // BLOCK
    length = keys.shape[1]
    any_spec = pl.BlockSpec(memory_space=pl.ANY)
    row_spec = pl.BlockSpec((None, BLOCK, D), lambda s, b, *_: (s, b, 0))
    return pl.pallas_call(
        forward_kernel,
        out_shape=[
            jax.ShapeDtypeStruct(q.shape, bf16),
            jax.ShapeDtypeStruct((seq_count, nb, 8, ROWS), f32),
        ],
        grid_spec=pltpu.PrefetchScalarGridSpec(
            num_scalar_prefetch=2,
            grid=(seq_count, nb),
            in_specs=[
                row_spec,
                pl.BlockSpec((None,) + table.shape[1:], lambda s, b, *_: (s, 0, 0, 0)),
                any_spec,
                any_spec,
            ],
            out_specs=[
                row_spec,
                pl.BlockSpec((None, None, 8, ROWS), lambda s, b, *_: (s, b, 0, 0)),
            ],
            scratch_shapes=[
                pltpu.VMEM((length // BLOCK, BLOCK, D), bf16),
                pltpu.VMEM((length // BLOCK, BLOCK, D), bf16),
                pltpu.VMEM((length // KEYS, ROWS, KEYS), f32),
                pltpu.SemaphoreType.DMA((2,)),
            ],
        ),
        compiler_params=pltpu.CompilerParams(vmem_limit_bytes=VMEM_LIMIT),
        name="attend",
    )(rand, meta, q, table, as_blocks(keys), as_blocks(values))


def attend_back(tables, q, grad_mixed, mixed, lse, keys, values, pieces):
    rand, meta, table = tables
    seq_count, piece_len, _ = q.shape
    nb = piece_len // BLOCK
    length = keys.shape[1]
    any_spec = pl.BlockSpec(memory_space=pl.ANY)
    row_spec = pl.BlockSpec((None, BLOCK, D), lambda s, b, *_: (s, b, 0))
    part_specs = [pl.BlockSpec((None, rows, D), lambda s, b, *_: (s, 0, 0)) for rows in pieces]
    part_shapes = [jax.ShapeDtypeStruct((seq_count, rows, D), bf16) for rows in pieces]
    out = pl.pallas_call(
        partial(backward_kernel, len(pieces)),
        out_shape=[jax.ShapeDtypeStruct(q.shape, bf16)] + part_shapes * 2,
        grid_spec=pltpu.PrefetchScalarGridSpec(
            num_scalar_prefetch=2,
            grid=(seq_count, nb),
            in_specs=[
                row_spec,
                row_spec,
                row_spec,
                pl.BlockSpec((None, None, 8, ROWS), lambda s, b, *_: (s, b, 0, 0)),
                pl.BlockSpec((None,) + table.shape[1:], lambda s, b, *_: (s, 0, 0, 0)),
                any_spec,
                any_spec,
            ],
            out_specs=[row_spec] + part_specs * 2,
            scratch_shapes=[
                pltpu.VMEM((length // BLOCK, BLOCK, D), bf16),
                pltpu.VMEM((length // BLOCK, BLOCK, D), bf16),
                pltpu.VMEM((length + BLOCK, D), f32),
                pltpu.VMEM((length + BLOCK, D), f32),
                pltpu.SemaphoreType.DMA((2,)),
            ],
        ),
        compiler_params=pltpu.CompilerParams(vmem_limit_bytes=VMEM_LIMIT),
        cost_estimate=pl.CostEstimate(
            flops=seq_count * nb * GROUPS * 10 * ROWS * KEYS * GROUP,
            bytes_accessed=seq_count * (3 * piece_len + 4 * length) * D * 2,
            transcendentals=seq_count * nb * GROUPS * ROWS * KEYS,
        ),
        name="attend_back",
    )(rand, meta, q, grad_mixed, mixed, lse, table, as_blocks(keys), as_blocks(values))
    return out[0], out[1 : 1 + len(pieces)], out[1 + len(pieces) :]


def norm_parts(hidden):
    centred = hidden - jnp.mean(hidden, axis=-1, keepdims=True)
    scale = lax.rsqrt(jnp.mean(centred * centred, axis=-1, keepdims=True) + norm_eps)
    return centred * scale, scale


def norm_back(grad, unit, scale, gain):
    inner = grad * gain
    return scale * (
        inner
        - jnp.mean(inner, axis=-1, keepdims=True)
        - unit * jnp.mean(inner * unit, axis=-1, keepdims=True)
    )


def gelu_and_slope(pre):
    bell = jnp.exp(-0.5 * pre * pre)
    t = 1.0 / (1.0 + (0.3275911 * 0.5**0.5) * jnp.abs(pre))
    poly = 0.5 * 1.061405429
    for coefficient in (-1.453152027, 1.421413741, -0.284496736, 0.254829592):
        poly = poly * t + 0.5 * coefficient
    tail = poly * t * bell
    phi = jnp.where(pre >= 0.0, 1.0 - tail, tail)
    return pre * phi, phi + pre * bell * 0.3989422804014327


def column_total(array):
    return jnp.sum(array.astype(f32), axis=0, keepdims=True)


def up_kernel(
    chunk,
    x_ref,
    mixed_ref,
    cot_ref,
    wo_ref,
    w1_ref,
    w2_ref,
    hid_ref,
    vec_ref,
    act_ref,
    slope_ref,
    h1_ref,
    res_ref,
    gs_ref,
    sums_ref,
    low,
    down,
):
    step = pl.program_id(0)
    chunks = x_ref.shape[0] // chunk

    @pl.when(step == 0)
    def _():
        @pl.loop(0, chunks)
        def _(i):
            rows = pl.ds(pl.multiple_of(i * chunk, chunk), chunk)
            h1 = x_ref[rows, :].astype(f32) + matmul_nt(mixed_ref[rows, :], wo_ref[...])
            h1 = h1 + vec_ref[4:5, :]
            h1_ref[rows, :] = h1
            unit, _scale = norm_parts(h1)
            low[rows, :] = (unit * vec_ref[0:1, :] + vec_ref[1:2, :]).astype(bf16)
            down[rows, :] = jnp.zeros((chunk, D), f32)

    for i in range(chunks):
        rows = slice(i * chunk, (i + 1) * chunk)
        pre = matmul(low[rows, :], w1_ref[...]) + hid_ref[...]
        act, slope = gelu_and_slope(pre)
        act = act.astype(bf16)
        act_ref[rows, :] = act
        slope_ref[rows, :] = slope.astype(bf16)
        down[rows, :] += matmul_nt(act, w2_ref[...])

    @pl.when(step == pl.num_programs(0) - 1)
    def _():
        sums_ref[...] = jnp.zeros_like(sums_ref)

        @pl.loop(0, chunks)
        def _(i):
            rows = pl.ds(pl.multiple_of(i * chunk, chunk), chunk)
            unit, _scale = norm_parts(h1_ref[rows, :])
            first = unit * vec_ref[0:1, :] + vec_ref[1:2, :]
            unit, scale = norm_parts(first + down[rows, :] + vec_ref[5:6, :])
            res_ref[rows, :] = (unit * vec_ref[2:3, :] + vec_ref[3:4, :]).astype(bf16)
            cot = cot_ref[rows, :].astype(f32)
            grad = norm_back(cot, unit, scale, vec_ref[2:3, :])
            gs_ref[rows, :] = grad
            sums_ref[0:1, :] += column_total(cot * unit)
            sums_ref[1:2, :] += column_total(cot)
            sums_ref[2:3, :] += column_total(grad.astype(bf16))


def feed_forward(x, mixed, cot, attn_full, ffn_full, hid_all, vec_par):
    rows = x.shape[0]
    chunk = min(256, rows)
    steps = FF // D
    whole = lambda shape: pl.BlockSpec(shape, lambda t: (0,) * len(shape))
    once = lambda shape: pl.BlockSpec(
        shape, lambda t: (0,) * len(shape), pipeline_mode=pl.Buffered(1)
    )
    hidden = pl.BlockSpec((rows, D), lambda t: (0, t))
    return pl.pallas_call(
        partial(up_kernel, chunk),
        out_shape=[
            jax.ShapeDtypeStruct((rows, FF), bf16),
            jax.ShapeDtypeStruct((rows, FF), bf16),
            jax.ShapeDtypeStruct((rows, D), f32),
            jax.ShapeDtypeStruct((rows, D), bf16),
            jax.ShapeDtypeStruct((rows, D), f32),
            jax.ShapeDtypeStruct((8, D), f32),
        ],
        grid=(steps,),
        in_specs=[
            once((rows, D)),
            once((rows, D)),
            once((rows, D)),
            pl.BlockSpec((None, D, D), lambda t: (3, 0, 0), pipeline_mode=pl.Buffered(1)),
            pl.BlockSpec((None, D, D), lambda t: (0, 0, t)),
            pl.BlockSpec((None, D, D), lambda t: (1, 0, t)),
            pl.BlockSpec((1, D), lambda t: (0, t)),
            whole((6, D)),
        ],
        out_specs=[
            hidden,
            hidden,
            whole((rows, D)),
            whole((rows, D)),
            whole((rows, D)),
            whole((8, D)),
        ],
        scratch_shapes=[pltpu.VMEM((rows, D), bf16), pltpu.VMEM((rows, D), f32)],
        compiler_params=pltpu.CompilerParams(vmem_limit_bytes=VMEM_LIMIT),
        cost_estimate=pl.CostEstimate(
            flops=2 * rows * D * (D + 2 * FF),
            bytes_accessed=rows * D * 30 + 2 * D * FF * 2,
            transcendentals=2 * rows * FF,
        ),
        name="feed_forward",
    )(x, mixed, cot, attn_full, ffn_full, ffn_full, hid_all.reshape(1, FF), vec_par)


def down_kernel(
    chunk,
    gs_ref,
    h1_ref,
    mixed_ref,
    wo_ref,
    w1_ref,
    w2_ref,
    act_ref,
    slope_ref,
    vec_ref,
    dw1_ref,
    dw2_ref,
    dwo_ref,
    gh1_ref,
    gm_ref,
    hid_ref,
    sums_ref,
    turned,
    low_t,
    pre,
    total,
):
    step = pl.program_id(0)
    n_rows = gs_ref.shape[0]
    chunks = n_rows // chunk

    @pl.when(step == 0)
    def _():
        @pl.loop(0, chunks)
        def _(i):
            rows = pl.ds(pl.multiple_of(i * chunk, chunk), chunk)
            unit, _scale = norm_parts(h1_ref[rows, :])
            low = unit * vec_ref[0:1, :] + vec_ref[1:2, :]
            low_t[:, rows] = low.T.astype(bf16)
            turned[:, rows] = gs_ref[rows, :].T.astype(bf16)
            total[rows, :] = gs_ref[rows, :]

    for i in range(chunks):
        rows = slice(i * chunk, (i + 1) * chunk)
        grad_act = matmul(gs_ref[rows, :].astype(bf16), w2_ref[...]).astype(bf16).astype(f32)
        grad_pre = (grad_act * slope_ref[rows, :].astype(f32)).astype(bf16)
        pre[rows, :] = grad_pre
        total[rows, :] += matmul_nt(grad_pre, w1_ref[...])
    hid_ref[...] = column_total(pre[...])
    part = D // 4
    for j in range(4):
        out = slice(j * part, (j + 1) * part)
        dw1_ref[out, :] = matmul(low_t[out, :], pre[...]).astype(bf16)
        dw2_ref[out, :] = matmul(turned[out, :], act_ref[...]).astype(bf16)

    @pl.when(step == pl.num_programs(0) - 1)
    def _():
        sums_ref[...] = jnp.zeros_like(sums_ref)

        @pl.loop(0, chunks)
        def _(i):
            rows = pl.ds(pl.multiple_of(i * chunk, chunk), chunk)
            unit, scale = norm_parts(h1_ref[rows, :])
            grad_first = total[rows, :]
            grad_h1 = norm_back(grad_first, unit, scale, vec_ref[0:1, :])
            gh1_ref[rows, :] = grad_h1
            low = grad_h1.astype(bf16)
            gm_ref[rows, :] = matmul(low, wo_ref[...]).astype(bf16)
            turned[:, rows] = grad_h1.T.astype(bf16)
            sums_ref[0:1, :] += column_total(grad_first * unit)
            sums_ref[1:2, :] += column_total(grad_first)
            sums_ref[2:3, :] += column_total(low)

        @pl.loop(0, 4)
        def _(j):
            out = pl.ds(pl.multiple_of(j * part, part), part)
            dwo_ref[out, :] = matmul(turned[out, :], mixed_ref[...]).astype(bf16)


def feed_back(gs, h1, mixed, attn_full, ffn_full, act, slope, vec_par):
    rows = gs.shape[0]
    chunk = min(256, rows)
    steps = FF // D
    whole = lambda shape: pl.BlockSpec(shape, lambda t: (0,) * len(shape))
    once = lambda shape: pl.BlockSpec(
        shape, lambda t: (0,) * len(shape), pipeline_mode=pl.Buffered(1)
    )
    hidden = pl.BlockSpec((rows, D), lambda t: (0, t))
    slab = pl.BlockSpec((D, D), lambda t: (0, t))
    return pl.pallas_call(
        partial(down_kernel, chunk),
        out_shape=[
            jax.ShapeDtypeStruct((D, FF), bf16),
            jax.ShapeDtypeStruct((D, FF), bf16),
            jax.ShapeDtypeStruct((D, D), bf16),
            jax.ShapeDtypeStruct((rows, D), f32),
            jax.ShapeDtypeStruct((rows, D), bf16),
            jax.ShapeDtypeStruct((1, FF), f32),
            jax.ShapeDtypeStruct((8, D), f32),
        ],
        grid=(steps,),
        in_specs=[
            once((rows, D)),
            once((rows, D)),
            once((rows, D)),
            pl.BlockSpec((None, D, D), lambda t: (3, 0, 0), pipeline_mode=pl.Buffered(1)),
            pl.BlockSpec((None, D, D), lambda t: (0, 0, t)),
            pl.BlockSpec((None, D, D), lambda t: (1, 0, t)),
            hidden,
            hidden,
            whole((6, D)),
        ],
        out_specs=[
            slab,
            slab,
            whole((D, D)),
            whole((rows, D)),
            whole((rows, D)),
            pl.BlockSpec((1, D), lambda t: (0, t)),
            whole((8, D)),
        ],
        scratch_shapes=[
            pltpu.VMEM((D, rows), bf16),
            pltpu.VMEM((D, rows), bf16),
            pltpu.VMEM((rows, D), bf16),
            pltpu.VMEM((rows, D), f32),
        ],
        compiler_params=pltpu.CompilerParams(vmem_limit_bytes=VMEM_LIMIT),
        cost_estimate=pl.CostEstimate(
            flops=2 * rows * D * (2 * D + 4 * FF),
            bytes_accessed=rows * D * 30 + 4 * D * FF * 2,
            transcendentals=0,
        ),
        name="feed_back",
    )(gs, h1, mixed, attn_full, ffn_full, ffn_full, act, slope, vec_par)


WIDE = 1536
STRIP = 96
PIECES = 8
ITEM = 128
LINE_ITEMS = 5
MESH = pl.DeviceIdType.MESH


def remote(src, dst, send, recv, where):
    return pltpu.make_async_remote_copy(
        src_ref=src,
        dst_ref=dst,
        send_sem=send,
        recv_sem=recv,
        device_id=where,
        device_id_type=MESH,
    )


def greet(partners):
    barrier = pltpu.get_barrier_semaphore()
    for where in partners:
        pl.semaphore_signal(barrier, inc=1, device_id=where, device_id_type=MESH)
    pl.semaphore_wait(barrier, len(partners))


def places(n_tensor):
    s, c, t = lax.axis_index("shard"), lax.axis_index("ctx"), lax.axis_index("tensor")
    x, core = s // 2, s % 2
    sibling = (x * 2 + 1 - core, c, t)
    over_x = ((1 - x) * 2 + core, c, t)
    over_y = (s, 1 - c, t)
    across = (x * 2 + 1 - core, 1 - c, t)
    along_z = [(s, c, lax.rem(t + k, n_tensor)) for k in range(1, n_tensor)]
    return s, c, t, x, core, sibling, over_x, over_y, across, along_z


class Line:
    def __init__(self, s, c, t, last, items, rows, array, up, down):
        self.s, self.c, self.t, self.last, self.items = s, c, t, last, items
        self.rows, self.array, self.up, self.down = rows, array, up, down

    def hop(self, i, src_t, sems, n, to):
        ref = self.array.at[src_t, pl.ds(i * self.rows, self.rows)]
        return remote(ref, ref, sems[0].at[n], sems[1].at[n], (self.s, self.c, to))

    def send_own(self, i):
        t = self.t

        @pl.when(t < self.last)
        def _():
            self.hop(i, t, self.up, i, t + 1).start()

        @pl.when(t > 0)
        def _():
            self.hop(i, t, self.down, i, t - 1).start()

    def tick(self, j):
        t, last = self.t, self.last
        i, hops, n = j % self.items, j // self.items + 1, j + self.items

        @pl.when(t >= hops)
        def _():
            self.hop(i, t - hops, self.up, j, t - 1).wait_recv()

            @pl.when(t < last)
            def _():
                self.hop(i, t - hops, self.up, n, t + 1).start()

        @pl.when(t + hops <= last)
        def _():
            self.hop(i, t + hops, self.down, j, t + 1).wait_recv()

            @pl.when(t > 0)
            def _():
                self.hop(i, t + hops, self.down, n, t - 1).start()

    def settle(self, j):
        t, last = self.t, self.last
        i, hops = j % self.items, j // self.items

        @pl.when((t < last) & (t >= hops))
        def _():
            self.hop(i, t - hops, self.up, j, t + 1).wait_send()

        @pl.when((t > 0) & (t + hops <= last))
        def _():
            self.hop(i, t + hops, self.down, j, t - 1).wait_send()


def start_kernel(n_tensor, *refs):
    attn_ref, ffn_ref, qv_ref, hid_ref, tab_ref, rand, tokens = refs[:7]
    attn_out, ffn_out, hid_out, x_out, q_out, k_out, v_out, mixed_out, lse_out = refs[7:16]
    low, low_z, bias, bias_z, bias_qv, ffn_low, full, xs, qs, ms, k_buf, v_buf, s_buf = refs[16:29]
    (
        z_send,
        z_recv,
        b_send,
        b_recv,
        fz_send,
        fz_recv,
        x_send,
        x_recv,
        g_send,
        g_recv,
        p_send,
        p_recv,
        fg_send,
        fg_recv,
        fp_send,
        fp_recv,
        kv_send,
        kv_recv,
        own_sem,
    ) = refs[29:]
    s, c, t, x, core, sibling, over_x, over_y, across, along_z = places(n_tensor)
    own_cols, own_ff = D // n_tensor, FF // n_tensor
    n_rows = xs.shape[0]

    for m in range(4):
        low[:, m * own_cols : (m + 1) * own_cols] = attn_ref[m].astype(bf16)
    for m in range(2):
        ffn_low[m] = ffn_ref[m].astype(bf16)
    bias[0:2, 0:own_cols] = qv_ref[...]
    bias[2:3, 0:own_ff] = hid_ref[...]

    greet([sibling, over_x, over_y, across] + along_z)

    sent = []

    def put(copy):
        copy.start()
        sent.append(copy)

    half = 2 * own_cols

    def z_hop(path, k, u):
        cols = pl.ds(path * half, half)
        n = path * n_tensor
        return remote(
            low.at[:, cols], low_z.at[u, :, cols], z_send.at[n + k], z_recv.at[n + u], along_z[k]
        )

    for path in range(2):
        for k in range(n_tensor - 1):
            put(z_hop(path, k, t))

    def keep_rows(src, dst, n):
        return pltpu.make_async_copy(src.at[t], dst, x_recv.at[n])

    def swap_rows(src, dst, n):
        return remote(src.at[t], dst, x_send.at[n], x_recv.at[n], across)

    @pl.when(core == c)
    def _():
        keep_rows(tokens, xs, 0).start()

    @pl.when(core != c)
    def _():
        swap_rows(tokens, xs, 0).start()

    low_z[t] = low[...]
    bias_z[t] = bias[...]

    def strip(shard, ctx):
        return pl.ds(pl.multiple_of((2 * shard + ctx) * STRIP, STRIP), STRIP)

    here = strip(s, c)

    def lay_out(path):
        for k, where in enumerate(along_z):
            z_hop(path, k, where[2]).wait_recv()
        for n in range(n_tensor):
            for m in range(2 * path, 2 * path + 2):
                piece = low_z[n, :, m * own_cols : (m + 1) * own_cols]
                full[m, here, n * own_cols : (n + 1) * own_cols] = piece

    far_x, far_y = over_x[0], 1 - c
    labels = ["own", "x", "y", "xy"]
    rows = {
        "own": here,
        "x": strip(far_x, c),
        "y": strip(s, far_y),
        "xy": strip(far_x, far_y),
    }
    far_rows = {
        "own": strip(sibling[0], c),
        "x": strip(2 * (1 - x) + 1 - core, c),
        "y": strip(sibling[0], far_y),
        "xy": strip(2 * (1 - x) + 1 - core, far_y),
    }

    def attn_block(path, at):
        return full.at[pl.ds(2 * path, 2), at, :]

    def ffn_block(path, at):
        return ffn_out.at[path, at, :]

    class Gather:
        def __init__(self, block, ways, gs, gr, ps, pr):
            self.block, self.gs, self.gr, self.ps, self.pr = block, gs, gr, ps, pr
            x_first = (("x", over_x), ("y", over_y))
            self.ways = [x_first if way == 0 else x_first[::-1] for way in ways]

        def hop(self, path, name, label, where):
            n = path * 3 + labels.index(label) - 1
            ref = self.block(path, rows[name])
            return remote(ref, ref, self.gs.at[n], self.gr.at[n], where)

        def give(self, path, name, label, where):
            put(self.hop(path, name, label, where))

        def take(self, path, label):
            self.hop(path, label, label, over_x).wait_recv()

        def share(self, path, name):
            put(self.shared(path, name))

        def take_shared(self, path):
            for n, name in enumerate(labels):
                ref = self.block(path, far_rows[name])
                n = path * 4 + n
                remote(ref, ref, self.ps.at[n], self.pr.at[n], sibling).wait_recv()

        def shared(self, path, name):
            n = path * 4 + labels.index(name)
            ref = self.block(path, rows[name])
            return remote(ref, ref, self.ps.at[n], self.pr.at[n], sibling)

        def again(self, path, number):
            near, far = self.ways[path]
            if number == 1:
                sent.append(self.hop(path, near[0], "xy", far[1]))
            sent.append(self.shared(path, {1: near[0], 2: far[0], 3: "xy"}[number]))

        def step(self, path, number):
            near, far = self.ways[path]
            if number == 0:
                self.give(path, "own", near[0], near[1])
                self.give(path, "own", far[0], far[1])
                self.share(path, "own")
            elif number == 1:
                self.take(path, near[0])
                self.give(path, near[0], "xy", far[1])
                self.share(path, near[0])
            elif number == 2:
                self.take(path, far[0])
                self.share(path, far[0])
            else:
                self.take(path, "xy")
                self.share(path, "xy")

    attn = Gather(attn_block, (1, 1), g_send, g_recv, p_send, p_recv)
    ffn = Gather(ffn_block, (0, 1), fg_send, fg_recv, fp_send, fp_recv)

    def ffn_cols(path, u):
        return ffn_out.at[path, here, pl.ds(pl.multiple_of(u * own_ff, own_ff), own_ff)]

    def ffn_hop(path, k, u):
        n = path * n_tensor
        return remote(
            ffn_low.at[path],
            ffn_cols(path, u),
            fz_send.at[n + k],
            fz_recv.at[n + u],
            along_z[k],
        )

    local = []

    def write(src, dst, n):
        copy = pltpu.make_async_copy(src, dst, own_sem.at[n])
        copy.start()
        local.append(copy)

    def ffn_along_z(path):
        for k in range(n_tensor - 1):
            put(ffn_hop(path, k, t))
        write(ffn_low.at[path], ffn_cols(path, t), 5 + path)

    def ffn_ready(path):
        for k, where in enumerate(along_z):
            ffn_hop(path, k, where[2]).wait_recv()
        local[path].wait()
        ffn.step(path, 0)

    lay_out(0)
    attn.step(0, 0)
    lay_out(1)
    attn.step(1, 0)
    ffn_along_z(0)
    ffn_along_z(1)
    for k, where in enumerate(along_z):
        put(remote(bias, bias_z.at[t], b_send.at[k], b_recv.at[t], where))
    attn.step(0, 1)
    attn.step(1, 1)
    ffn_ready(0)
    attn.step(0, 2)
    attn.step(1, 2)
    attn.step(0, 3)
    attn.step(1, 3)
    for k, where in enumerate(along_z):
        u = where[2]
        remote(bias, bias_z.at[u], b_send.at[k], b_recv.at[u], where).wait_recv()
    for n in range(n_tensor):
        cols = slice(n * own_cols, (n + 1) * own_cols)
        bias_qv[0:2, cols] = bias_z[n, 0:2, 0:own_cols]
        hid_out[:, n * own_ff : (n + 1) * own_ff] = bias_z[n, 2:3, 0:own_ff]

    @pl.when(core == c)
    def _():
        keep_rows(tokens, xs, 0).wait()

    @pl.when(core != c)
    def _():
        swap_rows(tokens, xs, 0).wait()

    chunk = 256
    chunks = n_rows // chunk
    per = chunk // BLOCK

    def kv_hop(buf, i, n):
        at, to = pl.ds(i * per, per), pl.ds(n_rows // BLOCK + i * per, per)
        return remote(buf.at[at], buf.at[to], kv_send.at[n], kv_recv.at[n], sibling)

    attn.take_shared(0)
    for i in range(chunks):
        at = pl.ds(i * chunk, chunk)
        k = matmul(xs[at, :], full[1]).astype(bf16)
        k_buf[pl.ds(i * per, per)] = k.reshape(per, BLOCK, D)
        put(kv_hop(k_buf, i, i))
    ffn_ready(1)
    for i in range(chunks):
        at = pl.ds(i * chunk, chunk)
        q = matmul(xs[at, :], full[0]) + bias_qv[0:1, :]
        qs[at, :] = (q.astype(bf16).astype(f32) * 0.125).astype(bf16)
    attn.take_shared(1)
    for i in range(chunks):
        at = pl.ds(i * chunk, chunk)
        v = (matmul(xs[at, :], full[2]) + bias_qv[1:2, :]).astype(bf16)
        v_buf[pl.ds(i * per, per)] = v.reshape(per, BLOCK, D)
        put(kv_hop(v_buf, i, chunks + i))
    ffn.step(0, 1)
    write(xs, x_out, 0)
    write(qs, q_out, 1)
    write(full, attn_out, 2)
    for i in range(chunks):
        kv_hop(k_buf, i, i).wait_recv()
        kv_hop(v_buf, i, chunks + i).wait_recv()
    write(k_buf, k_out, 3)
    write(v_buf, v_out, 4)

    nb = n_rows // BLOCK
    first = core * nb
    stops = {0: [(1, 1)], 1: [(0, 2), (1, 2)], 9: [(0, 3), (1, 3)]}

    @pl.loop(0, nb)
    def _(blk):
        at = pl.ds(pl.multiple_of(blk * BLOCK, BLOCK), BLOCK)
        forward_block(
            qs.at[at],
            ms.at[at],
            lse_out.at[blk],
            k_buf,
            v_buf,
            s_buf,
            tab_ref,
            rand,
            blk * (LISTED - 5),
            blk,
            first,
            0,
        )

        for at_block, moves in stops.items():

            @pl.when(blk == at_block)
            def _():
                mark = len(sent)
                for path, number in moves:
                    ffn.step(path, number)
                del sent[mark:]

    write(ms, mixed_out, 7)
    for path, number in [move for moves in stops.values() for move in moves]:
        ffn.again(path, number)
    ffn.take_shared(0)
    ffn.take_shared(1)

    for copy in sent:
        copy.wait_send()
    for copy in local[2:]:
        copy.wait()


def start(n_tensor, attn_w, ffn_w, qv_bias, hid_bias, table, rand, tokens):
    rows = tokens.shape[1]
    own_ff = FF // n_tensor
    dma = pltpu.SemaphoreType.DMA
    vmem, anywhere = pl.BlockSpec(memory_space=pltpu.VMEM), pl.BlockSpec(memory_space=pl.ANY)
    smem = pl.BlockSpec(memory_space=pltpu.SMEM)
    tall = jax.ShapeDtypeStruct((rows, D), bf16)
    both = jax.ShapeDtypeStruct((2 * rows // BLOCK, BLOCK, D), bf16)
    items = 2 * (rows // 256)
    return pl.pallas_call(
        partial(start_kernel, n_tensor),
        out_shape=[
            jax.ShapeDtypeStruct((4, D, D), bf16),
            jax.ShapeDtypeStruct((2, D, FF), bf16),
            jax.ShapeDtypeStruct((1, FF), f32),
            tall,
            tall,
            both,
            both,
            tall,
            jax.ShapeDtypeStruct((rows // BLOCK, 8, ROWS), f32),
        ],
        in_specs=[vmem] * 5 + [smem, anywhere],
        out_specs=[anywhere, anywhere, vmem] + [anywhere] * 5 + [vmem],
        scratch_shapes=[
            pltpu.VMEM((STRIP, D), bf16),
            pltpu.VMEM((n_tensor, STRIP, D), bf16),
            pltpu.VMEM((8, D), f32),
            pltpu.VMEM((n_tensor, 8, D), f32),
            pltpu.VMEM((8, D), f32),
            pltpu.VMEM((2, STRIP, own_ff), bf16),
            pltpu.VMEM((4, D, D), bf16),
            pltpu.VMEM((rows, D), bf16),
            pltpu.VMEM((rows, D), bf16),
            pltpu.VMEM((rows, D), bf16),
            pltpu.VMEM((2 * rows // BLOCK, BLOCK, D), bf16),
            pltpu.VMEM((2 * rows // BLOCK, BLOCK, D), bf16),
            pltpu.VMEM((2 * rows // KEYS, ROWS, KEYS), f32),
            dma((2 * n_tensor,)),
            dma((2 * n_tensor,)),
            dma((n_tensor,)),
            dma((n_tensor,)),
            dma((2 * n_tensor,)),
            dma((2 * n_tensor,)),
            dma((2,)),
            dma((2,)),
            dma((6,)),
            dma((6,)),
            dma((8,)),
            dma((8,)),
            dma((6,)),
            dma((6,)),
            dma((8,)),
            dma((8,)),
            dma((items,)),
            dma((items,)),
            dma((8,)),
        ],
        compiler_params=pltpu.CompilerParams(
            collective_id=2, has_side_effects=True, vmem_limit_bytes=VMEM_LIMIT
        ),
        cost_estimate=pl.CostEstimate(
            flops=6 * rows * D * D, bytes_accessed=100 * 2**20, transcendentals=0
        ),
        name="start",
    )(attn_w, ffn_w, qv_bias, hid_bias.reshape(1, own_ff), table, rand, tokens)


def middle_kernel(n_tensor, *refs):
    x_ref, mixed_ref, hid_ref, vec_ref, cotangent, attn_full, ffn_full = refs[:7]
    out_a, out_b, dw1, dw2, dwo, gh1, gm, hid_out, sums_out = refs[7:16]
    w, wo, act, slope, h1, total, gs_low, low_t, turned, pre, dw_s, cot, ready, low, down = refs[16:31]
    (
        w_sem,
        c_send,
        c_recv,
        h_send,
        h_recv,
        up_send,
        up_recv,
        dn_send,
        dn_recv,
        dw_sem,
        own_sem,
    ) = refs[31:]
    s, c, t, x, core, sibling, over_x, over_y, across, along_z = places(n_tensor)
    n_rows = x_ref.shape[0]
    chunk = 256
    chunks = n_rows // chunk
    steps = FF // D
    items, all_items = LINE_ITEMS, n_rows // ITEM
    last = n_tensor - 1

    def block(i):
        return pl.ds(pl.multiple_of(i * D, D), D)

    fetch_o = pltpu.make_async_copy(attn_full.at[3], wo, w_sem.at[2 * steps])
    fetch_o.start()

    def fetch(m, i):
        at = w.at[m, :, block(i)]
        return pltpu.make_async_copy(ffn_full.at[m, :, block(i)], at, w_sem.at[m * steps + i])

    for i in range(steps):
        for m in range(2):
            fetch(m, i).start()

    greet([over_y, across] + along_z)

    def keep_cot():
        return pltpu.make_async_copy(cotangent.at[t], cot, c_recv.at[0])

    def swap_cot():
        return remote(cotangent.at[t], cot, c_send.at[0], c_recv.at[0], across)

    def home_ref(i):
        if i < items:
            return out_a.at[t, pl.ds(i * ITEM, ITEM)]
        return out_b.at[pl.ds((i - items) * ITEM, ITEM)]

    def keep_home(i):
        return pltpu.make_async_copy(ready.at[pl.ds(i * ITEM, ITEM)], home_ref(i), h_recv.at[i])

    def send_home(i):
        src = ready.at[pl.ds(i * ITEM, ITEM)]
        return remote(src, home_ref(i), h_send.at[i], h_recv.at[i], across)

    def if_home(at_home, away):
        @pl.when(core == c)
        def _():
            at_home()

        @pl.when(core != c)
        def _():
            away()

    if_home(lambda: keep_cot().start(), lambda: swap_cot().start())

    up, down_line = (up_send, up_recv), (dn_send, dn_recv)
    chain = Line(s, c, t, last, items, ITEM, out_a, up, down_line)

    def own_ready(i):
        if_home(lambda: keep_home(i).wait(), lambda: send_home(i).wait_recv())

    per = chunk // ITEM
    for i in range(chunks):
        rows = slice(i * chunk, (i + 1) * chunk)
        if i == 0:
            fetch_o.wait()
        pre1 = x_ref[rows, :].astype(f32) + matmul_nt(mixed_ref[rows, :], wo[...])
        pre1 = pre1 + vec_ref[4:5, :]
        h1[rows, :] = pre1
        unit, _scale = norm_parts(pre1)
        first = unit * vec_ref[0:1, :] + vec_ref[1:2, :]
        low[...] = first.astype(bf16)
        down[...] = first + vec_ref[5:6, :]

        @pl.loop(0, steps)
        def _(j):
            if i == 0:
                fetch(0, j).wait()
                fetch(1, j).wait()
            else:

                @pl.when(j == steps // 2)
                def _():
                    for n in range((i - 1) * per, min(i * per, items)):
                        own_ready(n)
                        chain.send_own(n)

            hidden = matmul(low[...], w[0, :, block(j)]) + hid_ref[:, block(j)]
            act_now, slope_now = gelu_and_slope(hidden)
            act_now = act_now.astype(bf16)
            act[rows, block(j)] = act_now
            slope[rows, block(j)] = slope_now.astype(bf16)
            down[...] += matmul_nt(act_now, w[1, :, block(j)])

        second = down[...]
        total[rows, :] = second
        unit, _scale = norm_parts(second)
        ready[rows, :] = (unit * vec_ref[2:3, :] + vec_ref[3:4, :]).astype(bf16)
        for n in range(i * chunk // ITEM, (i + 1) * chunk // ITEM):
            if_home(lambda: keep_home(n).start(), lambda: send_home(n).start())
        if i == chunks - 1:
            chain.tick(0)
            chain.tick(1)
            chain.tick(2)

    if_home(lambda: keep_cot().wait(), lambda: swap_cot().wait())
    sums_out[...] = jnp.zeros_like(sums_out)

    @pl.loop(0, chunks)
    def _(i):
        rows = pl.ds(pl.multiple_of(i * chunk, chunk), chunk)
        unit, scale = norm_parts(total[rows, :])
        grad_out = cot[rows, :].astype(f32)
        grad = norm_back(grad_out, unit, scale, vec_ref[2:3, :])
        sums_out[2:3, :] += column_total(grad_out * unit)
        sums_out[3:4, :] += column_total(grad_out)
        total[rows, :] = grad
        grad_low = grad.astype(bf16)
        gs_low[rows, :] = grad_low
        sums_out[5:6, :] += column_total(grad_low)
        turned[:, rows] = grad.T.astype(bf16)
        unit, _scale = norm_parts(h1[rows, :])
        first = unit * vec_ref[0:1, :] + vec_ref[1:2, :]
        low_t[:, rows] = first.T.astype(bf16)

    chain.tick(3)
    chain.tick(4)
    part = D // 4

    def dw_copy(slot, m, j):
        return pltpu.make_async_copy(
            dw_s.at[slot, m], (dw1, dw2)[m].at[:, block(j)], dw_sem.at[2 * slot + m]
        )

    ticks = {0: [5, 6], 1: [7, 8], 2: [9, 10], 3: [11, 12]}

    @pl.loop(0, steps)
    def _(j):
        slot = lax.rem(j, 2)
        for i in range(chunks):
            rows = slice(i * chunk, (i + 1) * chunk)
            grad_act = matmul(gs_low[rows, :], w[1, :, block(j)]).astype(bf16).astype(f32)
            grad_pre = (grad_act * slope[rows, block(j)].astype(f32)).astype(bf16)
            pre[rows, :] = grad_pre
            total[rows, :] += matmul_nt(grad_pre, w[0, :, block(j)])
        hid_out[:, block(j)] = column_total(pre[...])

        @pl.when(j >= 2)
        def _():
            for m in range(2):
                dw_copy(slot, m, j - 2).wait()

        for n in range(4):
            out = slice(n * part, (n + 1) * part)
            dw_s[slot, 0, out, :] = matmul(low_t[out, :], pre[...]).astype(bf16)
            dw_s[slot, 1, out, :] = matmul(turned[out, :], act[:, block(j)]).astype(bf16)
        for m in range(2):
            dw_copy(slot, m, j).start()
        for at, numbers in ticks.items():

            @pl.when(j == at)
            def _():
                for n in numbers:
                    chain.tick(n)

    gm_s = gs_low

    @pl.loop(0, chunks)
    def _(i):
        rows = pl.ds(pl.multiple_of(i * chunk, chunk), chunk)
        unit, scale = norm_parts(h1[rows, :])
        grad_first = total[rows, :]
        grad_h1 = norm_back(grad_first, unit, scale, vec_ref[0:1, :])
        total[rows, :] = grad_h1
        grad_low = grad_h1.astype(bf16)
        gm_s[rows, :] = matmul(grad_low, wo[...]).astype(bf16)
        turned[:, rows] = grad_h1.T.astype(bf16)
        sums_out[0:1, :] += column_total(grad_first * unit)
        sums_out[1:2, :] += column_total(grad_first)
        sums_out[4:5, :] += column_total(grad_low)

    local = [
        pltpu.make_async_copy(total, gh1, own_sem.at[0]),
        pltpu.make_async_copy(gm_s, gm, own_sem.at[1]),
    ]
    for copy in local:
        copy.start()
    for j in range(steps - 2, steps):
        for m in range(2):
            dw_copy(j % 2, m, j).wait()

    @pl.loop(0, 4)
    def _(n):
        out = pl.ds(pl.multiple_of(n * part, part), part)
        dw_s[0, 0, out, :] = matmul(turned[out, :], mixed_ref[...]).astype(bf16)

    local.append(pltpu.make_async_copy(dw_s.at[0, 0], dwo, own_sem.at[2]))
    local[-1].start()
    for j in range(13, items * last):
        chain.tick(j)
    for i in range(items, all_items):
        own_ready(i)
    for i in range(all_items):

        @pl.when(core != c)
        def _():
            send_home(i).wait_send()

    for j in range(items * last):
        chain.settle(j)
    for copy in local:
        copy.wait()


def middle(n_tensor, x, mixed, hid_all, vec_par, cotangent, attn_full, ffn_full):
    rows = x.shape[0]
    steps = FF // D
    items, all_items = LINE_ITEMS, rows // ITEM
    dma = pltpu.SemaphoreType.DMA
    vmem, anywhere = pl.BlockSpec(memory_space=pltpu.VMEM), pl.BlockSpec(memory_space=pl.ANY)
    low, wide = pltpu.VMEM((rows, D), bf16), pltpu.VMEM((rows, D), f32)
    return pl.pallas_call(
        partial(middle_kernel, n_tensor),
        out_shape=[
            jax.ShapeDtypeStruct((n_tensor, items * ITEM, D), bf16),
            jax.ShapeDtypeStruct((rows - items * ITEM, D), bf16),
            jax.ShapeDtypeStruct((D, FF), bf16),
            jax.ShapeDtypeStruct((D, FF), bf16),
            jax.ShapeDtypeStruct((D, D), bf16),
            jax.ShapeDtypeStruct((rows, D), f32),
            jax.ShapeDtypeStruct((rows, D), bf16),
            jax.ShapeDtypeStruct((1, FF), f32),
            jax.ShapeDtypeStruct((8, D), f32),
        ],
        in_specs=[vmem] * 4 + [anywhere] * 3,
        out_specs=[anywhere] * 7 + [vmem] * 2,
        scratch_shapes=[
            pltpu.VMEM((2, D, FF), bf16),
            pltpu.VMEM((D, D), bf16),
            pltpu.VMEM((rows, FF), bf16),
            pltpu.VMEM((rows, FF), bf16),
            wide,
            wide,
            low,
            pltpu.VMEM((D, rows), bf16),
            pltpu.VMEM((D, rows), bf16),
            low,
            pltpu.VMEM((2, 2, D, D), bf16),
            low,
            low,
            pltpu.VMEM((256, D), bf16),
            pltpu.VMEM((256, D), f32),
            dma((2 * steps + 1,)),
            dma((1,)),
            dma((1,)),
            dma((all_items,)),
            dma((all_items,)),
            dma((items * n_tensor,)),
            dma((items * n_tensor,)),
            dma((items * n_tensor,)),
            dma((items * n_tensor,)),
            dma((4,)),
            dma((3,)),
        ],
        compiler_params=pltpu.CompilerParams(
            collective_id=3, has_side_effects=True, vmem_limit_bytes=VMEM_LIMIT
        ),
        cost_estimate=pl.CostEstimate(
            flops=2 * rows * D * (3 * D + 6 * FF),
            bytes_accessed=60 * 2**20,
            transcendentals=2 * rows * FF,
        ),
        name="middle",
    )(x, mixed, hid_all, vec_par, cotangent, attn_full, ffn_full)


def finish_kernel(n_tensor, *refs):
    dq, dk_own, dk_far, dv_own, dv_far, gh1, x_ref, weights = refs[:8]
    dw1, dw2, dwo, vec_sums, hid_sums = refs[8:13]
    attn_out, ffn_out, vec_out, qv_out, hid_out, tokens_out = refs[13:19]
    (
        dk_got,
        dv_got,
        dk,
        dv,
        x_t,
        partial_sum,
        ready,
        dws,
        acc,
        got0,
        got1a,
        got1b,
        got2,
        zf,
        zf_got,
        za,
        za_got,
        run,
        run_got,
        run_z,
        wts,
    ) = refs[19:40]
    (
        e_send,
        e_recv,
        own_sem,
        s0,
        r0,
        s1,
        r1,
        s2,
        r2,
        zf_send,
        zf_recv,
        za_send,
        za_recv,
        sm,
        rm,
        h_send,
        h_recv,
        up_send,
        up_recv,
        dn_send,
        dn_recv,
        w_sem,
    ) = refs[40:]
    s, c, t, x, core, sibling, over_x, over_y, across, along_z = places(n_tensor)
    n_rows = dq.shape[0]
    rows_each = n_rows // PIECES
    last = n_tensor - 1

    def pieces(path, i):
        if i < 2:
            return [(dw1 if path == 0 else dw2, i * WIDE, WIDE, 0)]
        if path == 0:
            return [(dws.at[0], 0, D, 0), (dws.at[1], 0, D, D)]
        return [(dws.at[2], 0, D, 0), (dwo, 0, D, D)]

    def slot(path, i):
        return path * 3 + i

    order = [(path, i) for i in range(3) for path in range(2)]

    def rows_of(xx, cc):
        return pl.ds(pl.multiple_of((4 * xx + 2 * cc) * STRIP, 2 * STRIP), 2 * STRIP)

    own, first = {}, {}
    for path, i in order:
        k = slot(path, i)
        own[k], first[k] = [], []
        for xx in range(2):
            for j, (ref, col, width, at) in enumerate(pieces(path, i)):
                n = (k * 2 + xx) * 2 + j
                cols, to = pl.ds(col, width), pl.ds(at, width)
                own[k].append(
                    pltpu.make_async_copy(
                        ref.at[rows_of(xx, core), cols], acc.at[k, xx, :, to], own_sem.at[n]
                    )
                )
                first[k].append(
                    remote(
                        ref.at[rows_of(xx, 1 - core), cols],
                        got0.at[k, xx, :, to],
                        s0.at[n],
                        r0.at[n],
                        sibling,
                    )
                )

    def start_own(i):
        for path in range(2):
            for copy in own[slot(path, i)]:
                copy.start()

    def start_first(i):
        for path in range(2):
            for copy in first[slot(path, i)]:
                copy.start()

    fetch = pltpu.make_async_copy(weights.at[pl.ds(0, 3)], wts, w_sem.at[0])
    fetch.start()
    start_own(0)
    start_own(1)
    greet([sibling, over_x, over_y, across] + along_z)

    swaps = [
        remote(dk_far, dk_got, e_send.at[0], e_recv.at[0], sibling),
        remote(dv_far, dv_got, e_send.at[1], e_recv.at[1], sibling),
    ]
    for copy in swaps:
        copy.start()
    start_first(0)

    fetch.wait()
    chunk = 256
    for i in range(n_rows // chunk):
        at = slice(i * chunk, (i + 1) * chunk)
        partial_sum[at, :] = gh1[at, :] + matmul_nt(dq[at, :], wts[0])
        x_t[:, at] = x_ref[at, :].T
    run[0] = jnp.zeros(run.shape[1:], f32)
    run[0, 0:6, :] = vec_sums[0:6, :]
    run[0, 6:7, :] = column_total(dq[...])
    for n in range(FF // D):
        run[0, 8 + n : 9 + n, :] = hid_sums[:, n * D : (n + 1) * D]

    for copy in swaps:
        copy.wait_recv()

    def keep_home(i):
        at = pl.ds(i * rows_each, rows_each)
        return pltpu.make_async_copy(ready.at[at], tokens_out.at[t, at], h_recv.at[i])

    def send_home(i):
        at = pl.ds(i * rows_each, rows_each)
        return remote(ready.at[at], tokens_out.at[t, at], h_send.at[i], h_recv.at[i], across)

    for i in range(PIECES):
        at = slice(i * rows_each, (i + 1) * rows_each)
        dk_piece = (dk_own[at, :].astype(f32) + dk_got[at, :].astype(f32)).astype(bf16)
        dv_piece = (dv_own[at, :].astype(f32) + dv_got[at, :].astype(f32)).astype(bf16)
        dk[at, :] = dk_piece
        dv[at, :] = dv_piece
        total = partial_sum[at, :] + matmul_nt(dk_piece, wts[1]) + matmul_nt(dv_piece, wts[2])
        ready[at, :] = total.astype(bf16)

        @pl.when(core == c)
        def _():
            keep_home(i).start()

        @pl.when(core != c)
        def _():
            send_home(i).start()

    chain = Line(
        s, c, t, last, PIECES, rows_each, tokens_out, (up_send, up_recv), (dn_send, dn_recv)
    )
    tick, settle = chain.tick, chain.settle

    def send_own(i):
        @pl.when(core == c)
        def _():
            keep_home(i).wait()

        @pl.when(core != c)
        def _():
            send_home(i).wait_recv()

        chain.send_own(i)

    def add_rows(target, source, count):
        @pl.loop(0, count // 16)
        def _(j):
            rows = pl.ds(pl.multiple_of(j * 16, 16), 16)
            total = target[rows, :].astype(f32) + source[rows, :].astype(f32)
            target[rows, :] = total.astype(bf16)

    def half(cc):
        return pl.ds(pl.multiple_of(cc * STRIP, STRIP), STRIP)

    second, third = {}, {}

    def stage1(path, i):
        k = slot(path, i)
        for copy in own[k]:
            copy.wait()
        for copy in first[k]:
            copy.wait_recv()
        for xx in range(2):
            add_rows(acc.at[k, xx], got0.at[k, xx], 2 * STRIP)
        if path == 0:
            second[k] = remote(acc.at[k, 1 - x], got1a.at[i], s1.at[k], r1.at[k], over_x)
        else:
            second[k] = remote(
                acc.at[k, :, half(1 - c), :], got1b.at[i], s1.at[k], r1.at[k], over_y
            )
        second[k].start()

    def stage2(path, i):
        k = slot(path, i)
        second[k].wait_recv()
        if path == 0:
            add_rows(acc.at[k, x], got1a.at[i], 2 * STRIP)
            third[k] = remote(
                acc.at[k, x, half(1 - c), :], got2.at[k], s2.at[k], r2.at[k], over_y
            )
        else:
            for xx in range(2):
                add_rows(acc.at[k, xx, half(c), :], got1b.at[i, xx], STRIP)
            third[k] = remote(
                acc.at[k, 1 - x, half(c), :], got2.at[k], s2.at[k], r2.at[k], over_x
            )
        third[k].start()

    own_cols = D // n_tensor
    own_ff = FF // n_tensor
    per = WIDE // own_ff

    def stage3(path, i):
        k = slot(path, i)
        third[k].wait_recv()

        @pl.loop(0, STRIP // 16)
        def _(j):
            rows = pl.ds(pl.multiple_of(j * 16, 16), 16)
            here = pl.ds(pl.multiple_of(c * STRIP + j * 16, 16), 16)
            total = acc[k, x, here, :].astype(f32) + got2[k, rows, :].astype(f32)
            if i < 2:
                for n in range(per):
                    piece = total[:, n * own_ff : (n + 1) * own_ff].astype(bf16)
                    zf[per * i + n, rows, path * own_ff : (path + 1) * own_ff] = piece
            else:
                for n in range(n_tensor):
                    for m in range(2):
                        at = m * D + n * own_cols
                        to = (2 * path + m) * own_cols
                        piece = total[:, at : at + own_cols].astype(bf16)
                        za[n, rows, to : to + own_cols] = piece

    z_sent = []

    def z_step(k, buf, got, send, recv):
        @pl.when(t == k)
        def _():
            for d in range(last, k, -1):
                if k > 0:
                    hop(buf, got, send, recv, d, 0, k - 1).wait_recv()
                    add_rows(buf.at[d], got.at[0, d], STRIP)
                hop(buf, got, send, recv, d, 0, k + 1).start()

        @pl.when(t == last - k)
        def _():
            for d in range(0, last - k):
                if k > 0:
                    hop(buf, got, send, recv, d, 1, last - k + 1).wait_recv()
                    add_rows(buf.at[d], got.at[1, d], STRIP)
                hop(buf, got, send, recv, d, 1, last - k - 1).start()

    def hop(buf, got, send, recv, d, way, to):
        n = way * n_tensor + d
        return remote(buf.at[d], got.at[way, d], send.at[n], recv.at[n], (s, c, to))

    def z_collect(buf, got, send, recv, emit):
        @pl.when(t > 0)
        def _():
            hop(buf, got, send, recv, t, 0, t - 1).wait_recv()
            add_rows(buf.at[t], got.at[0, t], STRIP)

        @pl.when(t < last)
        def _():
            hop(buf, got, send, recv, t, 1, t + 1).wait_recv()
            add_rows(buf.at[t], got.at[1, t], STRIP)

        @pl.loop(0, STRIP // 16)
        def _(j):
            rows = pl.ds(pl.multiple_of(j * 16, 16), 16)
            emit(rows, buf[t, rows, :].astype(f32))

    def z_settle(buf, got, send, recv):
        for d in range(n_tensor):

            @pl.when(t < d)
            def _():
                hop(buf, got, send, recv, d, 0, t + 1).wait_send()

            @pl.when(t > d)
            def _():
                hop(buf, got, send, recv, d, 1, t - 1).wait_send()

    ffn_z = (zf, zf_got, zf_send, zf_recv)
    attn_z = (za, za_got, za_send, za_recv)

    small = []

    def small_send(n, where):
        small.append(remote(run.at[n], run_got.at[n], sm.at[n], rm.at[n], where))
        small[n].start()

    def small_add(n):
        small[n].wait_recv()
        run[n + 1] = run[n] + run_got[n]

    dws[0] = matmul(x_t[...], dq[...]).astype(bf16)
    send_own(0)
    send_own(1)
    start_first(1)
    dws[1] = matmul(x_t[...], dk[...]).astype(bf16)
    send_own(2)
    send_own(3)
    dws[2] = matmul(x_t[...], dv[...]).astype(bf16)
    start_own(2)
    start_first(2)
    run[0, 7:8, :] = column_total(dv[...])
    small_send(0, sibling)
    stage1(0, 0)
    stage1(1, 0)
    send_own(4)
    send_own(5)
    stage1(0, 1)
    stage1(1, 1)
    send_own(6)
    send_own(7)
    tick(0)
    stage1(0, 2)
    stage1(1, 2)
    small_add(0)
    small_send(1, over_x)
    tick(1)
    tick(2)
    tick(3)
    stage2(0, 0)
    stage2(1, 0)
    tick(4)
    tick(5)
    small_add(1)
    small_send(2, over_y)
    tick(6)
    stage2(0, 1)
    stage2(1, 1)
    tick(7)
    tick(8)
    small_add(2)
    run_z[t] = run[3]
    for k, where in enumerate(along_z):
        copy = remote(run.at[3], run_z.at[t], sm.at[3 + k], rm.at[3 + t], where)
        copy.start()
        z_sent.append(copy)
    stage3(0, 0)
    stage3(1, 0)
    stage2(0, 2)
    stage2(1, 2)
    tick(9)
    tick(10)
    stage3(0, 1)
    stage3(1, 1)
    z_step(0, *ffn_z)
    tick(11)
    tick(12)
    z_step(1, *ffn_z)
    stage3(0, 2)
    stage3(1, 2)
    z_step(0, *attn_z)
    tick(13)
    tick(14)
    z_step(2, *ffn_z)
    z_step(1, *attn_z)
    tick(15)
    tick(16)
    z_step(2, *attn_z)
    for j in range(17, PIECES * last):
        tick(j)

    for k, where in enumerate(along_z):
        u = where[2]
        remote(run.at[3], run_z.at[u], sm.at[3 + k], rm.at[3 + u], where).wait_recv()
    total = run_z[0]
    for n in range(1, n_tensor):
        total = total + run_z[n]
    vec_out[...] = total[0:6, :]
    for n in range(n_tensor):

        @pl.when(t == n)
        def _():
            qv_out[...] = total[6:8, n * own_cols : (n + 1) * own_cols]
            hid_out[...] = total[8 + n : 9 + n, :]


    def emit_ffn(rows, total):
        for m in range(2):
            ffn_out[m, rows, :] = total[:, m * own_ff : (m + 1) * own_ff]

    def emit_attn(rows, total):
        for m in range(4):
            attn_out[m, rows, :] = total[:, m * own_cols : (m + 1) * own_cols]

    z_collect(*ffn_z, emit_ffn)
    z_collect(*attn_z, emit_attn)
    z_settle(*ffn_z)
    z_settle(*attn_z)

    for copy in swaps:
        copy.wait_send()
    for path, i in order:
        k = slot(path, i)
        for copy in first[k]:
            copy.wait_send()
        second[k].wait_send()
        third[k].wait_send()
    for copy in small + z_sent:
        copy.wait_send()

    @pl.when(core != c)
    def _():
        for i in range(PIECES):
            send_home(i).wait_send()

    for j in range(PIECES * last):
        settle(j)


def finish_all(n_tensor, grads, gh1, x, attn_full, dws, sums):
    rows = x.shape[0]
    own_cols, own_ff = D // n_tensor, FF // n_tensor
    dma = pltpu.SemaphoreType.DMA
    vmem, anywhere = pl.BlockSpec(memory_space=pltpu.VMEM), pl.BlockSpec(memory_space=pl.ANY)
    dq, dk_own, dk_far, dv_own, dv_far = grads
    tall = pltpu.VMEM((rows, D), bf16)
    items = PIECES * (n_tensor - 1)
    return pl.pallas_call(
        partial(finish_kernel, n_tensor),
        out_shape=[
            jax.ShapeDtypeStruct((4, STRIP, own_cols), f32),
            jax.ShapeDtypeStruct((2, STRIP, own_ff), f32),
            jax.ShapeDtypeStruct((6, D), f32),
            jax.ShapeDtypeStruct((2, own_cols), f32),
            jax.ShapeDtypeStruct((1, own_ff), f32),
            jax.ShapeDtypeStruct((n_tensor, rows, D), bf16),
        ],
        in_specs=[vmem, vmem, anywhere, vmem, anywhere, vmem, vmem, anywhere]
        + [anywhere] * 3
        + [vmem] * 2,
        out_specs=[vmem] * 5 + [anywhere],
        scratch_shapes=[
            tall,
            tall,
            tall,
            tall,
            pltpu.VMEM((D, rows), bf16),
            pltpu.VMEM((rows, D), f32),
            tall,
            pltpu.VMEM((3, D, D), bf16),
            pltpu.VMEM((6, 2, 2 * STRIP, WIDE), bf16),
            pltpu.VMEM((6, 2, 2 * STRIP, WIDE), bf16),
            pltpu.VMEM((3, 2 * STRIP, WIDE), bf16),
            pltpu.VMEM((3, 2, STRIP, WIDE), bf16),
            pltpu.VMEM((6, STRIP, WIDE), bf16),
            pltpu.VMEM((n_tensor, STRIP, 2 * own_ff), bf16),
            pltpu.VMEM((2, n_tensor, STRIP, 2 * own_ff), bf16),
            pltpu.VMEM((n_tensor, STRIP, 4 * own_cols), bf16),
            pltpu.VMEM((2, n_tensor, STRIP, 4 * own_cols), bf16),
            pltpu.VMEM((4, 16, D), f32),
            pltpu.VMEM((3, 16, D), f32),
            pltpu.VMEM((n_tensor, 16, D), f32),
            pltpu.VMEM((3, D, D), bf16),
            dma((2,)),
            dma((2,)),
            dma((24,)),
            dma((24,)),
            dma((24,)),
            dma((6,)),
            dma((6,)),
            dma((6,)),
            dma((6,)),
            dma((2 * n_tensor,)),
            dma((2 * n_tensor,)),
            dma((2 * n_tensor,)),
            dma((2 * n_tensor,)),
            dma((3 + n_tensor,)),
            dma((3 + n_tensor,)),
            dma((PIECES,)),
            dma((PIECES,)),
            dma((items + PIECES,)),
            dma((items + PIECES,)),
            dma((items + PIECES,)),
            dma((items + PIECES,)),
            dma((1,)),
        ],
        compiler_params=pltpu.CompilerParams(
            collective_id=1, has_side_effects=True, vmem_limit_bytes=VMEM_LIMIT
        ),
        cost_estimate=pl.CostEstimate(
            flops=12 * rows * D * D, bytes_accessed=400 * 2**20, transcendentals=0
        ),
        name="finish",
    )(dq, dk_own, dk_far, dv_own, dv_far, gh1, x, attn_full, *dws, *sums)


GROUP_RATES = (
    [2.0 / D**0.5] * 3 + [2.0 / (D // (4 * BLOCK)) ** 0.5],
    [2.0 / D**0.5, 2.0 / FF**0.5],
)


def last_kernel(tokens_ref, out_a, out_b, *refs):
    attn_g, attn_w, attn_m, attn_v, ffn_g, ffn_w, ffn_m, ffn_v = refs[:8]
    plain = [refs[8 + 4 * n : 12 + 4 * n] for n in range(3)]
    tokens_out, output = refs[20:22]
    attn_moment, attn_square, out_states, attn_new, attn_copy = refs[22:27]
    ffn_moment, ffn_square, ffn_new, ffn_copy = refs[27:31]
    plain_out = [refs[31 + 3 * n : 34 + 3 * n] for n in range(3)]
    step = pl.program_id(0)
    rows_a = out_a.shape[1]

    @pl.when(step == 0)
    def _():
        for m in range(4):
            moment, square, new = adam_update(
                attn_w[m], attn_m[m], attn_v[m], attn_g[m], GROUP_RATES[0][m], decay_rate
            )
            if m < 3:
                attn_moment[m], attn_square[m] = moment, square
            else:
                out_states[0], out_states[1] = moment, square
            attn_new[m], attn_copy[m] = new, new.astype(bf16)
        for m in range(2):
            moment, square, new = adam_update(
                ffn_w[m], ffn_m[m], ffn_v[m], ffn_g[m], GROUP_RATES[1][m], decay_rate
            )
            ffn_moment[m], ffn_square[m] = moment, square
            ffn_new[m], ffn_copy[m] = new, new.astype(bf16)
        for (g, w, m, v), outs in zip(plain, plain_out):
            for ref, value in zip(outs, adam_update(w[...], m[...], v[...], g[...], 0.5, 0.0)):
                ref[...] = value

    tokens_out[...] = tokens_ref[...].astype(f32)

    @pl.when(step % 2 == 0)
    def _():
        output[:, :rows_a] = out_a[...]

    @pl.when(step % 2 == 1)
    def _():
        output[:, rows_a:] = out_b[...]


def last(tokens_low, out_a, out_b, attn, ffn, plain):
    count, rows, _ = tokens_low.shape
    tile = lambda size, index: pl.BlockSpec((1, size, D), index)
    whole = lambda shape: pl.BlockSpec(
        shape, lambda i: (0,) * len(shape), pipeline_mode=pl.Buffered(1)
    )
    a, f = attn[0].shape, ffn[0].shape
    shapes = [
        ((3,) + a[1:], f32),
        ((3,) + a[1:], f32),
        ((2,) + a[1:], f32),
        (a, f32),
        (a, bf16),
        (f, f32),
        (f, f32),
        (f, f32),
        (f, bf16),
    ]
    for group in plain:
        shapes += [(group[0].shape, f32)] * 3
    inputs = list(attn) + list(ffn) + [array for group in plain for array in group]
    by_half = lambda i: (i // 2, i % 2, 0)
    by_one = lambda i: (i // 2, 0, 0)
    return pl.pallas_call(
        last_kernel,
        out_shape=[
            jax.ShapeDtypeStruct(tokens_low.shape, f32),
            jax.ShapeDtypeStruct(tokens_low.shape, bf16),
        ]
        + [jax.ShapeDtypeStruct(*entry) for entry in shapes],
        grid=(count * 2,),
        in_specs=[
            tile(rows // 2, by_half),
            tile(out_a.shape[1], by_one),
            tile(out_b.shape[1], by_one),
        ]
        + [whole(array.shape) for array in inputs],
        out_specs=[tile(rows // 2, by_half), tile(rows, by_one)]
        + [whole(shape) for shape, _ in shapes],
        compiler_params=pltpu.CompilerParams(vmem_limit_bytes=VMEM_LIMIT),
        name="last",
    )(tokens_low, out_a, out_b, *inputs)


def make_body(mesh):
    n_shard, n_ctx, n_tensor = mesh.shape["shard"], mesh.shape["ctx"], mesh.shape["tensor"]
    rows_axes = ("shard", "ctx")
    all_axes = ("shard", "ctx", "tensor")
    paired = n_ctx == 2 and n_shard == 4 and n_tensor == 4

    def swapped(s, c):
        return (s - s % 2 + c, s % 2)

    def swap(array):
        if not paired:
            return array
        pairs = []
        for s in range(n_shard):
            for c in range(n_ctx):
                s_to, c_to = swapped(s, c)
                pairs.append((s * n_ctx + c, s_to * n_ctx + c_to))
        return lax.ppermute(array, rows_axes, pairs)

    def spread(array):
        return lax.all_gather(swap(array), "tensor", axis=0, tiled=True)

    def body(
        tokens,
        cotangent,
        segments,
        rand_blocks,
        attn_w,
        attn_m,
        attn_v,
        ffn_w,
        ffn_m,
        ffn_v,
        qv_bias,
        qv_m,
        qv_v,
        hid_bias,
        hid_m,
        hid_v,
        vec_par,
        vec_m,
        vec_v,
    ):
        t_index = lax.axis_index("tensor")
        nseq = tokens.shape[0] // n_tensor
        piece_len = tokens.shape[1]
        nb = piece_len // BLOCK
        own_rows, own_cols = attn_w.shape[1], attn_w.shape[2]
        own_ff = ffn_w.shape[2]

        def mine(array):
            return lax.dynamic_slice_in_dim(array, t_index * nseq, nseq, 0)

        ints = jnp.concatenate(
            [mine(segments), mine(rand_blocks).reshape(nseq, -1)], axis=1
        )
        ints = swap(ints)
        length = segments.shape[1]
        segs, rand = ints[:, :length], ints[:, length:].reshape(nseq, length // BLOCK, -1)
        piece = lax.axis_index("shard") % 2 if paired else lax.axis_index("ctx")
        tables = attention_tables(segs, rand, piece, nb, paired)

        if paired:
            rand_own, _meta, table = tables
            attn_full, ffn_full, hid_all, x, queries, keys, values, mixed, lse = start(
                n_tensor, attn_w, ffn_w, qv_bias, hid_bias, table[0], rand_own, tokens
            )
            flat = x
            x, queries = x[None], queries[None]
            keys, values = keys.reshape(1, length, D), values.reshape(1, length, D)
            pieces = [piece_len, piece_len]
        else:
            x, cot = mine(tokens), mine(cotangent)
            pieces = [length]
            ffn_z = lax.all_gather(ffn_w.astype(bf16), "tensor", axis=0, tiled=False)
            ffn_z = ffn_z.transpose(1, 2, 0, 3).reshape(2, own_rows, FF)
            ffn_full = lax.all_gather(ffn_z, rows_axes, axis=1, tiled=True)
            flat = x.reshape(-1, D)
            attn_low = attn_w.astype(bf16)
            attn_low = jnp.concatenate([attn_low[i] for i in range(4)], axis=1)
            attn_z = lax.all_gather(attn_low, "tensor", axis=0, tiled=False)
            attn_z = attn_z.reshape(n_tensor, own_rows, 4, own_cols).transpose(2, 1, 0, 3)
            attn_full = lax.all_gather(
                attn_z.reshape(4, own_rows, D), rows_axes, axis=1, tiled=True
            )
            bias_own = jnp.concatenate([qv_bias.reshape(-1), hid_bias])
            bias_all = lax.all_gather(bias_own, "tensor", axis=0, tiled=False)
            qv_all = bias_all[:, : 2 * own_cols].reshape(n_tensor, 2, own_cols)
            qv_all = qv_all.transpose(1, 0, 2).reshape(2, D)
            hid_all = bias_all[:, 2 * own_cols :].reshape(FF)
            keys = matmul(flat, attn_full[1]).astype(bf16).reshape(x.shape)
            values = (matmul(flat, attn_full[2]) + qv_all[1]).astype(bf16).reshape(x.shape)
            keys = lax.all_gather(keys, "ctx", axis=1, tiled=True)
            values = lax.all_gather(values, "ctx", axis=1, tiled=True)
            queries = (matmul(flat, attn_full[0]) + qv_all[0]).astype(bf16) * 0.125
            queries = queries.reshape(x.shape)
            mixed, lse = attend(tables, queries, keys, values)
        mixed_low = mixed.reshape(-1, D)
        if paired:
            out_a, out_b, dw1, dw2, dwo, grad_first_in, grad_mixed, hid_sum, vec_sums = middle(
                n_tensor, flat, mixed_low, hid_all, vec_par, cotangent, attn_full, ffn_full
            )
            out_b = lax.all_gather(out_b, "tensor", axis=0, tiled=False)
        else:
            act, slope, h1, result, grad_second, second_sums = feed_forward(
                flat, mixed_low, cot.reshape(-1, D), attn_full, ffn_full, hid_all, vec_par
            )
            output = spread(result.reshape(x.shape))
            dw1, dw2, dwo, grad_first_in, grad_mixed, hid_sum, first_sums = feed_back(
                grad_second, h1, mixed_low, attn_full, ffn_full, act, slope, vec_par
            )

        grad_mixed = grad_mixed.reshape(x.shape)
        grad_query, dk_parts, dv_parts = attend_back(
            tables,
            queries,
            grad_mixed,
            mixed.reshape(x.shape),
            lse.reshape(nseq, nb, 8, ROWS),
            keys,
            values,
            pieces,
        )

        grad_query_low = grad_query.reshape(-1, D)
        if paired:
            attn_grad, ffn_grad, vec_grad, qv_grad, hid_grad, grad_tokens = finish_all(
                n_tensor,
                [grad_query_low] + [part[0] for part in list(dk_parts) + list(dv_parts)],
                grad_first_in,
                flat,
                attn_full,
                (dw1, dw2, dwo),
                (vec_sums, hid_sum),
            )
        else:
            grad_keys = lax.psum_scatter(dk_parts[0], "ctx", scatter_dimension=1, tiled=True)
            grad_values = lax.psum_scatter(dv_parts[0], "ctx", scatter_dimension=1, tiled=True)
            grad_keys_low = grad_keys.reshape(-1, D)
            grad_values_low = grad_values.reshape(-1, D)
            into_tokens = (
                matmul_nt(grad_query_low, attn_full[0])
                + matmul_nt(grad_keys_low, attn_full[1])
                + matmul_nt(grad_values_low, attn_full[2])
            )
            grad_tokens = spread((grad_first_in + into_tokens).astype(bf16).reshape(x.shape))
            dwq = matmul_tn(flat, grad_query_low).astype(bf16)
            dwk = matmul_tn(flat, grad_keys_low).astype(bf16)
            dwv = matmul_tn(flat, grad_values_low).astype(bf16)
            small = jnp.concatenate(
                [
                    first_sums[0],
                    first_sums[1],
                    second_sums[0],
                    second_sums[1],
                    first_sums[2],
                    second_sums[2],
                    column_sum(grad_query_low),
                    column_sum(grad_values_low),
                    hid_sum[0],
                ]
            )
            ffn_grad = lax.psum_scatter(
                jnp.stack([dw1, dw2]), rows_axes, scatter_dimension=1, tiled=True
            )
            ffn_grad = ffn_grad.reshape(2, own_rows, n_tensor, own_ff).transpose(2, 0, 1, 3)
            ffn_grad = lax.psum_scatter(ffn_grad, "tensor", scatter_dimension=0, tiled=False)
            ffn_grad = ffn_grad.astype(f32)
            attn_grad = lax.psum_scatter(
                jnp.stack([dwq, dwk, dwv, dwo]), rows_axes, scatter_dimension=1, tiled=True
            )
            attn_grad = attn_grad.reshape(4, own_rows, n_tensor, own_cols).transpose(2, 1, 0, 3)
            attn_grad = lax.psum_scatter(
                attn_grad.reshape(n_tensor, own_rows, D), "tensor", scatter_dimension=0
            )
            attn_grad = attn_grad.reshape(own_rows, 4, own_cols).transpose(1, 0, 2).astype(f32)
            small = lax.psum(small, all_axes)
            vec_grad = small[: 6 * D].reshape(6, D)
            qv_grad = lax.dynamic_slice_in_dim(
                small[6 * D : 8 * D].reshape(2, D), t_index * own_cols, own_cols, 1
            )
            hid_grad = lax.dynamic_slice_in_dim(
                small[8 * D : 8 * D + FF], t_index * own_ff, own_ff, 0
            )
            out_a, out_b = output[:, : piece_len // 2], output[:, piece_len // 2 :]

        row = lambda array: array.reshape(1, own_ff)
        grad_tokens, output, *updated = last(
            grad_tokens,
            out_a,
            out_b,
            (attn_grad, attn_w, attn_m, attn_v),
            (ffn_grad, ffn_w, ffn_m, ffn_v),
            [
                (qv_grad, qv_bias, qv_m, qv_v),
                (row(hid_grad), row(hid_bias), row(hid_m), row(hid_v)),
                (vec_grad, vec_par, vec_m, vec_v),
            ],
        )
        updated[12:15] = [array.reshape(own_ff) for array in updated[12:15]]
        return (output, grad_tokens, *updated)

    return body


def solution(mesh):
    rows = P("shard", "ctx", None)
    weight = P(None, ("shard", "ctx"), "tensor")
    in_specs = (
        (rows, rows, P("shard", None), P("shard", None, None))
        + (weight,) * 6
        + (P(None, "tensor"),) * 3
        + (P("tensor"),) * 3
        + (P(),) * 3
    )
    out_specs = (
        (rows, rows)
        + (weight,) * 9
        + (P(None, "tensor"),) * 3
        + (P("tensor"),) * 3
        + (P(),) * 3
    )
    return jax.shard_map(
        make_body(mesh), mesh=mesh, in_specs=in_specs, out_specs=out_specs, check_vma=False
    )
```

```python
from functools import partial

import jax
import jax.numpy as jnp
from jax import lax
from jax.experimental import pallas as pl
from jax.experimental.pallas import tpu as pltpu
from jax.sharding import PartitionSpec as P

D = 768
HEAD_DIM = 64
FF = 3072
BLOCK = 64
STEP = 5
GROUP = 4 * HEAD_DIM
GROUPS = D // GROUP
ROWS = 4 * BLOCK
LISTED = 8
KEYS = LISTED * BLOCK
VMEM_LIMIT = 60 * 2**20

beta_first = 0.9
beta_second = 0.999
adam_eps = 1e-08
decay_rate = 0.01
norm_eps = 1e-06
neg_large = -1e30

f32 = jnp.float32
bf16 = jnp.bfloat16


def matmul(left, right):
    return jnp.dot(left, right, preferred_element_type=f32)


def matmul_tn(left, right):
    return lax.dot_general(left, right, (((0,), (0,)), ((), ())), preferred_element_type=f32)


def matmul_nt(left, right):
    return lax.dot_general(left, right, (((1,), (1,)), ((), ())), preferred_element_type=f32)


def column_sum(array_in):
    return jnp.sum(array_in.astype(f32), axis=0)


def adam_update(weight, moment, square, gradient, step_rates, decay_on):
    moment_new = beta_first * moment + (1.0 - beta_first) * gradient
    square_new = beta_second * square + (1.0 - beta_second) * gradient * gradient
    step_ratio = (
        moment_new
        / (1.0 - beta_first**STEP)
        / (jnp.sqrt(square_new / (1.0 - beta_second**STEP)) + adam_eps)
    )
    weight_new = weight - step_rates * (step_ratio + decay_on * weight)
    return (moment_new, square_new, weight_new)


def same_head():
    row_head = lax.broadcasted_iota(jnp.int32, (ROWS, GROUP), 0) // BLOCK
    col_head = lax.broadcasted_iota(jnp.int32, (ROWS, GROUP), 1) // HEAD_DIM
    return row_head == col_head


def spread_heads(block, keep):
    stacked = jnp.concatenate([block] * 4, axis=0)
    return jnp.where(keep, stacked, jnp.zeros_like(stacked))


def fold_heads(full, keep):
    kept = jnp.where(keep, full, 0.0)
    return sum(kept[h * BLOCK : (h + 1) * BLOCK] for h in range(4))


def load_keys(k_all, v_all, seq, k_buf, v_buf, sems):
    return [
        pltpu.make_async_copy(k_all.at[seq], k_buf, sems.at[0]),
        pltpu.make_async_copy(v_all.at[seq], v_buf, sems.at[1]),
    ]


def picked_rows(buf, spots, cols):
    return jnp.concatenate([buf[at, :, cols] for at in spots], axis=0)


def chunk_rows(buf, i, cols):
    blocks = buf[pl.ds(i * LISTED, LISTED), :, cols]
    return blocks.reshape(KEYS, GROUP)


def listed_blocks(rand, base, blk, first, own, total):
    one = lambda condition: condition.astype(jnp.int32)
    me = first + blk
    ids = [me - 1, me, me + 1, me * 0, me * 0 + 1] + [rand[base + n] for n in range(LISTED - 5)]
    spots, unused, common = [], [], []
    for n, block in enumerate(ids):
        out = one(block < 0) + one(block >= total)
        for earlier in ids[:n]:
            out = out + one(block == earlier)
        out = lax.min(out, jnp.int32(1))
        at = lax.max(jnp.int32(0), lax.min(block, jnp.int32(total - 1))) - first + own
        spots.append(at + total * one(at < 0))
        unused.append(out)
        common.append(one(block < 2) * (1 - out))
    return spots, unused, common


def code_rows(tab_ref, spots, unused, common):
    low_half = lax.broadcasted_iota(jnp.int32, (1, 2 * BLOCK), 1) < BLOCK

    def one(n):
        plain = (1 - unused[n] - common[n]).astype(f32)
        return tab_ref[spots[n]] * plain - (unused[n] + 2 * common[n]).astype(f32)

    return [jnp.where(low_half, one(n), one(n + 1)) for n in range(0, LISTED, 2)]


def column_of(row):
    return jnp.broadcast_to(row, (2 * BLOCK, 2 * BLOCK)).T


def mask_bias(document, code):
    return jnp.where((document == code) | (code == -2.0), 0.0, neg_large)


def row_of(column):
    return jnp.broadcast_to(column, (ROWS, 2 * BLOCK)).T[0:1, :]


def forward_block(q_ref, out_ref, lse_ref, k_buf, v_buf, s_buf, tab_ref, rand, base, blk, first, own):
    keep = same_head()
    total_blocks = k_buf.shape[0]
    chunks = total_blocks // LISTED
    is_global = first + blk < 2

    @pl.when(jnp.logical_not(is_global))
    def _():
        spots, unused, common = listed_blocks(rand, base, blk, first, own, total_blocks)
        mine = column_of(tab_ref[own + blk])[:BLOCK]
        mine = jnp.concatenate([mine] * 4, axis=0)
        codes = code_rows(tab_ref, spots, unused, common)
        bias = jnp.concatenate([mask_bias(mine, code) for code in codes], axis=1)
        for g in range(GROUPS):
            cols = slice(g * GROUP, (g + 1) * GROUP)
            q_full = spread_heads(q_ref[:, cols], keep)
            scores = matmul_nt(q_full, picked_rows(k_buf, spots, cols)) + bias
            largest = jnp.max(scores, axis=-1, keepdims=True)
            weights = jnp.exp(scores - largest)
            total = jnp.sum(weights, axis=-1, keepdims=True)
            full = matmul(weights.astype(bf16), picked_rows(v_buf, spots, cols))
            out_ref[:, cols] = fold_heads(full * (1.0 / total), keep).astype(bf16)
            lse_ref[g : g + 1, :] = row_of(largest + jnp.log(total))

    @pl.when(is_global)
    def _():
        for g in range(GROUPS):
            cols = slice(g * GROUP, (g + 1) * GROUP)
            q_full = spread_heads(q_ref[:, cols], keep)

            def score_chunk(i, largest):
                scores = matmul_nt(q_full, chunk_rows(k_buf, i, cols))
                s_buf[i] = scores
                return jnp.maximum(largest, jnp.max(scores, axis=-1, keepdims=True))

            largest = lax.fori_loop(0, chunks, score_chunk, jnp.full((ROWS, 1), neg_large, f32))

            def mix_chunk(i, carry):
                total, full = carry
                weights = jnp.exp(s_buf[i] - largest)
                total = total + jnp.sum(weights, axis=-1, keepdims=True)
                return total, full + matmul(weights.astype(bf16), chunk_rows(v_buf, i, cols))

            total, full = lax.fori_loop(
                0, chunks, mix_chunk, (jnp.zeros((ROWS, 1), f32), jnp.zeros((ROWS, GROUP), f32))
            )
            out_ref[:, cols] = fold_heads(full * (1.0 / total), keep).astype(bf16)
            lse_ref[g : g + 1, :] = row_of(largest + jnp.log(total))


def forward_kernel(
    rand, meta, q_ref, tab_ref, k_all, v_all, out_ref, lse_ref, k_buf, v_buf, s_buf, sems
):
    seq, blk = pl.program_id(0), pl.program_id(1)
    nb = pl.num_programs(1)

    @pl.when(blk == 0)
    def _():
        copies = load_keys(k_all, v_all, seq, k_buf, v_buf, sems)
        for c in copies:
            c.start()
        for c in copies:
            c.wait()

    base = (seq * nb + blk) * (LISTED - 5)
    forward_block(
        q_ref, out_ref, lse_ref, k_buf, v_buf, s_buf, tab_ref, rand, base, blk, meta[0], meta[1]
    )


def back_tile(k_rows, v_rows, q_full, go_full, bias, lse, centre):
    scores = matmul_nt(k_rows, q_full)
    if bias is not None:
        scores = scores + bias
    probs = jnp.exp(scores - lse)
    grad_probs = matmul_nt(v_rows, go_full)
    grad_scores = (probs * (grad_probs - centre)).astype(bf16)
    dv_rows = matmul(probs.astype(bf16), go_full)
    dk_rows = matmul(grad_scores, q_full)
    return matmul_tn(grad_scores, k_rows), dk_rows, dv_rows


def backward_kernel(
    n_out, rand, meta, q_ref, go_ref, mixed_ref, lse_ref, tab_ref, k_all, v_all, dq_ref, *rest
):
    dk_refs, dv_refs = rest[:n_out], rest[n_out : 2 * n_out]
    k_buf, v_buf, dk_acc, dv_acc, sems = rest[2 * n_out :]
    seq, blk = pl.program_id(0), pl.program_id(1)
    nb = pl.num_programs(1)
    total_blocks = k_buf.shape[0]
    chunks = total_blocks // LISTED

    @pl.when(blk == 0)
    def _():
        copies = load_keys(k_all, v_all, seq, k_buf, v_buf, sems)
        for c in copies:
            c.start()
        dk_acc[...] = jnp.zeros_like(dk_acc)
        dv_acc[...] = jnp.zeros_like(dv_acc)
        for c in copies:
            c.wait()

    keep = same_head()
    is_global = meta[0] + blk < 2
    base = (seq * nb + blk) * (LISTED - 5)

    def operands(g):
        cols = slice(g * GROUP, (g + 1) * GROUP)
        q_full = spread_heads(q_ref[:, cols], keep)
        go_full = spread_heads(go_ref[:, cols], keep)
        mixed = jnp.concatenate([mixed_ref[:, cols]] * 4, axis=0)
        product = go_full.astype(f32) * mixed.astype(f32)
        centre = row_of(jnp.sum(product, axis=-1, keepdims=True))
        return cols, q_full, go_full, lse_ref[g : g + 1, :], centre

    @pl.when(jnp.logical_not(is_global))
    def _():
        spots, unused, common = listed_blocks(rand, base, blk, meta[0], meta[1], total_blocks)
        stores = [at + (total_blocks - at) * out for at, out in zip(spots, unused)]
        own = tab_ref[meta[1] + blk]
        codes = code_rows(tab_ref, spots, unused, common)
        bias = jnp.concatenate([mask_bias(own, column_of(code)) for code in codes], axis=0)
        bias = jnp.concatenate([bias, bias], axis=1)
        for g in range(GROUPS):
            cols, q_full, go_full, lse, centre = operands(g)
            k_rows, v_rows = picked_rows(k_buf, spots, cols), picked_rows(v_buf, spots, cols)
            dq_full, dk_rows, dv_rows = back_tile(
                k_rows, v_rows, q_full, go_full, bias, lse, centre
            )
            dq_ref[:, cols] = (fold_heads(dq_full, keep) * 0.125).astype(bf16)
            places = [pl.ds(pl.multiple_of(at * BLOCK, BLOCK), BLOCK) for at in stores]
            dk_old = [dk_acc[at, cols] for at in places]
            dv_old = [dv_acc[at, cols] for at in places]
            for n, at in enumerate(places):
                own_rows = slice(n * BLOCK, (n + 1) * BLOCK)
                dk_acc[at, cols] = dk_old[n] + dk_rows[own_rows]
                dv_acc[at, cols] = dv_old[n] + dv_rows[own_rows]

    @pl.when(is_global)
    def _():
        for g in range(GROUPS):
            cols, q_full, go_full, lse, centre = operands(g)

            def chunk_back(i, dq_full):
                rows = pl.ds(pl.multiple_of(i * KEYS, KEYS), KEYS)
                dq_now, dk_rows, dv_rows = back_tile(
                    chunk_rows(k_buf, i, cols),
                    chunk_rows(v_buf, i, cols),
                    q_full,
                    go_full,
                    None,
                    lse,
                    centre,
                )
                dk_acc[rows, cols] += dk_rows
                dv_acc[rows, cols] += dv_rows
                return dq_full + dq_now

            dq_full = lax.fori_loop(0, chunks, chunk_back, jnp.zeros((ROWS, GROUP), f32))
            dq_ref[:, cols] = (fold_heads(dq_full, keep) * 0.125).astype(bf16)

    @pl.when(blk == nb - 1)
    def _():
        row = 0
        for dk_ref, dv_ref in zip(dk_refs, dv_refs):
            rows = dk_ref.shape[0]
            dk_ref[...] = dk_acc[row : row + rows].astype(bf16)
            dv_ref[...] = dv_acc[row : row + rows].astype(bf16)
            row += rows


def attention_tables(segments, random, piece, nb, own_first):
    seq_count, length = segments.shape
    total = length // BLOCK
    first = piece * nb
    rand = lax.dynamic_slice_in_dim(random, first, nb, 1).reshape(-1)
    table = segments.reshape(seq_count, total, BLOCK).astype(f32)
    table = jnp.concatenate([table, table], axis=2)[:, :, None, :]
    if own_first:
        table = lax.dynamic_slice_in_dim(jnp.concatenate([table, table], axis=1), first, total, 1)
    meta = jnp.stack([first, jnp.zeros_like(first) if own_first else first]).astype(jnp.int32)
    return rand, meta, table


def as_blocks(rows):
    return rows.reshape(rows.shape[0], -1, BLOCK, D)


def attend(tables, q, keys, values):
    rand, meta, table = tables
    seq_count, piece_len, _ = q.shape
    nb = piece_len // BLOCK
    length = keys.shape[1]
    any_spec = pl.BlockSpec(memory_space=pl.ANY)
    row_spec = pl.BlockSpec((None, BLOCK, D), lambda s, b, *_: (s, b, 0))
    return pl.pallas_call(
        forward_kernel,
        out_shape=[
            jax.ShapeDtypeStruct(q.shape, bf16),
            jax.ShapeDtypeStruct((seq_count, nb, 8, ROWS), f32),
        ],
        grid_spec=pltpu.PrefetchScalarGridSpec(
            num_scalar_prefetch=2,
            grid=(seq_count, nb),
            in_specs=[
                row_spec,
                pl.BlockSpec((None,) + table.shape[1:], lambda s, b, *_: (s, 0, 0, 0)),
                any_spec,
                any_spec,
            ],
            out_specs=[
                row_spec,
                pl.BlockSpec((None, None, 8, ROWS), lambda s, b, *_: (s, b, 0, 0)),
            ],
            scratch_shapes=[
                pltpu.VMEM((length // BLOCK, BLOCK, D), bf16),
                pltpu.VMEM((length // BLOCK, BLOCK, D), bf16),
                pltpu.VMEM((length // KEYS, ROWS, KEYS), f32),
                pltpu.SemaphoreType.DMA((2,)),
            ],
        ),
        compiler_params=pltpu.CompilerParams(vmem_limit_bytes=VMEM_LIMIT),
        name="attend",
    )(rand, meta, q, table, as_blocks(keys), as_blocks(values))


def attend_back(tables, q, grad_mixed, mixed, lse, keys, values, pieces):
    rand, meta, table = tables
    seq_count, piece_len, _ = q.shape
    nb = piece_len // BLOCK
    length = keys.shape[1]
    any_spec = pl.BlockSpec(memory_space=pl.ANY)
    row_spec = pl.BlockSpec((None, BLOCK, D), lambda s, b, *_: (s, b, 0))
    part_specs = [pl.BlockSpec((None, rows, D), lambda s, b, *_: (s, 0, 0)) for rows in pieces]
    part_shapes = [jax.ShapeDtypeStruct((seq_count, rows, D), bf16) for rows in pieces]
    out = pl.pallas_call(
        partial(backward_kernel, len(pieces)),
        out_shape=[jax.ShapeDtypeStruct(q.shape, bf16)] + part_shapes * 2,
        grid_spec=pltpu.PrefetchScalarGridSpec(
            num_scalar_prefetch=2,
            grid=(seq_count, nb),
            in_specs=[
                row_spec,
                row_spec,
                row_spec,
                pl.BlockSpec((None, None, 8, ROWS), lambda s, b, *_: (s, b, 0, 0)),
                pl.BlockSpec((None,) + table.shape[1:], lambda s, b, *_: (s, 0, 0, 0)),
                any_spec,
                any_spec,
            ],
            out_specs=[row_spec] + part_specs * 2,
            scratch_shapes=[
                pltpu.VMEM((length // BLOCK, BLOCK, D), bf16),
                pltpu.VMEM((length // BLOCK, BLOCK, D), bf16),
                pltpu.VMEM((length + BLOCK, D), f32),
                pltpu.VMEM((length + BLOCK, D), f32),
                pltpu.SemaphoreType.DMA((2,)),
            ],
        ),
        compiler_params=pltpu.CompilerParams(vmem_limit_bytes=VMEM_LIMIT),
        cost_estimate=pl.CostEstimate(
            flops=seq_count * nb * GROUPS * 10 * ROWS * KEYS * GROUP,
            bytes_accessed=seq_count * (3 * piece_len + 4 * length) * D * 2,
            transcendentals=seq_count * nb * GROUPS * ROWS * KEYS,
        ),
        name="attend_back",
    )(rand, meta, q, grad_mixed, mixed, lse, table, as_blocks(keys), as_blocks(values))
    return out[0], out[1 : 1 + len(pieces)], out[1 + len(pieces) :]


def norm_parts(hidden):
    centred = hidden - jnp.mean(hidden, axis=-1, keepdims=True)
    scale = lax.rsqrt(jnp.mean(centred * centred, axis=-1, keepdims=True) + norm_eps)
    return centred * scale, scale


def norm_back(grad, unit, scale, gain):
    inner = grad * gain
    return scale * (
        inner
        - jnp.mean(inner, axis=-1, keepdims=True)
        - unit * jnp.mean(inner * unit, axis=-1, keepdims=True)
    )


def gelu_and_slope(pre):
    bell = jnp.exp(-0.5 * pre * pre)
    t = 1.0 / (1.0 + (0.3275911 * 0.5**0.5) * jnp.abs(pre))
    poly = 0.5 * 1.061405429
    for coefficient in (-1.453152027, 1.421413741, -0.284496736, 0.254829592):
        poly = poly * t + 0.5 * coefficient
    tail = poly * t * bell
    phi = jnp.where(pre >= 0.0, 1.0 - tail, tail)
    return pre * phi, phi + pre * bell * 0.3989422804014327


def column_total(array):
    return jnp.sum(array.astype(f32), axis=0, keepdims=True)


def up_kernel(
    chunk,
    x_ref,
    mixed_ref,
    cot_ref,
    wo_ref,
    w1_ref,
    w2_ref,
    hid_ref,
    vec_ref,
    act_ref,
    slope_ref,
    h1_ref,
    res_ref,
    gs_ref,
    sums_ref,
    low,
    down,
):
    step = pl.program_id(0)
    chunks = x_ref.shape[0] // chunk

    @pl.when(step == 0)
    def _():
        @pl.loop(0, chunks)
        def _(i):
            rows = pl.ds(pl.multiple_of(i * chunk, chunk), chunk)
            h1 = x_ref[rows, :].astype(f32) + matmul_nt(mixed_ref[rows, :], wo_ref[...])
            h1 = h1 + vec_ref[4:5, :]
            h1_ref[rows, :] = h1
            unit, _scale = norm_parts(h1)
            low[rows, :] = (unit * vec_ref[0:1, :] + vec_ref[1:2, :]).astype(bf16)
            down[rows, :] = jnp.zeros((chunk, D), f32)

    for i in range(chunks):
        rows = slice(i * chunk, (i + 1) * chunk)
        pre = matmul(low[rows, :], w1_ref[...]) + hid_ref[...]
        act, slope = gelu_and_slope(pre)
        act = act.astype(bf16)
        act_ref[rows, :] = act
        slope_ref[rows, :] = slope.astype(bf16)
        down[rows, :] += matmul_nt(act, w2_ref[...])

    @pl.when(step == pl.num_programs(0) - 1)
    def _():
        sums_ref[...] = jnp.zeros_like(sums_ref)

        @pl.loop(0, chunks)
        def _(i):
            rows = pl.ds(pl.multiple_of(i * chunk, chunk), chunk)
            unit, _scale = norm_parts(h1_ref[rows, :])
            first = unit * vec_ref[0:1, :] + vec_ref[1:2, :]
            unit, scale = norm_parts(first + down[rows, :] + vec_ref[5:6, :])
            res_ref[rows, :] = (unit * vec_ref[2:3, :] + vec_ref[3:4, :]).astype(bf16)
            cot = cot_ref[rows, :].astype(f32)
            grad = norm_back(cot, unit, scale, vec_ref[2:3, :])
            gs_ref[rows, :] = grad
            sums_ref[0:1, :] += column_total(cot * unit)
            sums_ref[1:2, :] += column_total(cot)
            sums_ref[2:3, :] += column_total(grad.astype(bf16))


def feed_forward(x, mixed, cot, attn_full, ffn_full, hid_all, vec_par):
    rows = x.shape[0]
    chunk = min(256, rows)
    steps = FF // D
    whole = lambda shape: pl.BlockSpec(shape, lambda t: (0,) * len(shape))
    once = lambda shape: pl.BlockSpec(
        shape, lambda t: (0,) * len(shape), pipeline_mode=pl.Buffered(1)
    )
    hidden = pl.BlockSpec((rows, D), lambda t: (0, t))
    return pl.pallas_call(
        partial(up_kernel, chunk),
        out_shape=[
            jax.ShapeDtypeStruct((rows, FF), bf16),
            jax.ShapeDtypeStruct((rows, FF), bf16),
            jax.ShapeDtypeStruct((rows, D), f32),
            jax.ShapeDtypeStruct((rows, D), bf16),
            jax.ShapeDtypeStruct((rows, D), f32),
            jax.ShapeDtypeStruct((8, D), f32),
        ],
        grid=(steps,),
        in_specs=[
            once((rows, D)),
            once((rows, D)),
            once((rows, D)),
            pl.BlockSpec((None, D, D), lambda t: (3, 0, 0), pipeline_mode=pl.Buffered(1)),
            pl.BlockSpec((None, D, D), lambda t: (0, 0, t)),
            pl.BlockSpec((None, D, D), lambda t: (1, 0, t)),
            pl.BlockSpec((1, D), lambda t: (0, t)),
            whole((6, D)),
        ],
        out_specs=[
            hidden,
            hidden,
            whole((rows, D)),
            whole((rows, D)),
            whole((rows, D)),
            whole((8, D)),
        ],
        scratch_shapes=[pltpu.VMEM((rows, D), bf16), pltpu.VMEM((rows, D), f32)],
        compiler_params=pltpu.CompilerParams(vmem_limit_bytes=VMEM_LIMIT),
        cost_estimate=pl.CostEstimate(
            flops=2 * rows * D * (D + 2 * FF),
            bytes_accessed=rows * D * 30 + 2 * D * FF * 2,
            transcendentals=2 * rows * FF,
        ),
        name="feed_forward",
    )(x, mixed, cot, attn_full, ffn_full, ffn_full, hid_all.reshape(1, FF), vec_par)


def down_kernel(
    chunk,
    gs_ref,
    h1_ref,
    mixed_ref,
    wo_ref,
    w1_ref,
    w2_ref,
    act_ref,
    slope_ref,
    vec_ref,
    dw1_ref,
    dw2_ref,
    dwo_ref,
    gh1_ref,
    gm_ref,
    hid_ref,
    sums_ref,
    turned,
    low_t,
    pre,
    total,
):
    step = pl.program_id(0)
    n_rows = gs_ref.shape[0]
    chunks = n_rows // chunk

    @pl.when(step == 0)
    def _():
        @pl.loop(0, chunks)
        def _(i):
            rows = pl.ds(pl.multiple_of(i * chunk, chunk), chunk)
            unit, _scale = norm_parts(h1_ref[rows, :])
            low = unit * vec_ref[0:1, :] + vec_ref[1:2, :]
            low_t[:, rows] = low.T.astype(bf16)
            turned[:, rows] = gs_ref[rows, :].T.astype(bf16)
            total[rows, :] = gs_ref[rows, :]

    for i in range(chunks):
        rows = slice(i * chunk, (i + 1) * chunk)
        grad_act = matmul(gs_ref[rows, :].astype(bf16), w2_ref[...]).astype(bf16).astype(f32)
        grad_pre = (grad_act * slope_ref[rows, :].astype(f32)).astype(bf16)
        pre[rows, :] = grad_pre
        total[rows, :] += matmul_nt(grad_pre, w1_ref[...])
    hid_ref[...] = column_total(pre[...])
    part = D // 4
    for j in range(4):
        out = slice(j * part, (j + 1) * part)
        dw1_ref[out, :] = matmul(low_t[out, :], pre[...]).astype(bf16)
        dw2_ref[out, :] = matmul(turned[out, :], act_ref[...]).astype(bf16)

    @pl.when(step == pl.num_programs(0) - 1)
    def _():
        sums_ref[...] = jnp.zeros_like(sums_ref)

        @pl.loop(0, chunks)
        def _(i):
            rows = pl.ds(pl.multiple_of(i * chunk, chunk), chunk)
            unit, scale = norm_parts(h1_ref[rows, :])
            grad_first = total[rows, :]
            grad_h1 = norm_back(grad_first, unit, scale, vec_ref[0:1, :])
            gh1_ref[rows, :] = grad_h1
            low = grad_h1.astype(bf16)
            gm_ref[rows, :] = matmul(low, wo_ref[...]).astype(bf16)
            turned[:, rows] = grad_h1.T.astype(bf16)
            sums_ref[0:1, :] += column_total(grad_first * unit)
            sums_ref[1:2, :] += column_total(grad_first)
            sums_ref[2:3, :] += column_total(low)

        @pl.loop(0, 4)
        def _(j):
            out = pl.ds(pl.multiple_of(j * part, part), part)
            dwo_ref[out, :] = matmul(turned[out, :], mixed_ref[...]).astype(bf16)


def feed_back(gs, h1, mixed, attn_full, ffn_full, act, slope, vec_par):
    rows = gs.shape[0]
    chunk = min(256, rows)
    steps = FF // D
    whole = lambda shape: pl.BlockSpec(shape, lambda t: (0,) * len(shape))
    once = lambda shape: pl.BlockSpec(
        shape, lambda t: (0,) * len(shape), pipeline_mode=pl.Buffered(1)
    )
    hidden = pl.BlockSpec((rows, D), lambda t: (0, t))
    slab = pl.BlockSpec((D, D), lambda t: (0, t))
    return pl.pallas_call(
        partial(down_kernel, chunk),
        out_shape=[
            jax.ShapeDtypeStruct((D, FF), bf16),
            jax.ShapeDtypeStruct((D, FF), bf16),
            jax.ShapeDtypeStruct((D, D), bf16),
            jax.ShapeDtypeStruct((rows, D), f32),
            jax.ShapeDtypeStruct((rows, D), bf16),
            jax.ShapeDtypeStruct((1, FF), f32),
            jax.ShapeDtypeStruct((8, D), f32),
        ],
        grid=(steps,),
        in_specs=[
            once((rows, D)),
            once((rows, D)),
            once((rows, D)),
            pl.BlockSpec((None, D, D), lambda t: (3, 0, 0), pipeline_mode=pl.Buffered(1)),
            pl.BlockSpec((None, D, D), lambda t: (0, 0, t)),
            pl.BlockSpec((None, D, D), lambda t: (1, 0, t)),
            hidden,
            hidden,
            whole((6, D)),
        ],
        out_specs=[
            slab,
            slab,
            whole((D, D)),
            whole((rows, D)),
            whole((rows, D)),
            pl.BlockSpec((1, D), lambda t: (0, t)),
            whole((8, D)),
        ],
        scratch_shapes=[
            pltpu.VMEM((D, rows), bf16),
            pltpu.VMEM((D, rows), bf16),
            pltpu.VMEM((rows, D), bf16),
            pltpu.VMEM((rows, D), f32),
        ],
        compiler_params=pltpu.CompilerParams(vmem_limit_bytes=VMEM_LIMIT),
        cost_estimate=pl.CostEstimate(
            flops=2 * rows * D * (2 * D + 4 * FF),
            bytes_accessed=rows * D * 30 + 4 * D * FF * 2,
            transcendentals=0,
        ),
        name="feed_back",
    )(gs, h1, mixed, attn_full, ffn_full, ffn_full, act, slope, vec_par)


WIDE = 1536
STRIP = 96
PIECES = 8
ITEM = 128
LINE_ITEMS = 5
MESH = pl.DeviceIdType.MESH


def remote(src, dst, send, recv, where):
    return pltpu.make_async_remote_copy(
        src_ref=src,
        dst_ref=dst,
        send_sem=send,
        recv_sem=recv,
        device_id=where,
        device_id_type=MESH,
    )


def greet(partners):
    barrier = pltpu.get_barrier_semaphore()
    for where in partners:
        pl.semaphore_signal(barrier, inc=1, device_id=where, device_id_type=MESH)
    pl.semaphore_wait(barrier, len(partners))


def places(n_tensor):
    s, c, t = lax.axis_index("shard"), lax.axis_index("ctx"), lax.axis_index("tensor")
    x, core = s // 2, s % 2
    sibling = (x * 2 + 1 - core, c, t)
    over_x = ((1 - x) * 2 + core, c, t)
    over_y = (s, 1 - c, t)
    across = (x * 2 + 1 - core, 1 - c, t)
    along_z = [(s, c, lax.rem(t + k, n_tensor)) for k in range(1, n_tensor)]
    return s, c, t, x, core, sibling, over_x, over_y, across, along_z


class Line:
    def __init__(self, s, c, t, last, items, rows, array, out, up, down, copied):
        self.s, self.c, self.t, self.last, self.items = s, c, t, last, items
        self.rows, self.array, self.out, self.up, self.down = rows, array, out, up, down
        self.copied = copied

    def hop(self, i, src_t, sems, n, to):
        ref = self.array.at[src_t, pl.ds(i * self.rows, self.rows)]
        return remote(ref, ref, sems[0].at[n], sems[1].at[n], (self.s, self.c, to))

    def keep(self, src_t, n):
        return pltpu.make_async_copy(self.array.at[src_t], self.out.at[src_t], self.copied.at[n])

    def send_own(self, i):
        t = self.t

        @pl.when(t < self.last)
        def _():
            self.hop(i, t, self.up, i, t + 1).start()

        @pl.when(t > 0)
        def _():
            self.hop(i, t, self.down, i, t - 1).start()

        if i == self.items - 1:
            self.keep(t, 2 * self.last).start()

    def tick(self, j):
        t, last = self.t, self.last
        i, hops, n = j % self.items, j // self.items + 1, j + self.items

        @pl.when(t >= hops)
        def _():
            self.hop(i, t - hops, self.up, j, t - 1).wait_recv()

            @pl.when(t < last)
            def _():
                self.hop(i, t - hops, self.up, n, t + 1).start()

            if i == self.items - 1:
                self.keep(t - hops, hops - 1).start()

        @pl.when(t + hops <= last)
        def _():
            self.hop(i, t + hops, self.down, j, t + 1).wait_recv()

            @pl.when(t > 0)
            def _():
                self.hop(i, t + hops, self.down, n, t - 1).start()

            if i == self.items - 1:
                self.keep(t + hops, last + hops - 1).start()

    def settle(self):
        t, last = self.t, self.last
        for j in range(self.items * last):
            i, hops = j % self.items, j // self.items

            @pl.when((t < last) & (t >= hops))
            def _():
                self.hop(i, t - hops, self.up, j, t + 1).wait_send()

            @pl.when((t > 0) & (t + hops <= last))
            def _():
                self.hop(i, t + hops, self.down, j, t - 1).wait_send()

        self.keep(t, 2 * last).wait()
        for hops in range(1, last + 1):

            @pl.when(t >= hops)
            def _():
                self.keep(t - hops, hops - 1).wait()

            @pl.when(t + hops <= last)
            def _():
                self.keep(t + hops, last + hops - 1).wait()


def start_kernel(n_tensor, *refs):
    attn_ref, ffn_ref, qv_ref, hid_ref, tab_ref, rand, tokens = refs[:7]
    attn_out, ffn_out, hid_out, x_out, q_out, k_out, v_out, mixed_out, lse_out = refs[7:16]
    low, low_z, bias, bias_z, bias_qv, ffn_low, full, xs, qs, ms, k_buf, v_buf, s_buf, ffn_full = refs[16:30]
    (
        z_send,
        z_recv,
        b_send,
        b_recv,
        fz_send,
        fz_recv,
        x_send,
        x_recv,
        g_send,
        g_recv,
        p_send,
        p_recv,
        fg_send,
        fg_recv,
        fp_send,
        fp_recv,
        kv_send,
        kv_recv,
        own_sem,
    ) = refs[30:]
    s, c, t, x, core, sibling, over_x, over_y, across, along_z = places(n_tensor)
    own_cols, own_ff = D // n_tensor, FF // n_tensor
    n_rows = xs.shape[0]

    for m in range(4):
        low[:, m * own_cols : (m + 1) * own_cols] = attn_ref[m].astype(bf16)
    for m in range(2):
        ffn_low[m] = ffn_ref[m].astype(bf16)
    bias[0:2, 0:own_cols] = qv_ref[...]
    bias[2:3, 0:own_ff] = hid_ref[...]

    greet([sibling, over_x, over_y, across] + along_z)

    sent = []

    def put(copy):
        copy.start()
        sent.append(copy)

    half = 2 * own_cols

    def z_hop(path, k, u):
        cols = pl.ds(path * half, half)
        n = path * n_tensor
        return remote(
            low.at[:, cols], low_z.at[u, :, cols], z_send.at[n + k], z_recv.at[n + u], along_z[k]
        )

    for path in range(2):
        for k in range(n_tensor - 1):
            put(z_hop(path, k, t))

    def keep_rows(src, dst, n):
        return pltpu.make_async_copy(src.at[t], dst, x_recv.at[n])

    def swap_rows(src, dst, n):
        return remote(src.at[t], dst, x_send.at[n], x_recv.at[n], across)

    @pl.when(core == c)
    def _():
        keep_rows(tokens, xs, 0).start()

    @pl.when(core != c)
    def _():
        swap_rows(tokens, xs, 0).start()

    low_z[t] = low[...]
    bias_z[t] = bias[...]

    def strip(shard, ctx):
        return pl.ds(pl.multiple_of((2 * shard + ctx) * STRIP, STRIP), STRIP)

    here = strip(s, c)

    def lay_out(path):
        for k, where in enumerate(along_z):
            z_hop(path, k, where[2]).wait_recv()
        for n in range(n_tensor):
            for m in range(2 * path, 2 * path + 2):
                piece = low_z[n, :, m * own_cols : (m + 1) * own_cols]
                full[m, here, n * own_cols : (n + 1) * own_cols] = piece

    far_x, far_y = over_x[0], 1 - c
    labels = ["own", "x", "y", "xy"]
    rows = {
        "own": here,
        "x": strip(far_x, c),
        "y": strip(s, far_y),
        "xy": strip(far_x, far_y),
    }
    far_rows = {
        "own": strip(sibling[0], c),
        "x": strip(2 * (1 - x) + 1 - core, c),
        "y": strip(sibling[0], far_y),
        "xy": strip(2 * (1 - x) + 1 - core, far_y),
    }

    def attn_block(path, at):
        return full.at[pl.ds(2 * path, 2), at, :]

    def ffn_block(path, at):
        return ffn_full.at[path, at, :]

    class Gather:
        def __init__(self, block, ways, gs, gr, ps, pr):
            self.block, self.gs, self.gr, self.ps, self.pr = block, gs, gr, ps, pr
            x_first = (("x", over_x), ("y", over_y))
            self.ways = [x_first if way == 0 else x_first[::-1] for way in ways]

        def hop(self, path, name, label, where):
            n = path * 3 + labels.index(label) - 1
            ref = self.block(path, rows[name])
            return remote(ref, ref, self.gs.at[n], self.gr.at[n], where)

        def give(self, path, name, label, where):
            put(self.hop(path, name, label, where))

        def take(self, path, label):
            self.hop(path, label, label, over_x).wait_recv()

        def share(self, path, name):
            put(self.shared(path, name))

        def take_shared(self, path):
            for n, name in enumerate(labels):
                ref = self.block(path, far_rows[name])
                n = path * 4 + n
                remote(ref, ref, self.ps.at[n], self.pr.at[n], sibling).wait_recv()

        def shared(self, path, name):
            n = path * 4 + labels.index(name)
            ref = self.block(path, rows[name])
            return remote(ref, ref, self.ps.at[n], self.pr.at[n], sibling)

        def again(self, path, number):
            near, far = self.ways[path]
            if number == 1:
                sent.append(self.hop(path, near[0], "xy", far[1]))
            sent.append(self.shared(path, {1: near[0], 2: far[0], 3: "xy"}[number]))

        def step(self, path, number):
            near, far = self.ways[path]
            if number == 0:
                self.give(path, "own", near[0], near[1])
                self.give(path, "own", far[0], far[1])
                self.share(path, "own")
            elif number == 1:
                self.take(path, near[0])
                self.give(path, near[0], "xy", far[1])
                self.share(path, near[0])
            elif number == 2:
                self.take(path, far[0])
                self.share(path, far[0])
            else:
                self.take(path, "xy")
                self.share(path, "xy")

    attn = Gather(attn_block, (1, 1), g_send, g_recv, p_send, p_recv)
    ffn = Gather(ffn_block, (0, 1), fg_send, fg_recv, fp_send, fp_recv)

    def ffn_cols(path, u):
        return ffn_full.at[path, here, pl.ds(pl.multiple_of(u * own_ff, own_ff), own_ff)]

    def ffn_hop(path, k, u):
        n = path * n_tensor
        return remote(
            ffn_low.at[path],
            ffn_cols(path, u),
            fz_send.at[n + k],
            fz_recv.at[n + u],
            along_z[k],
        )

    local = []

    def write(src, dst, n):
        copy = pltpu.make_async_copy(src, dst, own_sem.at[n])
        copy.start()
        local.append(copy)

    def ffn_along_z(path):
        for k in range(n_tensor - 1):
            put(ffn_hop(path, k, t))
        write(ffn_low.at[path], ffn_cols(path, t), 5 + path)

    def ffn_ready(path):
        for k, where in enumerate(along_z):
            ffn_hop(path, k, where[2]).wait_recv()
        local[path].wait()
        ffn.step(path, 0)

    lay_out(0)
    attn.step(0, 0)
    lay_out(1)
    attn.step(1, 0)
    ffn_along_z(0)
    ffn_along_z(1)
    for k, where in enumerate(along_z):
        put(remote(bias, bias_z.at[t], b_send.at[k], b_recv.at[t], where))
    attn.step(0, 1)
    attn.step(1, 1)
    ffn_ready(0)
    attn.step(0, 2)
    attn.step(1, 2)
    attn.step(0, 3)
    attn.step(1, 3)
    for k, where in enumerate(along_z):
        u = where[2]
        remote(bias, bias_z.at[u], b_send.at[k], b_recv.at[u], where).wait_recv()
    for n in range(n_tensor):
        cols = slice(n * own_cols, (n + 1) * own_cols)
        bias_qv[0:2, cols] = bias_z[n, 0:2, 0:own_cols]
        hid_out[:, n * own_ff : (n + 1) * own_ff] = bias_z[n, 2:3, 0:own_ff]

    @pl.when(core == c)
    def _():
        keep_rows(tokens, xs, 0).wait()

    @pl.when(core != c)
    def _():
        swap_rows(tokens, xs, 0).wait()

    chunk = 256
    chunks = n_rows // chunk
    per = chunk // BLOCK

    def kv_hop(buf, i, n):
        at, to = pl.ds(i * per, per), pl.ds(n_rows // BLOCK + i * per, per)
        return remote(buf.at[at], buf.at[to], kv_send.at[n], kv_recv.at[n], sibling)

    attn.take_shared(0)
    for i in range(chunks):
        at = pl.ds(i * chunk, chunk)
        k = matmul(xs[at, :], full[1]).astype(bf16)
        k_buf[pl.ds(i * per, per)] = k.reshape(per, BLOCK, D)
        put(kv_hop(k_buf, i, i))
    ffn_ready(1)
    for i in range(chunks):
        at = pl.ds(i * chunk, chunk)
        q = matmul(xs[at, :], full[0]) + bias_qv[0:1, :]
        qs[at, :] = (q.astype(bf16).astype(f32) * 0.125).astype(bf16)
    attn.take_shared(1)
    for i in range(chunks):
        at = pl.ds(i * chunk, chunk)
        v = (matmul(xs[at, :], full[2]) + bias_qv[1:2, :]).astype(bf16)
        v_buf[pl.ds(i * per, per)] = v.reshape(per, BLOCK, D)
        put(kv_hop(v_buf, i, chunks + i))
    ffn.step(0, 1)
    write(xs, x_out, 0)
    write(qs, q_out, 1)
    write(full, attn_out, 2)
    for i in range(chunks):
        kv_hop(k_buf, i, i).wait_recv()
        kv_hop(v_buf, i, chunks + i).wait_recv()
    write(k_buf, k_out, 3)
    write(v_buf, v_out, 4)

    nb = n_rows // BLOCK
    first = core * nb
    stops = {0: [(1, 1)], 1: [(0, 2), (1, 2)], 9: [(0, 3), (1, 3)]}

    @pl.loop(0, nb)
    def _(blk):
        at = pl.ds(pl.multiple_of(blk * BLOCK, BLOCK), BLOCK)
        forward_block(
            qs.at[at],
            ms.at[at],
            lse_out.at[blk],
            k_buf,
            v_buf,
            s_buf,
            tab_ref,
            rand,
            blk * (LISTED - 5),
            blk,
            first,
            0,
        )

        for at_block, moves in stops.items():

            @pl.when(blk == at_block)
            def _():
                mark = len(sent)
                for path, number in moves:
                    ffn.step(path, number)
                del sent[mark:]

    write(ms, mixed_out, 7)
    for path, number in [move for moves in stops.values() for move in moves]:
        ffn.again(path, number)
    for path in range(2):
        ffn.take_shared(path)
        write(ffn_full.at[path], ffn_out.at[path], 8 + path)

    for copy in sent:
        copy.wait_send()
    for copy in local[2:]:
        copy.wait()


def start(n_tensor, attn_w, ffn_w, qv_bias, hid_bias, table, rand, tokens):
    rows = tokens.shape[1]
    own_ff = FF // n_tensor
    dma = pltpu.SemaphoreType.DMA
    vmem, anywhere = pl.BlockSpec(memory_space=pltpu.VMEM), pl.BlockSpec(memory_space=pl.ANY)
    smem = pl.BlockSpec(memory_space=pltpu.SMEM)
    tall = jax.ShapeDtypeStruct((rows, D), bf16)
    both = jax.ShapeDtypeStruct((2 * rows // BLOCK, BLOCK, D), bf16)
    items = 2 * (rows // 256)
    return pl.pallas_call(
        partial(start_kernel, n_tensor),
        out_shape=[
            jax.ShapeDtypeStruct((4, D, D), bf16),
            jax.ShapeDtypeStruct((2, D, FF), bf16),
            jax.ShapeDtypeStruct((1, FF), f32),
            tall,
            tall,
            both,
            both,
            tall,
            jax.ShapeDtypeStruct((rows // BLOCK, 8, ROWS), f32),
        ],
        in_specs=[vmem] * 5 + [smem, anywhere],
        out_specs=[anywhere, anywhere, vmem] + [anywhere] * 5 + [vmem],
        scratch_shapes=[
            pltpu.VMEM((STRIP, D), bf16),
            pltpu.VMEM((n_tensor, STRIP, D), bf16),
            pltpu.VMEM((8, D), f32),
            pltpu.VMEM((n_tensor, 8, D), f32),
            pltpu.VMEM((8, D), f32),
            pltpu.VMEM((2, STRIP, own_ff), bf16),
            pltpu.VMEM((4, D, D), bf16),
            pltpu.VMEM((rows, D), bf16),
            pltpu.VMEM((rows, D), bf16),
            pltpu.VMEM((rows, D), bf16),
            pltpu.VMEM((2 * rows // BLOCK, BLOCK, D), bf16),
            pltpu.VMEM((2 * rows // BLOCK, BLOCK, D), bf16),
            pltpu.VMEM((2 * rows // KEYS, ROWS, KEYS), f32),
            pltpu.VMEM((2, D, FF), bf16),
            dma((2 * n_tensor,)),
            dma((2 * n_tensor,)),
            dma((n_tensor,)),
            dma((n_tensor,)),
            dma((2 * n_tensor,)),
            dma((2 * n_tensor,)),
            dma((2,)),
            dma((2,)),
            dma((6,)),
            dma((6,)),
            dma((8,)),
            dma((8,)),
            dma((6,)),
            dma((6,)),
            dma((8,)),
            dma((8,)),
            dma((items,)),
            dma((items,)),
            dma((10,)),
        ],
        compiler_params=pltpu.CompilerParams(
            collective_id=2, has_side_effects=True, vmem_limit_bytes=VMEM_LIMIT
        ),
        cost_estimate=pl.CostEstimate(
            flops=6 * rows * D * D, bytes_accessed=100 * 2**20, transcendentals=0
        ),
        name="start",
    )(attn_w, ffn_w, qv_bias, hid_bias.reshape(1, own_ff), table, rand, tokens)


def middle_kernel(n_tensor, *refs):
    x_ref, mixed_ref, hid_ref, vec_ref, cotangent, attn_full, ffn_full = refs[:7]
    out_a, out_b, dw1, dw2, dwo, gh1, gm, hid_out, sums_out = refs[7:16]
    w, wo, act, slope, h1, total, gs_low, low_t, turned, pre, dw_s, cot, ready, low, down, held = refs[16:32]
    (
        w_sem,
        c_send,
        c_recv,
        h_send,
        h_recv,
        up_send,
        up_recv,
        dn_send,
        dn_recv,
        dw_sem,
        own_sem,
        copied,
    ) = refs[32:]
    s, c, t, x, core, sibling, over_x, over_y, across, along_z = places(n_tensor)
    n_rows = x_ref.shape[0]
    chunk = 256
    chunks = n_rows // chunk
    steps = FF // D
    items, all_items = LINE_ITEMS, n_rows // ITEM
    last = n_tensor - 1

    def block(i):
        return pl.ds(pl.multiple_of(i * D, D), D)

    fetch_o = pltpu.make_async_copy(attn_full.at[3], wo, w_sem.at[2 * steps])
    fetch_o.start()

    def fetch(m, i):
        at = w.at[m, :, block(i)]
        return pltpu.make_async_copy(ffn_full.at[m, :, block(i)], at, w_sem.at[m * steps + i])

    for i in range(steps):
        for m in range(2):
            fetch(m, i).start()

    greet([over_y, across] + along_z)

    def keep_cot():
        return pltpu.make_async_copy(cotangent.at[t], cot, c_recv.at[0])

    def swap_cot():
        return remote(cotangent.at[t], cot, c_send.at[0], c_recv.at[0], across)

    def home_ref(i):
        if i < items:
            return held.at[t, pl.ds(i * ITEM, ITEM)]
        return out_b.at[pl.ds((i - items) * ITEM, ITEM)]

    def keep_home(i):
        return pltpu.make_async_copy(ready.at[pl.ds(i * ITEM, ITEM)], home_ref(i), h_recv.at[i])

    def send_home(i):
        src = ready.at[pl.ds(i * ITEM, ITEM)]
        return remote(src, home_ref(i), h_send.at[i], h_recv.at[i], across)

    def if_home(at_home, away):
        @pl.when(core == c)
        def _():
            at_home()

        @pl.when(core != c)
        def _():
            away()

    if_home(lambda: keep_cot().start(), lambda: swap_cot().start())

    up, down_line = (up_send, up_recv), (dn_send, dn_recv)
    chain = Line(s, c, t, last, items, ITEM, held, out_a, up, down_line, copied)

    def own_ready(i):
        if_home(lambda: keep_home(i).wait(), lambda: send_home(i).wait_recv())

    per = chunk // ITEM
    for i in range(chunks):
        rows = slice(i * chunk, (i + 1) * chunk)
        if i == 0:
            fetch_o.wait()
        pre1 = x_ref[rows, :].astype(f32) + matmul_nt(mixed_ref[rows, :], wo[...])
        pre1 = pre1 + vec_ref[4:5, :]
        h1[rows, :] = pre1
        unit, _scale = norm_parts(pre1)
        first = unit * vec_ref[0:1, :] + vec_ref[1:2, :]
        low[...] = first.astype(bf16)
        down[...] = first + vec_ref[5:6, :]

        @pl.loop(0, steps)
        def _(j):
            if i == 0:
                fetch(0, j).wait()
                fetch(1, j).wait()
            else:

                @pl.when(j == steps // 2)
                def _():
                    for n in range((i - 1) * per, min(i * per, items)):
                        own_ready(n)
                        chain.send_own(n)

            hidden = matmul(low[...], w[0, :, block(j)]) + hid_ref[:, block(j)]
            act_now, slope_now = gelu_and_slope(hidden)
            act_now = act_now.astype(bf16)
            act[rows, block(j)] = act_now
            slope[rows, block(j)] = slope_now.astype(bf16)
            down[...] += matmul_nt(act_now, w[1, :, block(j)])

        second = down[...]
        total[rows, :] = second
        unit, _scale = norm_parts(second)
        ready[rows, :] = (unit * vec_ref[2:3, :] + vec_ref[3:4, :]).astype(bf16)
        for n in range(i * chunk // ITEM, (i + 1) * chunk // ITEM):
            if_home(lambda: keep_home(n).start(), lambda: send_home(n).start())
        if i == chunks - 1:
            chain.tick(0)
            chain.tick(1)
            chain.tick(2)

    if_home(lambda: keep_cot().wait(), lambda: swap_cot().wait())
    sums_out[...] = jnp.zeros_like(sums_out)

    @pl.loop(0, chunks)
    def _(i):
        rows = pl.ds(pl.multiple_of(i * chunk, chunk), chunk)
        unit, scale = norm_parts(total[rows, :])
        grad_out = cot[rows, :].astype(f32)
        grad = norm_back(grad_out, unit, scale, vec_ref[2:3, :])
        sums_out[2:3, :] += column_total(grad_out * unit)
        sums_out[3:4, :] += column_total(grad_out)
        total[rows, :] = grad
        grad_low = grad.astype(bf16)
        gs_low[rows, :] = grad_low
        sums_out[5:6, :] += column_total(grad_low)
        turned[:, rows] = grad.T.astype(bf16)
        unit, _scale = norm_parts(h1[rows, :])
        first = unit * vec_ref[0:1, :] + vec_ref[1:2, :]
        low_t[:, rows] = first.T.astype(bf16)

    chain.tick(3)
    chain.tick(4)
    part = D // 4

    def dw_copy(slot, m, j):
        return pltpu.make_async_copy(
            dw_s.at[slot, m], (dw1, dw2)[m].at[:, block(j)], dw_sem.at[2 * slot + m]
        )

    ticks = {0: [5, 6], 1: [7, 8], 2: [9, 10], 3: [11, 12]}

    @pl.loop(0, steps)
    def _(j):
        slot = lax.rem(j, 2)
        for i in range(chunks):
            rows = slice(i * chunk, (i + 1) * chunk)
            grad_act = matmul(gs_low[rows, :], w[1, :, block(j)]).astype(bf16).astype(f32)
            grad_pre = (grad_act * slope[rows, block(j)].astype(f32)).astype(bf16)
            pre[rows, :] = grad_pre
            total[rows, :] += matmul_nt(grad_pre, w[0, :, block(j)])
        hid_out[:, block(j)] = column_total(pre[...])

        @pl.when(j >= 2)
        def _():
            for m in range(2):
                dw_copy(slot, m, j - 2).wait()

        for n in range(4):
            out = slice(n * part, (n + 1) * part)
            dw_s[slot, 0, out, :] = matmul(low_t[out, :], pre[...]).astype(bf16)
            dw_s[slot, 1, out, :] = matmul(turned[out, :], act[:, block(j)]).astype(bf16)
        for m in range(2):
            dw_copy(slot, m, j).start()
        for at, numbers in ticks.items():

            @pl.when(j == at)
            def _():
                for n in numbers:
                    chain.tick(n)

    gm_s = gs_low

    @pl.loop(0, chunks)
    def _(i):
        rows = pl.ds(pl.multiple_of(i * chunk, chunk), chunk)
        unit, scale = norm_parts(h1[rows, :])
        grad_first = total[rows, :]
        grad_h1 = norm_back(grad_first, unit, scale, vec_ref[0:1, :])
        total[rows, :] = grad_h1
        grad_low = grad_h1.astype(bf16)
        gm_s[rows, :] = matmul(grad_low, wo[...]).astype(bf16)
        turned[:, rows] = grad_h1.T.astype(bf16)
        sums_out[0:1, :] += column_total(grad_first * unit)
        sums_out[1:2, :] += column_total(grad_first)
        sums_out[4:5, :] += column_total(grad_low)

    local = [
        pltpu.make_async_copy(total, gh1, own_sem.at[0]),
        pltpu.make_async_copy(gm_s, gm, own_sem.at[1]),
    ]
    for copy in local:
        copy.start()
    for j in range(steps - 2, steps):
        for m in range(2):
            dw_copy(j % 2, m, j).wait()

    @pl.loop(0, 4)
    def _(n):
        out = pl.ds(pl.multiple_of(n * part, part), part)
        dw_s[0, 0, out, :] = matmul(turned[out, :], mixed_ref[...]).astype(bf16)

    local.append(pltpu.make_async_copy(dw_s.at[0, 0], dwo, own_sem.at[2]))
    local[-1].start()
    for j in range(13, items * last):
        chain.tick(j)
    for i in range(items, all_items):
        own_ready(i)
    for i in range(all_items):

        @pl.when(core != c)
        def _():
            send_home(i).wait_send()

    chain.settle()
    for copy in local:
        copy.wait()


def middle(n_tensor, x, mixed, hid_all, vec_par, cotangent, attn_full, ffn_full):
    rows = x.shape[0]
    steps = FF // D
    items, all_items = LINE_ITEMS, rows // ITEM
    dma = pltpu.SemaphoreType.DMA
    vmem, anywhere = pl.BlockSpec(memory_space=pltpu.VMEM), pl.BlockSpec(memory_space=pl.ANY)
    low, wide = pltpu.VMEM((rows, D), bf16), pltpu.VMEM((rows, D), f32)
    return pl.pallas_call(
        partial(middle_kernel, n_tensor),
        out_shape=[
            jax.ShapeDtypeStruct((n_tensor, items * ITEM, D), bf16),
            jax.ShapeDtypeStruct((rows - items * ITEM, D), bf16),
            jax.ShapeDtypeStruct((D, FF), bf16),
            jax.ShapeDtypeStruct((D, FF), bf16),
            jax.ShapeDtypeStruct((D, D), bf16),
            jax.ShapeDtypeStruct((rows, D), f32),
            jax.ShapeDtypeStruct((rows, D), bf16),
            jax.ShapeDtypeStruct((1, FF), f32),
            jax.ShapeDtypeStruct((8, D), f32),
        ],
        in_specs=[vmem] * 4 + [anywhere] * 3,
        out_specs=[anywhere] * 7 + [vmem] * 2,
        scratch_shapes=[
            pltpu.VMEM((2, D, FF), bf16),
            pltpu.VMEM((D, D), bf16),
            pltpu.VMEM((rows, FF), bf16),
            pltpu.VMEM((rows, FF), bf16),
            wide,
            wide,
            low,
            pltpu.VMEM((D, rows), bf16),
            pltpu.VMEM((D, rows), bf16),
            low,
            pltpu.VMEM((2, 2, D, D), bf16),
            low,
            low,
            pltpu.VMEM((256, D), bf16),
            pltpu.VMEM((256, D), f32),
            pltpu.VMEM((n_tensor, items * ITEM, D), bf16),
            dma((2 * steps + 1,)),
            dma((1,)),
            dma((1,)),
            dma((all_items,)),
            dma((all_items,)),
            dma((items * n_tensor,)),
            dma((items * n_tensor,)),
            dma((items * n_tensor,)),
            dma((items * n_tensor,)),
            dma((4,)),
            dma((3,)),
            dma((2 * n_tensor - 1,)),
        ],
        compiler_params=pltpu.CompilerParams(
            collective_id=3, has_side_effects=True, vmem_limit_bytes=VMEM_LIMIT
        ),
        cost_estimate=pl.CostEstimate(
            flops=2 * rows * D * (3 * D + 6 * FF),
            bytes_accessed=60 * 2**20,
            transcendentals=2 * rows * FF,
        ),
        name="middle",
    )(x, mixed, hid_all, vec_par, cotangent, attn_full, ffn_full)


def finish_kernel(n_tensor, *refs):
    dq, dk_own, dk_far, dv_own, dv_far, gh1, x_ref, weights = refs[:8]
    dw1, dw2, dwo, vec_sums, hid_sums = refs[8:13]
    attn_out, ffn_out, vec_out, qv_out, hid_out, tokens_out = refs[13:19]
    (
        dk,
        dv,
        xs,
        held,
        x_t,
        partial_sum,
        ready,
        dws,
        acc,
        got0,
        got1a,
        got1b,
        got2,
        zf,
        zf_got,
        za,
        za_got,
        run,
        run_got,
        run_z,
        wts,
    ) = refs[19:40]
    (
        e_send,
        e_recv,
        own_sem,
        s0,
        r0,
        s1,
        r1,
        s2,
        r2,
        zf_send,
        zf_recv,
        za_send,
        za_recv,
        sm,
        rm,
        h_send,
        h_recv,
        up_send,
        up_recv,
        dn_send,
        dn_recv,
        w_sem,
        copied,
    ) = refs[40:]
    s, c, t, x, core, sibling, over_x, over_y, across, along_z = places(n_tensor)
    n_rows = dq.shape[0]
    rows_each = n_rows // PIECES
    last = n_tensor - 1

    def pieces(path, i):
        if i < 2:
            return [(dw1 if path == 0 else dw2, i * WIDE, WIDE, 0)]
        if path == 0:
            return [(dws.at[0], 0, D, 0), (dws.at[1], 0, D, D)]
        return [(dws.at[2], 0, D, 0), (dwo, 0, D, D)]

    def slot(path, i):
        return path * 3 + i

    order = [(path, i) for i in range(3) for path in range(2)]

    def rows_of(xx, cc):
        return pl.ds(pl.multiple_of((4 * xx + 2 * cc) * STRIP, 2 * STRIP), 2 * STRIP)

    own, first = {}, {}
    for path, i in order:
        k = slot(path, i)
        own[k], first[k] = [], []
        for xx in range(2):
            for j, (ref, col, width, at) in enumerate(pieces(path, i)):
                n = (k * 2 + xx) * 2 + j
                cols, to = pl.ds(col, width), pl.ds(at, width)
                own[k].append(
                    pltpu.make_async_copy(
                        ref.at[rows_of(xx, core), cols], acc.at[k, xx, :, to], own_sem.at[n]
                    )
                )
                first[k].append(
                    remote(
                        ref.at[rows_of(xx, 1 - core), cols],
                        got0.at[k, xx, :, to],
                        s0.at[n],
                        r0.at[n],
                        sibling,
                    )
                )

    def start_own(i):
        for path in range(2):
            for copy in own[slot(path, i)]:
                copy.start()

    def start_first(i):
        for path in range(2):
            for copy in first[slot(path, i)]:
                copy.start()

    fetches = [
        pltpu.make_async_copy(gh1, partial_sum, w_sem.at[1]),
        pltpu.make_async_copy(weights.at[pl.ds(0, 3)], wts, w_sem.at[0]),
        pltpu.make_async_copy(x_ref, xs, w_sem.at[2]),
    ]
    for copy in fetches:
        copy.start()
    start_own(0)
    start_own(1)
    greet([sibling, over_x, over_y, across] + along_z)

    chunk = 256
    chunks = n_rows // chunk

    def exchange(i, n):
        at = pl.ds(i * chunk, chunk)
        src, dst = ((dk_far, dk), (dv_far, dv))[n]
        k = 2 * i + n
        return remote(src.at[at], dst.at[at], e_send.at[k], e_recv.at[k], sibling)

    swaps = [exchange(i, n) for i in range(chunks) for n in range(2)]
    for copy in swaps:
        copy.start()
    start_first(0)
    fetches[0].wait()
    fetches[1].wait()

    run[0] = jnp.zeros(run.shape[1:], f32)
    run[0, 0:6, :] = vec_sums[0:6, :]
    for n in range(FF // D):
        run[0, 8 + n : 9 + n, :] = hid_sums[:, n * D : (n + 1) * D]

    def keep_home(i):
        at = pl.ds(i * rows_each, rows_each)
        return pltpu.make_async_copy(ready.at[at], held.at[t, at], h_recv.at[i])

    def send_home(i):
        at = pl.ds(i * rows_each, rows_each)
        return remote(ready.at[at], held.at[t, at], h_send.at[i], h_recv.at[i], across)

    chain = Line(
        s,
        c,
        t,
        last,
        PIECES,
        rows_each,
        held,
        tokens_out,
        (up_send, up_recv),
        (dn_send, dn_recv),
        copied,
    )
    tick = chain.tick

    def send_own(i):
        @pl.when(core == c)
        def _():
            keep_home(i).wait()

        @pl.when(core != c)
        def _():
            send_home(i).wait_recv()

        chain.send_own(i)

    for i in range(PIECES):
        at = slice(i * rows_each, (i + 1) * rows_each)
        if i * rows_each % chunk == 0:
            for n in range(2):
                exchange(i * rows_each // chunk, n).wait_recv()
        dk_piece = (dk_own[at, :].astype(f32) + dk[at, :].astype(f32)).astype(bf16)
        dv_piece = (dv_own[at, :].astype(f32) + dv[at, :].astype(f32)).astype(bf16)
        dk[at, :] = dk_piece
        dv[at, :] = dv_piece
        total = partial_sum[at, :] + matmul_nt(dq[at, :], wts[0])
        total = total + matmul_nt(dk_piece, wts[1]) + matmul_nt(dv_piece, wts[2])
        ready[at, :] = total.astype(bf16)

        @pl.when(core == c)
        def _():
            keep_home(i).start()

        @pl.when(core != c)
        def _():
            send_home(i).start()

        if i > 0:
            send_own(i - 1)

    def add_rows(target, source, count):
        @pl.loop(0, count // 16)
        def _(j):
            rows = pl.ds(pl.multiple_of(j * 16, 16), 16)
            total = target[rows, :].astype(f32) + source[rows, :].astype(f32)
            target[rows, :] = total.astype(bf16)

    def half(cc):
        return pl.ds(pl.multiple_of(cc * STRIP, STRIP), STRIP)

    second, third = {}, {}

    def stage1(path, i):
        k = slot(path, i)
        for copy in own[k]:
            copy.wait()
        for copy in first[k]:
            copy.wait_recv()
        for xx in range(2):
            add_rows(acc.at[k, xx], got0.at[k, xx], 2 * STRIP)
        if path == 0:
            second[k] = remote(acc.at[k, 1 - x], got1a.at[i], s1.at[k], r1.at[k], over_x)
        else:
            second[k] = remote(
                acc.at[k, :, half(1 - c), :], got1b.at[i], s1.at[k], r1.at[k], over_y
            )
        second[k].start()

    def stage2(path, i):
        k = slot(path, i)
        second[k].wait_recv()
        if path == 0:
            add_rows(acc.at[k, x], got1a.at[i], 2 * STRIP)
            third[k] = remote(
                acc.at[k, x, half(1 - c), :], got2.at[k], s2.at[k], r2.at[k], over_y
            )
        else:
            for xx in range(2):
                add_rows(acc.at[k, xx, half(c), :], got1b.at[i, xx], STRIP)
            third[k] = remote(
                acc.at[k, 1 - x, half(c), :], got2.at[k], s2.at[k], r2.at[k], over_x
            )
        third[k].start()

    own_cols = D // n_tensor
    own_ff = FF // n_tensor
    per = WIDE // own_ff

    def stage3(path, i):
        k = slot(path, i)
        third[k].wait_recv()

        @pl.loop(0, STRIP // 16)
        def _(j):
            rows = pl.ds(pl.multiple_of(j * 16, 16), 16)
            here = pl.ds(pl.multiple_of(c * STRIP + j * 16, 16), 16)
            total = acc[k, x, here, :].astype(f32) + got2[k, rows, :].astype(f32)
            if i < 2:
                for n in range(per):
                    piece = total[:, n * own_ff : (n + 1) * own_ff].astype(bf16)
                    zf[per * i + n, rows, path * own_ff : (path + 1) * own_ff] = piece
            else:
                for n in range(n_tensor):
                    for m in range(2):
                        at = m * D + n * own_cols
                        to = (2 * path + m) * own_cols
                        piece = total[:, at : at + own_cols].astype(bf16)
                        za[n, rows, to : to + own_cols] = piece

    z_sent = []

    def z_step(k, buf, got, send, recv):
        @pl.when(t == k)
        def _():
            for d in range(last, k, -1):
                if k > 0:
                    hop(buf, got, send, recv, d, 0, k - 1).wait_recv()
                    add_rows(buf.at[d], got.at[0, d], STRIP)
                hop(buf, got, send, recv, d, 0, k + 1).start()

        @pl.when(t == last - k)
        def _():
            for d in range(0, last - k):
                if k > 0:
                    hop(buf, got, send, recv, d, 1, last - k + 1).wait_recv()
                    add_rows(buf.at[d], got.at[1, d], STRIP)
                hop(buf, got, send, recv, d, 1, last - k - 1).start()

    def hop(buf, got, send, recv, d, way, to):
        n = way * n_tensor + d
        return remote(buf.at[d], got.at[way, d], send.at[n], recv.at[n], (s, c, to))

    def z_collect(buf, got, send, recv, emit):
        @pl.when(t > 0)
        def _():
            hop(buf, got, send, recv, t, 0, t - 1).wait_recv()
            add_rows(buf.at[t], got.at[0, t], STRIP)

        @pl.when(t < last)
        def _():
            hop(buf, got, send, recv, t, 1, t + 1).wait_recv()
            add_rows(buf.at[t], got.at[1, t], STRIP)

        @pl.loop(0, STRIP // 16)
        def _(j):
            rows = pl.ds(pl.multiple_of(j * 16, 16), 16)
            emit(rows, buf[t, rows, :].astype(f32))

    def z_settle(buf, got, send, recv):
        for d in range(n_tensor):

            @pl.when(t < d)
            def _():
                hop(buf, got, send, recv, d, 0, t + 1).wait_send()

            @pl.when(t > d)
            def _():
                hop(buf, got, send, recv, d, 1, t - 1).wait_send()

    ffn_z = (zf, zf_got, zf_send, zf_recv)
    attn_z = (za, za_got, za_send, za_recv)

    small = []

    def small_send(n, where):
        small.append(remote(run.at[n], run_got.at[n], sm.at[n], rm.at[n], where))
        small[n].start()

    def small_add(n):
        small[n].wait_recv()
        run[n + 1] = run[n] + run_got[n]

    start_first(1)
    fetches[2].wait()
    for i in range(chunks):
        at = slice(i * chunk, (i + 1) * chunk)
        x_t[:, at] = xs[at, :].T
    dws[0] = matmul(x_t[...], dq[...]).astype(bf16)
    send_own(7)
    dws[1] = matmul(x_t[...], dk[...]).astype(bf16)
    dws[2] = matmul(x_t[...], dv[...]).astype(bf16)
    start_own(2)
    start_first(2)
    run[0, 6:7, :] = column_total(dq[...])
    run[0, 7:8, :] = column_total(dv[...])
    small_send(0, sibling)
    stage1(0, 0)
    stage1(1, 0)
    stage1(0, 1)
    stage1(1, 1)
    tick(0)
    stage1(0, 2)
    stage1(1, 2)
    small_add(0)
    small_send(1, over_x)
    tick(1)
    tick(2)
    tick(3)
    stage2(0, 0)
    stage2(1, 0)
    tick(4)
    tick(5)
    small_add(1)
    small_send(2, over_y)
    tick(6)
    stage2(0, 1)
    stage2(1, 1)
    tick(7)
    tick(8)
    small_add(2)
    run_z[t] = run[3]
    for k, where in enumerate(along_z):
        copy = remote(run.at[3], run_z.at[t], sm.at[3 + k], rm.at[3 + t], where)
        copy.start()
        z_sent.append(copy)
    stage3(0, 0)
    stage3(1, 0)
    stage2(0, 2)
    stage2(1, 2)
    tick(9)
    tick(10)
    stage3(0, 1)
    stage3(1, 1)
    z_step(0, *ffn_z)
    tick(11)
    tick(12)
    z_step(1, *ffn_z)
    stage3(0, 2)
    stage3(1, 2)
    z_step(0, *attn_z)
    tick(13)
    tick(14)
    z_step(2, *ffn_z)
    z_step(1, *attn_z)
    tick(15)
    tick(16)
    z_step(2, *attn_z)
    for j in range(17, PIECES * last):
        tick(j)

    for k, where in enumerate(along_z):
        u = where[2]
        remote(run.at[3], run_z.at[u], sm.at[3 + k], rm.at[3 + u], where).wait_recv()
    total = run_z[0]
    for n in range(1, n_tensor):
        total = total + run_z[n]
    vec_out[...] = total[0:6, :]
    for n in range(n_tensor):

        @pl.when(t == n)
        def _():
            qv_out[...] = total[6:8, n * own_cols : (n + 1) * own_cols]
            hid_out[...] = total[8 + n : 9 + n, :]


    def emit_ffn(rows, total):
        for m in range(2):
            ffn_out[m, rows, :] = total[:, m * own_ff : (m + 1) * own_ff]

    def emit_attn(rows, total):
        for m in range(4):
            attn_out[m, rows, :] = total[:, m * own_cols : (m + 1) * own_cols]

    z_collect(*ffn_z, emit_ffn)
    z_collect(*attn_z, emit_attn)
    z_settle(*ffn_z)
    z_settle(*attn_z)

    for copy in swaps:
        copy.wait_send()
    for path, i in order:
        k = slot(path, i)
        for copy in first[k]:
            copy.wait_send()
        second[k].wait_send()
        third[k].wait_send()
    for copy in small + z_sent:
        copy.wait_send()

    @pl.when(core != c)
    def _():
        for i in range(PIECES):
            send_home(i).wait_send()

    chain.settle()


def finish_all(n_tensor, grads, gh1, x, attn_full, dws, sums):
    rows = x.shape[0]
    own_cols, own_ff = D // n_tensor, FF // n_tensor
    dma = pltpu.SemaphoreType.DMA
    vmem, anywhere = pl.BlockSpec(memory_space=pltpu.VMEM), pl.BlockSpec(memory_space=pl.ANY)
    dq, dk_own, dk_far, dv_own, dv_far = grads
    tall = pltpu.VMEM((rows, D), bf16)
    items = PIECES * (n_tensor - 1)
    return pl.pallas_call(
        partial(finish_kernel, n_tensor),
        out_shape=[
            jax.ShapeDtypeStruct((4, STRIP, own_cols), f32),
            jax.ShapeDtypeStruct((2, STRIP, own_ff), f32),
            jax.ShapeDtypeStruct((6, D), f32),
            jax.ShapeDtypeStruct((2, own_cols), f32),
            jax.ShapeDtypeStruct((1, own_ff), f32),
            jax.ShapeDtypeStruct((n_tensor, rows, D), bf16),
        ],
        in_specs=[vmem, vmem, anywhere, vmem, anywhere] + [anywhere] * 6
        + [vmem] * 2,
        out_specs=[vmem] * 5 + [anywhere],
        scratch_shapes=[
            tall,
            tall,
            tall,
            pltpu.VMEM((n_tensor, rows, D), bf16),
            pltpu.VMEM((D, rows), bf16),
            pltpu.VMEM((rows, D), f32),
            tall,
            pltpu.VMEM((3, D, D), bf16),
            pltpu.VMEM((6, 2, 2 * STRIP, WIDE), bf16),
            pltpu.VMEM((6, 2, 2 * STRIP, WIDE), bf16),
            pltpu.VMEM((3, 2 * STRIP, WIDE), bf16),
            pltpu.VMEM((3, 2, STRIP, WIDE), bf16),
            pltpu.VMEM((6, STRIP, WIDE), bf16),
            pltpu.VMEM((n_tensor, STRIP, 2 * own_ff), bf16),
            pltpu.VMEM((2, n_tensor, STRIP, 2 * own_ff), bf16),
            pltpu.VMEM((n_tensor, STRIP, 4 * own_cols), bf16),
            pltpu.VMEM((2, n_tensor, STRIP, 4 * own_cols), bf16),
            pltpu.VMEM((4, 16, D), f32),
            pltpu.VMEM((3, 16, D), f32),
            pltpu.VMEM((n_tensor, 16, D), f32),
            pltpu.VMEM((3, D, D), bf16),
            dma((2 * rows // 256,)),
            dma((2 * rows // 256,)),
            dma((24,)),
            dma((24,)),
            dma((24,)),
            dma((6,)),
            dma((6,)),
            dma((6,)),
            dma((6,)),
            dma((2 * n_tensor,)),
            dma((2 * n_tensor,)),
            dma((2 * n_tensor,)),
            dma((2 * n_tensor,)),
            dma((3 + n_tensor,)),
            dma((3 + n_tensor,)),
            dma((PIECES,)),
            dma((PIECES,)),
            dma((items + PIECES,)),
            dma((items + PIECES,)),
            dma((items + PIECES,)),
            dma((items + PIECES,)),
            dma((3,)),
            dma((2 * n_tensor - 1,)),
        ],
        compiler_params=pltpu.CompilerParams(
            collective_id=1, has_side_effects=True, vmem_limit_bytes=VMEM_LIMIT
        ),
        cost_estimate=pl.CostEstimate(
            flops=12 * rows * D * D, bytes_accessed=400 * 2**20, transcendentals=0
        ),
        name="finish",
    )(dq, dk_own, dk_far, dv_own, dv_far, gh1, x, attn_full, *dws, *sums)


GROUP_RATES = (
    [2.0 / D**0.5] * 3 + [2.0 / (D // (4 * BLOCK)) ** 0.5],
    [2.0 / D**0.5, 2.0 / FF**0.5],
)


def last_kernel(tokens_ref, out_a, out_b, *refs):
    attn_g, attn_w, attn_m, attn_v, ffn_g, ffn_w, ffn_m, ffn_v = refs[:8]
    plain = [refs[8 + 4 * n : 12 + 4 * n] for n in range(3)]
    tokens_out, output = refs[20:22]
    attn_moment, attn_square, out_states, attn_new, attn_copy = refs[22:27]
    ffn_moment, ffn_square, ffn_new, ffn_copy = refs[27:31]
    plain_out = [refs[31 + 3 * n : 34 + 3 * n] for n in range(3)]
    step = pl.program_id(0)
    rows_a = out_a.shape[1]

    @pl.when(step == 0)
    def _():
        for m in range(4):
            moment, square, new = adam_update(
                attn_w[m], attn_m[m], attn_v[m], attn_g[m], GROUP_RATES[0][m], decay_rate
            )
            if m < 3:
                attn_moment[m], attn_square[m] = moment, square
            else:
                out_states[0], out_states[1] = moment, square
            attn_new[m], attn_copy[m] = new, new.astype(bf16)
        for m in range(2):
            moment, square, new = adam_update(
                ffn_w[m], ffn_m[m], ffn_v[m], ffn_g[m], GROUP_RATES[1][m], decay_rate
            )
            ffn_moment[m], ffn_square[m] = moment, square
            ffn_new[m], ffn_copy[m] = new, new.astype(bf16)
        for (g, w, m, v), outs in zip(plain, plain_out):
            for ref, value in zip(outs, adam_update(w[...], m[...], v[...], g[...], 0.5, 0.0)):
                ref[...] = value

    tokens_out[...] = tokens_ref[...].astype(f32)

    @pl.when(step % 2 == 0)
    def _():
        output[:, :rows_a] = out_a[...]

    @pl.when(step % 2 == 1)
    def _():
        output[:, rows_a:] = out_b[...]


def last(tokens_low, out_a, out_b, attn, ffn, plain):
    count, rows, _ = tokens_low.shape
    tile = lambda size, index: pl.BlockSpec((1, size, D), index)
    whole = lambda shape: pl.BlockSpec(
        shape, lambda i: (0,) * len(shape), pipeline_mode=pl.Buffered(1)
    )
    a, f = attn[0].shape, ffn[0].shape
    shapes = [
        ((3,) + a[1:], f32),
        ((3,) + a[1:], f32),
        ((2,) + a[1:], f32),
        (a, f32),
        (a, bf16),
        (f, f32),
        (f, f32),
        (f, f32),
        (f, bf16),
    ]
    for group in plain:
        shapes += [(group[0].shape, f32)] * 3
    inputs = list(attn) + list(ffn) + [array for group in plain for array in group]
    by_half = lambda i: (i // 2, i % 2, 0)
    by_one = lambda i: (i // 2, 0, 0)
    return pl.pallas_call(
        last_kernel,
        out_shape=[
            jax.ShapeDtypeStruct(tokens_low.shape, f32),
            jax.ShapeDtypeStruct(tokens_low.shape, bf16),
        ]
        + [jax.ShapeDtypeStruct(*entry) for entry in shapes],
        grid=(count * 2,),
        in_specs=[
            tile(rows // 2, by_half),
            tile(out_a.shape[1], by_one),
            tile(out_b.shape[1], by_one),
        ]
        + [whole(array.shape) for array in inputs],
        out_specs=[tile(rows // 2, by_half), tile(rows, by_one)]
        + [whole(shape) for shape, _ in shapes],
        compiler_params=pltpu.CompilerParams(vmem_limit_bytes=VMEM_LIMIT),
        name="last",
    )(tokens_low, out_a, out_b, *inputs)


def make_body(mesh):
    n_shard, n_ctx, n_tensor = mesh.shape["shard"], mesh.shape["ctx"], mesh.shape["tensor"]
    rows_axes = ("shard", "ctx")
    all_axes = ("shard", "ctx", "tensor")
    paired = n_ctx == 2 and n_shard == 4 and n_tensor == 4

    def swapped(s, c):
        return (s - s % 2 + c, s % 2)

    def swap(array):
        if not paired:
            return array
        pairs = []
        for s in range(n_shard):
            for c in range(n_ctx):
                s_to, c_to = swapped(s, c)
                pairs.append((s * n_ctx + c, s_to * n_ctx + c_to))
        return lax.ppermute(array, rows_axes, pairs)

    def spread(array):
        return lax.all_gather(swap(array), "tensor", axis=0, tiled=True)

    def body(
        tokens,
        cotangent,
        segments,
        rand_blocks,
        attn_w,
        attn_m,
        attn_v,
        ffn_w,
        ffn_m,
        ffn_v,
        qv_bias,
        qv_m,
        qv_v,
        hid_bias,
        hid_m,
        hid_v,
        vec_par,
        vec_m,
        vec_v,
    ):
        t_index = lax.axis_index("tensor")
        nseq = tokens.shape[0] // n_tensor
        piece_len = tokens.shape[1]
        nb = piece_len // BLOCK
        own_rows, own_cols = attn_w.shape[1], attn_w.shape[2]
        own_ff = ffn_w.shape[2]

        def mine(array):
            return lax.dynamic_slice_in_dim(array, t_index * nseq, nseq, 0)

        ints = jnp.concatenate(
            [mine(segments), mine(rand_blocks).reshape(nseq, -1)], axis=1
        )
        ints = swap(ints)
        length = segments.shape[1]
        segs, rand = ints[:, :length], ints[:, length:].reshape(nseq, length // BLOCK, -1)
        piece = lax.axis_index("shard") % 2 if paired else lax.axis_index("ctx")
        tables = attention_tables(segs, rand, piece, nb, paired)

        if paired:
            rand_own, _meta, table = tables
            attn_full, ffn_full, hid_all, x, queries, keys, values, mixed, lse = start(
                n_tensor, attn_w, ffn_w, qv_bias, hid_bias, table[0], rand_own, tokens
            )
            flat = x
            x, queries = x[None], queries[None]
            keys, values = keys.reshape(1, length, D), values.reshape(1, length, D)
            pieces = [piece_len, piece_len]
        else:
            x, cot = mine(tokens), mine(cotangent)
            pieces = [length]
            ffn_z = lax.all_gather(ffn_w.astype(bf16), "tensor", axis=0, tiled=False)
            ffn_z = ffn_z.transpose(1, 2, 0, 3).reshape(2, own_rows, FF)
            ffn_full = lax.all_gather(ffn_z, rows_axes, axis=1, tiled=True)
            flat = x.reshape(-1, D)
            attn_low = attn_w.astype(bf16)
            attn_low = jnp.concatenate([attn_low[i] for i in range(4)], axis=1)
            attn_z = lax.all_gather(attn_low, "tensor", axis=0, tiled=False)
            attn_z = attn_z.reshape(n_tensor, own_rows, 4, own_cols).transpose(2, 1, 0, 3)
            attn_full = lax.all_gather(
                attn_z.reshape(4, own_rows, D), rows_axes, axis=1, tiled=True
            )
            bias_own = jnp.concatenate([qv_bias.reshape(-1), hid_bias])
            bias_all = lax.all_gather(bias_own, "tensor", axis=0, tiled=False)
            qv_all = bias_all[:, : 2 * own_cols].reshape(n_tensor, 2, own_cols)
            qv_all = qv_all.transpose(1, 0, 2).reshape(2, D)
            hid_all = bias_all[:, 2 * own_cols :].reshape(FF)
            keys = matmul(flat, attn_full[1]).astype(bf16).reshape(x.shape)
            values = (matmul(flat, attn_full[2]) + qv_all[1]).astype(bf16).reshape(x.shape)
            keys = lax.all_gather(keys, "ctx", axis=1, tiled=True)
            values = lax.all_gather(values, "ctx", axis=1, tiled=True)
            queries = (matmul(flat, attn_full[0]) + qv_all[0]).astype(bf16) * 0.125
            queries = queries.reshape(x.shape)
            mixed, lse = attend(tables, queries, keys, values)
        mixed_low = mixed.reshape(-1, D)
        if paired:
            out_a, out_b, dw1, dw2, dwo, grad_first_in, grad_mixed, hid_sum, vec_sums = middle(
                n_tensor, flat, mixed_low, hid_all, vec_par, cotangent, attn_full, ffn_full
            )
            out_b = lax.all_gather(out_b, "tensor", axis=0, tiled=False)
        else:
            act, slope, h1, result, grad_second, second_sums = feed_forward(
                flat, mixed_low, cot.reshape(-1, D), attn_full, ffn_full, hid_all, vec_par
            )
            output = spread(result.reshape(x.shape))
            dw1, dw2, dwo, grad_first_in, grad_mixed, hid_sum, first_sums = feed_back(
                grad_second, h1, mixed_low, attn_full, ffn_full, act, slope, vec_par
            )

        grad_mixed = grad_mixed.reshape(x.shape)
        grad_query, dk_parts, dv_parts = attend_back(
            tables,
            queries,
            grad_mixed,
            mixed.reshape(x.shape),
            lse.reshape(nseq, nb, 8, ROWS),
            keys,
            values,
            pieces,
        )

        grad_query_low = grad_query.reshape(-1, D)
        if paired:
            attn_grad, ffn_grad, vec_grad, qv_grad, hid_grad, grad_tokens = finish_all(
                n_tensor,
                [grad_query_low] + [part[0] for part in list(dk_parts) + list(dv_parts)],
                grad_first_in,
                flat,
                attn_full,
                (dw1, dw2, dwo),
                (vec_sums, hid_sum),
            )
        else:
            grad_keys = lax.psum_scatter(dk_parts[0], "ctx", scatter_dimension=1, tiled=True)
            grad_values = lax.psum_scatter(dv_parts[0], "ctx", scatter_dimension=1, tiled=True)
            grad_keys_low = grad_keys.reshape(-1, D)
            grad_values_low = grad_values.reshape(-1, D)
            into_tokens = (
                matmul_nt(grad_query_low, attn_full[0])
                + matmul_nt(grad_keys_low, attn_full[1])
                + matmul_nt(grad_values_low, attn_full[2])
            )
            grad_tokens = spread((grad_first_in + into_tokens).astype(bf16).reshape(x.shape))
            dwq = matmul_tn(flat, grad_query_low).astype(bf16)
            dwk = matmul_tn(flat, grad_keys_low).astype(bf16)
            dwv = matmul_tn(flat, grad_values_low).astype(bf16)
            small = jnp.concatenate(
                [
                    first_sums[0],
                    first_sums[1],
                    second_sums[0],
                    second_sums[1],
                    first_sums[2],
                    second_sums[2],
                    column_sum(grad_query_low),
                    column_sum(grad_values_low),
                    hid_sum[0],
                ]
            )
            ffn_grad = lax.psum_scatter(
                jnp.stack([dw1, dw2]), rows_axes, scatter_dimension=1, tiled=True
            )
            ffn_grad = ffn_grad.reshape(2, own_rows, n_tensor, own_ff).transpose(2, 0, 1, 3)
            ffn_grad = lax.psum_scatter(ffn_grad, "tensor", scatter_dimension=0, tiled=False)
            ffn_grad = ffn_grad.astype(f32)
            attn_grad = lax.psum_scatter(
                jnp.stack([dwq, dwk, dwv, dwo]), rows_axes, scatter_dimension=1, tiled=True
            )
            attn_grad = attn_grad.reshape(4, own_rows, n_tensor, own_cols).transpose(2, 1, 0, 3)
            attn_grad = lax.psum_scatter(
                attn_grad.reshape(n_tensor, own_rows, D), "tensor", scatter_dimension=0
            )
            attn_grad = attn_grad.reshape(own_rows, 4, own_cols).transpose(1, 0, 2).astype(f32)
            small = lax.psum(small, all_axes)
            vec_grad = small[: 6 * D].reshape(6, D)
            qv_grad = lax.dynamic_slice_in_dim(
                small[6 * D : 8 * D].reshape(2, D), t_index * own_cols, own_cols, 1
            )
            hid_grad = lax.dynamic_slice_in_dim(
                small[8 * D : 8 * D + FF], t_index * own_ff, own_ff, 0
            )
            out_a, out_b = output[:, : piece_len // 2], output[:, piece_len // 2 :]

        grad_tokens, output, *updated = last(
            grad_tokens,
            out_a,
            out_b,
            (attn_grad, attn_w, attn_m, attn_v),
            (ffn_grad, ffn_w, ffn_m, ffn_v),
            [
                (qv_grad, qv_bias, qv_m, qv_v),
                (hid_grad.reshape(own_ff), hid_bias, hid_m, hid_v),
                (vec_grad, vec_par, vec_m, vec_v),
            ],
        )
        return (output, grad_tokens, *updated)

    return body


def solution(mesh):
    rows = P("shard", "ctx", None)
    weight = P(None, ("shard", "ctx"), "tensor")
    in_specs = (
        (rows, rows, P("shard", None), P("shard", None, None))
        + (weight,) * 6
        + (P(None, "tensor"),) * 3
        + (P("tensor"),) * 3
        + (P(),) * 3
    )
    out_specs = (
        (rows, rows)
        + (weight,) * 9
        + (P(None, "tensor"),) * 3
        + (P("tensor"),) * 3
        + (P(),) * 3
    )
    return jax.shard_map(
        make_body(mesh), mesh=mesh, in_specs=in_specs, out_specs=out_specs, check_vma=False
    )
```

```python
from functools import partial

import jax
import jax.numpy as jnp
from jax import lax
from jax.experimental import pallas as pl
from jax.experimental.pallas import tpu as pltpu
from jax.sharding import PartitionSpec as P

D = 768
HEAD_DIM = 64
FF = 3072
BLOCK = 64
STEP = 5
GROUP = 4 * HEAD_DIM
GROUPS = D // GROUP
ROWS = 4 * BLOCK
LISTED = 8
KEYS = LISTED * BLOCK
VMEM_LIMIT = 60 * 2**20

beta_first = 0.9
beta_second = 0.999
adam_eps = 1e-08
decay_rate = 0.01
norm_eps = 1e-06
neg_large = -1e30

f32 = jnp.float32
bf16 = jnp.bfloat16


def matmul(left, right):
    return jnp.dot(left, right, preferred_element_type=f32)


def matmul_tn(left, right):
    return lax.dot_general(left, right, (((0,), (0,)), ((), ())), preferred_element_type=f32)


def matmul_nt(left, right):
    return lax.dot_general(left, right, (((1,), (1,)), ((), ())), preferred_element_type=f32)


def column_sum(array_in):
    return jnp.sum(array_in.astype(f32), axis=0)


def adam_update(weight, moment, square, gradient, step_rates, decay_on):
    moment_new = beta_first * moment + (1.0 - beta_first) * gradient
    square_new = beta_second * square + (1.0 - beta_second) * gradient * gradient
    step_ratio = (
        moment_new
        / (1.0 - beta_first**STEP)
        / (jnp.sqrt(square_new / (1.0 - beta_second**STEP)) + adam_eps)
    )
    weight_new = weight - step_rates * (step_ratio + decay_on * weight)
    return (moment_new, square_new, weight_new)


def same_head():
    row_head = lax.broadcasted_iota(jnp.int32, (ROWS, GROUP), 0) // BLOCK
    col_head = lax.broadcasted_iota(jnp.int32, (ROWS, GROUP), 1) // HEAD_DIM
    return row_head == col_head


def spread_heads(block, keep):
    stacked = jnp.concatenate([block] * 4, axis=0)
    return jnp.where(keep, stacked, jnp.zeros_like(stacked))


def fold_heads(full, keep):
    kept = jnp.where(keep, full, 0.0)
    return sum(kept[h * BLOCK : (h + 1) * BLOCK] for h in range(4))


def load_keys(k_all, v_all, seq, k_buf, v_buf, sems):
    return [
        pltpu.make_async_copy(k_all.at[seq], k_buf, sems.at[0]),
        pltpu.make_async_copy(v_all.at[seq], v_buf, sems.at[1]),
    ]


def picked_rows(buf, spots, cols):
    return jnp.concatenate([buf[at, :, cols] for at in spots], axis=0)


def chunk_rows(buf, i, cols):
    blocks = buf[pl.ds(i * LISTED, LISTED), :, cols]
    return blocks.reshape(KEYS, GROUP)


def listed_blocks(rand, base, blk, first, own, total):
    one = lambda condition: condition.astype(jnp.int32)
    me = first + blk
    ids = [me - 1, me, me + 1, me * 0, me * 0 + 1] + [rand[base + n] for n in range(LISTED - 5)]
    spots, unused, common = [], [], []
    for n, block in enumerate(ids):
        out = one(block < 0) + one(block >= total)
        for earlier in ids[:n]:
            out = out + one(block == earlier)
        out = lax.min(out, jnp.int32(1))
        at = lax.max(jnp.int32(0), lax.min(block, jnp.int32(total - 1))) - first + own
        spots.append(at + total * one(at < 0))
        unused.append(out)
        common.append(one(block < 2) * (1 - out))
    return spots, unused, common


def code_rows(tab_ref, spots, unused, common):
    low_half = lax.broadcasted_iota(jnp.int32, (1, 2 * BLOCK), 1) < BLOCK

    def one(n):
        plain = (1 - unused[n] - common[n]).astype(f32)
        return tab_ref[spots[n]] * plain - (unused[n] + 2 * common[n]).astype(f32)

    return [jnp.where(low_half, one(n), one(n + 1)) for n in range(0, LISTED, 2)]


def column_of(row):
    return jnp.broadcast_to(row, (2 * BLOCK, 2 * BLOCK)).T


def mask_bias(document, code):
    return jnp.where((document == code) | (code == -2.0), 0.0, neg_large)


def row_of(column):
    return jnp.broadcast_to(column, (ROWS, 2 * BLOCK)).T[0:1, :]


def forward_block(q_ref, out_ref, lse_ref, k_buf, v_buf, s_buf, tab_ref, rand, base, blk, first, own):
    keep = same_head()
    total_blocks = k_buf.shape[0]
    chunks = total_blocks // LISTED
    is_global = first + blk < 2

    @pl.when(jnp.logical_not(is_global))
    def _():
        spots, unused, common = listed_blocks(rand, base, blk, first, own, total_blocks)
        mine = column_of(tab_ref[own + blk])[:BLOCK]
        mine = jnp.concatenate([mine] * 4, axis=0)
        codes = code_rows(tab_ref, spots, unused, common)
        bias = jnp.concatenate([mask_bias(mine, code) for code in codes], axis=1)
        for g in range(GROUPS):
            cols = slice(g * GROUP, (g + 1) * GROUP)
            q_full = spread_heads(q_ref[:, cols], keep)
            scores = matmul_nt(q_full, picked_rows(k_buf, spots, cols)) + bias
            largest = jnp.max(scores, axis=-1, keepdims=True)
            weights = jnp.exp(scores - largest)
            total = jnp.sum(weights, axis=-1, keepdims=True)
            full = matmul(weights.astype(bf16), picked_rows(v_buf, spots, cols))
            out_ref[:, cols] = fold_heads(full * (1.0 / total), keep).astype(bf16)
            lse_ref[g : g + 1, :] = row_of(largest + jnp.log(total))

    @pl.when(is_global)
    def _():
        for g in range(GROUPS):
            cols = slice(g * GROUP, (g + 1) * GROUP)
            q_full = spread_heads(q_ref[:, cols], keep)

            def score_chunk(i, largest):
                scores = matmul_nt(q_full, chunk_rows(k_buf, i, cols))
                s_buf[i] = scores
                return jnp.maximum(largest, jnp.max(scores, axis=-1, keepdims=True))

            largest = lax.fori_loop(0, chunks, score_chunk, jnp.full((ROWS, 1), neg_large, f32))

            def mix_chunk(i, carry):
                total, full = carry
                weights = jnp.exp(s_buf[i] - largest)
                total = total + jnp.sum(weights, axis=-1, keepdims=True)
                return total, full + matmul(weights.astype(bf16), chunk_rows(v_buf, i, cols))

            total, full = lax.fori_loop(
                0, chunks, mix_chunk, (jnp.zeros((ROWS, 1), f32), jnp.zeros((ROWS, GROUP), f32))
            )
            out_ref[:, cols] = fold_heads(full * (1.0 / total), keep).astype(bf16)
            lse_ref[g : g + 1, :] = row_of(largest + jnp.log(total))


def forward_kernel(
    rand, meta, q_ref, tab_ref, k_all, v_all, out_ref, lse_ref, k_buf, v_buf, s_buf, sems
):
    seq, blk = pl.program_id(0), pl.program_id(1)
    nb = pl.num_programs(1)

    @pl.when(blk == 0)
    def _():
        copies = load_keys(k_all, v_all, seq, k_buf, v_buf, sems)
        for c in copies:
            c.start()
        for c in copies:
            c.wait()

    base = (seq * nb + blk) * (LISTED - 5)
    forward_block(
        q_ref, out_ref, lse_ref, k_buf, v_buf, s_buf, tab_ref, rand, base, blk, meta[0], meta[1]
    )


def back_tile(k_rows, v_rows, q_full, go_full, bias, lse, centre):
    scores = matmul_nt(k_rows, q_full)
    if bias is not None:
        scores = scores + bias
    probs = jnp.exp(scores - lse)
    grad_probs = matmul_nt(v_rows, go_full)
    grad_scores = (probs * (grad_probs - centre)).astype(bf16)
    dv_rows = matmul(probs.astype(bf16), go_full)
    dk_rows = matmul(grad_scores, q_full)
    return matmul_tn(grad_scores, k_rows), dk_rows, dv_rows


def backward_kernel(
    n_out, rand, meta, q_ref, go_ref, mixed_ref, lse_ref, tab_ref, out_a, k_all, v_all, *rest
):
    dq_ref, out_ref, *rest = rest
    dk_refs, dv_refs = rest[:n_out], rest[n_out : 2 * n_out]
    k_buf, v_buf, dk_acc, dv_acc, sems = rest[2 * n_out :]
    seq, blk = pl.program_id(0), pl.program_id(1)
    nb = pl.num_programs(1)
    total_blocks = k_buf.shape[0]
    chunks = total_blocks // LISTED

    out_ref[...] = out_a[...]

    @pl.when(blk == 0)
    def _():
        copies = load_keys(k_all, v_all, seq, k_buf, v_buf, sems)
        for c in copies:
            c.start()
        dk_acc[...] = jnp.zeros_like(dk_acc)
        dv_acc[...] = jnp.zeros_like(dv_acc)
        for c in copies:
            c.wait()

    keep = same_head()
    is_global = meta[0] + blk < 2
    base = (seq * nb + blk) * (LISTED - 5)

    def operands(g):
        cols = slice(g * GROUP, (g + 1) * GROUP)
        q_full = spread_heads(q_ref[:, cols], keep)
        go_full = spread_heads(go_ref[:, cols], keep)
        mixed = jnp.concatenate([mixed_ref[:, cols]] * 4, axis=0)
        product = go_full.astype(f32) * mixed.astype(f32)
        centre = row_of(jnp.sum(product, axis=-1, keepdims=True))
        return cols, q_full, go_full, lse_ref[g : g + 1, :], centre

    @pl.when(jnp.logical_not(is_global))
    def _():
        spots, unused, common = listed_blocks(rand, base, blk, meta[0], meta[1], total_blocks)
        stores = [at + (total_blocks - at) * out for at, out in zip(spots, unused)]
        own = tab_ref[meta[1] + blk]
        codes = code_rows(tab_ref, spots, unused, common)
        bias = jnp.concatenate([mask_bias(own, column_of(code)) for code in codes], axis=0)
        bias = jnp.concatenate([bias, bias], axis=1)
        for g in range(GROUPS):
            cols, q_full, go_full, lse, centre = operands(g)
            k_rows, v_rows = picked_rows(k_buf, spots, cols), picked_rows(v_buf, spots, cols)
            dq_full, dk_rows, dv_rows = back_tile(
                k_rows, v_rows, q_full, go_full, bias, lse, centre
            )
            dq_ref[:, cols] = (fold_heads(dq_full, keep) * 0.125).astype(bf16)
            places = [pl.ds(pl.multiple_of(at * BLOCK, BLOCK), BLOCK) for at in stores]
            dk_old = [dk_acc[at, cols] for at in places]
            dv_old = [dv_acc[at, cols] for at in places]
            for n, at in enumerate(places):
                own_rows = slice(n * BLOCK, (n + 1) * BLOCK)
                dk_acc[at, cols] = dk_old[n] + dk_rows[own_rows]
                dv_acc[at, cols] = dv_old[n] + dv_rows[own_rows]

    @pl.when(is_global)
    def _():
        for g in range(GROUPS):
            cols, q_full, go_full, lse, centre = operands(g)

            def chunk_back(i, dq_full):
                rows = pl.ds(pl.multiple_of(i * KEYS, KEYS), KEYS)
                dq_now, dk_rows, dv_rows = back_tile(
                    chunk_rows(k_buf, i, cols),
                    chunk_rows(v_buf, i, cols),
                    q_full,
                    go_full,
                    None,
                    lse,
                    centre,
                )
                dk_acc[rows, cols] += dk_rows
                dv_acc[rows, cols] += dv_rows
                return dq_full + dq_now

            dq_full = lax.fori_loop(0, chunks, chunk_back, jnp.zeros((ROWS, GROUP), f32))
            dq_ref[:, cols] = (fold_heads(dq_full, keep) * 0.125).astype(bf16)

    @pl.when(blk == nb - 1)
    def _():
        row = 0
        for dk_ref, dv_ref in zip(dk_refs, dv_refs):
            rows = dk_ref.shape[0]
            dk_ref[...] = dk_acc[row : row + rows].astype(bf16)
            dv_ref[...] = dv_acc[row : row + rows].astype(bf16)
            row += rows


def attention_tables(segments, random, piece, nb, own_first):
    seq_count, length = segments.shape
    total = length // BLOCK
    first = piece * nb
    rand = lax.dynamic_slice_in_dim(random, first, nb, 1).reshape(-1)
    table = segments.reshape(seq_count, total, BLOCK).astype(f32)
    table = jnp.concatenate([table, table], axis=2)[:, :, None, :]
    if own_first:
        table = lax.dynamic_slice_in_dim(jnp.concatenate([table, table], axis=1), first, total, 1)
    meta = jnp.stack([first, jnp.zeros_like(first) if own_first else first]).astype(jnp.int32)
    return rand, meta, table


def as_blocks(rows):
    return rows.reshape(rows.shape[0], -1, BLOCK, D)


def attend(tables, q, keys, values):
    rand, meta, table = tables
    seq_count, piece_len, _ = q.shape
    nb = piece_len // BLOCK
    length = keys.shape[1]
    any_spec = pl.BlockSpec(memory_space=pl.ANY)
    row_spec = pl.BlockSpec((None, BLOCK, D), lambda s, b, *_: (s, b, 0))
    return pl.pallas_call(
        forward_kernel,
        out_shape=[
            jax.ShapeDtypeStruct(q.shape, bf16),
            jax.ShapeDtypeStruct((seq_count, nb, 8, ROWS), f32),
        ],
        grid_spec=pltpu.PrefetchScalarGridSpec(
            num_scalar_prefetch=2,
            grid=(seq_count, nb),
            in_specs=[
                row_spec,
                pl.BlockSpec((None,) + table.shape[1:], lambda s, b, *_: (s, 0, 0, 0)),
                any_spec,
                any_spec,
            ],
            out_specs=[
                row_spec,
                pl.BlockSpec((None, None, 8, ROWS), lambda s, b, *_: (s, b, 0, 0)),
            ],
            scratch_shapes=[
                pltpu.VMEM((length // BLOCK, BLOCK, D), bf16),
                pltpu.VMEM((length // BLOCK, BLOCK, D), bf16),
                pltpu.VMEM((length // KEYS, ROWS, KEYS), f32),
                pltpu.SemaphoreType.DMA((2,)),
            ],
        ),
        compiler_params=pltpu.CompilerParams(vmem_limit_bytes=VMEM_LIMIT),
        name="attend",
    )(rand, meta, q, table, as_blocks(keys), as_blocks(values))


def attend_back(tables, q, grad_mixed, mixed, lse, out_a, keys, values, pieces):
    rand, meta, table = tables
    seq_count, piece_len, _ = q.shape
    nb = piece_len // BLOCK
    length = keys.shape[1]
    any_spec = pl.BlockSpec(memory_space=pl.ANY)
    row_spec = pl.BlockSpec((None, BLOCK, D), lambda s, b, *_: (s, b, 0))
    count, half, _ = out_a.shape
    share = count * half // (seq_count * nb)
    if share <= half:
        per = half // share
        tile = pl.BlockSpec(
            (None, share, D), lambda s, b, *_: ((s * nb + b) // per, (s * nb + b) % per, 0)
        )
    else:
        tile = pl.BlockSpec((share // half, half, D), lambda s, b, *_: (s * nb + b, 0, 0))
    part_specs = [pl.BlockSpec((None, rows, D), lambda s, b, *_: (s, 0, 0)) for rows in pieces]
    part_shapes = [jax.ShapeDtypeStruct((seq_count, rows, D), bf16) for rows in pieces]
    out = pl.pallas_call(
        partial(backward_kernel, len(pieces)),
        out_shape=[
            jax.ShapeDtypeStruct(q.shape, bf16),
            jax.ShapeDtypeStruct((count, 2 * half, D), bf16),
        ]
        + part_shapes * 2,
        grid_spec=pltpu.PrefetchScalarGridSpec(
            num_scalar_prefetch=2,
            grid=(seq_count, nb),
            in_specs=[
                row_spec,
                row_spec,
                row_spec,
                pl.BlockSpec((None, None, 8, ROWS), lambda s, b, *_: (s, b, 0, 0)),
                pl.BlockSpec((None,) + table.shape[1:], lambda s, b, *_: (s, 0, 0, 0)),
                tile,
                any_spec,
                any_spec,
            ],
            out_specs=[row_spec, tile] + part_specs * 2,
            scratch_shapes=[
                pltpu.VMEM((length // BLOCK, BLOCK, D), bf16),
                pltpu.VMEM((length // BLOCK, BLOCK, D), bf16),
                pltpu.VMEM((length + BLOCK, D), f32),
                pltpu.VMEM((length + BLOCK, D), f32),
                pltpu.SemaphoreType.DMA((2,)),
            ],
        ),
        compiler_params=pltpu.CompilerParams(vmem_limit_bytes=VMEM_LIMIT),
        cost_estimate=pl.CostEstimate(
            flops=seq_count * nb * GROUPS * 10 * ROWS * KEYS * GROUP,
            bytes_accessed=seq_count * (3 * piece_len + 4 * length) * D * 2,
            transcendentals=seq_count * nb * GROUPS * ROWS * KEYS,
        ),
        name="attend_back",
    )(rand, meta, q, grad_mixed, mixed, lse, table, out_a, as_blocks(keys), as_blocks(values))
    return out[0], out[1], out[2 : 2 + len(pieces)], out[2 + len(pieces) :]


def norm_parts(hidden):
    centred = hidden - jnp.mean(hidden, axis=-1, keepdims=True)
    scale = lax.rsqrt(jnp.mean(centred * centred, axis=-1, keepdims=True) + norm_eps)
    return centred * scale, scale


def norm_back(grad, unit, scale, gain):
    inner = grad * gain
    return scale * (
        inner
        - jnp.mean(inner, axis=-1, keepdims=True)
        - unit * jnp.mean(inner * unit, axis=-1, keepdims=True)
    )


def gelu_and_slope(pre):
    bell = jnp.exp(-0.5 * pre * pre)
    t = 1.0 / (1.0 + (0.3275911 * 0.5**0.5) * jnp.abs(pre))
    poly = 0.5 * 1.061405429
    for coefficient in (-1.453152027, 1.421413741, -0.284496736, 0.254829592):
        poly = poly * t + 0.5 * coefficient
    tail = poly * t * bell
    phi = jnp.where(pre >= 0.0, 1.0 - tail, tail)
    return pre * phi, phi + pre * bell * 0.3989422804014327


def column_total(array):
    return jnp.sum(array.astype(f32), axis=0, keepdims=True)


def up_kernel(
    chunk,
    x_ref,
    mixed_ref,
    cot_ref,
    wo_ref,
    w1_ref,
    w2_ref,
    hid_ref,
    vec_ref,
    act_ref,
    slope_ref,
    h1_ref,
    res_ref,
    gs_ref,
    sums_ref,
    low,
    down,
):
    step = pl.program_id(0)
    chunks = x_ref.shape[0] // chunk

    @pl.when(step == 0)
    def _():
        @pl.loop(0, chunks)
        def _(i):
            rows = pl.ds(pl.multiple_of(i * chunk, chunk), chunk)
            h1 = x_ref[rows, :].astype(f32) + matmul_nt(mixed_ref[rows, :], wo_ref[...])
            h1 = h1 + vec_ref[4:5, :]
            h1_ref[rows, :] = h1
            unit, _scale = norm_parts(h1)
            low[rows, :] = (unit * vec_ref[0:1, :] + vec_ref[1:2, :]).astype(bf16)
            down[rows, :] = jnp.zeros((chunk, D), f32)

    for i in range(chunks):
        rows = slice(i * chunk, (i + 1) * chunk)
        pre = matmul(low[rows, :], w1_ref[...]) + hid_ref[...]
        act, slope = gelu_and_slope(pre)
        act = act.astype(bf16)
        act_ref[rows, :] = act
        slope_ref[rows, :] = slope.astype(bf16)
        down[rows, :] += matmul_nt(act, w2_ref[...])

    @pl.when(step == pl.num_programs(0) - 1)
    def _():
        sums_ref[...] = jnp.zeros_like(sums_ref)

        @pl.loop(0, chunks)
        def _(i):
            rows = pl.ds(pl.multiple_of(i * chunk, chunk), chunk)
            unit, _scale = norm_parts(h1_ref[rows, :])
            first = unit * vec_ref[0:1, :] + vec_ref[1:2, :]
            unit, scale = norm_parts(first + down[rows, :] + vec_ref[5:6, :])
            res_ref[rows, :] = (unit * vec_ref[2:3, :] + vec_ref[3:4, :]).astype(bf16)
            cot = cot_ref[rows, :].astype(f32)
            grad = norm_back(cot, unit, scale, vec_ref[2:3, :])
            gs_ref[rows, :] = grad
            sums_ref[0:1, :] += column_total(cot * unit)
            sums_ref[1:2, :] += column_total(cot)
            sums_ref[2:3, :] += column_total(grad.astype(bf16))


def feed_forward(x, mixed, cot, attn_full, ffn_full, hid_all, vec_par):
    rows = x.shape[0]
    chunk = min(256, rows)
    steps = FF // D
    whole = lambda shape: pl.BlockSpec(shape, lambda t: (0,) * len(shape))
    once = lambda shape: pl.BlockSpec(
        shape, lambda t: (0,) * len(shape), pipeline_mode=pl.Buffered(1)
    )
    hidden = pl.BlockSpec((rows, D), lambda t: (0, t))
    return pl.pallas_call(
        partial(up_kernel, chunk),
        out_shape=[
            jax.ShapeDtypeStruct((rows, FF), bf16),
            jax.ShapeDtypeStruct((rows, FF), bf16),
            jax.ShapeDtypeStruct((rows, D), f32),
            jax.ShapeDtypeStruct((rows, D), bf16),
            jax.ShapeDtypeStruct((rows, D), f32),
            jax.ShapeDtypeStruct((8, D), f32),
        ],
        grid=(steps,),
        in_specs=[
            once((rows, D)),
            once((rows, D)),
            once((rows, D)),
            pl.BlockSpec((None, D, D), lambda t: (3, 0, 0), pipeline_mode=pl.Buffered(1)),
            pl.BlockSpec((None, D, D), lambda t: (0, 0, t)),
            pl.BlockSpec((None, D, D), lambda t: (1, 0, t)),
            pl.BlockSpec((1, D), lambda t: (0, t)),
            whole((6, D)),
        ],
        out_specs=[
            hidden,
            hidden,
            whole((rows, D)),
            whole((rows, D)),
            whole((rows, D)),
            whole((8, D)),
        ],
        scratch_shapes=[pltpu.VMEM((rows, D), bf16), pltpu.VMEM((rows, D), f32)],
        compiler_params=pltpu.CompilerParams(vmem_limit_bytes=VMEM_LIMIT),
        cost_estimate=pl.CostEstimate(
            flops=2 * rows * D * (D + 2 * FF),
            bytes_accessed=rows * D * 30 + 2 * D * FF * 2,
            transcendentals=2 * rows * FF,
        ),
        name="feed_forward",
    )(x, mixed, cot, attn_full, ffn_full, ffn_full, hid_all.reshape(1, FF), vec_par)


def down_kernel(
    chunk,
    gs_ref,
    h1_ref,
    mixed_ref,
    wo_ref,
    w1_ref,
    w2_ref,
    act_ref,
    slope_ref,
    vec_ref,
    dw1_ref,
    dw2_ref,
    dwo_ref,
    gh1_ref,
    gm_ref,
    hid_ref,
    sums_ref,
    turned,
    low_t,
    pre,
    total,
):
    step = pl.program_id(0)
    n_rows = gs_ref.shape[0]
    chunks = n_rows // chunk

    @pl.when(step == 0)
    def _():
        @pl.loop(0, chunks)
        def _(i):
            rows = pl.ds(pl.multiple_of(i * chunk, chunk), chunk)
            unit, _scale = norm_parts(h1_ref[rows, :])
            low = unit * vec_ref[0:1, :] + vec_ref[1:2, :]
            low_t[:, rows] = low.T.astype(bf16)
            turned[:, rows] = gs_ref[rows, :].T.astype(bf16)
            total[rows, :] = gs_ref[rows, :]

    for i in range(chunks):
        rows = slice(i * chunk, (i + 1) * chunk)
        grad_act = matmul(gs_ref[rows, :].astype(bf16), w2_ref[...]).astype(bf16).astype(f32)
        grad_pre = (grad_act * slope_ref[rows, :].astype(f32)).astype(bf16)
        pre[rows, :] = grad_pre
        total[rows, :] += matmul_nt(grad_pre, w1_ref[...])
    hid_ref[...] = column_total(pre[...])
    part = D // 4
    for j in range(4):
        out = slice(j * part, (j + 1) * part)
        dw1_ref[out, :] = matmul(low_t[out, :], pre[...]).astype(bf16)
        dw2_ref[out, :] = matmul(turned[out, :], act_ref[...]).astype(bf16)

    @pl.when(step == pl.num_programs(0) - 1)
    def _():
        sums_ref[...] = jnp.zeros_like(sums_ref)

        @pl.loop(0, chunks)
        def _(i):
            rows = pl.ds(pl.multiple_of(i * chunk, chunk), chunk)
            unit, scale = norm_parts(h1_ref[rows, :])
            grad_first = total[rows, :]
            grad_h1 = norm_back(grad_first, unit, scale, vec_ref[0:1, :])
            gh1_ref[rows, :] = grad_h1
            low = grad_h1.astype(bf16)
            gm_ref[rows, :] = matmul(low, wo_ref[...]).astype(bf16)
            turned[:, rows] = grad_h1.T.astype(bf16)
            sums_ref[0:1, :] += column_total(grad_first * unit)
            sums_ref[1:2, :] += column_total(grad_first)
            sums_ref[2:3, :] += column_total(low)

        @pl.loop(0, 4)
        def _(j):
            out = pl.ds(pl.multiple_of(j * part, part), part)
            dwo_ref[out, :] = matmul(turned[out, :], mixed_ref[...]).astype(bf16)


def feed_back(gs, h1, mixed, attn_full, ffn_full, act, slope, vec_par):
    rows = gs.shape[0]
    chunk = min(256, rows)
    steps = FF // D
    whole = lambda shape: pl.BlockSpec(shape, lambda t: (0,) * len(shape))
    once = lambda shape: pl.BlockSpec(
        shape, lambda t: (0,) * len(shape), pipeline_mode=pl.Buffered(1)
    )
    hidden = pl.BlockSpec((rows, D), lambda t: (0, t))
    slab = pl.BlockSpec((D, D), lambda t: (0, t))
    return pl.pallas_call(
        partial(down_kernel, chunk),
        out_shape=[
            jax.ShapeDtypeStruct((D, FF), bf16),
            jax.ShapeDtypeStruct((D, FF), bf16),
            jax.ShapeDtypeStruct((D, D), bf16),
            jax.ShapeDtypeStruct((rows, D), f32),
            jax.ShapeDtypeStruct((rows, D), bf16),
            jax.ShapeDtypeStruct((1, FF), f32),
            jax.ShapeDtypeStruct((8, D), f32),
        ],
        grid=(steps,),
        in_specs=[
            once((rows, D)),
            once((rows, D)),
            once((rows, D)),
            pl.BlockSpec((None, D, D), lambda t: (3, 0, 0), pipeline_mode=pl.Buffered(1)),
            pl.BlockSpec((None, D, D), lambda t: (0, 0, t)),
            pl.BlockSpec((None, D, D), lambda t: (1, 0, t)),
            hidden,
            hidden,
            whole((6, D)),
        ],
        out_specs=[
            slab,
            slab,
            whole((D, D)),
            whole((rows, D)),
            whole((rows, D)),
            pl.BlockSpec((1, D), lambda t: (0, t)),
            whole((8, D)),
        ],
        scratch_shapes=[
            pltpu.VMEM((D, rows), bf16),
            pltpu.VMEM((D, rows), bf16),
            pltpu.VMEM((rows, D), bf16),
            pltpu.VMEM((rows, D), f32),
        ],
        compiler_params=pltpu.CompilerParams(vmem_limit_bytes=VMEM_LIMIT),
        cost_estimate=pl.CostEstimate(
            flops=2 * rows * D * (2 * D + 4 * FF),
            bytes_accessed=rows * D * 30 + 4 * D * FF * 2,
            transcendentals=0,
        ),
        name="feed_back",
    )(gs, h1, mixed, attn_full, ffn_full, ffn_full, act, slope, vec_par)


WIDE = 1536
STRIP = 96
PIECES = 8
ITEM = 128
LINE_ITEMS = 4
MESH = pl.DeviceIdType.MESH


def remote(src, dst, send, recv, where):
    return pltpu.make_async_remote_copy(
        src_ref=src,
        dst_ref=dst,
        send_sem=send,
        recv_sem=recv,
        device_id=where,
        device_id_type=MESH,
    )


def greet(partners):
    barrier = pltpu.get_barrier_semaphore()
    for where in partners:
        pl.semaphore_signal(barrier, inc=1, device_id=where, device_id_type=MESH)
    pl.semaphore_wait(barrier, len(partners))


def places(n_tensor):
    s, c, t = lax.axis_index("shard"), lax.axis_index("ctx"), lax.axis_index("tensor")
    x, core = s // 2, s % 2
    sibling = (x * 2 + 1 - core, c, t)
    over_x = ((1 - x) * 2 + core, c, t)
    over_y = (s, 1 - c, t)
    across = (x * 2 + 1 - core, 1 - c, t)
    along_z = [(s, c, lax.rem(t + k, n_tensor)) for k in range(1, n_tensor)]
    return s, c, t, x, core, sibling, over_x, over_y, across, along_z


class Line:
    def __init__(self, s, c, t, last, items, rows, array, out, up, down, copied):
        self.s, self.c, self.t, self.last, self.items = s, c, t, last, items
        self.rows, self.array, self.out, self.up, self.down = rows, array, out, up, down
        self.copied = copied

    def hop(self, i, src_t, sems, n, to):
        ref = self.array.at[src_t, pl.ds(i * self.rows, self.rows)]
        return remote(ref, ref, sems[0].at[n], sems[1].at[n], (self.s, self.c, to))

    def keep(self, src_t, n):
        return pltpu.make_async_copy(self.array.at[src_t], self.out.at[src_t], self.copied.at[n])

    def send_own(self, i):
        t = self.t

        @pl.when(t < self.last)
        def _():
            self.hop(i, t, self.up, i, t + 1).start()

        @pl.when(t > 0)
        def _():
            self.hop(i, t, self.down, i, t - 1).start()

        if i == self.items - 1:
            self.keep(t, 2 * self.last).start()

    def tick(self, j):
        t, last = self.t, self.last
        i, hops, n = j % self.items, j // self.items + 1, j + self.items

        @pl.when(t >= hops)
        def _():
            self.hop(i, t - hops, self.up, j, t - 1).wait_recv()

            @pl.when(t < last)
            def _():
                self.hop(i, t - hops, self.up, n, t + 1).start()

            if i == self.items - 1:
                self.keep(t - hops, hops - 1).start()

        @pl.when(t + hops <= last)
        def _():
            self.hop(i, t + hops, self.down, j, t + 1).wait_recv()

            @pl.when(t > 0)
            def _():
                self.hop(i, t + hops, self.down, n, t - 1).start()

            if i == self.items - 1:
                self.keep(t + hops, last + hops - 1).start()

    def settle(self):
        t, last = self.t, self.last
        for j in range(self.items * last):
            i, hops = j % self.items, j // self.items

            @pl.when((t < last) & (t >= hops))
            def _():
                self.hop(i, t - hops, self.up, j, t + 1).wait_send()

            @pl.when((t > 0) & (t + hops <= last))
            def _():
                self.hop(i, t + hops, self.down, j, t - 1).wait_send()

        self.keep(t, 2 * last).wait()
        for hops in range(1, last + 1):

            @pl.when(t >= hops)
            def _():
                self.keep(t - hops, hops - 1).wait()

            @pl.when(t + hops <= last)
            def _():
                self.keep(t + hops, last + hops - 1).wait()


def start_kernel(n_tensor, *refs):
    attn_ref, ffn_ref, qv_ref, hid_ref, tab_ref, rand, tokens = refs[:7]
    attn_out, ffn_out, hid_out, x_out, q_out, k_out, v_out, mixed_out, lse_out = refs[7:16]
    low, low_z, bias, bias_z, bias_qv, ffn_low, full, xs, qs, ms, k_buf, v_buf, s_buf, ffn_full = refs[16:30]
    (
        z_send,
        z_recv,
        b_send,
        b_recv,
        fz_send,
        fz_recv,
        x_send,
        x_recv,
        g_send,
        g_recv,
        p_send,
        p_recv,
        fg_send,
        fg_recv,
        fp_send,
        fp_recv,
        kv_send,
        kv_recv,
        own_sem,
    ) = refs[30:]
    s, c, t, x, core, sibling, over_x, over_y, across, along_z = places(n_tensor)
    own_cols, own_ff = D // n_tensor, FF // n_tensor
    n_rows = xs.shape[0]

    for m in range(4):
        low[:, m * own_cols : (m + 1) * own_cols] = attn_ref[m].astype(bf16)
    for m in range(2):
        ffn_low[m] = ffn_ref[m].astype(bf16)
    bias[0:2, 0:own_cols] = qv_ref[...]
    bias[2:3, 0:own_ff] = hid_ref[...]

    greet([sibling, over_x, over_y, across] + along_z)

    sent = []

    def put(copy):
        copy.start()
        sent.append(copy)

    half = 2 * own_cols

    def z_hop(path, k, u):
        cols = pl.ds(path * half, half)
        n = path * n_tensor
        return remote(
            low.at[:, cols], low_z.at[u, :, cols], z_send.at[n + k], z_recv.at[n + u], along_z[k]
        )

    for path in range(2):
        for k in range(n_tensor - 1):
            put(z_hop(path, k, t))

    def keep_rows(src, dst, n):
        return pltpu.make_async_copy(src.at[t], dst, x_recv.at[n])

    def swap_rows(src, dst, n):
        return remote(src.at[t], dst, x_send.at[n], x_recv.at[n], across)

    @pl.when(core == c)
    def _():
        keep_rows(tokens, xs, 0).start()

    @pl.when(core != c)
    def _():
        swap_rows(tokens, xs, 0).start()

    low_z[t] = low[...]
    bias_z[t] = bias[...]

    def strip(shard, ctx):
        return pl.ds(pl.multiple_of((2 * shard + ctx) * STRIP, STRIP), STRIP)

    here = strip(s, c)

    def lay_out(path):
        for k, where in enumerate(along_z):
            z_hop(path, k, where[2]).wait_recv()
        for n in range(n_tensor):
            for m in range(2 * path, 2 * path + 2):
                piece = low_z[n, :, m * own_cols : (m + 1) * own_cols]
                full[m, here, n * own_cols : (n + 1) * own_cols] = piece

    far_x, far_y = over_x[0], 1 - c
    labels = ["own", "x", "y", "xy"]
    rows = {
        "own": here,
        "x": strip(far_x, c),
        "y": strip(s, far_y),
        "xy": strip(far_x, far_y),
    }
    far_rows = {
        "own": strip(sibling[0], c),
        "x": strip(2 * (1 - x) + 1 - core, c),
        "y": strip(sibling[0], far_y),
        "xy": strip(2 * (1 - x) + 1 - core, far_y),
    }

    def attn_block(path, at):
        return full.at[pl.ds(2 * path, 2), at, :]

    def ffn_block(path, at):
        return ffn_full.at[path, at, :]

    class Gather:
        def __init__(self, block, ways, gs, gr, ps, pr):
            self.block, self.gs, self.gr, self.ps, self.pr = block, gs, gr, ps, pr
            x_first = (("x", over_x), ("y", over_y))
            self.ways = [x_first if way == 0 else x_first[::-1] for way in ways]

        def hop(self, path, name, label, where):
            n = path * 3 + labels.index(label) - 1
            ref = self.block(path, rows[name])
            return remote(ref, ref, self.gs.at[n], self.gr.at[n], where)

        def give(self, path, name, label, where):
            put(self.hop(path, name, label, where))

        def take(self, path, label):
            self.hop(path, label, label, over_x).wait_recv()

        def share(self, path, name):
            put(self.shared(path, name))

        def take_shared(self, path):
            for n, name in enumerate(labels):
                ref = self.block(path, far_rows[name])
                n = path * 4 + n
                remote(ref, ref, self.ps.at[n], self.pr.at[n], sibling).wait_recv()

        def shared(self, path, name):
            n = path * 4 + labels.index(name)
            ref = self.block(path, rows[name])
            return remote(ref, ref, self.ps.at[n], self.pr.at[n], sibling)

        def again(self, path, number):
            near, far = self.ways[path]
            if number == 1:
                sent.append(self.hop(path, near[0], "xy", far[1]))
            sent.append(self.shared(path, {1: near[0], 2: far[0], 3: "xy"}[number]))

        def step(self, path, number):
            near, far = self.ways[path]
            if number == 0:
                self.give(path, "own", near[0], near[1])
                self.give(path, "own", far[0], far[1])
                self.share(path, "own")
            elif number == 1:
                self.take(path, near[0])
                self.give(path, near[0], "xy", far[1])
                self.share(path, near[0])
            elif number == 2:
                self.take(path, far[0])
                self.share(path, far[0])
            else:
                self.take(path, "xy")
                self.share(path, "xy")

    attn = Gather(attn_block, (1, 1), g_send, g_recv, p_send, p_recv)
    ffn = Gather(ffn_block, (0, 1), fg_send, fg_recv, fp_send, fp_recv)

    def ffn_cols(path, u):
        return ffn_full.at[path, here, pl.ds(pl.multiple_of(u * own_ff, own_ff), own_ff)]

    def ffn_hop(path, k, u):
        n = path * n_tensor
        return remote(
            ffn_low.at[path],
            ffn_cols(path, u),
            fz_send.at[n + k],
            fz_recv.at[n + u],
            along_z[k],
        )

    local = []

    def write(src, dst, n):
        copy = pltpu.make_async_copy(src, dst, own_sem.at[n])
        copy.start()
        local.append(copy)

    def ffn_along_z(path):
        for k in range(n_tensor - 1):
            put(ffn_hop(path, k, t))
        write(ffn_low.at[path], ffn_cols(path, t), 5 + path)

    def ffn_ready(path):
        for k, where in enumerate(along_z):
            ffn_hop(path, k, where[2]).wait_recv()
        local[path].wait()
        ffn.step(path, 0)

    lay_out(0)
    attn.step(0, 0)
    lay_out(1)
    attn.step(1, 0)
    ffn_along_z(0)
    ffn_along_z(1)
    for k, where in enumerate(along_z):
        put(remote(bias, bias_z.at[t], b_send.at[k], b_recv.at[t], where))
    attn.step(0, 1)
    attn.step(1, 1)
    ffn_ready(0)
    attn.step(0, 2)
    attn.step(1, 2)
    attn.step(0, 3)
    attn.step(1, 3)
    for k, where in enumerate(along_z):
        u = where[2]
        remote(bias, bias_z.at[u], b_send.at[k], b_recv.at[u], where).wait_recv()
    for n in range(n_tensor):
        cols = slice(n * own_cols, (n + 1) * own_cols)
        bias_qv[0:2, cols] = bias_z[n, 0:2, 0:own_cols]
        hid_out[:, n * own_ff : (n + 1) * own_ff] = bias_z[n, 2:3, 0:own_ff]

    @pl.when(core == c)
    def _():
        keep_rows(tokens, xs, 0).wait()

    @pl.when(core != c)
    def _():
        swap_rows(tokens, xs, 0).wait()

    chunk = 256
    chunks = n_rows // chunk
    per = chunk // BLOCK

    def kv_hop(buf, i, n):
        at, to = pl.ds(i * per, per), pl.ds(n_rows // BLOCK + i * per, per)
        return remote(buf.at[at], buf.at[to], kv_send.at[n], kv_recv.at[n], sibling)

    attn.take_shared(0)
    for i in range(chunks):
        at = pl.ds(i * chunk, chunk)
        k = matmul(xs[at, :], full[1]).astype(bf16)
        k_buf[pl.ds(i * per, per)] = k.reshape(per, BLOCK, D)
        put(kv_hop(k_buf, i, i))
    for i in range(chunks):
        at = pl.ds(i * chunk, chunk)
        q = matmul(xs[at, :], full[0]) + bias_qv[0:1, :]
        qs[at, :] = (q.astype(bf16).astype(f32) * 0.125).astype(bf16)
    attn.take_shared(1)
    for i in range(chunks):
        at = pl.ds(i * chunk, chunk)
        v = (matmul(xs[at, :], full[2]) + bias_qv[1:2, :]).astype(bf16)
        v_buf[pl.ds(i * per, per)] = v.reshape(per, BLOCK, D)
        put(kv_hop(v_buf, i, chunks + i))
    write(xs, x_out, 0)
    write(qs, q_out, 1)
    write(full, attn_out, 2)
    for i in range(chunks):
        kv_hop(k_buf, i, i).wait_recv()
        kv_hop(v_buf, i, chunks + i).wait_recv()
    write(k_buf, k_out, 3)
    write(v_buf, v_out, 4)
    ffn_ready(1)
    ffn.step(0, 1)

    nb = n_rows // BLOCK
    first = core * nb
    stops = {1: [(1, 1), (0, 2)], 3: [(1, 2)], 10: [(0, 3), (1, 3)]}

    @pl.loop(0, nb)
    def _(blk):
        at = pl.ds(pl.multiple_of(blk * BLOCK, BLOCK), BLOCK)
        forward_block(
            qs.at[at],
            ms.at[at],
            lse_out.at[blk],
            k_buf,
            v_buf,
            s_buf,
            tab_ref,
            rand,
            blk * (LISTED - 5),
            blk,
            first,
            0,
        )

        for at_block, moves in stops.items():

            @pl.when(blk == at_block)
            def _():
                mark = len(sent)
                for path, number in moves:
                    ffn.step(path, number)
                del sent[mark:]

    write(ms, mixed_out, 7)
    for path, number in [move for moves in stops.values() for move in moves]:
        ffn.again(path, number)
    for path in range(2):
        ffn.take_shared(path)
        write(ffn_full.at[path], ffn_out.at[path], 8 + path)

    for copy in sent:
        copy.wait_send()
    for copy in local[2:]:
        copy.wait()


def start(n_tensor, attn_w, ffn_w, qv_bias, hid_bias, table, rand, tokens):
    rows = tokens.shape[1]
    own_ff = FF // n_tensor
    dma = pltpu.SemaphoreType.DMA
    vmem, anywhere = pl.BlockSpec(memory_space=pltpu.VMEM), pl.BlockSpec(memory_space=pl.ANY)
    smem = pl.BlockSpec(memory_space=pltpu.SMEM)
    tall = jax.ShapeDtypeStruct((rows, D), bf16)
    both = jax.ShapeDtypeStruct((2 * rows // BLOCK, BLOCK, D), bf16)
    items = 2 * (rows // 256)
    return pl.pallas_call(
        partial(start_kernel, n_tensor),
        out_shape=[
            jax.ShapeDtypeStruct((4, D, D), bf16),
            jax.ShapeDtypeStruct((2, D, FF), bf16),
            jax.ShapeDtypeStruct((1, FF), f32),
            tall,
            tall,
            both,
            both,
            tall,
            jax.ShapeDtypeStruct((rows // BLOCK, 8, ROWS), f32),
        ],
        in_specs=[vmem] * 5 + [smem, anywhere],
        out_specs=[anywhere, anywhere, vmem] + [anywhere] * 5 + [vmem],
        scratch_shapes=[
            pltpu.VMEM((STRIP, D), bf16),
            pltpu.VMEM((n_tensor, STRIP, D), bf16),
            pltpu.VMEM((8, D), f32),
            pltpu.VMEM((n_tensor, 8, D), f32),
            pltpu.VMEM((8, D), f32),
            pltpu.VMEM((2, STRIP, own_ff), bf16),
            pltpu.VMEM((4, D, D), bf16),
            pltpu.VMEM((rows, D), bf16),
            pltpu.VMEM((rows, D), bf16),
            pltpu.VMEM((rows, D), bf16),
            pltpu.VMEM((2 * rows // BLOCK, BLOCK, D), bf16),
            pltpu.VMEM((2 * rows // BLOCK, BLOCK, D), bf16),
            pltpu.VMEM((2 * rows // KEYS, ROWS, KEYS), f32),
            pltpu.VMEM((2, D, FF), bf16),
            dma((2 * n_tensor,)),
            dma((2 * n_tensor,)),
            dma((n_tensor,)),
            dma((n_tensor,)),
            dma((2 * n_tensor,)),
            dma((2 * n_tensor,)),
            dma((2,)),
            dma((2,)),
            dma((6,)),
            dma((6,)),
            dma((8,)),
            dma((8,)),
            dma((6,)),
            dma((6,)),
            dma((8,)),
            dma((8,)),
            dma((items,)),
            dma((items,)),
            dma((10,)),
        ],
        compiler_params=pltpu.CompilerParams(
            collective_id=2, has_side_effects=True, vmem_limit_bytes=VMEM_LIMIT
        ),
        cost_estimate=pl.CostEstimate(
            flops=6 * rows * D * D, bytes_accessed=100 * 2**20, transcendentals=0
        ),
        name="start",
    )(attn_w, ffn_w, qv_bias, hid_bias.reshape(1, own_ff), table, rand, tokens)


def middle_kernel(n_tensor, *refs):
    x_ref, mixed_ref, hid_ref, vec_ref, cotangent, attn_full, ffn_full = refs[:7]
    out_a, out_b, dw1, dw2, dwo, gh1, gm, hid_out, sums_out = refs[7:16]
    w, wo, act, slope, h1, total, gs_low, low_t, turned, pre, dw_s, cot, ready, low, down, held = refs[16:32]
    (
        w_sem,
        c_send,
        c_recv,
        h_send,
        h_recv,
        up_send,
        up_recv,
        dn_send,
        dn_recv,
        dw_sem,
        own_sem,
        copied,
    ) = refs[32:]
    s, c, t, x, core, sibling, over_x, over_y, across, along_z = places(n_tensor)
    n_rows = x_ref.shape[0]
    chunk = 256
    chunks = n_rows // chunk
    steps = FF // D
    items, all_items = LINE_ITEMS, n_rows // ITEM
    last = n_tensor - 1

    def block(i):
        return pl.ds(pl.multiple_of(i * D, D), D)

    fetch_o = pltpu.make_async_copy(attn_full.at[3], wo, w_sem.at[2 * steps])
    fetch_o.start()

    def fetch(m, i):
        at = w.at[m, :, block(i)]
        return pltpu.make_async_copy(ffn_full.at[m, :, block(i)], at, w_sem.at[m * steps + i])

    for i in range(steps):
        for m in range(2):
            fetch(m, i).start()

    greet([over_y, across] + along_z)

    def keep_cot(i):
        at = pl.ds(i * chunk, chunk)
        return pltpu.make_async_copy(cotangent.at[t, at], cot.at[at], c_recv.at[i])

    def swap_cot(i):
        at = pl.ds(i * chunk, chunk)
        return remote(cotangent.at[t, at], cot.at[at], c_send.at[i], c_recv.at[i], across)

    def home_ref(i):
        if i < items:
            return held.at[t, pl.ds(i * ITEM, ITEM)]
        return out_b.at[pl.ds((i - items) * ITEM, ITEM)]

    def keep_home(i):
        return pltpu.make_async_copy(ready.at[pl.ds(i * ITEM, ITEM)], home_ref(i), h_recv.at[i])

    def send_home(i):
        src = ready.at[pl.ds(i * ITEM, ITEM)]
        return remote(src, home_ref(i), h_send.at[i], h_recv.at[i], across)

    def if_home(at_home, away):
        @pl.when(core == c)
        def _():
            at_home()

        @pl.when(core != c)
        def _():
            away()

    if_home(lambda: keep_cot(0).start(), lambda: swap_cot(0).start())

    up, down_line = (up_send, up_recv), (dn_send, dn_recv)
    chain = Line(s, c, t, last, items, ITEM, held, out_a, up, down_line, copied)

    def own_ready(i):
        if_home(lambda: keep_home(i).wait(), lambda: send_home(i).wait_recv())

    events = {
        (1, 1): ([0], []),
        (2, 1): ([1], []),
        (2, 2): ([2], []),
        (2, 3): ([], [0]),
        (3, 1): ([3], [1]),
        (3, 3): ([], [2]),
    }
    sizes = [ITEM] + [chunk] * (chunks - 1) + [chunk - ITEM]
    start_row = 0
    for i, size in enumerate(sizes):
        rows = slice(start_row, start_row + size)
        top = slice(0, size)
        if i == 0:
            fetch_o.wait()
        pre1 = x_ref[rows, :].astype(f32) + matmul_nt(mixed_ref[rows, :], wo[...])
        pre1 = pre1 + vec_ref[4:5, :]
        h1[rows, :] = pre1
        unit, _scale = norm_parts(pre1)
        first = unit * vec_ref[0:1, :] + vec_ref[1:2, :]
        low[top, :] = first.astype(bf16)
        down[top, :] = first + vec_ref[5:6, :]

        @pl.loop(0, steps)
        def _(j):
            if i == 0:
                fetch(0, j).wait()
                fetch(1, j).wait()
            for (at_chunk, at_step), (own, passing) in events.items():
                if at_chunk != i:
                    continue

                @pl.when(j == at_step)
                def _():
                    for n in own:
                        own_ready(n)
                        chain.send_own(n)
                    for n in passing:
                        chain.tick(n)

            hidden = matmul(low[top, :], w[0, :, block(j)]) + hid_ref[:, block(j)]
            act_now, slope_now = gelu_and_slope(hidden)
            act_now = act_now.astype(bf16)
            act[rows, block(j)] = act_now
            slope[rows, block(j)] = slope_now.astype(bf16)
            down[top, :] += matmul_nt(act_now, w[1, :, block(j)])

        second = down[top, :]
        total[rows, :] = second
        unit, _scale = norm_parts(second)
        ready[rows, :] = (unit * vec_ref[2:3, :] + vec_ref[3:4, :]).astype(bf16)
        for n in range(start_row // ITEM, (start_row + size) // ITEM):
            if_home(lambda: keep_home(n).start(), lambda: send_home(n).start())
        if i + 1 < chunks:
            if_home(lambda: keep_cot(i + 1).start(), lambda: swap_cot(i + 1).start())
        start_row += size
    chain.tick(3)
    chain.tick(4)

    sums_out[...] = jnp.zeros_like(sums_out)

    @pl.loop(0, chunks)
    def _(i):
        rows = pl.ds(pl.multiple_of(i * chunk, chunk), chunk)
        if_home(lambda: keep_cot(i).wait(), lambda: swap_cot(i).wait())
        unit, scale = norm_parts(total[rows, :])
        grad_out = cot[rows, :].astype(f32)
        grad = norm_back(grad_out, unit, scale, vec_ref[2:3, :])
        sums_out[2:3, :] += column_total(grad_out * unit)
        sums_out[3:4, :] += column_total(grad_out)
        total[rows, :] = grad
        grad_low = grad.astype(bf16)
        gs_low[rows, :] = grad_low
        sums_out[5:6, :] += column_total(grad_low)
        turned[:, rows] = grad.T.astype(bf16)
        unit, _scale = norm_parts(h1[rows, :])
        first = unit * vec_ref[0:1, :] + vec_ref[1:2, :]
        low_t[:, rows] = first.T.astype(bf16)

    chain.tick(5)
    part = D // 4

    def dw_copy(slot, m, j):
        return pltpu.make_async_copy(
            dw_s.at[slot, m], (dw1, dw2)[m].at[:, block(j)], dw_sem.at[2 * slot + m]
        )

    ticks = {0: [6, 7], 1: [8, 9], 2: [10, 11]}

    @pl.loop(0, steps)
    def _(j):
        slot = lax.rem(j, 2)
        for i in range(chunks):
            rows = slice(i * chunk, (i + 1) * chunk)
            grad_act = matmul(gs_low[rows, :], w[1, :, block(j)]).astype(bf16).astype(f32)
            grad_pre = (grad_act * slope[rows, block(j)].astype(f32)).astype(bf16)
            pre[rows, :] = grad_pre
            total[rows, :] += matmul_nt(grad_pre, w[0, :, block(j)])
        hid_out[:, block(j)] = column_total(pre[...])

        @pl.when(j >= 2)
        def _():
            for m in range(2):
                dw_copy(slot, m, j - 2).wait()

        for n in range(4):
            out = slice(n * part, (n + 1) * part)
            dw_s[slot, 0, out, :] = matmul(low_t[out, :], pre[...]).astype(bf16)
            dw_s[slot, 1, out, :] = matmul(turned[out, :], act[:, block(j)]).astype(bf16)
        for m in range(2):
            dw_copy(slot, m, j).start()
        for at, numbers in ticks.items():

            @pl.when(j == at)
            def _():
                for n in numbers:
                    chain.tick(n)

    gm_s = gs_low

    @pl.loop(0, chunks)
    def _(i):
        rows = pl.ds(pl.multiple_of(i * chunk, chunk), chunk)
        unit, scale = norm_parts(h1[rows, :])
        grad_first = total[rows, :]
        grad_h1 = norm_back(grad_first, unit, scale, vec_ref[0:1, :])
        total[rows, :] = grad_h1
        grad_low = grad_h1.astype(bf16)
        gm_s[rows, :] = matmul(grad_low, wo[...]).astype(bf16)
        turned[:, rows] = grad_h1.T.astype(bf16)
        sums_out[0:1, :] += column_total(grad_first * unit)
        sums_out[1:2, :] += column_total(grad_first)
        sums_out[4:5, :] += column_total(grad_low)

    local = [
        pltpu.make_async_copy(total, gh1, own_sem.at[0]),
        pltpu.make_async_copy(gm_s, gm, own_sem.at[1]),
    ]
    for copy in local:
        copy.start()
    for j in range(steps - 2, steps):
        for m in range(2):
            dw_copy(j % 2, m, j).wait()

    @pl.loop(0, 4)
    def _(n):
        out = pl.ds(pl.multiple_of(n * part, part), part)
        dw_s[0, 0, out, :] = matmul(turned[out, :], mixed_ref[...]).astype(bf16)

    local.append(pltpu.make_async_copy(dw_s.at[0, 0], dwo, own_sem.at[2]))
    local[-1].start()
    for i in range(items, all_items):
        own_ready(i)
    for i in range(all_items):

        @pl.when(core != c)
        def _():
            send_home(i).wait_send()

    chain.settle()
    for copy in local:
        copy.wait()


def middle(n_tensor, x, mixed, hid_all, vec_par, cotangent, attn_full, ffn_full):
    rows = x.shape[0]
    steps = FF // D
    items, all_items = LINE_ITEMS, rows // ITEM
    dma = pltpu.SemaphoreType.DMA
    vmem, anywhere = pl.BlockSpec(memory_space=pltpu.VMEM), pl.BlockSpec(memory_space=pl.ANY)
    low, wide = pltpu.VMEM((rows, D), bf16), pltpu.VMEM((rows, D), f32)
    return pl.pallas_call(
        partial(middle_kernel, n_tensor),
        out_shape=[
            jax.ShapeDtypeStruct((n_tensor, items * ITEM, D), bf16),
            jax.ShapeDtypeStruct((rows - items * ITEM, D), bf16),
            jax.ShapeDtypeStruct((D, FF), bf16),
            jax.ShapeDtypeStruct((D, FF), bf16),
            jax.ShapeDtypeStruct((D, D), bf16),
            jax.ShapeDtypeStruct((rows, D), f32),
            jax.ShapeDtypeStruct((rows, D), bf16),
            jax.ShapeDtypeStruct((1, FF), f32),
            jax.ShapeDtypeStruct((8, D), f32),
        ],
        in_specs=[vmem] * 4 + [anywhere] * 3,
        out_specs=[anywhere] * 7 + [vmem] * 2,
        scratch_shapes=[
            pltpu.VMEM((2, D, FF), bf16),
            pltpu.VMEM((D, D), bf16),
            pltpu.VMEM((rows, FF), bf16),
            pltpu.VMEM((rows, FF), bf16),
            wide,
            wide,
            low,
            pltpu.VMEM((D, rows), bf16),
            pltpu.VMEM((D, rows), bf16),
            low,
            pltpu.VMEM((2, 2, D, D), bf16),
            low,
            low,
            pltpu.VMEM((256, D), bf16),
            pltpu.VMEM((256, D), f32),
            pltpu.VMEM((n_tensor, items * ITEM, D), bf16),
            dma((2 * steps + 1,)),
            dma((rows // 256,)),
            dma((rows // 256,)),
            dma((all_items,)),
            dma((all_items,)),
            dma((items * n_tensor,)),
            dma((items * n_tensor,)),
            dma((items * n_tensor,)),
            dma((items * n_tensor,)),
            dma((4,)),
            dma((3,)),
            dma((2 * n_tensor - 1,)),
        ],
        compiler_params=pltpu.CompilerParams(
            collective_id=3, has_side_effects=True, vmem_limit_bytes=VMEM_LIMIT
        ),
        cost_estimate=pl.CostEstimate(
            flops=2 * rows * D * (3 * D + 6 * FF),
            bytes_accessed=60 * 2**20,
            transcendentals=2 * rows * FF,
        ),
        name="middle",
    )(x, mixed, hid_all, vec_par, cotangent, attn_full, ffn_full)


def finish_kernel(n_tensor, *refs):
    dq, dk_own, dk_far, dv_own, dv_far, gh1, x_ref, weights = refs[:8]
    dw1, dw2, dwo, vec_sums, hid_sums = refs[8:13]
    attn_out, ffn_out, vec_out, qv_out, hid_out, tokens_out = refs[13:19]
    (
        dk,
        dv,
        xs,
        held,
        x_t,
        partial_sum,
        ready,
        dws,
        acc,
        got0,
        got1a,
        got1b,
        got2,
        zf,
        zf_got,
        za,
        za_got,
        run,
        run_got,
        run_z,
        wts,
    ) = refs[19:40]
    (
        e_send,
        e_recv,
        own_sem,
        s0,
        r0,
        s1,
        r1,
        s2,
        r2,
        zf_send,
        zf_recv,
        za_send,
        za_recv,
        sm,
        rm,
        h_send,
        h_recv,
        up_send,
        up_recv,
        dn_send,
        dn_recv,
        w_sem,
        copied,
    ) = refs[40:]
    s, c, t, x, core, sibling, over_x, over_y, across, along_z = places(n_tensor)
    n_rows = dq.shape[0]
    rows_each = n_rows // PIECES
    last = n_tensor - 1

    def pieces(path, i):
        if i < 2:
            return [(dw1 if path == 0 else dw2, i * WIDE, WIDE, 0)]
        if path == 0:
            return [(dws.at[0], 0, D, 0), (dws.at[1], 0, D, D)]
        return [(dws.at[2], 0, D, 0), (dwo, 0, D, D)]

    def slot(path, i):
        return path * 3 + i

    order = [(path, i) for i in range(3) for path in range(2)]

    def rows_of(xx, cc):
        return pl.ds(pl.multiple_of((4 * xx + 2 * cc) * STRIP, 2 * STRIP), 2 * STRIP)

    own, first = {}, {}
    for path, i in order:
        k = slot(path, i)
        own[k], first[k] = [], []
        for xx in range(2):
            for j, (ref, col, width, at) in enumerate(pieces(path, i)):
                n = (k * 2 + xx) * 2 + j
                cols, to = pl.ds(col, width), pl.ds(at, width)
                own[k].append(
                    pltpu.make_async_copy(
                        ref.at[rows_of(xx, core), cols], acc.at[k, xx, :, to], own_sem.at[n]
                    )
                )
                first[k].append(
                    remote(
                        ref.at[rows_of(xx, 1 - core), cols],
                        got0.at[k, xx, :, to],
                        s0.at[n],
                        r0.at[n],
                        sibling,
                    )
                )

    def start_own(i):
        for path in range(2):
            for copy in own[slot(path, i)]:
                copy.start()

    def start_first(i):
        for path in range(2):
            for copy in first[slot(path, i)]:
                copy.start()

    fetches = [
        pltpu.make_async_copy(gh1, partial_sum, w_sem.at[1]),
        pltpu.make_async_copy(weights.at[pl.ds(0, 3)], wts, w_sem.at[0]),
        pltpu.make_async_copy(x_ref, xs, w_sem.at[2]),
    ]
    for copy in fetches:
        copy.start()
    start_own(0)
    start_own(1)
    greet([sibling, over_x, over_y, across] + along_z)

    chunk = 256
    chunks = n_rows // chunk

    def exchange(i, n):
        at = pl.ds(i * chunk, chunk)
        src, dst = ((dk_far, dk), (dv_far, dv))[n]
        k = 2 * i + n
        return remote(src.at[at], dst.at[at], e_send.at[k], e_recv.at[k], sibling)

    swaps = [exchange(i, n) for i in range(chunks) for n in range(2)]
    for copy in swaps:
        copy.start()
    start_first(0)
    fetches[0].wait()
    fetches[1].wait()

    run[0] = jnp.zeros(run.shape[1:], f32)
    run[0, 0:6, :] = vec_sums[0:6, :]
    for n in range(FF // D):
        run[0, 8 + n : 9 + n, :] = hid_sums[:, n * D : (n + 1) * D]

    def keep_home(i):
        at = pl.ds(i * rows_each, rows_each)
        return pltpu.make_async_copy(ready.at[at], held.at[t, at], h_recv.at[i])

    def send_home(i):
        at = pl.ds(i * rows_each, rows_each)
        return remote(ready.at[at], held.at[t, at], h_send.at[i], h_recv.at[i], across)

    chain = Line(
        s,
        c,
        t,
        last,
        PIECES,
        rows_each,
        held,
        tokens_out,
        (up_send, up_recv),
        (dn_send, dn_recv),
        copied,
    )
    tick = chain.tick

    def send_own(i):
        @pl.when(core == c)
        def _():
            keep_home(i).wait()

        @pl.when(core != c)
        def _():
            send_home(i).wait_recv()

        chain.send_own(i)

    for i in range(PIECES):
        at = slice(i * rows_each, (i + 1) * rows_each)
        if i * rows_each % chunk == 0:
            for n in range(2):
                exchange(i * rows_each // chunk, n).wait_recv()
        dk_piece = (dk_own[at, :].astype(f32) + dk[at, :].astype(f32)).astype(bf16)
        dv_piece = (dv_own[at, :].astype(f32) + dv[at, :].astype(f32)).astype(bf16)
        dk[at, :] = dk_piece
        dv[at, :] = dv_piece
        total = partial_sum[at, :] + matmul_nt(dq[at, :], wts[0])
        total = total + matmul_nt(dk_piece, wts[1]) + matmul_nt(dv_piece, wts[2])
        ready[at, :] = total.astype(bf16)

        @pl.when(core == c)
        def _():
            keep_home(i).start()

        @pl.when(core != c)
        def _():
            send_home(i).start()

        if i > 0:
            send_own(i - 1)

    def add_rows(target, source, count):
        @pl.loop(0, count // 16)
        def _(j):
            rows = pl.ds(pl.multiple_of(j * 16, 16), 16)
            total = target[rows, :].astype(f32) + source[rows, :].astype(f32)
            target[rows, :] = total.astype(bf16)

    def half(cc):
        return pl.ds(pl.multiple_of(cc * STRIP, STRIP), STRIP)

    second, third = {}, {}

    def stage1(path, i):
        k = slot(path, i)
        for copy in own[k]:
            copy.wait()
        for copy in first[k]:
            copy.wait_recv()
        for xx in range(2):
            add_rows(acc.at[k, xx], got0.at[k, xx], 2 * STRIP)
        if path == 0:
            second[k] = remote(acc.at[k, 1 - x], got1a.at[i], s1.at[k], r1.at[k], over_x)
        else:
            second[k] = remote(
                acc.at[k, :, half(1 - c), :], got1b.at[i], s1.at[k], r1.at[k], over_y
            )
        second[k].start()

    def stage2(path, i):
        k = slot(path, i)
        second[k].wait_recv()
        if path == 0:
            add_rows(acc.at[k, x], got1a.at[i], 2 * STRIP)
            third[k] = remote(
                acc.at[k, x, half(1 - c), :], got2.at[k], s2.at[k], r2.at[k], over_y
            )
        else:
            for xx in range(2):
                add_rows(acc.at[k, xx, half(c), :], got1b.at[i, xx], STRIP)
            third[k] = remote(
                acc.at[k, 1 - x, half(c), :], got2.at[k], s2.at[k], r2.at[k], over_x
            )
        third[k].start()

    own_cols = D // n_tensor
    own_ff = FF // n_tensor
    per = WIDE // own_ff

    def stage3(path, i):
        k = slot(path, i)
        third[k].wait_recv()

        @pl.loop(0, STRIP // 16)
        def _(j):
            rows = pl.ds(pl.multiple_of(j * 16, 16), 16)
            here = pl.ds(pl.multiple_of(c * STRIP + j * 16, 16), 16)
            total = acc[k, x, here, :].astype(f32) + got2[k, rows, :].astype(f32)
            if i < 2:
                for n in range(per):
                    piece = total[:, n * own_ff : (n + 1) * own_ff].astype(bf16)
                    zf[per * i + n, rows, path * own_ff : (path + 1) * own_ff] = piece
            else:
                for n in range(n_tensor):
                    for m in range(2):
                        at = m * D + n * own_cols
                        to = (2 * path + m) * own_cols
                        piece = total[:, at : at + own_cols].astype(bf16)
                        za[n, rows, to : to + own_cols] = piece

    z_sent = []

    def z_step(k, buf, got, send, recv):
        @pl.when(t == k)
        def _():
            for d in range(last, k, -1):
                if k > 0:
                    hop(buf, got, send, recv, d, 0, k - 1).wait_recv()
                    add_rows(buf.at[d], got.at[0, d], STRIP)
                hop(buf, got, send, recv, d, 0, k + 1).start()

        @pl.when(t == last - k)
        def _():
            for d in range(0, last - k):
                if k > 0:
                    hop(buf, got, send, recv, d, 1, last - k + 1).wait_recv()
                    add_rows(buf.at[d], got.at[1, d], STRIP)
                hop(buf, got, send, recv, d, 1, last - k - 1).start()

    def hop(buf, got, send, recv, d, way, to):
        n = way * n_tensor + d
        return remote(buf.at[d], got.at[way, d], send.at[n], recv.at[n], (s, c, to))

    def z_collect(buf, got, send, recv, emit):
        @pl.when(t > 0)
        def _():
            hop(buf, got, send, recv, t, 0, t - 1).wait_recv()
            add_rows(buf.at[t], got.at[0, t], STRIP)

        @pl.when(t < last)
        def _():
            hop(buf, got, send, recv, t, 1, t + 1).wait_recv()
            add_rows(buf.at[t], got.at[1, t], STRIP)

        @pl.loop(0, STRIP // 16)
        def _(j):
            rows = pl.ds(pl.multiple_of(j * 16, 16), 16)
            emit(rows, buf[t, rows, :].astype(f32))

    def z_settle(buf, got, send, recv):
        for d in range(n_tensor):

            @pl.when(t < d)
            def _():
                hop(buf, got, send, recv, d, 0, t + 1).wait_send()

            @pl.when(t > d)
            def _():
                hop(buf, got, send, recv, d, 1, t - 1).wait_send()

    ffn_z = (zf, zf_got, zf_send, zf_recv)
    attn_z = (za, za_got, za_send, za_recv)

    small = []

    def small_send(n, where):
        small.append(remote(run.at[n], run_got.at[n], sm.at[n], rm.at[n], where))
        small[n].start()

    def small_add(n):
        small[n].wait_recv()
        run[n + 1] = run[n] + run_got[n]

    start_first(1)
    fetches[2].wait()
    for i in range(chunks):
        at = slice(i * chunk, (i + 1) * chunk)
        x_t[:, at] = xs[at, :].T
    dws[0] = matmul(x_t[...], dq[...]).astype(bf16)
    send_own(7)
    dws[1] = matmul(x_t[...], dk[...]).astype(bf16)
    dws[2] = matmul(x_t[...], dv[...]).astype(bf16)
    start_own(2)
    start_first(2)
    run[0, 6:7, :] = column_total(dq[...])
    run[0, 7:8, :] = column_total(dv[...])
    small_send(0, sibling)
    stage1(0, 0)
    stage1(1, 0)
    stage1(0, 1)
    stage1(1, 1)
    tick(0)
    stage1(0, 2)
    stage1(1, 2)
    small_add(0)
    small_send(1, over_x)
    tick(1)
    tick(2)
    tick(3)
    stage2(0, 0)
    stage2(1, 0)
    tick(4)
    tick(5)
    small_add(1)
    small_send(2, over_y)
    tick(6)
    stage2(0, 1)
    stage2(1, 1)
    tick(7)
    tick(8)
    small_add(2)
    run_z[t] = run[3]
    for k, where in enumerate(along_z):
        copy = remote(run.at[3], run_z.at[t], sm.at[3 + k], rm.at[3 + t], where)
        copy.start()
        z_sent.append(copy)
    stage3(0, 0)
    stage3(1, 0)
    stage2(0, 2)
    stage2(1, 2)
    tick(9)
    tick(10)
    stage3(0, 1)
    stage3(1, 1)
    z_step(0, *ffn_z)
    tick(11)
    tick(12)
    z_step(1, *ffn_z)
    stage3(0, 2)
    stage3(1, 2)
    z_step(0, *attn_z)
    tick(13)
    tick(14)
    z_step(2, *ffn_z)
    z_step(1, *attn_z)
    tick(15)
    tick(16)
    z_step(2, *attn_z)
    for j in range(17, PIECES * last):
        tick(j)

    for k, where in enumerate(along_z):
        u = where[2]
        remote(run.at[3], run_z.at[u], sm.at[3 + k], rm.at[3 + u], where).wait_recv()
    total = run_z[0]
    for n in range(1, n_tensor):
        total = total + run_z[n]
    vec_out[...] = total[0:6, :]
    for n in range(n_tensor):

        @pl.when(t == n)
        def _():
            qv_out[...] = total[6:8, n * own_cols : (n + 1) * own_cols]
            hid_out[...] = total[8 + n : 9 + n, :]


    def emit_ffn(rows, total):
        for m in range(2):
            ffn_out[m, rows, :] = total[:, m * own_ff : (m + 1) * own_ff]

    def emit_attn(rows, total):
        for m in range(4):
            attn_out[m, rows, :] = total[:, m * own_cols : (m + 1) * own_cols]

    z_collect(*ffn_z, emit_ffn)
    z_collect(*attn_z, emit_attn)
    z_settle(*ffn_z)
    z_settle(*attn_z)

    for copy in swaps:
        copy.wait_send()
    for path, i in order:
        k = slot(path, i)
        for copy in first[k]:
            copy.wait_send()
        second[k].wait_send()
        third[k].wait_send()
    for copy in small + z_sent:
        copy.wait_send()

    @pl.when(core != c)
    def _():
        for i in range(PIECES):
            send_home(i).wait_send()

    chain.settle()


def finish_all(n_tensor, grads, gh1, x, attn_full, dws, sums):
    rows = x.shape[0]
    own_cols, own_ff = D // n_tensor, FF // n_tensor
    dma = pltpu.SemaphoreType.DMA
    vmem, anywhere = pl.BlockSpec(memory_space=pltpu.VMEM), pl.BlockSpec(memory_space=pl.ANY)
    dq, dk_own, dk_far, dv_own, dv_far = grads
    tall = pltpu.VMEM((rows, D), bf16)
    items = PIECES * (n_tensor - 1)
    return pl.pallas_call(
        partial(finish_kernel, n_tensor),
        out_shape=[
            jax.ShapeDtypeStruct((4, STRIP, own_cols), f32),
            jax.ShapeDtypeStruct((2, STRIP, own_ff), f32),
            jax.ShapeDtypeStruct((6, D), f32),
            jax.ShapeDtypeStruct((2, own_cols), f32),
            jax.ShapeDtypeStruct((1, own_ff), f32),
            jax.ShapeDtypeStruct((n_tensor, rows, D), bf16),
        ],
        in_specs=[vmem, vmem, anywhere, vmem, anywhere] + [anywhere] * 6
        + [vmem] * 2,
        out_specs=[vmem] * 5 + [anywhere],
        scratch_shapes=[
            tall,
            tall,
            tall,
            pltpu.VMEM((n_tensor, rows, D), bf16),
            pltpu.VMEM((D, rows), bf16),
            pltpu.VMEM((rows, D), f32),
            tall,
            pltpu.VMEM((3, D, D), bf16),
            pltpu.VMEM((6, 2, 2 * STRIP, WIDE), bf16),
            pltpu.VMEM((6, 2, 2 * STRIP, WIDE), bf16),
            pltpu.VMEM((3, 2 * STRIP, WIDE), bf16),
            pltpu.VMEM((3, 2, STRIP, WIDE), bf16),
            pltpu.VMEM((6, STRIP, WIDE), bf16),
            pltpu.VMEM((n_tensor, STRIP, 2 * own_ff), bf16),
            pltpu.VMEM((2, n_tensor, STRIP, 2 * own_ff), bf16),
            pltpu.VMEM((n_tensor, STRIP, 4 * own_cols), bf16),
            pltpu.VMEM((2, n_tensor, STRIP, 4 * own_cols), bf16),
            pltpu.VMEM((4, 16, D), f32),
            pltpu.VMEM((3, 16, D), f32),
            pltpu.VMEM((n_tensor, 16, D), f32),
            pltpu.VMEM((3, D, D), bf16),
            dma((2 * rows // 256,)),
            dma((2 * rows // 256,)),
            dma((24,)),
            dma((24,)),
            dma((24,)),
            dma((6,)),
            dma((6,)),
            dma((6,)),
            dma((6,)),
            dma((2 * n_tensor,)),
            dma((2 * n_tensor,)),
            dma((2 * n_tensor,)),
            dma((2 * n_tensor,)),
            dma((3 + n_tensor,)),
            dma((3 + n_tensor,)),
            dma((PIECES,)),
            dma((PIECES,)),
            dma((items + PIECES,)),
            dma((items + PIECES,)),
            dma((items + PIECES,)),
            dma((items + PIECES,)),
            dma((3,)),
            dma((2 * n_tensor - 1,)),
        ],
        compiler_params=pltpu.CompilerParams(
            collective_id=1, has_side_effects=True, vmem_limit_bytes=VMEM_LIMIT
        ),
        cost_estimate=pl.CostEstimate(
            flops=12 * rows * D * D, bytes_accessed=400 * 2**20, transcendentals=0
        ),
        name="finish",
    )(dq, dk_own, dk_far, dv_own, dv_far, gh1, x, attn_full, *dws, *sums)


GROUP_RATES = (
    [2.0 / D**0.5] * 3 + [2.0 / (D // (4 * BLOCK)) ** 0.5],
    [2.0 / D**0.5, 2.0 / FF**0.5],
)


def last_kernel(tokens_ref, out_b, _output_a, *refs):
    attn_g, attn_w, attn_m, attn_v, ffn_g, ffn_w, ffn_m, ffn_v = refs[:8]
    plain = [refs[8 + 4 * n : 12 + 4 * n] for n in range(3)]
    tokens_out, output = refs[20:22]
    attn_moment, attn_square, out_states, attn_new, attn_copy = refs[22:27]
    ffn_moment, ffn_square, ffn_new, ffn_copy = refs[27:31]
    plain_out = [refs[31 + 3 * n : 34 + 3 * n] for n in range(3)]
    step = pl.program_id(0)

    @pl.when(step == 0)
    def _():
        for m in range(4):
            moment, square, new = adam_update(
                attn_w[m], attn_m[m], attn_v[m], attn_g[m], GROUP_RATES[0][m], decay_rate
            )
            if m < 3:
                attn_moment[m], attn_square[m] = moment, square
            else:
                out_states[0], out_states[1] = moment, square
            attn_new[m], attn_copy[m] = new, new.astype(bf16)
        for m in range(2):
            moment, square, new = adam_update(
                ffn_w[m], ffn_m[m], ffn_v[m], ffn_g[m], GROUP_RATES[1][m], decay_rate
            )
            ffn_moment[m], ffn_square[m] = moment, square
            ffn_new[m], ffn_copy[m] = new, new.astype(bf16)
        for (g, w, m, v), outs in zip(plain, plain_out):
            for ref, value in zip(outs, adam_update(w[...], m[...], v[...], g[...], 0.5, 0.0)):
                ref[...] = value

    tokens_out[...] = tokens_ref[...].astype(f32)

    output[...] = out_b[...]


def last(tokens_low, output, out_b, attn, ffn, plain):
    count, rows, _ = tokens_low.shape
    tile = lambda size, index: pl.BlockSpec((1, size, D), index)
    whole = lambda shape: pl.BlockSpec(
        shape, lambda i: (0,) * len(shape), pipeline_mode=pl.Buffered(1)
    )
    a, f = attn[0].shape, ffn[0].shape
    shapes = [
        ((3,) + a[1:], f32),
        ((3,) + a[1:], f32),
        ((2,) + a[1:], f32),
        (a, f32),
        (a, bf16),
        (f, f32),
        (f, f32),
        (f, f32),
        (f, bf16),
    ]
    for group in plain:
        shapes += [(group[0].shape, f32)] * 3
    inputs = list(attn) + list(ffn) + [array for group in plain for array in group]
    by_half = lambda i: (i // 2, i % 2, 0)
    by_one = lambda i: (i // 2, i % 2, 0)
    second = lambda i: (i // 2, 2 + i % 2, 0)
    quarter = rows // 4
    return pl.pallas_call(
        last_kernel,
        out_shape=[
            jax.ShapeDtypeStruct(tokens_low.shape, f32),
            jax.ShapeDtypeStruct(tokens_low.shape, bf16),
        ]
        + [jax.ShapeDtypeStruct(*entry) for entry in shapes],
        grid=(count * 2,),
        in_specs=[
            tile(rows // 2, by_half),
            tile(quarter, by_one),
            pl.BlockSpec(memory_space=pl.ANY),
        ]
        + [whole(array.shape) for array in inputs],
        out_specs=[tile(rows // 2, by_half), tile(quarter, second)]
        + [whole(shape) for shape, _ in shapes],
        input_output_aliases={2: 1},
        compiler_params=pltpu.CompilerParams(vmem_limit_bytes=VMEM_LIMIT),
        name="last",
    )(tokens_low, out_b, output, *inputs)


def make_body(mesh):
    n_shard, n_ctx, n_tensor = mesh.shape["shard"], mesh.shape["ctx"], mesh.shape["tensor"]
    rows_axes = ("shard", "ctx")
    all_axes = ("shard", "ctx", "tensor")
    paired = n_ctx == 2 and n_shard == 4 and n_tensor == 4

    def swapped(s, c):
        return (s - s % 2 + c, s % 2)

    def swap(array):
        if not paired:
            return array
        pairs = []
        for s in range(n_shard):
            for c in range(n_ctx):
                s_to, c_to = swapped(s, c)
                pairs.append((s * n_ctx + c, s_to * n_ctx + c_to))
        return lax.ppermute(array, rows_axes, pairs)

    def spread(array):
        return lax.all_gather(swap(array), "tensor", axis=0, tiled=True)

    def body(
        tokens,
        cotangent,
        segments,
        rand_blocks,
        attn_w,
        attn_m,
        attn_v,
        ffn_w,
        ffn_m,
        ffn_v,
        qv_bias,
        qv_m,
        qv_v,
        hid_bias,
        hid_m,
        hid_v,
        vec_par,
        vec_m,
        vec_v,
    ):
        t_index = lax.axis_index("tensor")
        nseq = tokens.shape[0] // n_tensor
        piece_len = tokens.shape[1]
        nb = piece_len // BLOCK
        own_rows, own_cols = attn_w.shape[1], attn_w.shape[2]
        own_ff = ffn_w.shape[2]

        def mine(array):
            return lax.dynamic_slice_in_dim(array, t_index * nseq, nseq, 0)

        ints = jnp.concatenate(
            [mine(segments), mine(rand_blocks).reshape(nseq, -1)], axis=1
        )
        ints = swap(ints)
        length = segments.shape[1]
        segs, rand = ints[:, :length], ints[:, length:].reshape(nseq, length // BLOCK, -1)
        piece = lax.axis_index("shard") % 2 if paired else lax.axis_index("ctx")
        tables = attention_tables(segs, rand, piece, nb, paired)

        if paired:
            rand_own, _meta, table = tables
            attn_full, ffn_full, hid_all, x, queries, keys, values, mixed, lse = start(
                n_tensor, attn_w, ffn_w, qv_bias, hid_bias, table[0], rand_own, tokens
            )
            flat = x
            x, queries = x[None], queries[None]
            keys, values = keys.reshape(1, length, D), values.reshape(1, length, D)
            pieces = [piece_len, piece_len]
        else:
            x, cot = mine(tokens), mine(cotangent)
            pieces = [length]
            ffn_z = lax.all_gather(ffn_w.astype(bf16), "tensor", axis=0, tiled=False)
            ffn_z = ffn_z.transpose(1, 2, 0, 3).reshape(2, own_rows, FF)
            ffn_full = lax.all_gather(ffn_z, rows_axes, axis=1, tiled=True)
            flat = x.reshape(-1, D)
            attn_low = attn_w.astype(bf16)
            attn_low = jnp.concatenate([attn_low[i] for i in range(4)], axis=1)
            attn_z = lax.all_gather(attn_low, "tensor", axis=0, tiled=False)
            attn_z = attn_z.reshape(n_tensor, own_rows, 4, own_cols).transpose(2, 1, 0, 3)
            attn_full = lax.all_gather(
                attn_z.reshape(4, own_rows, D), rows_axes, axis=1, tiled=True
            )
            bias_own = jnp.concatenate([qv_bias.reshape(-1), hid_bias])
            bias_all = lax.all_gather(bias_own, "tensor", axis=0, tiled=False)
            qv_all = bias_all[:, : 2 * own_cols].reshape(n_tensor, 2, own_cols)
            qv_all = qv_all.transpose(1, 0, 2).reshape(2, D)
            hid_all = bias_all[:, 2 * own_cols :].reshape(FF)
            keys = matmul(flat, attn_full[1]).astype(bf16).reshape(x.shape)
            values = (matmul(flat, attn_full[2]) + qv_all[1]).astype(bf16).reshape(x.shape)
            keys = lax.all_gather(keys, "ctx", axis=1, tiled=True)
            values = lax.all_gather(values, "ctx", axis=1, tiled=True)
            queries = (matmul(flat, attn_full[0]) + qv_all[0]).astype(bf16) * 0.125
            queries = queries.reshape(x.shape)
            mixed, lse = attend(tables, queries, keys, values)
        mixed_low = mixed.reshape(-1, D)
        if paired:
            out_a, out_b, dw1, dw2, dwo, grad_first_in, grad_mixed, hid_sum, vec_sums = middle(
                n_tensor, flat, mixed_low, hid_all, vec_par, cotangent, attn_full, ffn_full
            )
            out_b = lax.all_gather(out_b, "tensor", axis=0, tiled=False)
        else:
            act, slope, h1, result, grad_second, second_sums = feed_forward(
                flat, mixed_low, cot.reshape(-1, D), attn_full, ffn_full, hid_all, vec_par
            )
            output = spread(result.reshape(x.shape))
            out_a, out_b = output[:, : piece_len // 2], output[:, piece_len // 2 :]
            dw1, dw2, dwo, grad_first_in, grad_mixed, hid_sum, first_sums = feed_back(
                grad_second, h1, mixed_low, attn_full, ffn_full, act, slope, vec_par
            )

        grad_mixed = grad_mixed.reshape(x.shape)
        grad_query, output, dk_parts, dv_parts = attend_back(
            tables,
            queries,
            grad_mixed,
            mixed.reshape(x.shape),
            lse.reshape(nseq, nb, 8, ROWS),
            out_a,
            keys,
            values,
            pieces,
        )

        grad_query_low = grad_query.reshape(-1, D)
        if paired:
            attn_grad, ffn_grad, vec_grad, qv_grad, hid_grad, grad_tokens = finish_all(
                n_tensor,
                [grad_query_low] + [part[0] for part in list(dk_parts) + list(dv_parts)],
                grad_first_in,
                flat,
                attn_full,
                (dw1, dw2, dwo),
                (vec_sums, hid_sum),
            )
        else:
            grad_keys = lax.psum_scatter(dk_parts[0], "ctx", scatter_dimension=1, tiled=True)
            grad_values = lax.psum_scatter(dv_parts[0], "ctx", scatter_dimension=1, tiled=True)
            grad_keys_low = grad_keys.reshape(-1, D)
            grad_values_low = grad_values.reshape(-1, D)
            into_tokens = (
                matmul_nt(grad_query_low, attn_full[0])
                + matmul_nt(grad_keys_low, attn_full[1])
                + matmul_nt(grad_values_low, attn_full[2])
            )
            grad_tokens = spread((grad_first_in + into_tokens).astype(bf16).reshape(x.shape))
            dwq = matmul_tn(flat, grad_query_low).astype(bf16)
            dwk = matmul_tn(flat, grad_keys_low).astype(bf16)
            dwv = matmul_tn(flat, grad_values_low).astype(bf16)
            small = jnp.concatenate(
                [
                    first_sums[0],
                    first_sums[1],
                    second_sums[0],
                    second_sums[1],
                    first_sums[2],
                    second_sums[2],
                    column_sum(grad_query_low),
                    column_sum(grad_values_low),
                    hid_sum[0],
                ]
            )
            ffn_grad = lax.psum_scatter(
                jnp.stack([dw1, dw2]), rows_axes, scatter_dimension=1, tiled=True
            )
            ffn_grad = ffn_grad.reshape(2, own_rows, n_tensor, own_ff).transpose(2, 0, 1, 3)
            ffn_grad = lax.psum_scatter(ffn_grad, "tensor", scatter_dimension=0, tiled=False)
            ffn_grad = ffn_grad.astype(f32)
            attn_grad = lax.psum_scatter(
                jnp.stack([dwq, dwk, dwv, dwo]), rows_axes, scatter_dimension=1, tiled=True
            )
            attn_grad = attn_grad.reshape(4, own_rows, n_tensor, own_cols).transpose(2, 1, 0, 3)
            attn_grad = lax.psum_scatter(
                attn_grad.reshape(n_tensor, own_rows, D), "tensor", scatter_dimension=0
            )
            attn_grad = attn_grad.reshape(own_rows, 4, own_cols).transpose(1, 0, 2).astype(f32)
            small = lax.psum(small, all_axes)
            vec_grad = small[: 6 * D].reshape(6, D)
            qv_grad = lax.dynamic_slice_in_dim(
                small[6 * D : 8 * D].reshape(2, D), t_index * own_cols, own_cols, 1
            )
            hid_grad = lax.dynamic_slice_in_dim(
                small[8 * D : 8 * D + FF], t_index * own_ff, own_ff, 0
            )

        grad_tokens, output, *updated = last(
            grad_tokens,
            output,
            out_b,
            (attn_grad, attn_w, attn_m, attn_v),
            (ffn_grad, ffn_w, ffn_m, ffn_v),
            [
                (qv_grad, qv_bias, qv_m, qv_v),
                (hid_grad.reshape(own_ff), hid_bias, hid_m, hid_v),
                (vec_grad, vec_par, vec_m, vec_v),
            ],
        )
        return (output, grad_tokens, *updated)

    return body


def solution(mesh):
    rows = P("shard", "ctx", None)
    weight = P(None, ("shard", "ctx"), "tensor")
    in_specs = (
        (rows, rows, P("shard", None), P("shard", None, None))
        + (weight,) * 6
        + (P(None, "tensor"),) * 3
        + (P("tensor"),) * 3
        + (P(),) * 3
    )
    out_specs = (
        (rows, rows)
        + (weight,) * 9
        + (P(None, "tensor"),) * 3
        + (P("tensor"),) * 3
        + (P(),) * 3
    )
    return jax.shard_map(
        make_body(mesh), mesh=mesh, in_specs=in_specs, out_specs=out_specs, check_vma=False
    )
```

```python
from functools import partial

import jax
import jax.numpy as jnp
from jax import lax
from jax.experimental import pallas as pl
from jax.experimental.pallas import tpu as pltpu
from jax.sharding import PartitionSpec as P

D = 768
HEAD_DIM = 64
FF = 3072
BLOCK = 64
STEP = 5
GROUP = 4 * HEAD_DIM
GROUPS = D // GROUP
ROWS = 4 * BLOCK
LISTED = 8
KEYS = LISTED * BLOCK
VMEM_LIMIT = 60 * 2**20

beta_first = 0.9
beta_second = 0.999
adam_eps = 1e-08
decay_rate = 0.01
norm_eps = 1e-06
neg_large = -1e30

f32 = jnp.float32
bf16 = jnp.bfloat16


def matmul(left, right):
    return jnp.dot(left, right, preferred_element_type=f32)


def matmul_tn(left, right):
    return lax.dot_general(left, right, (((0,), (0,)), ((), ())), preferred_element_type=f32)


def matmul_nt(left, right):
    return lax.dot_general(left, right, (((1,), (1,)), ((), ())), preferred_element_type=f32)


def column_sum(array_in):
    return jnp.sum(array_in.astype(f32), axis=0)


def adam_update(weight, moment, square, gradient, step_rates, decay_on):
    moment_new = beta_first * moment + (1.0 - beta_first) * gradient
    square_new = beta_second * square + (1.0 - beta_second) * gradient * gradient
    step_ratio = (
        moment_new
        / (1.0 - beta_first**STEP)
        / (jnp.sqrt(square_new / (1.0 - beta_second**STEP)) + adam_eps)
    )
    weight_new = weight - step_rates * (step_ratio + decay_on * weight)
    return (moment_new, square_new, weight_new)


def same_head():
    row_head = lax.broadcasted_iota(jnp.int32, (ROWS, GROUP), 0) // BLOCK
    col_head = lax.broadcasted_iota(jnp.int32, (ROWS, GROUP), 1) // HEAD_DIM
    return row_head == col_head


def spread_heads(block, keep):
    stacked = jnp.concatenate([block] * 4, axis=0)
    return jnp.where(keep, stacked, jnp.zeros_like(stacked))


def fold_heads(full, keep):
    kept = jnp.where(keep, full, 0.0)
    return sum(kept[h * BLOCK : (h + 1) * BLOCK] for h in range(4))


def load_keys(k_all, v_all, seq, k_buf, v_buf, sems):
    return [
        pltpu.make_async_copy(k_all.at[seq], k_buf, sems.at[0]),
        pltpu.make_async_copy(v_all.at[seq], v_buf, sems.at[1]),
    ]


def picked_rows(buf, spots, cols):
    return jnp.concatenate([buf[at, :, cols] for at in spots], axis=0)


def chunk_rows(buf, i, cols):
    blocks = buf[pl.ds(i * LISTED, LISTED), :, cols]
    return blocks.reshape(KEYS, GROUP)


def listed_blocks(rand, base, blk, first, own, total):
    one = lambda condition: condition.astype(jnp.int32)
    me = first + blk
    ids = [me - 1, me, me + 1, me * 0, me * 0 + 1] + [rand[base + n] for n in range(LISTED - 5)]
    spots, unused, common = [], [], []
    for n, block in enumerate(ids):
        out = one(block < 0) + one(block >= total)
        for earlier in ids[:n]:
            out = out + one(block == earlier)
        out = lax.min(out, jnp.int32(1))
        at = lax.max(jnp.int32(0), lax.min(block, jnp.int32(total - 1))) - first + own
        spots.append(at + total * one(at < 0))
        unused.append(out)
        common.append(one(block < 2) * (1 - out))
    return spots, unused, common


def code_rows(tab_ref, spots, unused, common):
    low_half = lax.broadcasted_iota(jnp.int32, (1, 2 * BLOCK), 1) < BLOCK

    def one(n):
        plain = (1 - unused[n] - common[n]).astype(f32)
        return tab_ref[spots[n]] * plain - (unused[n] + 2 * common[n]).astype(f32)

    return [jnp.where(low_half, one(n), one(n + 1)) for n in range(0, LISTED, 2)]


def column_of(row):
    return jnp.broadcast_to(row, (2 * BLOCK, 2 * BLOCK)).T


def mask_bias(document, code):
    return jnp.where((document == code) | (code == -2.0), 0.0, neg_large)


def row_of(column):
    return jnp.broadcast_to(column, (ROWS, 2 * BLOCK)).T[0:1, :]


def forward_block(q_ref, out_ref, lse_ref, k_buf, v_buf, s_buf, tab_ref, rand, base, blk, first, own):
    keep = same_head()
    total_blocks = k_buf.shape[0]
    chunks = total_blocks // LISTED
    is_global = first + blk < 2

    @pl.when(jnp.logical_not(is_global))
    def _():
        spots, unused, common = listed_blocks(rand, base, blk, first, own, total_blocks)
        mine = column_of(tab_ref[own + blk])[:BLOCK]
        mine = jnp.concatenate([mine] * 4, axis=0)
        codes = code_rows(tab_ref, spots, unused, common)
        bias = jnp.concatenate([mask_bias(mine, code) for code in codes], axis=1)
        for g in range(GROUPS):
            cols = slice(g * GROUP, (g + 1) * GROUP)
            q_full = spread_heads(q_ref[:, cols], keep)
            scores = matmul_nt(q_full, picked_rows(k_buf, spots, cols)) + bias
            largest = jnp.max(scores, axis=-1, keepdims=True)
            weights = jnp.exp(scores - largest)
            total = jnp.sum(weights, axis=-1, keepdims=True)
            full = matmul(weights.astype(bf16), picked_rows(v_buf, spots, cols))
            out_ref[:, cols] = fold_heads(full * (1.0 / total), keep).astype(bf16)
            lse_ref[g : g + 1, :] = row_of(largest + jnp.log(total))

    @pl.when(is_global)
    def _():
        for g in range(GROUPS):
            cols = slice(g * GROUP, (g + 1) * GROUP)
            q_full = spread_heads(q_ref[:, cols], keep)

            def score_chunk(i, largest):
                scores = matmul_nt(q_full, chunk_rows(k_buf, i, cols))
                s_buf[i] = scores
                return jnp.maximum(largest, jnp.max(scores, axis=-1, keepdims=True))

            largest = lax.fori_loop(0, chunks, score_chunk, jnp.full((ROWS, 1), neg_large, f32))

            def mix_chunk(i, carry):
                total, full = carry
                weights = jnp.exp(s_buf[i] - largest)
                total = total + jnp.sum(weights, axis=-1, keepdims=True)
                return total, full + matmul(weights.astype(bf16), chunk_rows(v_buf, i, cols))

            total, full = lax.fori_loop(
                0, chunks, mix_chunk, (jnp.zeros((ROWS, 1), f32), jnp.zeros((ROWS, GROUP), f32))
            )
            out_ref[:, cols] = fold_heads(full * (1.0 / total), keep).astype(bf16)
            lse_ref[g : g + 1, :] = row_of(largest + jnp.log(total))


def forward_kernel(
    rand, meta, q_ref, tab_ref, k_all, v_all, out_ref, lse_ref, k_buf, v_buf, s_buf, sems
):
    seq, blk = pl.program_id(0), pl.program_id(1)
    nb = pl.num_programs(1)

    @pl.when(blk == 0)
    def _():
        copies = load_keys(k_all, v_all, seq, k_buf, v_buf, sems)
        for c in copies:
            c.start()
        for c in copies:
            c.wait()

    base = (seq * nb + blk) * (LISTED - 5)
    forward_block(
        q_ref, out_ref, lse_ref, k_buf, v_buf, s_buf, tab_ref, rand, base, blk, meta[0], meta[1]
    )


def back_tile(k_rows, v_rows, q_full, go_full, bias, lse, centre):
    scores = matmul_nt(k_rows, q_full)
    if bias is not None:
        scores = scores + bias
    probs = jnp.exp(scores - lse)
    grad_probs = matmul_nt(v_rows, go_full)
    grad_scores = (probs * (grad_probs - centre)).astype(bf16)
    dv_rows = matmul(probs.astype(bf16), go_full)
    dk_rows = matmul(grad_scores, q_full)
    return matmul_tn(grad_scores, k_rows), dk_rows, dv_rows


def backward_kernel(
    n_out, rand, meta, q_ref, go_ref, mixed_ref, lse_ref, tab_ref, out_a, k_all, v_all, *rest
):
    dq_ref, out_ref, *rest = rest
    dk_refs, dv_refs = rest[:n_out], rest[n_out : 2 * n_out]
    k_buf, v_buf, dk_acc, dv_acc, sems = rest[2 * n_out :]
    seq, blk = pl.program_id(0), pl.program_id(1)
    nb = pl.num_programs(1)
    total_blocks = k_buf.shape[0]
    chunks = total_blocks // LISTED

    out_ref[...] = out_a[...]

    @pl.when(blk == 0)
    def _():
        copies = load_keys(k_all, v_all, seq, k_buf, v_buf, sems)
        for c in copies:
            c.start()
        dk_acc[...] = jnp.zeros_like(dk_acc)
        dv_acc[...] = jnp.zeros_like(dv_acc)
        for c in copies:
            c.wait()

    keep = same_head()
    is_global = meta[0] + blk < 2
    base = (seq * nb + blk) * (LISTED - 5)

    def operands(g):
        cols = slice(g * GROUP, (g + 1) * GROUP)
        q_full = spread_heads(q_ref[:, cols], keep)
        go_full = spread_heads(go_ref[:, cols], keep)
        mixed = jnp.concatenate([mixed_ref[:, cols]] * 4, axis=0)
        product = go_full.astype(f32) * mixed.astype(f32)
        centre = row_of(jnp.sum(product, axis=-1, keepdims=True))
        return cols, q_full, go_full, lse_ref[g : g + 1, :], centre

    @pl.when(jnp.logical_not(is_global))
    def _():
        spots, unused, common = listed_blocks(rand, base, blk, meta[0], meta[1], total_blocks)
        stores = [at + (total_blocks - at) * out for at, out in zip(spots, unused)]
        own = tab_ref[meta[1] + blk]
        codes = code_rows(tab_ref, spots, unused, common)
        bias = jnp.concatenate([mask_bias(own, column_of(code)) for code in codes], axis=0)
        bias = jnp.concatenate([bias, bias], axis=1)
        for g in range(GROUPS):
            cols, q_full, go_full, lse, centre = operands(g)
            k_rows, v_rows = picked_rows(k_buf, spots, cols), picked_rows(v_buf, spots, cols)
            dq_full, dk_rows, dv_rows = back_tile(
                k_rows, v_rows, q_full, go_full, bias, lse, centre
            )
            dq_ref[:, cols] = (fold_heads(dq_full, keep) * 0.125).astype(bf16)
            places = [pl.ds(pl.multiple_of(at * BLOCK, BLOCK), BLOCK) for at in stores]
            dk_old = [dk_acc[at, cols] for at in places]
            dv_old = [dv_acc[at, cols] for at in places]
            for n, at in enumerate(places):
                own_rows = slice(n * BLOCK, (n + 1) * BLOCK)
                dk_acc[at, cols] = dk_old[n] + dk_rows[own_rows]
                dv_acc[at, cols] = dv_old[n] + dv_rows[own_rows]

    @pl.when(is_global)
    def _():
        for g in range(GROUPS):
            cols, q_full, go_full, lse, centre = operands(g)

            def chunk_back(i, dq_full):
                rows = pl.ds(pl.multiple_of(i * KEYS, KEYS), KEYS)
                dq_now, dk_rows, dv_rows = back_tile(
                    chunk_rows(k_buf, i, cols),
                    chunk_rows(v_buf, i, cols),
                    q_full,
                    go_full,
                    None,
                    lse,
                    centre,
                )
                dk_acc[rows, cols] += dk_rows
                dv_acc[rows, cols] += dv_rows
                return dq_full + dq_now

            dq_full = lax.fori_loop(0, chunks, chunk_back, jnp.zeros((ROWS, GROUP), f32))
            dq_ref[:, cols] = (fold_heads(dq_full, keep) * 0.125).astype(bf16)

    @pl.when(blk == nb - 1)
    def _():
        row = 0
        for dk_ref, dv_ref in zip(dk_refs, dv_refs):
            rows = dk_ref.shape[0]
            dk_ref[...] = dk_acc[row : row + rows].astype(bf16)
            dv_ref[...] = dv_acc[row : row + rows].astype(bf16)
            row += rows


def attention_tables(segments, random, piece, nb, own_first):
    seq_count, length = segments.shape
    total = length // BLOCK
    first = piece * nb
    rand = lax.dynamic_slice_in_dim(random, first, nb, 1).reshape(-1)
    table = segments.reshape(seq_count, total, BLOCK).astype(f32)
    table = jnp.concatenate([table, table], axis=2)[:, :, None, :]
    if own_first:
        table = lax.dynamic_slice_in_dim(jnp.concatenate([table, table], axis=1), first, total, 1)
    meta = jnp.stack([first, jnp.zeros_like(first) if own_first else first]).astype(jnp.int32)
    return rand, meta, table


def as_blocks(rows):
    return rows.reshape(rows.shape[0], -1, BLOCK, D)


def attend(tables, q, keys, values):
    rand, meta, table = tables
    seq_count, piece_len, _ = q.shape
    nb = piece_len // BLOCK
    length = keys.shape[1]
    any_spec = pl.BlockSpec(memory_space=pl.ANY)
    row_spec = pl.BlockSpec((None, BLOCK, D), lambda s, b, *_: (s, b, 0))
    return pl.pallas_call(
        forward_kernel,
        out_shape=[
            jax.ShapeDtypeStruct(q.shape, bf16),
            jax.ShapeDtypeStruct((seq_count, nb, 8, ROWS), f32),
        ],
        grid_spec=pltpu.PrefetchScalarGridSpec(
            num_scalar_prefetch=2,
            grid=(seq_count, nb),
            in_specs=[
                row_spec,
                pl.BlockSpec((None,) + table.shape[1:], lambda s, b, *_: (s, 0, 0, 0)),
                any_spec,
                any_spec,
            ],
            out_specs=[
                row_spec,
                pl.BlockSpec((None, None, 8, ROWS), lambda s, b, *_: (s, b, 0, 0)),
            ],
            scratch_shapes=[
                pltpu.VMEM((length // BLOCK, BLOCK, D), bf16),
                pltpu.VMEM((length // BLOCK, BLOCK, D), bf16),
                pltpu.VMEM((length // KEYS, ROWS, KEYS), f32),
                pltpu.SemaphoreType.DMA((2,)),
            ],
        ),
        compiler_params=pltpu.CompilerParams(vmem_limit_bytes=VMEM_LIMIT),
        name="attend",
    )(rand, meta, q, table, as_blocks(keys), as_blocks(values))


def attend_back(tables, q, grad_mixed, mixed, lse, out_a, keys, values, pieces):
    rand, meta, table = tables
    seq_count, piece_len, _ = q.shape
    nb = piece_len // BLOCK
    length = keys.shape[1]
    any_spec = pl.BlockSpec(memory_space=pl.ANY)
    row_spec = pl.BlockSpec((None, BLOCK, D), lambda s, b, *_: (s, b, 0))
    count, half, _ = out_a.shape
    share = count * half // (seq_count * nb)
    if share <= half:
        per = half // share
        tile = pl.BlockSpec(
            (None, share, D), lambda s, b, *_: ((s * nb + b) // per, (s * nb + b) % per, 0)
        )
    else:
        tile = pl.BlockSpec((share // half, half, D), lambda s, b, *_: (s * nb + b, 0, 0))
    part_specs = [pl.BlockSpec((None, rows, D), lambda s, b, *_: (s, 0, 0)) for rows in pieces]
    part_shapes = [jax.ShapeDtypeStruct((seq_count, rows, D), bf16) for rows in pieces]
    out = pl.pallas_call(
        partial(backward_kernel, len(pieces)),
        out_shape=[
            jax.ShapeDtypeStruct(q.shape, bf16),
            jax.ShapeDtypeStruct((count, 2 * half, D), bf16),
        ]
        + part_shapes * 2,
        grid_spec=pltpu.PrefetchScalarGridSpec(
            num_scalar_prefetch=2,
            grid=(seq_count, nb),
            in_specs=[
                row_spec,
                row_spec,
                row_spec,
                pl.BlockSpec((None, None, 8, ROWS), lambda s, b, *_: (s, b, 0, 0)),
                pl.BlockSpec((None,) + table.shape[1:], lambda s, b, *_: (s, 0, 0, 0)),
                tile,
                any_spec,
                any_spec,
            ],
            out_specs=[row_spec, tile] + part_specs * 2,
            scratch_shapes=[
                pltpu.VMEM((length // BLOCK, BLOCK, D), bf16),
                pltpu.VMEM((length // BLOCK, BLOCK, D), bf16),
                pltpu.VMEM((length + BLOCK, D), f32),
                pltpu.VMEM((length + BLOCK, D), f32),
                pltpu.SemaphoreType.DMA((2,)),
            ],
        ),
        compiler_params=pltpu.CompilerParams(vmem_limit_bytes=VMEM_LIMIT),
        cost_estimate=pl.CostEstimate(
            flops=seq_count * nb * GROUPS * 10 * ROWS * KEYS * GROUP,
            bytes_accessed=seq_count * (3 * piece_len + 4 * length) * D * 2,
            transcendentals=seq_count * nb * GROUPS * ROWS * KEYS,
        ),
        name="attend_back",
    )(rand, meta, q, grad_mixed, mixed, lse, table, out_a, as_blocks(keys), as_blocks(values))
    return out[0], out[1], out[2 : 2 + len(pieces)], out[2 + len(pieces) :]


def norm_parts(hidden):
    centred = hidden - jnp.mean(hidden, axis=-1, keepdims=True)
    scale = lax.rsqrt(jnp.mean(centred * centred, axis=-1, keepdims=True) + norm_eps)
    return centred * scale, scale


def norm_back(grad, unit, scale, gain):
    inner = grad * gain
    return scale * (
        inner
        - jnp.mean(inner, axis=-1, keepdims=True)
        - unit * jnp.mean(inner * unit, axis=-1, keepdims=True)
    )


def gelu_and_slope(pre):
    bell = jnp.exp(-0.5 * pre * pre)
    t = 1.0 / (1.0 + (0.3275911 * 0.5**0.5) * jnp.abs(pre))
    poly = 0.5 * 1.061405429
    for coefficient in (-1.453152027, 1.421413741, -0.284496736, 0.254829592):
        poly = poly * t + 0.5 * coefficient
    tail = poly * t * bell
    phi = jnp.where(pre >= 0.0, 1.0 - tail, tail)
    return pre * phi, phi + pre * bell * 0.3989422804014327


def column_total(array):
    return jnp.sum(array.astype(f32), axis=0, keepdims=True)


def up_kernel(
    chunk,
    x_ref,
    mixed_ref,
    cot_ref,
    wo_ref,
    w1_ref,
    w2_ref,
    hid_ref,
    vec_ref,
    act_ref,
    slope_ref,
    h1_ref,
    res_ref,
    gs_ref,
    sums_ref,
    low,
    down,
):
    step = pl.program_id(0)
    chunks = x_ref.shape[0] // chunk

    @pl.when(step == 0)
    def _():
        @pl.loop(0, chunks)
        def _(i):
            rows = pl.ds(pl.multiple_of(i * chunk, chunk), chunk)
            h1 = x_ref[rows, :].astype(f32) + matmul_nt(mixed_ref[rows, :], wo_ref[...])
            h1 = h1 + vec_ref[4:5, :]
            h1_ref[rows, :] = h1
            unit, _scale = norm_parts(h1)
            low[rows, :] = (unit * vec_ref[0:1, :] + vec_ref[1:2, :]).astype(bf16)
            down[rows, :] = jnp.zeros((chunk, D), f32)

    for i in range(chunks):
        rows = slice(i * chunk, (i + 1) * chunk)
        pre = matmul(low[rows, :], w1_ref[...]) + hid_ref[...]
        act, slope = gelu_and_slope(pre)
        act = act.astype(bf16)
        act_ref[rows, :] = act
        slope_ref[rows, :] = slope.astype(bf16)
        down[rows, :] += matmul_nt(act, w2_ref[...])

    @pl.when(step == pl.num_programs(0) - 1)
    def _():
        sums_ref[...] = jnp.zeros_like(sums_ref)

        @pl.loop(0, chunks)
        def _(i):
            rows = pl.ds(pl.multiple_of(i * chunk, chunk), chunk)
            unit, _scale = norm_parts(h1_ref[rows, :])
            first = unit * vec_ref[0:1, :] + vec_ref[1:2, :]
            unit, scale = norm_parts(first + down[rows, :] + vec_ref[5:6, :])
            res_ref[rows, :] = (unit * vec_ref[2:3, :] + vec_ref[3:4, :]).astype(bf16)
            cot = cot_ref[rows, :].astype(f32)
            grad = norm_back(cot, unit, scale, vec_ref[2:3, :])
            gs_ref[rows, :] = grad
            sums_ref[0:1, :] += column_total(cot * unit)
            sums_ref[1:2, :] += column_total(cot)
            sums_ref[2:3, :] += column_total(grad.astype(bf16))


def feed_forward(x, mixed, cot, attn_full, ffn_full, hid_all, vec_par):
    rows = x.shape[0]
    chunk = min(256, rows)
    steps = FF // D
    whole = lambda shape: pl.BlockSpec(shape, lambda t: (0,) * len(shape))
    once = lambda shape: pl.BlockSpec(
        shape, lambda t: (0,) * len(shape), pipeline_mode=pl.Buffered(1)
    )
    hidden = pl.BlockSpec((rows, D), lambda t: (0, t))
    return pl.pallas_call(
        partial(up_kernel, chunk),
        out_shape=[
            jax.ShapeDtypeStruct((rows, FF), bf16),
            jax.ShapeDtypeStruct((rows, FF), bf16),
            jax.ShapeDtypeStruct((rows, D), f32),
            jax.ShapeDtypeStruct((rows, D), bf16),
            jax.ShapeDtypeStruct((rows, D), f32),
            jax.ShapeDtypeStruct((8, D), f32),
        ],
        grid=(steps,),
        in_specs=[
            once((rows, D)),
            once((rows, D)),
            once((rows, D)),
            pl.BlockSpec((None, D, D), lambda t: (3, 0, 0), pipeline_mode=pl.Buffered(1)),
            pl.BlockSpec((None, D, D), lambda t: (0, 0, t)),
            pl.BlockSpec((None, D, D), lambda t: (1, 0, t)),
            pl.BlockSpec((1, D), lambda t: (0, t)),
            whole((6, D)),
        ],
        out_specs=[
            hidden,
            hidden,
            whole((rows, D)),
            whole((rows, D)),
            whole((rows, D)),
            whole((8, D)),
        ],
        scratch_shapes=[pltpu.VMEM((rows, D), bf16), pltpu.VMEM((rows, D), f32)],
        compiler_params=pltpu.CompilerParams(vmem_limit_bytes=VMEM_LIMIT),
        cost_estimate=pl.CostEstimate(
            flops=2 * rows * D * (D + 2 * FF),
            bytes_accessed=rows * D * 30 + 2 * D * FF * 2,
            transcendentals=2 * rows * FF,
        ),
        name="feed_forward",
    )(x, mixed, cot, attn_full, ffn_full, ffn_full, hid_all.reshape(1, FF), vec_par)


def down_kernel(
    chunk,
    gs_ref,
    h1_ref,
    mixed_ref,
    wo_ref,
    w1_ref,
    w2_ref,
    act_ref,
    slope_ref,
    vec_ref,
    dw1_ref,
    dw2_ref,
    dwo_ref,
    gh1_ref,
    gm_ref,
    hid_ref,
    sums_ref,
    turned,
    low_t,
    pre,
    total,
):
    step = pl.program_id(0)
    n_rows = gs_ref.shape[0]
    chunks = n_rows // chunk

    @pl.when(step == 0)
    def _():
        @pl.loop(0, chunks)
        def _(i):
            rows = pl.ds(pl.multiple_of(i * chunk, chunk), chunk)
            unit, _scale = norm_parts(h1_ref[rows, :])
            low = unit * vec_ref[0:1, :] + vec_ref[1:2, :]
            low_t[:, rows] = low.T.astype(bf16)
            turned[:, rows] = gs_ref[rows, :].T.astype(bf16)
            total[rows, :] = gs_ref[rows, :]

    for i in range(chunks):
        rows = slice(i * chunk, (i + 1) * chunk)
        grad_act = matmul(gs_ref[rows, :].astype(bf16), w2_ref[...]).astype(bf16).astype(f32)
        grad_pre = (grad_act * slope_ref[rows, :].astype(f32)).astype(bf16)
        pre[rows, :] = grad_pre
        total[rows, :] += matmul_nt(grad_pre, w1_ref[...])
    hid_ref[...] = column_total(pre[...])
    part = D // 4
    for j in range(4):
        out = slice(j * part, (j + 1) * part)
        dw1_ref[out, :] = matmul(low_t[out, :], pre[...]).astype(bf16)
        dw2_ref[out, :] = matmul(turned[out, :], act_ref[...]).astype(bf16)

    @pl.when(step == pl.num_programs(0) - 1)
    def _():
        sums_ref[...] = jnp.zeros_like(sums_ref)

        @pl.loop(0, chunks)
        def _(i):
            rows = pl.ds(pl.multiple_of(i * chunk, chunk), chunk)
            unit, scale = norm_parts(h1_ref[rows, :])
            grad_first = total[rows, :]
            grad_h1 = norm_back(grad_first, unit, scale, vec_ref[0:1, :])
            gh1_ref[rows, :] = grad_h1
            low = grad_h1.astype(bf16)
            gm_ref[rows, :] = matmul(low, wo_ref[...]).astype(bf16)
            turned[:, rows] = grad_h1.T.astype(bf16)
            sums_ref[0:1, :] += column_total(grad_first * unit)
            sums_ref[1:2, :] += column_total(grad_first)
            sums_ref[2:3, :] += column_total(low)

        @pl.loop(0, 4)
        def _(j):
            out = pl.ds(pl.multiple_of(j * part, part), part)
            dwo_ref[out, :] = matmul(turned[out, :], mixed_ref[...]).astype(bf16)


def feed_back(gs, h1, mixed, attn_full, ffn_full, act, slope, vec_par):
    rows = gs.shape[0]
    chunk = min(256, rows)
    steps = FF // D
    whole = lambda shape: pl.BlockSpec(shape, lambda t: (0,) * len(shape))
    once = lambda shape: pl.BlockSpec(
        shape, lambda t: (0,) * len(shape), pipeline_mode=pl.Buffered(1)
    )
    hidden = pl.BlockSpec((rows, D), lambda t: (0, t))
    slab = pl.BlockSpec((D, D), lambda t: (0, t))
    return pl.pallas_call(
        partial(down_kernel, chunk),
        out_shape=[
            jax.ShapeDtypeStruct((D, FF), bf16),
            jax.ShapeDtypeStruct((D, FF), bf16),
            jax.ShapeDtypeStruct((D, D), bf16),
            jax.ShapeDtypeStruct((rows, D), f32),
            jax.ShapeDtypeStruct((rows, D), bf16),
            jax.ShapeDtypeStruct((1, FF), f32),
            jax.ShapeDtypeStruct((8, D), f32),
        ],
        grid=(steps,),
        in_specs=[
            once((rows, D)),
            once((rows, D)),
            once((rows, D)),
            pl.BlockSpec((None, D, D), lambda t: (3, 0, 0), pipeline_mode=pl.Buffered(1)),
            pl.BlockSpec((None, D, D), lambda t: (0, 0, t)),
            pl.BlockSpec((None, D, D), lambda t: (1, 0, t)),
            hidden,
            hidden,
            whole((6, D)),
        ],
        out_specs=[
            slab,
            slab,
            whole((D, D)),
            whole((rows, D)),
            whole((rows, D)),
            pl.BlockSpec((1, D), lambda t: (0, t)),
            whole((8, D)),
        ],
        scratch_shapes=[
            pltpu.VMEM((D, rows), bf16),
            pltpu.VMEM((D, rows), bf16),
            pltpu.VMEM((rows, D), bf16),
            pltpu.VMEM((rows, D), f32),
        ],
        compiler_params=pltpu.CompilerParams(vmem_limit_bytes=VMEM_LIMIT),
        cost_estimate=pl.CostEstimate(
            flops=2 * rows * D * (2 * D + 4 * FF),
            bytes_accessed=rows * D * 30 + 4 * D * FF * 2,
            transcendentals=0,
        ),
        name="feed_back",
    )(gs, h1, mixed, attn_full, ffn_full, ffn_full, act, slope, vec_par)


WIDE = 1536
STRIP = 96
PIECES = 8
ITEM = 128
LINE_ITEMS = 4
MESH = pl.DeviceIdType.MESH


def remote(src, dst, send, recv, where):
    return pltpu.make_async_remote_copy(
        src_ref=src,
        dst_ref=dst,
        send_sem=send,
        recv_sem=recv,
        device_id=where,
        device_id_type=MESH,
    )


def greet(partners):
    barrier = pltpu.get_barrier_semaphore()
    for where in partners:
        pl.semaphore_signal(barrier, inc=1, device_id=where, device_id_type=MESH)
    pl.semaphore_wait(barrier, len(partners))


def places(n_tensor):
    s, c, t = lax.axis_index("shard"), lax.axis_index("ctx"), lax.axis_index("tensor")
    x, core = s // 2, s % 2
    sibling = (x * 2 + 1 - core, c, t)
    over_x = ((1 - x) * 2 + core, c, t)
    over_y = (s, 1 - c, t)
    across = (x * 2 + 1 - core, 1 - c, t)
    along_z = [(s, c, lax.rem(t + k, n_tensor)) for k in range(1, n_tensor)]
    return s, c, t, x, core, sibling, over_x, over_y, across, along_z


class Line:
    def __init__(self, s, c, t, last, items, rows, array, out, up, down, copied):
        self.s, self.c, self.t, self.last, self.items = s, c, t, last, items
        self.rows, self.array, self.out, self.up, self.down = rows, array, out, up, down
        self.copied = copied

    def hop(self, i, src_t, sems, n, to):
        ref = self.array.at[src_t, pl.ds(i * self.rows, self.rows)]
        return remote(ref, ref, sems[0].at[n], sems[1].at[n], (self.s, self.c, to))

    def keep(self, src_t, n):
        return pltpu.make_async_copy(self.array.at[src_t], self.out.at[src_t], self.copied.at[n])

    def send_own(self, i):
        t = self.t

        @pl.when(t < self.last)
        def _():
            self.hop(i, t, self.up, i, t + 1).start()

        @pl.when(t > 0)
        def _():
            self.hop(i, t, self.down, i, t - 1).start()

        if i == self.items - 1:
            self.keep(t, 2 * self.last).start()

    def tick(self, j):
        t, last = self.t, self.last
        i, hops, n = j % self.items, j // self.items + 1, j + self.items

        @pl.when(t >= hops)
        def _():
            self.hop(i, t - hops, self.up, j, t - 1).wait_recv()

            @pl.when(t < last)
            def _():
                self.hop(i, t - hops, self.up, n, t + 1).start()

            if i == self.items - 1:
                self.keep(t - hops, hops - 1).start()

        @pl.when(t + hops <= last)
        def _():
            self.hop(i, t + hops, self.down, j, t + 1).wait_recv()

            @pl.when(t > 0)
            def _():
                self.hop(i, t + hops, self.down, n, t - 1).start()

            if i == self.items - 1:
                self.keep(t + hops, last + hops - 1).start()

    def settle(self):
        t, last = self.t, self.last
        for j in range(self.items * last):
            i, hops = j % self.items, j // self.items

            @pl.when((t < last) & (t >= hops))
            def _():
                self.hop(i, t - hops, self.up, j, t + 1).wait_send()

            @pl.when((t > 0) & (t + hops <= last))
            def _():
                self.hop(i, t + hops, self.down, j, t - 1).wait_send()

        self.keep(t, 2 * last).wait()
        for hops in range(1, last + 1):

            @pl.when(t >= hops)
            def _():
                self.keep(t - hops, hops - 1).wait()

            @pl.when(t + hops <= last)
            def _():
                self.keep(t + hops, last + hops - 1).wait()


def start_kernel(n_tensor, *refs):
    attn_ref, ffn_ref, qv_ref, hid_ref, tab_ref, rand, tokens = refs[:7]
    attn_out, ffn_out, hid_out, x_out, q_out, k_out, v_out, mixed_out, lse_out = refs[7:16]
    low, low_z, bias, bias_z, bias_qv, ffn_low, full, xs, qs, ms, k_buf, v_buf, s_buf, ffn_full = refs[16:30]
    (
        z_send,
        z_recv,
        b_send,
        b_recv,
        fz_send,
        fz_recv,
        x_send,
        x_recv,
        g_send,
        g_recv,
        p_send,
        p_recv,
        fg_send,
        fg_recv,
        fp_send,
        fp_recv,
        kv_send,
        kv_recv,
        own_sem,
    ) = refs[30:]
    s, c, t, x, core, sibling, over_x, over_y, across, along_z = places(n_tensor)
    own_cols, own_ff = D // n_tensor, FF // n_tensor
    n_rows = xs.shape[0]

    for m in range(4):
        low[:, m * own_cols : (m + 1) * own_cols] = attn_ref[m].astype(bf16)
    for m in range(2):
        ffn_low[m] = ffn_ref[m].astype(bf16)
    bias[0:2, 0:own_cols] = qv_ref[...]
    bias[2:3, 0:own_ff] = hid_ref[...]

    greet([sibling, over_x, over_y, across] + along_z)

    sent = []

    def put(copy):
        copy.start()
        sent.append(copy)

    half = 2 * own_cols

    def z_hop(path, k, u):
        cols = pl.ds(path * half, half)
        n = path * n_tensor
        return remote(
            low.at[:, cols], low_z.at[u, :, cols], z_send.at[n + k], z_recv.at[n + u], along_z[k]
        )

    for path in range(2):
        for k in range(n_tensor - 1):
            put(z_hop(path, k, t))

    quarter = n_rows // 4

    def keep_rows(n):
        at = pl.ds(n * quarter, quarter)
        return pltpu.make_async_copy(tokens.at[t, at], xs.at[at], x_recv.at[n])

    def swap_rows(n):
        at = pl.ds(n * quarter, quarter)
        return remote(tokens.at[t, at], xs.at[at], x_send.at[n], x_recv.at[n], across)

    def start_rows(n):
        @pl.when(core == c)
        def _():
            keep_rows(n).start()

        @pl.when(core != c)
        def _():
            swap_rows(n).start()

    start_rows(0)
    start_rows(1)
    low_z[t] = low[...]
    bias_z[t] = bias[...]

    def strip(shard, ctx):
        return pl.ds(pl.multiple_of((2 * shard + ctx) * STRIP, STRIP), STRIP)

    here = strip(s, c)

    def lay_out(path):
        for k, where in enumerate(along_z):
            z_hop(path, k, where[2]).wait_recv()
        for n in range(n_tensor):
            for m in range(2 * path, 2 * path + 2):
                piece = low_z[n, :, m * own_cols : (m + 1) * own_cols]
                full[m, here, n * own_cols : (n + 1) * own_cols] = piece

    far_x, far_y = over_x[0], 1 - c
    labels = ["own", "x", "y", "xy"]
    rows = {
        "own": here,
        "x": strip(far_x, c),
        "y": strip(s, far_y),
        "xy": strip(far_x, far_y),
    }
    far_rows = {
        "own": strip(sibling[0], c),
        "x": strip(2 * (1 - x) + 1 - core, c),
        "y": strip(sibling[0], far_y),
        "xy": strip(2 * (1 - x) + 1 - core, far_y),
    }

    def attn_block(path, at):
        return full.at[pl.ds(2 * path, 2), at, :]

    def ffn_block(path, at):
        return ffn_full.at[path, at, :]

    class Gather:
        def __init__(self, block, ways, gs, gr, ps, pr):
            self.block, self.gs, self.gr, self.ps, self.pr = block, gs, gr, ps, pr
            x_first = (("x", over_x), ("y", over_y))
            self.ways = [x_first if way == 0 else x_first[::-1] for way in ways]

        def hop(self, path, name, label, where):
            n = path * 3 + labels.index(label) - 1
            ref = self.block(path, rows[name])
            return remote(ref, ref, self.gs.at[n], self.gr.at[n], where)

        def give(self, path, name, label, where):
            put(self.hop(path, name, label, where))

        def take(self, path, label):
            self.hop(path, label, label, over_x).wait_recv()

        def share(self, path, name):
            put(self.shared(path, name))

        def take_shared(self, path):
            for n, name in enumerate(labels):
                ref = self.block(path, far_rows[name])
                n = path * 4 + n
                remote(ref, ref, self.ps.at[n], self.pr.at[n], sibling).wait_recv()

        def shared(self, path, name):
            n = path * 4 + labels.index(name)
            ref = self.block(path, rows[name])
            return remote(ref, ref, self.ps.at[n], self.pr.at[n], sibling)

        def again(self, path, number):
            near, far = self.ways[path]
            if number == 1:
                sent.append(self.hop(path, near[0], "xy", far[1]))
            sent.append(self.shared(path, {1: near[0], 2: far[0], 3: "xy"}[number]))

        def step(self, path, number):
            near, far = self.ways[path]
            if number == 0:
                self.give(path, "own", near[0], near[1])
                self.give(path, "own", far[0], far[1])
                self.share(path, "own")
            elif number == 1:
                self.take(path, near[0])
                self.give(path, near[0], "xy", far[1])
                self.share(path, near[0])
            elif number == 2:
                self.take(path, far[0])
                self.share(path, far[0])
            else:
                self.take(path, "xy")
                self.share(path, "xy")

    attn = Gather(attn_block, (1, 1), g_send, g_recv, p_send, p_recv)
    ffn = Gather(ffn_block, (0, 1), fg_send, fg_recv, fp_send, fp_recv)

    def ffn_cols(path, u):
        return ffn_full.at[path, here, pl.ds(pl.multiple_of(u * own_ff, own_ff), own_ff)]

    def ffn_hop(path, k, u):
        n = path * n_tensor
        return remote(
            ffn_low.at[path],
            ffn_cols(path, u),
            fz_send.at[n + k],
            fz_recv.at[n + u],
            along_z[k],
        )

    local = []

    def write(src, dst, n):
        copy = pltpu.make_async_copy(src, dst, own_sem.at[n])
        copy.start()
        local.append(copy)

    def ffn_along_z(path):
        for k in range(n_tensor - 1):
            put(ffn_hop(path, k, t))
        write(ffn_low.at[path], ffn_cols(path, t), 5 + path)

    def ffn_ready(path):
        for k, where in enumerate(along_z):
            ffn_hop(path, k, where[2]).wait_recv()
        local[path].wait()
        ffn.step(path, 0)

    lay_out(0)
    attn.step(0, 0)
    start_rows(2)
    ffn_along_z(0)
    lay_out(1)
    attn.step(1, 0)
    start_rows(3)
    ffn_along_z(1)
    for k, where in enumerate(along_z):
        put(remote(bias, bias_z.at[t], b_send.at[k], b_recv.at[t], where))
    attn.step(0, 1)
    attn.step(1, 1)
    attn.step(0, 2)
    attn.step(0, 3)
    for k, where in enumerate(along_z):
        u = where[2]
        remote(bias, bias_z.at[u], b_send.at[k], b_recv.at[u], where).wait_recv()
    for n in range(n_tensor):
        cols = slice(n * own_cols, (n + 1) * own_cols)
        bias_qv[0:2, cols] = bias_z[n, 0:2, 0:own_cols]
        hid_out[:, n * own_ff : (n + 1) * own_ff] = bias_z[n, 2:3, 0:own_ff]

    for n in range(4):

        @pl.when(core == c)
        def _():
            keep_rows(n).wait()

        @pl.when(core != c)
        def _():
            swap_rows(n).wait()

    chunk = 256
    chunks = n_rows // chunk
    per = chunk // BLOCK

    def kv_hop(buf, i, n):
        at, to = pl.ds(i * per, per), pl.ds(n_rows // BLOCK + i * per, per)
        return remote(buf.at[at], buf.at[to], kv_send.at[n], kv_recv.at[n], sibling)

    attn.take_shared(0)
    for i in range(chunks):
        at = pl.ds(i * chunk, chunk)
        k = matmul(xs[at, :], full[1]).astype(bf16)
        k_buf[pl.ds(i * per, per)] = k.reshape(per, BLOCK, D)
        put(kv_hop(k_buf, i, i))
    for i in range(chunks):
        at = pl.ds(i * chunk, chunk)
        q = matmul(xs[at, :], full[0]) + bias_qv[0:1, :]
        qs[at, :] = (q.astype(bf16).astype(f32) * 0.125).astype(bf16)
    attn.step(1, 2)
    attn.step(1, 3)
    ffn_ready(0)
    attn.take_shared(1)
    for i in range(chunks):
        at = pl.ds(i * chunk, chunk)
        v = (matmul(xs[at, :], full[2]) + bias_qv[1:2, :]).astype(bf16)
        v_buf[pl.ds(i * per, per)] = v.reshape(per, BLOCK, D)
        put(kv_hop(v_buf, i, chunks + i))
    write(xs, x_out, 0)
    write(qs, q_out, 1)
    write(full, attn_out, 2)
    for i in range(chunks):
        kv_hop(k_buf, i, i).wait_recv()
        kv_hop(v_buf, i, chunks + i).wait_recv()
    write(k_buf, k_out, 3)
    write(v_buf, v_out, 4)
    ffn_ready(1)
    ffn.step(0, 1)

    nb = n_rows // BLOCK
    first = core * nb
    stops = {1: [(1, 1), (0, 2)], 3: [(1, 2)]}

    @pl.loop(0, nb)
    def _(blk):
        at = pl.ds(pl.multiple_of(blk * BLOCK, BLOCK), BLOCK)
        forward_block(
            qs.at[at],
            ms.at[at],
            lse_out.at[blk],
            k_buf,
            v_buf,
            s_buf,
            tab_ref,
            rand,
            blk * (LISTED - 5),
            blk,
            first,
            0,
        )

        for at_block, moves in stops.items():

            @pl.when(blk == at_block)
            def _():
                mark = len(sent)
                for path, number in moves:
                    ffn.step(path, number)
                del sent[mark:]

    write(ms, mixed_out, 7)
    for path, number in [move for moves in stops.values() for move in moves]:
        ffn.again(path, number)
    ffn.step(0, 3)
    ffn.step(1, 3)
    for path in range(2):
        ffn.take_shared(path)
        write(ffn_full.at[path], ffn_out.at[path], 8 + path)

    for copy in sent:
        copy.wait_send()
    for copy in local[2:]:
        copy.wait()


def start(n_tensor, attn_w, ffn_w, qv_bias, hid_bias, table, rand, tokens):
    rows = tokens.shape[1]
    own_ff = FF // n_tensor
    dma = pltpu.SemaphoreType.DMA
    vmem, anywhere = pl.BlockSpec(memory_space=pltpu.VMEM), pl.BlockSpec(memory_space=pl.ANY)
    smem = pl.BlockSpec(memory_space=pltpu.SMEM)
    tall = jax.ShapeDtypeStruct((rows, D), bf16)
    both = jax.ShapeDtypeStruct((2 * rows // BLOCK, BLOCK, D), bf16)
    items = 2 * (rows // 256)
    return pl.pallas_call(
        partial(start_kernel, n_tensor),
        out_shape=[
            jax.ShapeDtypeStruct((4, D, D), bf16),
            jax.ShapeDtypeStruct((2, D, FF), bf16),
            jax.ShapeDtypeStruct((1, FF), f32),
            tall,
            tall,
            both,
            both,
            tall,
            jax.ShapeDtypeStruct((rows // BLOCK, 8, ROWS), f32),
        ],
        in_specs=[vmem] * 5 + [smem, anywhere],
        out_specs=[anywhere, anywhere, vmem] + [anywhere] * 5 + [vmem],
        scratch_shapes=[
            pltpu.VMEM((STRIP, D), bf16),
            pltpu.VMEM((n_tensor, STRIP, D), bf16),
            pltpu.VMEM((8, D), f32),
            pltpu.VMEM((n_tensor, 8, D), f32),
            pltpu.VMEM((8, D), f32),
            pltpu.VMEM((2, STRIP, own_ff), bf16),
            pltpu.VMEM((4, D, D), bf16),
            pltpu.VMEM((rows, D), bf16),
            pltpu.VMEM((rows, D), bf16),
            pltpu.VMEM((rows, D), bf16),
            pltpu.VMEM((2 * rows // BLOCK, BLOCK, D), bf16),
            pltpu.VMEM((2 * rows // BLOCK, BLOCK, D), bf16),
            pltpu.VMEM((2 * rows // KEYS, ROWS, KEYS), f32),
            pltpu.VMEM((2, D, FF), bf16),
            dma((2 * n_tensor,)),
            dma((2 * n_tensor,)),
            dma((n_tensor,)),
            dma((n_tensor,)),
            dma((2 * n_tensor,)),
            dma((2 * n_tensor,)),
            dma((4,)),
            dma((4,)),
            dma((6,)),
            dma((6,)),
            dma((8,)),
            dma((8,)),
            dma((6,)),
            dma((6,)),
            dma((8,)),
            dma((8,)),
            dma((items,)),
            dma((items,)),
            dma((10,)),
        ],
        compiler_params=pltpu.CompilerParams(
            collective_id=2, has_side_effects=True, vmem_limit_bytes=VMEM_LIMIT
        ),
        cost_estimate=pl.CostEstimate(
            flops=6 * rows * D * D, bytes_accessed=100 * 2**20, transcendentals=0
        ),
        name="start",
    )(attn_w, ffn_w, qv_bias, hid_bias.reshape(1, own_ff), table, rand, tokens)


def middle_kernel(n_tensor, *refs):
    x_ref, mixed_ref, hid_ref, vec_ref, cotangent, attn_full, ffn_full = refs[:7]
    out_a, out_b, dw1, dw2, dwo, gh1, gm, hid_out, sums_out = refs[7:16]
    w, wo, act, slope, h1, total, gs_low, low_t, turned, pre, dw_s, cot, ready, low, down, held = refs[16:32]
    (
        w_sem,
        c_send,
        c_recv,
        h_send,
        h_recv,
        up_send,
        up_recv,
        dn_send,
        dn_recv,
        dw_sem,
        own_sem,
        copied,
    ) = refs[32:]
    s, c, t, x, core, sibling, over_x, over_y, across, along_z = places(n_tensor)
    n_rows = x_ref.shape[0]
    chunk = 256
    chunks = n_rows // chunk
    steps = FF // D
    items, all_items = LINE_ITEMS, n_rows // ITEM
    last = n_tensor - 1

    def block(i):
        return pl.ds(pl.multiple_of(i * D, D), D)

    fetch_o = pltpu.make_async_copy(attn_full.at[3], wo, w_sem.at[2 * steps])
    fetch_o.start()

    def fetch(m, i):
        at = w.at[m, :, block(i)]
        return pltpu.make_async_copy(ffn_full.at[m, :, block(i)], at, w_sem.at[m * steps + i])

    for i in range(steps):
        for m in range(2):
            fetch(m, i).start()

    greet([over_y, across] + along_z)

    def keep_cot(i):
        at = pl.ds(i * chunk, chunk)
        return pltpu.make_async_copy(cotangent.at[t, at], cot.at[at], c_recv.at[i])

    def swap_cot(i):
        at = pl.ds(i * chunk, chunk)
        return remote(cotangent.at[t, at], cot.at[at], c_send.at[i], c_recv.at[i], across)

    def home_ref(i):
        if i < items:
            return held.at[t, pl.ds(i * ITEM, ITEM)]
        return out_b.at[pl.ds((i - items) * ITEM, ITEM)]

    def keep_home(i):
        return pltpu.make_async_copy(ready.at[pl.ds(i * ITEM, ITEM)], home_ref(i), h_recv.at[i])

    def send_home(i):
        src = ready.at[pl.ds(i * ITEM, ITEM)]
        return remote(src, home_ref(i), h_send.at[i], h_recv.at[i], across)

    def if_home(at_home, away):
        @pl.when(core == c)
        def _():
            at_home()

        @pl.when(core != c)
        def _():
            away()

    if_home(lambda: keep_cot(0).start(), lambda: swap_cot(0).start())

    up, down_line = (up_send, up_recv), (dn_send, dn_recv)
    chain = Line(s, c, t, last, items, ITEM, held, out_a, up, down_line, copied)

    def own_ready(i):
        if_home(lambda: keep_home(i).wait(), lambda: send_home(i).wait_recv())

    events = {
        (1, 2): ([0], []),
        (2, 2): ([1], []),
        (2, 3): ([2], [0]),
        (3, 2): ([], [1]),
        (3, 3): ([3], []),
        (4, 0): ([], [2]),
    }
    sizes = [ITEM] + [chunk] * (chunks - 1) + [chunk - ITEM]
    start_row = 0
    for i, size in enumerate(sizes):
        rows = slice(start_row, start_row + size)
        top = slice(0, size)
        if i == 0:
            fetch_o.wait()
        pre1 = x_ref[rows, :].astype(f32) + matmul_nt(mixed_ref[rows, :], wo[...])
        pre1 = pre1 + vec_ref[4:5, :]
        h1[rows, :] = pre1
        unit, _scale = norm_parts(pre1)
        first = unit * vec_ref[0:1, :] + vec_ref[1:2, :]
        low[top, :] = first.astype(bf16)
        down[top, :] = first + vec_ref[5:6, :]

        @pl.loop(0, steps)
        def _(j):
            if i == 0:
                fetch(0, j).wait()
                fetch(1, j).wait()
            for (at_chunk, at_step), (own, passing) in events.items():
                if at_chunk != i:
                    continue

                @pl.when(j == at_step)
                def _():
                    for n in own:
                        own_ready(n)
                        chain.send_own(n)
                    for n in passing:
                        chain.tick(n)

            hidden = matmul(low[top, :], w[0, :, block(j)]) + hid_ref[:, block(j)]
            act_now, slope_now = gelu_and_slope(hidden)
            act_now = act_now.astype(bf16)
            act[rows, block(j)] = act_now
            slope[rows, block(j)] = slope_now.astype(bf16)
            down[top, :] += matmul_nt(act_now, w[1, :, block(j)])

        second = down[top, :]
        total[rows, :] = second
        unit, _scale = norm_parts(second)
        ready[rows, :] = (unit * vec_ref[2:3, :] + vec_ref[3:4, :]).astype(bf16)
        for n in range(start_row // ITEM, (start_row + size) // ITEM):
            if_home(lambda: keep_home(n).start(), lambda: send_home(n).start())
        if i + 1 < chunks:
            if_home(lambda: keep_cot(i + 1).start(), lambda: swap_cot(i + 1).start())
        start_row += size
    chain.tick(4)

    sums_out[...] = jnp.zeros_like(sums_out)

    @pl.loop(0, chunks)
    def _(i):
        rows = pl.ds(pl.multiple_of(i * chunk, chunk), chunk)
        if_home(lambda: keep_cot(i).wait(), lambda: swap_cot(i).wait())
        unit, scale = norm_parts(total[rows, :])
        grad_out = cot[rows, :].astype(f32)
        grad = norm_back(grad_out, unit, scale, vec_ref[2:3, :])
        sums_out[2:3, :] += column_total(grad_out * unit)
        sums_out[3:4, :] += column_total(grad_out)
        total[rows, :] = grad
        grad_low = grad.astype(bf16)
        gs_low[rows, :] = grad_low
        sums_out[5:6, :] += column_total(grad_low)
        turned[:, rows] = grad.T.astype(bf16)
        unit, _scale = norm_parts(h1[rows, :])
        first = unit * vec_ref[0:1, :] + vec_ref[1:2, :]
        low_t[:, rows] = first.T.astype(bf16)

    part = D // 4

    def dw_copy(slot, m, j):
        return pltpu.make_async_copy(
            dw_s.at[slot, m], (dw1, dw2)[m].at[:, block(j)], dw_sem.at[2 * slot + m]
        )

    ticks = {(0, 1): 5, (1, 0): 3, (1, 1): 6, (2, 0): 8, (2, 1): 9, (3, 0): 7, (3, 1): 10}

    def pass_on(j, when):
        for (at, place), n in ticks.items():
            if place == when:

                @pl.when(j == at)
                def _():
                    chain.tick(n)

    @pl.loop(0, steps)
    def _(j):
        slot = lax.rem(j, 2)
        pass_on(j, 0)
        for i in range(chunks):
            rows = slice(i * chunk, (i + 1) * chunk)
            grad_act = matmul(gs_low[rows, :], w[1, :, block(j)]).astype(bf16).astype(f32)
            grad_pre = (grad_act * slope[rows, block(j)].astype(f32)).astype(bf16)
            pre[rows, :] = grad_pre
            total[rows, :] += matmul_nt(grad_pre, w[0, :, block(j)])
        pass_on(j, 1)
        hid_out[:, block(j)] = column_total(pre[...])

        @pl.when(j >= 2)
        def _():
            for m in range(2):
                dw_copy(slot, m, j - 2).wait()

        for n in range(4):
            out = slice(n * part, (n + 1) * part)
            dw_s[slot, 0, out, :] = matmul(low_t[out, :], pre[...]).astype(bf16)
            dw_s[slot, 1, out, :] = matmul(turned[out, :], act[:, block(j)]).astype(bf16)
        for m in range(2):
            dw_copy(slot, m, j).start()

    gm_s = gs_low

    @pl.loop(0, chunks)
    def _(i):
        rows = pl.ds(pl.multiple_of(i * chunk, chunk), chunk)
        unit, scale = norm_parts(h1[rows, :])
        grad_first = total[rows, :]
        grad_h1 = norm_back(grad_first, unit, scale, vec_ref[0:1, :])
        total[rows, :] = grad_h1
        grad_low = grad_h1.astype(bf16)
        gm_s[rows, :] = matmul(grad_low, wo[...]).astype(bf16)
        turned[:, rows] = grad_h1.T.astype(bf16)
        sums_out[0:1, :] += column_total(grad_first * unit)
        sums_out[1:2, :] += column_total(grad_first)
        sums_out[4:5, :] += column_total(grad_low)

    local = [
        pltpu.make_async_copy(total, gh1, own_sem.at[0]),
        pltpu.make_async_copy(gm_s, gm, own_sem.at[1]),
    ]
    for copy in local:
        copy.start()
    for j in range(steps - 2, steps):
        for m in range(2):
            dw_copy(j % 2, m, j).wait()

    @pl.loop(0, 4)
    def _(n):
        out = pl.ds(pl.multiple_of(n * part, part), part)
        dw_s[0, 0, out, :] = matmul(turned[out, :], mixed_ref[...]).astype(bf16)

    local.append(pltpu.make_async_copy(dw_s.at[0, 0], dwo, own_sem.at[2]))
    local[-1].start()
    chain.tick(11)
    for i in range(items, all_items):
        own_ready(i)
    for i in range(all_items):

        @pl.when(core != c)
        def _():
            send_home(i).wait_send()

    chain.settle()
    for copy in local:
        copy.wait()


def middle(n_tensor, x, mixed, hid_all, vec_par, cotangent, attn_full, ffn_full):
    rows = x.shape[0]
    steps = FF // D
    items, all_items = LINE_ITEMS, rows // ITEM
    dma = pltpu.SemaphoreType.DMA
    vmem, anywhere = pl.BlockSpec(memory_space=pltpu.VMEM), pl.BlockSpec(memory_space=pl.ANY)
    low, wide = pltpu.VMEM((rows, D), bf16), pltpu.VMEM((rows, D), f32)
    return pl.pallas_call(
        partial(middle_kernel, n_tensor),
        out_shape=[
            jax.ShapeDtypeStruct((n_tensor, items * ITEM, D), bf16),
            jax.ShapeDtypeStruct((rows - items * ITEM, D), bf16),
            jax.ShapeDtypeStruct((D, FF), bf16),
            jax.ShapeDtypeStruct((D, FF), bf16),
            jax.ShapeDtypeStruct((D, D), bf16),
            jax.ShapeDtypeStruct((rows, D), f32),
            jax.ShapeDtypeStruct((rows, D), bf16),
            jax.ShapeDtypeStruct((1, FF), f32),
            jax.ShapeDtypeStruct((8, D), f32),
        ],
        in_specs=[vmem] * 4 + [anywhere] * 3,
        out_specs=[anywhere] * 7 + [vmem] * 2,
        scratch_shapes=[
            pltpu.VMEM((2, D, FF), bf16),
            pltpu.VMEM((D, D), bf16),
            pltpu.VMEM((rows, FF), bf16),
            pltpu.VMEM((rows, FF), bf16),
            wide,
            wide,
            low,
            pltpu.VMEM((D, rows), bf16),
            pltpu.VMEM((D, rows), bf16),
            low,
            pltpu.VMEM((2, 2, D, D), bf16),
            low,
            low,
            pltpu.VMEM((256, D), bf16),
            pltpu.VMEM((256, D), f32),
            pltpu.VMEM((n_tensor, items * ITEM, D), bf16),
            dma((2 * steps + 1,)),
            dma((rows // 256,)),
            dma((rows // 256,)),
            dma((all_items,)),
            dma((all_items,)),
            dma((items * n_tensor,)),
            dma((items * n_tensor,)),
            dma((items * n_tensor,)),
            dma((items * n_tensor,)),
            dma((4,)),
            dma((3,)),
            dma((2 * n_tensor - 1,)),
        ],
        compiler_params=pltpu.CompilerParams(
            collective_id=3, has_side_effects=True, vmem_limit_bytes=VMEM_LIMIT
        ),
        cost_estimate=pl.CostEstimate(
            flops=2 * rows * D * (3 * D + 6 * FF),
            bytes_accessed=60 * 2**20,
            transcendentals=2 * rows * FF,
        ),
        name="middle",
    )(x, mixed, hid_all, vec_par, cotangent, attn_full, ffn_full)


def finish_kernel(n_tensor, *refs):
    dq, dk_own, dk_far, dv_own, dv_far, gh1, x_ref, weights = refs[:8]
    dw1, dw2, dwo, vec_sums, hid_sums = refs[8:13]
    attn_out, ffn_out, vec_out, qv_out, hid_out, tokens_out = refs[13:19]
    (
        dk,
        dv,
        xs,
        held,
        x_t,
        partial_sum,
        ready,
        dws,
        acc,
        got0,
        got1a,
        got1b,
        got2,
        zf,
        zf_got,
        za,
        za_got,
        run,
        run_got,
        run_z,
        wts,
    ) = refs[19:40]
    (
        e_send,
        e_recv,
        own_sem,
        s0,
        r0,
        s1,
        r1,
        s2,
        r2,
        zf_send,
        zf_recv,
        za_send,
        za_recv,
        sm,
        rm,
        h_send,
        h_recv,
        up_send,
        up_recv,
        dn_send,
        dn_recv,
        w_sem,
        copied,
    ) = refs[40:]
    s, c, t, x, core, sibling, over_x, over_y, across, along_z = places(n_tensor)
    n_rows = dq.shape[0]
    rows_each = n_rows // PIECES
    last = n_tensor - 1

    def pieces(path, i):
        if i < 2:
            return [(dw1 if path == 0 else dw2, i * WIDE, WIDE, 0)]
        if path == 0:
            return [(dws.at[0], 0, D, 0), (dws.at[1], 0, D, D)]
        return [(dws.at[2], 0, D, 0), (dwo, 0, D, D)]

    def slot(path, i):
        return path * 3 + i

    order = [(path, i) for i in range(3) for path in range(2)]

    def rows_of(xx, cc):
        return pl.ds(pl.multiple_of((4 * xx + 2 * cc) * STRIP, 2 * STRIP), 2 * STRIP)

    own, first = {}, {}
    for path, i in order:
        k = slot(path, i)
        own[k], first[k] = [], []
        for xx in range(2):
            for j, (ref, col, width, at) in enumerate(pieces(path, i)):
                n = (k * 2 + xx) * 2 + j
                cols, to = pl.ds(col, width), pl.ds(at, width)
                own[k].append(
                    pltpu.make_async_copy(
                        ref.at[rows_of(xx, core), cols], acc.at[k, xx, :, to], own_sem.at[n]
                    )
                )
                first[k].append(
                    remote(
                        ref.at[rows_of(xx, 1 - core), cols],
                        got0.at[k, xx, :, to],
                        s0.at[n],
                        r0.at[n],
                        sibling,
                    )
                )

    def start_own(i):
        for path in range(2):
            for copy in own[slot(path, i)]:
                copy.start()

    def start_first(i):
        for path in range(2):
            for copy in first[slot(path, i)]:
                copy.start()

    fetches = [
        pltpu.make_async_copy(gh1, partial_sum, w_sem.at[1]),
        pltpu.make_async_copy(weights.at[pl.ds(0, 3)], wts, w_sem.at[0]),
        pltpu.make_async_copy(x_ref, xs, w_sem.at[2]),
    ]
    for copy in fetches:
        copy.start()
    start_own(0)
    start_own(1)
    greet([sibling, over_x, over_y, across] + along_z)

    chunk = 256
    chunks = n_rows // chunk

    def exchange(i, n):
        at = pl.ds(i * chunk, chunk)
        src, dst = ((dk_far, dk), (dv_far, dv))[n]
        k = 2 * i + n
        return remote(src.at[at], dst.at[at], e_send.at[k], e_recv.at[k], sibling)

    swaps = [exchange(i, n) for i in range(chunks) for n in range(2)]
    for copy in swaps:
        copy.start()
    start_first(0)
    fetches[0].wait()
    fetches[1].wait()

    run[0] = jnp.zeros(run.shape[1:], f32)
    run[0, 0:6, :] = vec_sums[0:6, :]
    for n in range(FF // D):
        run[0, 8 + n : 9 + n, :] = hid_sums[:, n * D : (n + 1) * D]

    def keep_home(i):
        at = pl.ds(i * rows_each, rows_each)
        return pltpu.make_async_copy(ready.at[at], held.at[t, at], h_recv.at[i])

    def send_home(i):
        at = pl.ds(i * rows_each, rows_each)
        return remote(ready.at[at], held.at[t, at], h_send.at[i], h_recv.at[i], across)

    chain = Line(
        s,
        c,
        t,
        last,
        PIECES,
        rows_each,
        held,
        tokens_out,
        (up_send, up_recv),
        (dn_send, dn_recv),
        copied,
    )
    tick = chain.tick

    def send_own(i):
        @pl.when(core == c)
        def _():
            keep_home(i).wait()

        @pl.when(core != c)
        def _():
            send_home(i).wait_recv()

        chain.send_own(i)

    for i in range(PIECES):
        at = slice(i * rows_each, (i + 1) * rows_each)
        if i * rows_each % chunk == 0:
            for n in range(2):
                exchange(i * rows_each // chunk, n).wait_recv()
        dk_piece = (dk_own[at, :].astype(f32) + dk[at, :].astype(f32)).astype(bf16)
        dv_piece = (dv_own[at, :].astype(f32) + dv[at, :].astype(f32)).astype(bf16)
        dk[at, :] = dk_piece
        dv[at, :] = dv_piece
        total = partial_sum[at, :] + matmul_nt(dq[at, :], wts[0])
        total = total + matmul_nt(dk_piece, wts[1]) + matmul_nt(dv_piece, wts[2])
        ready[at, :] = total.astype(bf16)

        @pl.when(core == c)
        def _():
            keep_home(i).start()

        @pl.when(core != c)
        def _():
            send_home(i).start()

        if i > 0:
            send_own(i - 1)

    def add_rows(target, source, count):
        @pl.loop(0, count // 16)
        def _(j):
            rows = pl.ds(pl.multiple_of(j * 16, 16), 16)
            total = target[rows, :].astype(f32) + source[rows, :].astype(f32)
            target[rows, :] = total.astype(bf16)

    def half(cc):
        return pl.ds(pl.multiple_of(cc * STRIP, STRIP), STRIP)

    second, third = {}, {}

    def stage1(path, i):
        k = slot(path, i)
        for copy in own[k]:
            copy.wait()
        for copy in first[k]:
            copy.wait_recv()
        for xx in range(2):
            add_rows(acc.at[k, xx], got0.at[k, xx], 2 * STRIP)
        if path == 0:
            second[k] = remote(acc.at[k, 1 - x], got1a.at[i], s1.at[k], r1.at[k], over_x)
        else:
            second[k] = remote(
                acc.at[k, :, half(1 - c), :], got1b.at[i], s1.at[k], r1.at[k], over_y
            )
        second[k].start()

    def stage2(path, i):
        k = slot(path, i)
        second[k].wait_recv()
        if path == 0:
            add_rows(acc.at[k, x], got1a.at[i], 2 * STRIP)
            third[k] = remote(
                acc.at[k, x, half(1 - c), :], got2.at[k], s2.at[k], r2.at[k], over_y
            )
        else:
            for xx in range(2):
                add_rows(acc.at[k, xx, half(c), :], got1b.at[i, xx], STRIP)
            third[k] = remote(
                acc.at[k, 1 - x, half(c), :], got2.at[k], s2.at[k], r2.at[k], over_x
            )
        third[k].start()

    own_cols = D // n_tensor
    own_ff = FF // n_tensor
    per = WIDE // own_ff

    def stage3(path, i):
        k = slot(path, i)
        third[k].wait_recv()

        @pl.loop(0, STRIP // 16)
        def _(j):
            rows = pl.ds(pl.multiple_of(j * 16, 16), 16)
            here = pl.ds(pl.multiple_of(c * STRIP + j * 16, 16), 16)
            total = acc[k, x, here, :].astype(f32) + got2[k, rows, :].astype(f32)
            if i < 2:
                for n in range(per):
                    piece = total[:, n * own_ff : (n + 1) * own_ff].astype(bf16)
                    zf[per * i + n, rows, path * own_ff : (path + 1) * own_ff] = piece
            else:
                for n in range(n_tensor):
                    for m in range(2):
                        at = m * D + n * own_cols
                        to = (2 * path + m) * own_cols
                        piece = total[:, at : at + own_cols].astype(bf16)
                        za[n, rows, to : to + own_cols] = piece

    z_sent = []

    def z_step(k, buf, got, send, recv):
        @pl.when(t == k)
        def _():
            for d in range(last, k, -1):
                if k > 0:
                    hop(buf, got, send, recv, d, 0, k - 1).wait_recv()
                    add_rows(buf.at[d], got.at[0, d], STRIP)
                hop(buf, got, send, recv, d, 0, k + 1).start()

        @pl.when(t == last - k)
        def _():
            for d in range(0, last - k):
                if k > 0:
                    hop(buf, got, send, recv, d, 1, last - k + 1).wait_recv()
                    add_rows(buf.at[d], got.at[1, d], STRIP)
                hop(buf, got, send, recv, d, 1, last - k - 1).start()

    def hop(buf, got, send, recv, d, way, to):
        n = way * n_tensor + d
        return remote(buf.at[d], got.at[way, d], send.at[n], recv.at[n], (s, c, to))

    def z_collect(buf, got, send, recv, emit):
        @pl.when(t > 0)
        def _():
            hop(buf, got, send, recv, t, 0, t - 1).wait_recv()
            add_rows(buf.at[t], got.at[0, t], STRIP)

        @pl.when(t < last)
        def _():
            hop(buf, got, send, recv, t, 1, t + 1).wait_recv()
            add_rows(buf.at[t], got.at[1, t], STRIP)

        @pl.loop(0, STRIP // 16)
        def _(j):
            rows = pl.ds(pl.multiple_of(j * 16, 16), 16)
            emit(rows, buf[t, rows, :].astype(f32))

    def z_settle(buf, got, send, recv):
        for d in range(n_tensor):

            @pl.when(t < d)
            def _():
                hop(buf, got, send, recv, d, 0, t + 1).wait_send()

            @pl.when(t > d)
            def _():
                hop(buf, got, send, recv, d, 1, t - 1).wait_send()

    ffn_z = (zf, zf_got, zf_send, zf_recv)
    attn_z = (za, za_got, za_send, za_recv)

    small = []

    def small_send(n, where):
        small.append(remote(run.at[n], run_got.at[n], sm.at[n], rm.at[n], where))
        small[n].start()

    def small_add(n):
        small[n].wait_recv()
        run[n + 1] = run[n] + run_got[n]

    start_first(1)
    fetches[2].wait()
    for i in range(chunks):
        at = slice(i * chunk, (i + 1) * chunk)
        x_t[:, at] = xs[at, :].T
    dws[0] = matmul(x_t[...], dq[...]).astype(bf16)
    send_own(7)
    dws[1] = matmul(x_t[...], dk[...]).astype(bf16)
    dws[2] = matmul(x_t[...], dv[...]).astype(bf16)
    start_own(2)
    start_first(2)
    run[0, 6:7, :] = column_total(dq[...])
    run[0, 7:8, :] = column_total(dv[...])
    small_send(0, sibling)
    stage1(0, 0)
    stage1(1, 0)
    stage1(0, 1)
    stage1(1, 1)
    tick(0)
    stage1(0, 2)
    stage1(1, 2)
    small_add(0)
    small_send(1, over_x)
    tick(1)
    tick(2)
    tick(3)
    stage2(0, 0)
    stage2(1, 0)
    tick(4)
    tick(5)
    small_add(1)
    small_send(2, over_y)
    tick(6)
    stage2(0, 1)
    stage2(1, 1)
    tick(7)
    tick(8)
    small_add(2)
    run_z[t] = run[3]
    for k, where in enumerate(along_z):
        copy = remote(run.at[3], run_z.at[t], sm.at[3 + k], rm.at[3 + t], where)
        copy.start()
        z_sent.append(copy)
    stage3(0, 0)
    stage3(1, 0)
    stage2(0, 2)
    stage2(1, 2)
    tick(9)
    tick(10)
    stage3(0, 1)
    stage3(1, 1)
    z_step(0, *ffn_z)
    tick(11)
    tick(12)
    z_step(1, *ffn_z)
    stage3(0, 2)
    stage3(1, 2)
    z_step(0, *attn_z)
    tick(13)
    tick(14)
    z_step(2, *ffn_z)
    z_step(1, *attn_z)
    tick(15)
    tick(16)
    z_step(2, *attn_z)
    for j in range(17, PIECES * last):
        tick(j)

    for k, where in enumerate(along_z):
        u = where[2]
        remote(run.at[3], run_z.at[u], sm.at[3 + k], rm.at[3 + u], where).wait_recv()
    total = run_z[0]
    for n in range(1, n_tensor):
        total = total + run_z[n]
    vec_out[...] = total[0:6, :]
    for n in range(n_tensor):

        @pl.when(t == n)
        def _():
            qv_out[...] = total[6:8, n * own_cols : (n + 1) * own_cols]
            hid_out[...] = total[8 + n : 9 + n, :]


    def emit_ffn(rows, total):
        for m in range(2):
            ffn_out[m, rows, :] = total[:, m * own_ff : (m + 1) * own_ff]

    def emit_attn(rows, total):
        for m in range(4):
            attn_out[m, rows, :] = total[:, m * own_cols : (m + 1) * own_cols]

    z_collect(*ffn_z, emit_ffn)
    z_collect(*attn_z, emit_attn)
    z_settle(*ffn_z)
    z_settle(*attn_z)

    for copy in swaps:
        copy.wait_send()
    for path, i in order:
        k = slot(path, i)
        for copy in first[k]:
            copy.wait_send()
        second[k].wait_send()
        third[k].wait_send()
    for copy in small + z_sent:
        copy.wait_send()

    @pl.when(core != c)
    def _():
        for i in range(PIECES):
            send_home(i).wait_send()

    chain.settle()


def finish_all(n_tensor, grads, gh1, x, attn_full, dws, sums):
    rows = x.shape[0]
    own_cols, own_ff = D // n_tensor, FF // n_tensor
    dma = pltpu.SemaphoreType.DMA
    vmem, anywhere = pl.BlockSpec(memory_space=pltpu.VMEM), pl.BlockSpec(memory_space=pl.ANY)
    dq, dk_own, dk_far, dv_own, dv_far = grads
    tall = pltpu.VMEM((rows, D), bf16)
    items = PIECES * (n_tensor - 1)
    return pl.pallas_call(
        partial(finish_kernel, n_tensor),
        out_shape=[
            jax.ShapeDtypeStruct((4, STRIP, own_cols), f32),
            jax.ShapeDtypeStruct((2, STRIP, own_ff), f32),
            jax.ShapeDtypeStruct((6, D), f32),
            jax.ShapeDtypeStruct((2, own_cols), f32),
            jax.ShapeDtypeStruct((1, own_ff), f32),
            jax.ShapeDtypeStruct((n_tensor, rows, D), bf16),
        ],
        in_specs=[vmem, vmem, anywhere, vmem, anywhere] + [anywhere] * 6
        + [vmem] * 2,
        out_specs=[vmem] * 5 + [anywhere],
        scratch_shapes=[
            tall,
            tall,
            tall,
            pltpu.VMEM((n_tensor, rows, D), bf16),
            pltpu.VMEM((D, rows), bf16),
            pltpu.VMEM((rows, D), f32),
            tall,
            pltpu.VMEM((3, D, D), bf16),
            pltpu.VMEM((6, 2, 2 * STRIP, WIDE), bf16),
            pltpu.VMEM((6, 2, 2 * STRIP, WIDE), bf16),
            pltpu.VMEM((3, 2 * STRIP, WIDE), bf16),
            pltpu.VMEM((3, 2, STRIP, WIDE), bf16),
            pltpu.VMEM((6, STRIP, WIDE), bf16),
            pltpu.VMEM((n_tensor, STRIP, 2 * own_ff), bf16),
            pltpu.VMEM((2, n_tensor, STRIP, 2 * own_ff), bf16),
            pltpu.VMEM((n_tensor, STRIP, 4 * own_cols), bf16),
            pltpu.VMEM((2, n_tensor, STRIP, 4 * own_cols), bf16),
            pltpu.VMEM((4, 16, D), f32),
            pltpu.VMEM((3, 16, D), f32),
            pltpu.VMEM((n_tensor, 16, D), f32),
            pltpu.VMEM((3, D, D), bf16),
            dma((2 * rows // 256,)),
            dma((2 * rows // 256,)),
            dma((24,)),
            dma((24,)),
            dma((24,)),
            dma((6,)),
            dma((6,)),
            dma((6,)),
            dma((6,)),
            dma((2 * n_tensor,)),
            dma((2 * n_tensor,)),
            dma((2 * n_tensor,)),
            dma((2 * n_tensor,)),
            dma((3 + n_tensor,)),
            dma((3 + n_tensor,)),
            dma((PIECES,)),
            dma((PIECES,)),
            dma((items + PIECES,)),
            dma((items + PIECES,)),
            dma((items + PIECES,)),
            dma((items + PIECES,)),
            dma((3,)),
            dma((2 * n_tensor - 1,)),
        ],
        compiler_params=pltpu.CompilerParams(
            collective_id=1, has_side_effects=True, vmem_limit_bytes=VMEM_LIMIT
        ),
        cost_estimate=pl.CostEstimate(
            flops=12 * rows * D * D, bytes_accessed=400 * 2**20, transcendentals=0
        ),
        name="finish",
    )(dq, dk_own, dk_far, dv_own, dv_far, gh1, x, attn_full, *dws, *sums)


GROUP_RATES = (
    [2.0 / D**0.5] * 3 + [2.0 / (D // (4 * BLOCK)) ** 0.5],
    [2.0 / D**0.5, 2.0 / FF**0.5],
)


def last_kernel(tokens_ref, out_b, _output_a, *refs):
    attn_g, attn_w, attn_m, attn_v, ffn_g, ffn_w, ffn_m, ffn_v = refs[:8]
    plain = [refs[8 + 4 * n : 12 + 4 * n] for n in range(3)]
    tokens_out, output = refs[20:22]
    attn_moment, attn_square, out_states, attn_new, attn_copy = refs[22:27]
    ffn_moment, ffn_square, ffn_new, ffn_copy = refs[27:31]
    plain_out = [refs[31 + 3 * n : 34 + 3 * n] for n in range(3)]
    step = pl.program_id(0)

    @pl.when(step == 0)
    def _():
        for m in range(4):
            moment, square, new = adam_update(
                attn_w[m], attn_m[m], attn_v[m], attn_g[m], GROUP_RATES[0][m], decay_rate
            )
            if m < 3:
                attn_moment[m], attn_square[m] = moment, square
            else:
                out_states[0], out_states[1] = moment, square
            attn_new[m], attn_copy[m] = new, new.astype(bf16)
        for m in range(2):
            moment, square, new = adam_update(
                ffn_w[m], ffn_m[m], ffn_v[m], ffn_g[m], GROUP_RATES[1][m], decay_rate
            )
            ffn_moment[m], ffn_square[m] = moment, square
            ffn_new[m], ffn_copy[m] = new, new.astype(bf16)
        for (g, w, m, v), outs in zip(plain, plain_out):
            for ref, value in zip(outs, adam_update(w[...], m[...], v[...], g[...], 0.5, 0.0)):
                ref[...] = value

    tokens_out[...] = tokens_ref[...].astype(f32)

    output[...] = out_b[...]


def last(tokens_low, output, out_b, attn, ffn, plain):
    count, rows, _ = tokens_low.shape
    tile = lambda size, index: pl.BlockSpec((1, size, D), index)
    whole = lambda shape: pl.BlockSpec(
        shape, lambda i: (0,) * len(shape), pipeline_mode=pl.Buffered(1)
    )
    a, f = attn[0].shape, ffn[0].shape
    shapes = [
        ((3,) + a[1:], f32),
        ((3,) + a[1:], f32),
        ((2,) + a[1:], f32),
        (a, f32),
        (a, bf16),
        (f, f32),
        (f, f32),
        (f, f32),
        (f, bf16),
    ]
    for group in plain:
        shapes += [(group[0].shape, f32)] * 3
    inputs = list(attn) + list(ffn) + [array for group in plain for array in group]
    by_half = lambda i: (i // 2, i % 2, 0)
    by_one = lambda i: (i // 2, i % 2, 0)
    second = lambda i: (i // 2, 2 + i % 2, 0)
    quarter = rows // 4
    return pl.pallas_call(
        last_kernel,
        out_shape=[
            jax.ShapeDtypeStruct(tokens_low.shape, f32),
            jax.ShapeDtypeStruct(tokens_low.shape, bf16),
        ]
        + [jax.ShapeDtypeStruct(*entry) for entry in shapes],
        grid=(count * 2,),
        in_specs=[
            tile(rows // 2, by_half),
            tile(quarter, by_one),
            pl.BlockSpec(memory_space=pl.ANY),
        ]
        + [whole(array.shape) for array in inputs],
        out_specs=[tile(rows // 2, by_half), tile(quarter, second)]
        + [whole(shape) for shape, _ in shapes],
        input_output_aliases={2: 1},
        compiler_params=pltpu.CompilerParams(vmem_limit_bytes=VMEM_LIMIT),
        name="last",
    )(tokens_low, out_b, output, *inputs)


def make_body(mesh):
    n_shard, n_ctx, n_tensor = mesh.shape["shard"], mesh.shape["ctx"], mesh.shape["tensor"]
    rows_axes = ("shard", "ctx")
    all_axes = ("shard", "ctx", "tensor")
    paired = n_ctx == 2 and n_shard == 4 and n_tensor == 4

    def swapped(s, c):
        return (s - s % 2 + c, s % 2)

    def swap(array):
        if not paired:
            return array
        pairs = []
        for s in range(n_shard):
            for c in range(n_ctx):
                s_to, c_to = swapped(s, c)
                pairs.append((s * n_ctx + c, s_to * n_ctx + c_to))
        return lax.ppermute(array, rows_axes, pairs)

    def spread(array):
        return lax.all_gather(swap(array), "tensor", axis=0, tiled=True)

    def body(
        tokens,
        cotangent,
        segments,
        rand_blocks,
        attn_w,
        attn_m,
        attn_v,
        ffn_w,
        ffn_m,
        ffn_v,
        qv_bias,
        qv_m,
        qv_v,
        hid_bias,
        hid_m,
        hid_v,
        vec_par,
        vec_m,
        vec_v,
    ):
        t_index = lax.axis_index("tensor")
        nseq = tokens.shape[0] // n_tensor
        piece_len = tokens.shape[1]
        nb = piece_len // BLOCK
        own_rows, own_cols = attn_w.shape[1], attn_w.shape[2]
        own_ff = ffn_w.shape[2]

        def mine(array):
            return lax.dynamic_slice_in_dim(array, t_index * nseq, nseq, 0)

        ints = jnp.concatenate(
            [mine(segments), mine(rand_blocks).reshape(nseq, -1)], axis=1
        )
        ints = swap(ints)
        length = segments.shape[1]
        segs, rand = ints[:, :length], ints[:, length:].reshape(nseq, length // BLOCK, -1)
        piece = lax.axis_index("shard") % 2 if paired else lax.axis_index("ctx")
        tables = attention_tables(segs, rand, piece, nb, paired)

        if paired:
            rand_own, _meta, table = tables
            attn_full, ffn_full, hid_all, x, queries, keys, values, mixed, lse = start(
                n_tensor, attn_w, ffn_w, qv_bias, hid_bias, table[0], rand_own, tokens
            )
            flat = x
            x, queries = x[None], queries[None]
            keys, values = keys.reshape(1, length, D), values.reshape(1, length, D)
            pieces = [piece_len, piece_len]
        else:
            x, cot = mine(tokens), mine(cotangent)
            pieces = [length]
            ffn_z = lax.all_gather(ffn_w.astype(bf16), "tensor", axis=0, tiled=False)
            ffn_z = ffn_z.transpose(1, 2, 0, 3).reshape(2, own_rows, FF)
            ffn_full = lax.all_gather(ffn_z, rows_axes, axis=1, tiled=True)
            flat = x.reshape(-1, D)
            attn_low = attn_w.astype(bf16)
            attn_low = jnp.concatenate([attn_low[i] for i in range(4)], axis=1)
            attn_z = lax.all_gather(attn_low, "tensor", axis=0, tiled=False)
            attn_z = attn_z.reshape(n_tensor, own_rows, 4, own_cols).transpose(2, 1, 0, 3)
            attn_full = lax.all_gather(
                attn_z.reshape(4, own_rows, D), rows_axes, axis=1, tiled=True
            )
            bias_own = jnp.concatenate([qv_bias.reshape(-1), hid_bias])
            bias_all = lax.all_gather(bias_own, "tensor", axis=0, tiled=False)
            qv_all = bias_all[:, : 2 * own_cols].reshape(n_tensor, 2, own_cols)
            qv_all = qv_all.transpose(1, 0, 2).reshape(2, D)
            hid_all = bias_all[:, 2 * own_cols :].reshape(FF)
            keys = matmul(flat, attn_full[1]).astype(bf16).reshape(x.shape)
            values = (matmul(flat, attn_full[2]) + qv_all[1]).astype(bf16).reshape(x.shape)
            keys = lax.all_gather(keys, "ctx", axis=1, tiled=True)
            values = lax.all_gather(values, "ctx", axis=1, tiled=True)
            queries = (matmul(flat, attn_full[0]) + qv_all[0]).astype(bf16) * 0.125
            queries = queries.reshape(x.shape)
            mixed, lse = attend(tables, queries, keys, values)
        mixed_low = mixed.reshape(-1, D)
        if paired:
            out_a, out_b, dw1, dw2, dwo, grad_first_in, grad_mixed, hid_sum, vec_sums = middle(
                n_tensor, flat, mixed_low, hid_all, vec_par, cotangent, attn_full, ffn_full
            )
            out_b = lax.all_gather(out_b, "tensor", axis=0, tiled=False)
        else:
            act, slope, h1, result, grad_second, second_sums = feed_forward(
                flat, mixed_low, cot.reshape(-1, D), attn_full, ffn_full, hid_all, vec_par
            )
            output = spread(result.reshape(x.shape))
            out_a, out_b = output[:, : piece_len // 2], output[:, piece_len // 2 :]
            dw1, dw2, dwo, grad_first_in, grad_mixed, hid_sum, first_sums = feed_back(
                grad_second, h1, mixed_low, attn_full, ffn_full, act, slope, vec_par
            )

        grad_mixed = grad_mixed.reshape(x.shape)
        grad_query, output, dk_parts, dv_parts = attend_back(
            tables,
            queries,
            grad_mixed,
            mixed.reshape(x.shape),
            lse.reshape(nseq, nb, 8, ROWS),
            out_a,
            keys,
            values,
            pieces,
        )

        grad_query_low = grad_query.reshape(-1, D)
        if paired:
            attn_grad, ffn_grad, vec_grad, qv_grad, hid_grad, grad_tokens = finish_all(
                n_tensor,
                [grad_query_low] + [part[0] for part in list(dk_parts) + list(dv_parts)],
                grad_first_in,
                flat,
                attn_full,
                (dw1, dw2, dwo),
                (vec_sums, hid_sum),
            )
        else:
            grad_keys = lax.psum_scatter(dk_parts[0], "ctx", scatter_dimension=1, tiled=True)
            grad_values = lax.psum_scatter(dv_parts[0], "ctx", scatter_dimension=1, tiled=True)
            grad_keys_low = grad_keys.reshape(-1, D)
            grad_values_low = grad_values.reshape(-1, D)
            into_tokens = (
                matmul_nt(grad_query_low, attn_full[0])
                + matmul_nt(grad_keys_low, attn_full[1])
                + matmul_nt(grad_values_low, attn_full[2])
            )
            grad_tokens = spread((grad_first_in + into_tokens).astype(bf16).reshape(x.shape))
            dwq = matmul_tn(flat, grad_query_low).astype(bf16)
            dwk = matmul_tn(flat, grad_keys_low).astype(bf16)
            dwv = matmul_tn(flat, grad_values_low).astype(bf16)
            small = jnp.concatenate(
                [
                    first_sums[0],
                    first_sums[1],
                    second_sums[0],
                    second_sums[1],
                    first_sums[2],
                    second_sums[2],
                    column_sum(grad_query_low),
                    column_sum(grad_values_low),
                    hid_sum[0],
                ]
            )
            ffn_grad = lax.psum_scatter(
                jnp.stack([dw1, dw2]), rows_axes, scatter_dimension=1, tiled=True
            )
            ffn_grad = ffn_grad.reshape(2, own_rows, n_tensor, own_ff).transpose(2, 0, 1, 3)
            ffn_grad = lax.psum_scatter(ffn_grad, "tensor", scatter_dimension=0, tiled=False)
            ffn_grad = ffn_grad.astype(f32)
            attn_grad = lax.psum_scatter(
                jnp.stack([dwq, dwk, dwv, dwo]), rows_axes, scatter_dimension=1, tiled=True
            )
            attn_grad = attn_grad.reshape(4, own_rows, n_tensor, own_cols).transpose(2, 1, 0, 3)
            attn_grad = lax.psum_scatter(
                attn_grad.reshape(n_tensor, own_rows, D), "tensor", scatter_dimension=0
            )
            attn_grad = attn_grad.reshape(own_rows, 4, own_cols).transpose(1, 0, 2).astype(f32)
            small = lax.psum(small, all_axes)
            vec_grad = small[: 6 * D].reshape(6, D)
            qv_grad = lax.dynamic_slice_in_dim(
                small[6 * D : 8 * D].reshape(2, D), t_index * own_cols, own_cols, 1
            )
            hid_grad = lax.dynamic_slice_in_dim(
                small[8 * D : 8 * D + FF], t_index * own_ff, own_ff, 0
            )

        grad_tokens, output, *updated = last(
            grad_tokens,
            output,
            out_b,
            (attn_grad, attn_w, attn_m, attn_v),
            (ffn_grad, ffn_w, ffn_m, ffn_v),
            [
                (qv_grad, qv_bias, qv_m, qv_v),
                (hid_grad.reshape(own_ff), hid_bias, hid_m, hid_v),
                (vec_grad, vec_par, vec_m, vec_v),
            ],
        )
        return (output, grad_tokens, *updated)

    return body


def solution(mesh):
    rows = P("shard", "ctx", None)
    weight = P(None, ("shard", "ctx"), "tensor")
    in_specs = (
        (rows, rows, P("shard", None), P("shard", None, None))
        + (weight,) * 6
        + (P(None, "tensor"),) * 3
        + (P("tensor"),) * 3
        + (P(),) * 3
    )
    out_specs = (
        (rows, rows)
        + (weight,) * 9
        + (P(None, "tensor"),) * 3
        + (P("tensor"),) * 3
        + (P(),) * 3
    )
    return jax.shard_map(
        make_body(mesh), mesh=mesh, in_specs=in_specs, out_specs=out_specs, check_vma=False
    )
```

```python
from functools import partial

import jax
import jax.numpy as jnp
from jax import lax
from jax.experimental import pallas as pl
from jax.experimental.pallas import tpu as pltpu
from jax.sharding import PartitionSpec as P

D = 768
HEAD_DIM = 64
FF = 3072
BLOCK = 64
STEP = 5
GROUP = 4 * HEAD_DIM
GROUPS = D // GROUP
ROWS = 4 * BLOCK
LISTED = 8
KEYS = LISTED * BLOCK
VMEM_LIMIT = 60 * 2**20

beta_first = 0.9
beta_second = 0.999
adam_eps = 1e-08
decay_rate = 0.01
norm_eps = 1e-06
neg_large = -1e30

f32 = jnp.float32
bf16 = jnp.bfloat16


def matmul(left, right):
    return jnp.dot(left, right, preferred_element_type=f32)


def matmul_tn(left, right):
    return lax.dot_general(left, right, (((0,), (0,)), ((), ())), preferred_element_type=f32)


def matmul_nt(left, right):
    return lax.dot_general(left, right, (((1,), (1,)), ((), ())), preferred_element_type=f32)


def column_sum(array_in):
    return jnp.sum(array_in.astype(f32), axis=0)


def adam_update(weight, moment, square, gradient, step_rates, decay_on):
    moment_new = beta_first * moment + (1.0 - beta_first) * gradient
    square_new = beta_second * square + (1.0 - beta_second) * gradient * gradient
    step_ratio = (
        moment_new
        / (1.0 - beta_first**STEP)
        / (jnp.sqrt(square_new / (1.0 - beta_second**STEP)) + adam_eps)
    )
    weight_new = weight - step_rates * (step_ratio + decay_on * weight)
    return (moment_new, square_new, weight_new)


def same_head():
    row_head = lax.broadcasted_iota(jnp.int32, (ROWS, GROUP), 0) // BLOCK
    col_head = lax.broadcasted_iota(jnp.int32, (ROWS, GROUP), 1) // HEAD_DIM
    return row_head == col_head


def spread_heads(block, keep):
    stacked = jnp.concatenate([block] * 4, axis=0)
    return jnp.where(keep, stacked, jnp.zeros_like(stacked))


def fold_heads(full, keep):
    kept = jnp.where(keep, full, 0.0)
    return sum(kept[h * BLOCK : (h + 1) * BLOCK] for h in range(4))


def load_keys(k_all, v_all, seq, k_buf, v_buf, sems):
    return [
        pltpu.make_async_copy(k_all.at[seq], k_buf, sems.at[0]),
        pltpu.make_async_copy(v_all.at[seq], v_buf, sems.at[1]),
    ]


def picked_rows(buf, spots, cols):
    return jnp.concatenate([buf[at, :, cols] for at in spots], axis=0)


def chunk_rows(buf, i, cols):
    blocks = buf[pl.ds(i * LISTED, LISTED), :, cols]
    return blocks.reshape(KEYS, GROUP)


def listed_blocks(rand, base, blk, first, own, total):
    one = lambda condition: condition.astype(jnp.int32)
    me = first + blk
    ids = [me - 1, me, me + 1, me * 0, me * 0 + 1] + [rand[base + n] for n in range(LISTED - 5)]
    spots, unused, common = [], [], []
    for n, block in enumerate(ids):
        out = one(block < 0) + one(block >= total)
        for earlier in ids[:n]:
            out = out + one(block == earlier)
        out = lax.min(out, jnp.int32(1))
        at = lax.max(jnp.int32(0), lax.min(block, jnp.int32(total - 1))) - first + own
        spots.append(at + total * one(at < 0))
        unused.append(out)
        common.append(one(block < 2) * (1 - out))
    return spots, unused, common


def code_rows(tab_ref, spots, unused, common):
    low_half = lax.broadcasted_iota(jnp.int32, (1, 2 * BLOCK), 1) < BLOCK

    def one(n):
        plain = (1 - unused[n] - common[n]).astype(f32)
        return tab_ref[spots[n]] * plain - (unused[n] + 2 * common[n]).astype(f32)

    return [jnp.where(low_half, one(n), one(n + 1)) for n in range(0, LISTED, 2)]


def column_of(row):
    return jnp.broadcast_to(row, (2 * BLOCK, 2 * BLOCK)).T


def mask_bias(document, code):
    return jnp.where((document == code) | (code == -2.0), 0.0, neg_large)


def row_of(column):
    return jnp.broadcast_to(column, (ROWS, 2 * BLOCK)).T[0:1, :]


def forward_block(q_ref, out_ref, lse_ref, k_buf, v_buf, s_buf, tab_ref, rand, base, blk, first, own):
    keep = same_head()
    total_blocks = k_buf.shape[0]
    chunks = total_blocks // LISTED
    is_global = first + blk < 2

    @pl.when(jnp.logical_not(is_global))
    def _():
        spots, unused, common = listed_blocks(rand, base, blk, first, own, total_blocks)
        mine = column_of(tab_ref[own + blk])[:BLOCK]
        mine = jnp.concatenate([mine] * 4, axis=0)
        codes = code_rows(tab_ref, spots, unused, common)
        bias = jnp.concatenate([mask_bias(mine, code) for code in codes], axis=1)
        for g in range(GROUPS):
            cols = slice(g * GROUP, (g + 1) * GROUP)
            q_full = spread_heads(q_ref[:, cols], keep)
            scores = matmul_nt(q_full, picked_rows(k_buf, spots, cols)) + bias
            largest = jnp.max(scores, axis=-1, keepdims=True)
            weights = jnp.exp(scores - largest)
            total = jnp.sum(weights, axis=-1, keepdims=True)
            full = matmul(weights.astype(bf16), picked_rows(v_buf, spots, cols))
            out_ref[:, cols] = fold_heads(full * (1.0 / total), keep).astype(bf16)
            lse_ref[g : g + 1, :] = row_of(largest + jnp.log(total))

    @pl.when(is_global)
    def _():
        for g in range(GROUPS):
            cols = slice(g * GROUP, (g + 1) * GROUP)
            q_full = spread_heads(q_ref[:, cols], keep)

            def score_chunk(i, largest):
                scores = matmul_nt(q_full, chunk_rows(k_buf, i, cols))
                s_buf[i] = scores
                return jnp.maximum(largest, jnp.max(scores, axis=-1, keepdims=True))

            largest = lax.fori_loop(0, chunks, score_chunk, jnp.full((ROWS, 1), neg_large, f32))

            def mix_chunk(i, carry):
                total, full = carry
                weights = jnp.exp(s_buf[i] - largest)
                total = total + jnp.sum(weights, axis=-1, keepdims=True)
                return total, full + matmul(weights.astype(bf16), chunk_rows(v_buf, i, cols))

            total, full = lax.fori_loop(
                0, chunks, mix_chunk, (jnp.zeros((ROWS, 1), f32), jnp.zeros((ROWS, GROUP), f32))
            )
            out_ref[:, cols] = fold_heads(full * (1.0 / total), keep).astype(bf16)
            lse_ref[g : g + 1, :] = row_of(largest + jnp.log(total))


def forward_kernel(
    rand, meta, q_ref, tab_ref, k_all, v_all, out_ref, lse_ref, k_buf, v_buf, s_buf, sems
):
    seq, blk = pl.program_id(0), pl.program_id(1)
    nb = pl.num_programs(1)

    @pl.when(blk == 0)
    def _():
        copies = load_keys(k_all, v_all, seq, k_buf, v_buf, sems)
        for c in copies:
            c.start()
        for c in copies:
            c.wait()

    base = (seq * nb + blk) * (LISTED - 5)
    forward_block(
        q_ref, out_ref, lse_ref, k_buf, v_buf, s_buf, tab_ref, rand, base, blk, meta[0], meta[1]
    )


def back_tile(k_rows, v_rows, q_full, go_full, bias, lse, centre):
    scores = matmul_nt(k_rows, q_full)
    if bias is not None:
        scores = scores + bias
    probs = jnp.exp(scores - lse)
    grad_probs = matmul_nt(v_rows, go_full)
    grad_scores = (probs * (grad_probs - centre)).astype(bf16)
    dv_rows = matmul(probs.astype(bf16), go_full)
    dk_rows = matmul(grad_scores, q_full)
    return matmul_tn(grad_scores, k_rows), dk_rows, dv_rows


def backward_kernel(
    n_out, rand, meta, q_ref, go_ref, mixed_ref, lse_ref, tab_ref, out_a, k_all, v_all, *rest
):
    dq_ref, out_ref, *rest = rest
    dk_refs, dv_refs = rest[:n_out], rest[n_out : 2 * n_out]
    k_buf, v_buf, dk_acc, dv_acc, sems = rest[2 * n_out :]
    seq, blk = pl.program_id(0), pl.program_id(1)
    nb = pl.num_programs(1)
    total_blocks = k_buf.shape[0]
    chunks = total_blocks // LISTED

    out_ref[...] = out_a[...]

    @pl.when(blk == 0)
    def _():
        copies = load_keys(k_all, v_all, seq, k_buf, v_buf, sems)
        for c in copies:
            c.start()
        dk_acc[...] = jnp.zeros_like(dk_acc)
        dv_acc[...] = jnp.zeros_like(dv_acc)
        for c in copies:
            c.wait()

    keep = same_head()
    is_global = meta[0] + blk < 2
    base = (seq * nb + blk) * (LISTED - 5)

    def operands(g):
        cols = slice(g * GROUP, (g + 1) * GROUP)
        q_full = spread_heads(q_ref[:, cols], keep)
        go_full = spread_heads(go_ref[:, cols], keep)
        mixed = jnp.concatenate([mixed_ref[:, cols]] * 4, axis=0)
        product = go_full.astype(f32) * mixed.astype(f32)
        centre = row_of(jnp.sum(product, axis=-1, keepdims=True))
        return cols, q_full, go_full, lse_ref[g : g + 1, :], centre

    @pl.when(jnp.logical_not(is_global))
    def _():
        spots, unused, common = listed_blocks(rand, base, blk, meta[0], meta[1], total_blocks)
        stores = [at + (total_blocks - at) * out for at, out in zip(spots, unused)]
        own = tab_ref[meta[1] + blk]
        codes = code_rows(tab_ref, spots, unused, common)
        bias = jnp.concatenate([mask_bias(own, column_of(code)) for code in codes], axis=0)
        bias = jnp.concatenate([bias, bias], axis=1)
        for g in range(GROUPS):
            cols, q_full, go_full, lse, centre = operands(g)
            k_rows, v_rows = picked_rows(k_buf, spots, cols), picked_rows(v_buf, spots, cols)
            dq_full, dk_rows, dv_rows = back_tile(
                k_rows, v_rows, q_full, go_full, bias, lse, centre
            )
            dq_ref[:, cols] = (fold_heads(dq_full, keep) * 0.125).astype(bf16)
            places = [pl.ds(pl.multiple_of(at * BLOCK, BLOCK), BLOCK) for at in stores]
            dk_old = [dk_acc[at, cols] for at in places]
            dv_old = [dv_acc[at, cols] for at in places]
            for n, at in enumerate(places):
                own_rows = slice(n * BLOCK, (n + 1) * BLOCK)
                dk_acc[at, cols] = dk_old[n] + dk_rows[own_rows]
                dv_acc[at, cols] = dv_old[n] + dv_rows[own_rows]

    @pl.when(is_global)
    def _():
        for g in range(GROUPS):
            cols, q_full, go_full, lse, centre = operands(g)

            def chunk_back(i, dq_full):
                rows = pl.ds(pl.multiple_of(i * KEYS, KEYS), KEYS)
                dq_now, dk_rows, dv_rows = back_tile(
                    chunk_rows(k_buf, i, cols),
                    chunk_rows(v_buf, i, cols),
                    q_full,
                    go_full,
                    None,
                    lse,
                    centre,
                )
                dk_acc[rows, cols] += dk_rows
                dv_acc[rows, cols] += dv_rows
                return dq_full + dq_now

            dq_full = lax.fori_loop(0, chunks, chunk_back, jnp.zeros((ROWS, GROUP), f32))
            dq_ref[:, cols] = (fold_heads(dq_full, keep) * 0.125).astype(bf16)

    @pl.when(blk == nb - 1)
    def _():
        row = 0
        for dk_ref, dv_ref in zip(dk_refs, dv_refs):
            rows = dk_ref.shape[0]
            dk_ref[...] = dk_acc[row : row + rows].astype(bf16)
            dv_ref[...] = dv_acc[row : row + rows].astype(bf16)
            row += rows


def attention_tables(segments, random, piece, nb, own_first):
    seq_count, length = segments.shape
    total = length // BLOCK
    first = piece * nb
    rand = lax.dynamic_slice_in_dim(random, first, nb, 1).reshape(-1)
    table = segments.reshape(seq_count, total, BLOCK).astype(f32)
    table = jnp.concatenate([table, table], axis=2)[:, :, None, :]
    if own_first:
        table = lax.dynamic_slice_in_dim(jnp.concatenate([table, table], axis=1), first, total, 1)
    meta = jnp.stack([first, jnp.zeros_like(first) if own_first else first]).astype(jnp.int32)
    return rand, meta, table


def as_blocks(rows):
    return rows.reshape(rows.shape[0], -1, BLOCK, D)


def attend(tables, q, keys, values):
    rand, meta, table = tables
    seq_count, piece_len, _ = q.shape
    nb = piece_len // BLOCK
    length = keys.shape[1]
    any_spec = pl.BlockSpec(memory_space=pl.ANY)
    row_spec = pl.BlockSpec((None, BLOCK, D), lambda s, b, *_: (s, b, 0))
    return pl.pallas_call(
        forward_kernel,
        out_shape=[
            jax.ShapeDtypeStruct(q.shape, bf16),
            jax.ShapeDtypeStruct((seq_count, nb, 8, ROWS), f32),
        ],
        grid_spec=pltpu.PrefetchScalarGridSpec(
            num_scalar_prefetch=2,
            grid=(seq_count, nb),
            in_specs=[
                row_spec,
                pl.BlockSpec((None,) + table.shape[1:], lambda s, b, *_: (s, 0, 0, 0)),
                any_spec,
                any_spec,
            ],
            out_specs=[
                row_spec,
                pl.BlockSpec((None, None, 8, ROWS), lambda s, b, *_: (s, b, 0, 0)),
            ],
            scratch_shapes=[
                pltpu.VMEM((length // BLOCK, BLOCK, D), bf16),
                pltpu.VMEM((length // BLOCK, BLOCK, D), bf16),
                pltpu.VMEM((length // KEYS, ROWS, KEYS), f32),
                pltpu.SemaphoreType.DMA((2,)),
            ],
        ),
        compiler_params=pltpu.CompilerParams(vmem_limit_bytes=VMEM_LIMIT),
        name="attend",
    )(rand, meta, q, table, as_blocks(keys), as_blocks(values))


def attend_back(tables, q, grad_mixed, mixed, lse, out_a, keys, values, pieces):
    rand, meta, table = tables
    seq_count, piece_len, _ = q.shape
    nb = piece_len // BLOCK
    length = keys.shape[1]
    any_spec = pl.BlockSpec(memory_space=pl.ANY)
    row_spec = pl.BlockSpec((None, BLOCK, D), lambda s, b, *_: (s, b, 0))
    count, half, _ = out_a.shape
    share = count * half // (seq_count * nb)
    if share <= half:
        per = half // share
        tile = pl.BlockSpec(
            (None, share, D), lambda s, b, *_: ((s * nb + b) // per, (s * nb + b) % per, 0)
        )
    else:
        tile = pl.BlockSpec((share // half, half, D), lambda s, b, *_: (s * nb + b, 0, 0))
    part_specs = [pl.BlockSpec((None, rows, D), lambda s, b, *_: (s, 0, 0)) for rows in pieces]
    part_shapes = [jax.ShapeDtypeStruct((seq_count, rows, D), bf16) for rows in pieces]
    out = pl.pallas_call(
        partial(backward_kernel, len(pieces)),
        out_shape=[
            jax.ShapeDtypeStruct(q.shape, bf16),
            jax.ShapeDtypeStruct((count, 2 * half, D), bf16),
        ]
        + part_shapes * 2,
        grid_spec=pltpu.PrefetchScalarGridSpec(
            num_scalar_prefetch=2,
            grid=(seq_count, nb),
            in_specs=[
                row_spec,
                row_spec,
                row_spec,
                pl.BlockSpec((None, None, 8, ROWS), lambda s, b, *_: (s, b, 0, 0)),
                pl.BlockSpec((None,) + table.shape[1:], lambda s, b, *_: (s, 0, 0, 0)),
                tile,
                any_spec,
                any_spec,
            ],
            out_specs=[row_spec, tile] + part_specs * 2,
            scratch_shapes=[
                pltpu.VMEM((length // BLOCK, BLOCK, D), bf16),
                pltpu.VMEM((length // BLOCK, BLOCK, D), bf16),
                pltpu.VMEM((length + BLOCK, D), f32),
                pltpu.VMEM((length + BLOCK, D), f32),
                pltpu.SemaphoreType.DMA((2,)),
            ],
        ),
        compiler_params=pltpu.CompilerParams(vmem_limit_bytes=VMEM_LIMIT),
        cost_estimate=pl.CostEstimate(
            flops=seq_count * nb * GROUPS * 10 * ROWS * KEYS * GROUP,
            bytes_accessed=seq_count * (3 * piece_len + 4 * length) * D * 2,
            transcendentals=seq_count * nb * GROUPS * ROWS * KEYS,
        ),
        name="attend_back",
    )(rand, meta, q, grad_mixed, mixed, lse, table, out_a, as_blocks(keys), as_blocks(values))
    return out[0], out[1], out[2 : 2 + len(pieces)], out[2 + len(pieces) :]


def norm_parts(hidden):
    centred = hidden - jnp.mean(hidden, axis=-1, keepdims=True)
    scale = lax.rsqrt(jnp.mean(centred * centred, axis=-1, keepdims=True) + norm_eps)
    return centred * scale, scale


def norm_back(grad, unit, scale, gain):
    inner = grad * gain
    return scale * (
        inner
        - jnp.mean(inner, axis=-1, keepdims=True)
        - unit * jnp.mean(inner * unit, axis=-1, keepdims=True)
    )


def gelu_and_slope(pre):
    bell = jnp.exp(-0.5 * pre * pre)
    t = 1.0 / (1.0 + (0.3275911 * 0.5**0.5) * jnp.abs(pre))
    poly = 0.5 * 1.061405429
    for coefficient in (-1.453152027, 1.421413741, -0.284496736, 0.254829592):
        poly = poly * t + 0.5 * coefficient
    tail = poly * t * bell
    phi = jnp.where(pre >= 0.0, 1.0 - tail, tail)
    return pre * phi, phi + pre * bell * 0.3989422804014327


def column_total(array):
    return jnp.sum(array.astype(f32), axis=0, keepdims=True)


def up_kernel(
    chunk,
    x_ref,
    mixed_ref,
    cot_ref,
    wo_ref,
    w1_ref,
    w2_ref,
    hid_ref,
    vec_ref,
    act_ref,
    slope_ref,
    h1_ref,
    res_ref,
    gs_ref,
    sums_ref,
    low,
    down,
):
    step = pl.program_id(0)
    chunks = x_ref.shape[0] // chunk

    @pl.when(step == 0)
    def _():
        @pl.loop(0, chunks)
        def _(i):
            rows = pl.ds(pl.multiple_of(i * chunk, chunk), chunk)
            h1 = x_ref[rows, :].astype(f32) + matmul_nt(mixed_ref[rows, :], wo_ref[...])
            h1 = h1 + vec_ref[4:5, :]
            h1_ref[rows, :] = h1
            unit, _scale = norm_parts(h1)
            low[rows, :] = (unit * vec_ref[0:1, :] + vec_ref[1:2, :]).astype(bf16)
            down[rows, :] = jnp.zeros((chunk, D), f32)

    for i in range(chunks):
        rows = slice(i * chunk, (i + 1) * chunk)
        pre = matmul(low[rows, :], w1_ref[...]) + hid_ref[...]
        act, slope = gelu_and_slope(pre)
        act = act.astype(bf16)
        act_ref[rows, :] = act
        slope_ref[rows, :] = slope.astype(bf16)
        down[rows, :] += matmul_nt(act, w2_ref[...])

    @pl.when(step == pl.num_programs(0) - 1)
    def _():
        sums_ref[...] = jnp.zeros_like(sums_ref)

        @pl.loop(0, chunks)
        def _(i):
            rows = pl.ds(pl.multiple_of(i * chunk, chunk), chunk)
            unit, _scale = norm_parts(h1_ref[rows, :])
            first = unit * vec_ref[0:1, :] + vec_ref[1:2, :]
            unit, scale = norm_parts(first + down[rows, :] + vec_ref[5:6, :])
            res_ref[rows, :] = (unit * vec_ref[2:3, :] + vec_ref[3:4, :]).astype(bf16)
            cot = cot_ref[rows, :].astype(f32)
            grad = norm_back(cot, unit, scale, vec_ref[2:3, :])
            gs_ref[rows, :] = grad
            sums_ref[0:1, :] += column_total(cot * unit)
            sums_ref[1:2, :] += column_total(cot)
            sums_ref[2:3, :] += column_total(grad.astype(bf16))


def feed_forward(x, mixed, cot, attn_full, ffn_full, hid_all, vec_par):
    rows = x.shape[0]
    chunk = min(256, rows)
    steps = FF // D
    whole = lambda shape: pl.BlockSpec(shape, lambda t: (0,) * len(shape))
    once = lambda shape: pl.BlockSpec(
        shape, lambda t: (0,) * len(shape), pipeline_mode=pl.Buffered(1)
    )
    hidden = pl.BlockSpec((rows, D), lambda t: (0, t))
    return pl.pallas_call(
        partial(up_kernel, chunk),
        out_shape=[
            jax.ShapeDtypeStruct((rows, FF), bf16),
            jax.ShapeDtypeStruct((rows, FF), bf16),
            jax.ShapeDtypeStruct((rows, D), f32),
            jax.ShapeDtypeStruct((rows, D), bf16),
            jax.ShapeDtypeStruct((rows, D), f32),
            jax.ShapeDtypeStruct((8, D), f32),
        ],
        grid=(steps,),
        in_specs=[
            once((rows, D)),
            once((rows, D)),
            once((rows, D)),
            pl.BlockSpec((None, D, D), lambda t: (3, 0, 0), pipeline_mode=pl.Buffered(1)),
            pl.BlockSpec((None, D, D), lambda t: (0, 0, t)),
            pl.BlockSpec((None, D, D), lambda t: (1, 0, t)),
            pl.BlockSpec((1, D), lambda t: (0, t)),
            whole((6, D)),
        ],
        out_specs=[
            hidden,
            hidden,
            whole((rows, D)),
            whole((rows, D)),
            whole((rows, D)),
            whole((8, D)),
        ],
        scratch_shapes=[pltpu.VMEM((rows, D), bf16), pltpu.VMEM((rows, D), f32)],
        compiler_params=pltpu.CompilerParams(vmem_limit_bytes=VMEM_LIMIT),
        cost_estimate=pl.CostEstimate(
            flops=2 * rows * D * (D + 2 * FF),
            bytes_accessed=rows * D * 30 + 2 * D * FF * 2,
            transcendentals=2 * rows * FF,
        ),
        name="feed_forward",
    )(x, mixed, cot, attn_full, ffn_full, ffn_full, hid_all.reshape(1, FF), vec_par)


def down_kernel(
    chunk,
    gs_ref,
    h1_ref,
    mixed_ref,
    wo_ref,
    w1_ref,
    w2_ref,
    act_ref,
    slope_ref,
    vec_ref,
    dw1_ref,
    dw2_ref,
    dwo_ref,
    gh1_ref,
    gm_ref,
    hid_ref,
    sums_ref,
    turned,
    low_t,
    pre,
    total,
):
    step = pl.program_id(0)
    n_rows = gs_ref.shape[0]
    chunks = n_rows // chunk

    @pl.when(step == 0)
    def _():
        @pl.loop(0, chunks)
        def _(i):
            rows = pl.ds(pl.multiple_of(i * chunk, chunk), chunk)
            unit, _scale = norm_parts(h1_ref[rows, :])
            low = unit * vec_ref[0:1, :] + vec_ref[1:2, :]
            low_t[:, rows] = low.T.astype(bf16)
            turned[:, rows] = gs_ref[rows, :].T.astype(bf16)
            total[rows, :] = gs_ref[rows, :]

    for i in range(chunks):
        rows = slice(i * chunk, (i + 1) * chunk)
        grad_act = matmul(gs_ref[rows, :].astype(bf16), w2_ref[...]).astype(bf16).astype(f32)
        grad_pre = (grad_act * slope_ref[rows, :].astype(f32)).astype(bf16)
        pre[rows, :] = grad_pre
        total[rows, :] += matmul_nt(grad_pre, w1_ref[...])
    hid_ref[...] = column_total(pre[...])
    part = D // 4
    for j in range(4):
        out = slice(j * part, (j + 1) * part)
        dw1_ref[out, :] = matmul(low_t[out, :], pre[...]).astype(bf16)
        dw2_ref[out, :] = matmul(turned[out, :], act_ref[...]).astype(bf16)

    @pl.when(step == pl.num_programs(0) - 1)
    def _():
        sums_ref[...] = jnp.zeros_like(sums_ref)

        @pl.loop(0, chunks)
        def _(i):
            rows = pl.ds(pl.multiple_of(i * chunk, chunk), chunk)
            unit, scale = norm_parts(h1_ref[rows, :])
            grad_first = total[rows, :]
            grad_h1 = norm_back(grad_first, unit, scale, vec_ref[0:1, :])
            gh1_ref[rows, :] = grad_h1
            low = grad_h1.astype(bf16)
            gm_ref[rows, :] = matmul(low, wo_ref[...]).astype(bf16)
            turned[:, rows] = grad_h1.T.astype(bf16)
            sums_ref[0:1, :] += column_total(grad_first * unit)
            sums_ref[1:2, :] += column_total(grad_first)
            sums_ref[2:3, :] += column_total(low)

        @pl.loop(0, 4)
        def _(j):
            out = pl.ds(pl.multiple_of(j * part, part), part)
            dwo_ref[out, :] = matmul(turned[out, :], mixed_ref[...]).astype(bf16)


def feed_back(gs, h1, mixed, attn_full, ffn_full, act, slope, vec_par):
    rows = gs.shape[0]
    chunk = min(256, rows)
    steps = FF // D
    whole = lambda shape: pl.BlockSpec(shape, lambda t: (0,) * len(shape))
    once = lambda shape: pl.BlockSpec(
        shape, lambda t: (0,) * len(shape), pipeline_mode=pl.Buffered(1)
    )
    hidden = pl.BlockSpec((rows, D), lambda t: (0, t))
    slab = pl.BlockSpec((D, D), lambda t: (0, t))
    return pl.pallas_call(
        partial(down_kernel, chunk),
        out_shape=[
            jax.ShapeDtypeStruct((D, FF), bf16),
            jax.ShapeDtypeStruct((D, FF), bf16),
            jax.ShapeDtypeStruct((D, D), bf16),
            jax.ShapeDtypeStruct((rows, D), f32),
            jax.ShapeDtypeStruct((rows, D), bf16),
            jax.ShapeDtypeStruct((1, FF), f32),
            jax.ShapeDtypeStruct((8, D), f32),
        ],
        grid=(steps,),
        in_specs=[
            once((rows, D)),
            once((rows, D)),
            once((rows, D)),
            pl.BlockSpec((None, D, D), lambda t: (3, 0, 0), pipeline_mode=pl.Buffered(1)),
            pl.BlockSpec((None, D, D), lambda t: (0, 0, t)),
            pl.BlockSpec((None, D, D), lambda t: (1, 0, t)),
            hidden,
            hidden,
            whole((6, D)),
        ],
        out_specs=[
            slab,
            slab,
            whole((D, D)),
            whole((rows, D)),
            whole((rows, D)),
            pl.BlockSpec((1, D), lambda t: (0, t)),
            whole((8, D)),
        ],
        scratch_shapes=[
            pltpu.VMEM((D, rows), bf16),
            pltpu.VMEM((D, rows), bf16),
            pltpu.VMEM((rows, D), bf16),
            pltpu.VMEM((rows, D), f32),
        ],
        compiler_params=pltpu.CompilerParams(vmem_limit_bytes=VMEM_LIMIT),
        cost_estimate=pl.CostEstimate(
            flops=2 * rows * D * (2 * D + 4 * FF),
            bytes_accessed=rows * D * 30 + 4 * D * FF * 2,
            transcendentals=0,
        ),
        name="feed_back",
    )(gs, h1, mixed, attn_full, ffn_full, ffn_full, act, slope, vec_par)


WIDE = 1536
STRIP = 96
PIECES = 8
ITEM = 128
LINE_ITEMS = 4
MESH = pl.DeviceIdType.MESH


def remote(src, dst, send, recv, where):
    return pltpu.make_async_remote_copy(
        src_ref=src,
        dst_ref=dst,
        send_sem=send,
        recv_sem=recv,
        device_id=where,
        device_id_type=MESH,
    )


def greet(partners):
    barrier = pltpu.get_barrier_semaphore()
    for where in partners:
        pl.semaphore_signal(barrier, inc=1, device_id=where, device_id_type=MESH)
    pl.semaphore_wait(barrier, len(partners))


def places(n_tensor):
    s, c, t = lax.axis_index("shard"), lax.axis_index("ctx"), lax.axis_index("tensor")
    x, core = s // 2, s % 2
    sibling = (x * 2 + 1 - core, c, t)
    over_x = ((1 - x) * 2 + core, c, t)
    over_y = (s, 1 - c, t)
    across = (x * 2 + 1 - core, 1 - c, t)
    along_z = [(s, c, lax.rem(t + k, n_tensor)) for k in range(1, n_tensor)]
    return s, c, t, x, core, sibling, over_x, over_y, across, along_z


class Line:
    def __init__(self, s, c, t, last, items, rows, array, out, up, down, copied):
        self.s, self.c, self.t, self.last, self.items = s, c, t, last, items
        self.rows, self.array, self.out, self.up, self.down = rows, array, out, up, down
        self.copied = copied

    def hop(self, i, src_t, sems, n, to):
        ref = self.array.at[src_t, pl.ds(i * self.rows, self.rows)]
        return remote(ref, ref, sems[0].at[n], sems[1].at[n], (self.s, self.c, to))

    def keep(self, src_t, n):
        return pltpu.make_async_copy(self.array.at[src_t], self.out.at[src_t], self.copied.at[n])

    def send_own(self, i):
        t = self.t

        @pl.when(t < self.last)
        def _():
            self.hop(i, t, self.up, i, t + 1).start()

        @pl.when(t > 0)
        def _():
            self.hop(i, t, self.down, i, t - 1).start()

        if i == self.items - 1:
            self.keep(t, 2 * self.last).start()

    def tick(self, j):
        t, last = self.t, self.last
        i, hops, n = j % self.items, j // self.items + 1, j + self.items

        @pl.when(t >= hops)
        def _():
            self.hop(i, t - hops, self.up, j, t - 1).wait_recv()

            @pl.when(t < last)
            def _():
                self.hop(i, t - hops, self.up, n, t + 1).start()

            if i == self.items - 1:
                self.keep(t - hops, hops - 1).start()

        @pl.when(t + hops <= last)
        def _():
            self.hop(i, t + hops, self.down, j, t + 1).wait_recv()

            @pl.when(t > 0)
            def _():
                self.hop(i, t + hops, self.down, n, t - 1).start()

            if i == self.items - 1:
                self.keep(t + hops, last + hops - 1).start()

    def settle(self):
        t, last = self.t, self.last
        for j in range(self.items * last):
            i, hops = j % self.items, j // self.items

            @pl.when((t < last) & (t >= hops))
            def _():
                self.hop(i, t - hops, self.up, j, t + 1).wait_send()

            @pl.when((t > 0) & (t + hops <= last))
            def _():
                self.hop(i, t + hops, self.down, j, t - 1).wait_send()

        self.keep(t, 2 * last).wait()
        for hops in range(1, last + 1):

            @pl.when(t >= hops)
            def _():
                self.keep(t - hops, hops - 1).wait()

            @pl.when(t + hops <= last)
            def _():
                self.keep(t + hops, last + hops - 1).wait()


def start_kernel(n_tensor, *refs):
    attn_ref, ffn_ref, qv_ref, hid_ref, tab_ref, rand, tokens = refs[:7]
    attn_out, ffn_out, hid_out, x_out, q_out, k_out, v_out, mixed_out, lse_out = refs[7:16]
    low, low_z, bias, bias_z, bias_qv, ffn_low, full, xs, qs, ms, k_buf, v_buf, s_buf = refs[16:29]
    (
        z_send,
        z_recv,
        b_send,
        b_recv,
        fz_send,
        fz_recv,
        x_send,
        x_recv,
        g_send,
        g_recv,
        p_send,
        p_recv,
        fg_send,
        fg_recv,
        fp_send,
        fp_recv,
        kv_send,
        kv_recv,
        own_sem,
    ) = refs[29:]
    s, c, t, x, core, sibling, over_x, over_y, across, along_z = places(n_tensor)
    own_cols, own_ff = D // n_tensor, FF // n_tensor
    n_rows = xs.shape[0]

    for m in range(4):
        low[:, m * own_cols : (m + 1) * own_cols] = attn_ref[m].astype(bf16)
    for m in range(2):
        ffn_low[m] = ffn_ref[m].astype(bf16)
    bias[0:2, 0:own_cols] = qv_ref[...]
    bias[2:3, 0:own_ff] = hid_ref[...]

    greet([sibling, over_x, over_y, across] + along_z)

    sent = []

    def put(copy):
        copy.start()
        sent.append(copy)

    half = 2 * own_cols

    def z_hop(path, k, u):
        cols = pl.ds(path * half, half)
        n = path * n_tensor
        return remote(
            low.at[:, cols], low_z.at[u, :, cols], z_send.at[n + k], z_recv.at[n + u], along_z[k]
        )

    for path in range(2):
        for k in range(n_tensor - 1):
            put(z_hop(path, k, t))

    def keep_rows(src, dst, n):
        return pltpu.make_async_copy(src.at[t], dst, x_recv.at[n])

    def swap_rows(src, dst, n):
        return remote(src.at[t], dst, x_send.at[n], x_recv.at[n], across)

    @pl.when(core == c)
    def _():
        keep_rows(tokens, xs, 0).start()

    @pl.when(core != c)
    def _():
        swap_rows(tokens, xs, 0).start()

    low_z[t] = low[...]
    bias_z[t] = bias[...]

    def strip(shard, ctx):
        return pl.ds(pl.multiple_of((2 * shard + ctx) * STRIP, STRIP), STRIP)

    here = strip(s, c)

    def lay_out(path):
        for k, where in enumerate(along_z):
            z_hop(path, k, where[2]).wait_recv()
        for n in range(n_tensor):
            for m in range(2 * path, 2 * path + 2):
                piece = low_z[n, :, m * own_cols : (m + 1) * own_cols]
                full[m, here, n * own_cols : (n + 1) * own_cols] = piece

    far_x, far_y = over_x[0], 1 - c
    labels = ["own", "x", "y", "xy"]
    rows = {
        "own": here,
        "x": strip(far_x, c),
        "y": strip(s, far_y),
        "xy": strip(far_x, far_y),
    }
    far_rows = {
        "own": strip(sibling[0], c),
        "x": strip(2 * (1 - x) + 1 - core, c),
        "y": strip(sibling[0], far_y),
        "xy": strip(2 * (1 - x) + 1 - core, far_y),
    }

    def attn_block(path, at):
        return full.at[pl.ds(2 * path, 2), at, :]

    def ffn_block(path, at):
        return ffn_out.at[path, at, :]

    class Gather:
        def __init__(self, block, ways, gs, gr, ps, pr):
            self.block, self.gs, self.gr, self.ps, self.pr = block, gs, gr, ps, pr
            x_first = (("x", over_x), ("y", over_y))
            self.ways = [x_first if way == 0 else x_first[::-1] for way in ways]

        def hop(self, path, name, label, where):
            n = path * 3 + labels.index(label) - 1
            ref = self.block(path, rows[name])
            return remote(ref, ref, self.gs.at[n], self.gr.at[n], where)

        def give(self, path, name, label, where):
            put(self.hop(path, name, label, where))

        def take(self, path, label):
            self.hop(path, label, label, over_x).wait_recv()

        def share(self, path, name):
            put(self.shared(path, name))

        def take_shared(self, path):
            for n, name in enumerate(labels):
                ref = self.block(path, far_rows[name])
                n = path * 4 + n
                remote(ref, ref, self.ps.at[n], self.pr.at[n], sibling).wait_recv()

        def shared(self, path, name):
            n = path * 4 + labels.index(name)
            ref = self.block(path, rows[name])
            return remote(ref, ref, self.ps.at[n], self.pr.at[n], sibling)

        def again(self, path, number):
            near, far = self.ways[path]
            if number == 1:
                sent.append(self.hop(path, near[0], "xy", far[1]))
            sent.append(self.shared(path, {1: near[0], 2: far[0], 3: "xy"}[number]))

        def step(self, path, number):
            near, far = self.ways[path]
            if number == 0:
                self.give(path, "own", near[0], near[1])
                self.give(path, "own", far[0], far[1])
                self.share(path, "own")
            elif number == 1:
                self.take(path, near[0])
                self.give(path, near[0], "xy", far[1])
                self.share(path, near[0])
            elif number == 2:
                self.take(path, far[0])
                self.share(path, far[0])
            else:
                self.take(path, "xy")
                self.share(path, "xy")

    attn = Gather(attn_block, (1, 1), g_send, g_recv, p_send, p_recv)
    ffn = Gather(ffn_block, (0, 1), fg_send, fg_recv, fp_send, fp_recv)

    def ffn_cols(path, u):
        return ffn_out.at[path, here, pl.ds(pl.multiple_of(u * own_ff, own_ff), own_ff)]

    def ffn_hop(path, k, u):
        n = path * n_tensor
        return remote(
            ffn_low.at[path],
            ffn_cols(path, u),
            fz_send.at[n + k],
            fz_recv.at[n + u],
            along_z[k],
        )

    local = []

    def write(src, dst, n):
        copy = pltpu.make_async_copy(src, dst, own_sem.at[n])
        copy.start()
        local.append(copy)

    def ffn_along_z(path):
        for k in range(n_tensor - 1):
            put(ffn_hop(path, k, t))
        write(ffn_low.at[path], ffn_cols(path, t), 5 + path)

    def ffn_ready(path):
        for k, where in enumerate(along_z):
            ffn_hop(path, k, where[2]).wait_recv()
        local[path].wait()
        ffn.step(path, 0)

    lay_out(0)
    attn.step(0, 0)
    lay_out(1)
    attn.step(1, 0)
    ffn_along_z(0)
    ffn_along_z(1)
    for k, where in enumerate(along_z):
        put(remote(bias, bias_z.at[t], b_send.at[k], b_recv.at[t], where))
    attn.step(0, 1)
    attn.step(1, 1)
    ffn_ready(0)
    attn.step(0, 2)
    attn.step(1, 2)
    attn.step(0, 3)
    attn.step(1, 3)
    for k, where in enumerate(along_z):
        u = where[2]
        remote(bias, bias_z.at[u], b_send.at[k], b_recv.at[u], where).wait_recv()
    for n in range(n_tensor):
        cols = slice(n * own_cols, (n + 1) * own_cols)
        bias_qv[0:2, cols] = bias_z[n, 0:2, 0:own_cols]
        hid_out[:, n * own_ff : (n + 1) * own_ff] = bias_z[n, 2:3, 0:own_ff]

    @pl.when(core == c)
    def _():
        keep_rows(tokens, xs, 0).wait()

    @pl.when(core != c)
    def _():
        swap_rows(tokens, xs, 0).wait()

    chunk = 256
    chunks = n_rows // chunk
    per = chunk // BLOCK

    def kv_hop(buf, i, n):
        at, to = pl.ds(i * per, per), pl.ds(n_rows // BLOCK + i * per, per)
        return remote(buf.at[at], buf.at[to], kv_send.at[n], kv_recv.at[n], sibling)

    attn.take_shared(0)
    for i in range(chunks):
        at = pl.ds(i * chunk, chunk)
        k = matmul(xs[at, :], full[1]).astype(bf16)
        k_buf[pl.ds(i * per, per)] = k.reshape(per, BLOCK, D)
        put(kv_hop(k_buf, i, i))
    ffn_ready(1)
    for i in range(chunks):
        at = pl.ds(i * chunk, chunk)
        q = matmul(xs[at, :], full[0]) + bias_qv[0:1, :]
        qs[at, :] = (q.astype(bf16).astype(f32) * 0.125).astype(bf16)
    attn.take_shared(1)
    for i in range(chunks):
        at = pl.ds(i * chunk, chunk)
        v = (matmul(xs[at, :], full[2]) + bias_qv[1:2, :]).astype(bf16)
        v_buf[pl.ds(i * per, per)] = v.reshape(per, BLOCK, D)
        put(kv_hop(v_buf, i, chunks + i))
    ffn.step(0, 1)
    write(xs, x_out, 0)
    write(qs, q_out, 1)
    write(full, attn_out, 2)
    for i in range(chunks):
        kv_hop(k_buf, i, i).wait_recv()
        kv_hop(v_buf, i, chunks + i).wait_recv()
    write(k_buf, k_out, 3)
    write(v_buf, v_out, 4)

    nb = n_rows // BLOCK
    first = core * nb
    stops = {0: [(1, 1)], 1: [(0, 2), (1, 2)], 9: [(0, 3), (1, 3)]}

    @pl.loop(0, nb)
    def _(blk):
        at = pl.ds(pl.multiple_of(blk * BLOCK, BLOCK), BLOCK)
        forward_block(
            qs.at[at],
            ms.at[at],
            lse_out.at[blk],
            k_buf,
            v_buf,
            s_buf,
            tab_ref,
            rand,
            blk * (LISTED - 5),
            blk,
            first,
            0,
        )

        for at_block, moves in stops.items():

            @pl.when(blk == at_block)
            def _():
                mark = len(sent)
                for path, number in moves:
                    ffn.step(path, number)
                del sent[mark:]

    write(ms, mixed_out, 7)
    for path, number in [move for moves in stops.values() for move in moves]:
        ffn.again(path, number)
    ffn.take_shared(0)
    ffn.take_shared(1)

    for copy in sent:
        copy.wait_send()
    for copy in local[2:]:
        copy.wait()


def start(n_tensor, attn_w, ffn_w, qv_bias, hid_bias, table, rand, tokens):
    rows = tokens.shape[1]
    own_ff = FF // n_tensor
    dma = pltpu.SemaphoreType.DMA
    vmem, anywhere = pl.BlockSpec(memory_space=pltpu.VMEM), pl.BlockSpec(memory_space=pl.ANY)
    smem = pl.BlockSpec(memory_space=pltpu.SMEM)
    tall = jax.ShapeDtypeStruct((rows, D), bf16)
    both = jax.ShapeDtypeStruct((2 * rows // BLOCK, BLOCK, D), bf16)
    items = 2 * (rows // 256)
    return pl.pallas_call(
        partial(start_kernel, n_tensor),
        out_shape=[
            jax.ShapeDtypeStruct((4, D, D), bf16),
            jax.ShapeDtypeStruct((2, D, FF), bf16),
            jax.ShapeDtypeStruct((1, FF), f32),
            tall,
            tall,
            both,
            both,
            tall,
            jax.ShapeDtypeStruct((rows // BLOCK, 8, ROWS), f32),
        ],
        in_specs=[vmem] * 5 + [smem, anywhere],
        out_specs=[anywhere, anywhere, vmem] + [anywhere] * 5 + [vmem],
        scratch_shapes=[
            pltpu.VMEM((STRIP, D), bf16),
            pltpu.VMEM((n_tensor, STRIP, D), bf16),
            pltpu.VMEM((8, D), f32),
            pltpu.VMEM((n_tensor, 8, D), f32),
            pltpu.VMEM((8, D), f32),
            pltpu.VMEM((2, STRIP, own_ff), bf16),
            pltpu.VMEM((4, D, D), bf16),
            pltpu.VMEM((rows, D), bf16),
            pltpu.VMEM((rows, D), bf16),
            pltpu.VMEM((rows, D), bf16),
            pltpu.VMEM((2 * rows // BLOCK, BLOCK, D), bf16),
            pltpu.VMEM((2 * rows // BLOCK, BLOCK, D), bf16),
            pltpu.VMEM((2 * rows // KEYS, ROWS, KEYS), f32),
            dma((2 * n_tensor,)),
            dma((2 * n_tensor,)),
            dma((n_tensor,)),
            dma((n_tensor,)),
            dma((2 * n_tensor,)),
            dma((2 * n_tensor,)),
            dma((2,)),
            dma((2,)),
            dma((6,)),
            dma((6,)),
            dma((8,)),
            dma((8,)),
            dma((6,)),
            dma((6,)),
            dma((8,)),
            dma((8,)),
            dma((items,)),
            dma((items,)),
            dma((8,)),
        ],
        compiler_params=pltpu.CompilerParams(
            collective_id=2, has_side_effects=True, vmem_limit_bytes=VMEM_LIMIT
        ),
        cost_estimate=pl.CostEstimate(
            flops=6 * rows * D * D, bytes_accessed=100 * 2**20, transcendentals=0
        ),
        name="start",
    )(attn_w, ffn_w, qv_bias, hid_bias.reshape(1, own_ff), table, rand, tokens)


def middle_kernel(n_tensor, *refs):
    x_ref, mixed_ref, hid_ref, vec_ref, cotangent, attn_full, ffn_full = refs[:7]
    out_a, out_b, dw1, dw2, dwo, gh1, gm, hid_out, sums_out = refs[7:16]
    w, wo, act, slope, h1, total, gs_low, low_t, turned, pre, dw_s, cot, ready, low, down, held = refs[16:32]
    (
        w_sem,
        c_send,
        c_recv,
        h_send,
        h_recv,
        up_send,
        up_recv,
        dn_send,
        dn_recv,
        dw_sem,
        own_sem,
        copied,
    ) = refs[32:]
    s, c, t, x, core, sibling, over_x, over_y, across, along_z = places(n_tensor)
    n_rows = x_ref.shape[0]
    chunk = 256
    chunks = n_rows // chunk
    steps = FF // D
    items, all_items = LINE_ITEMS, n_rows // ITEM
    last = n_tensor - 1

    def block(i):
        return pl.ds(pl.multiple_of(i * D, D), D)

    fetch_o = pltpu.make_async_copy(attn_full.at[3], wo, w_sem.at[2 * steps])
    fetch_o.start()

    def fetch(m, i):
        at = w.at[m, :, block(i)]
        return pltpu.make_async_copy(ffn_full.at[m, :, block(i)], at, w_sem.at[m * steps + i])

    for i in range(steps):
        for m in range(2):
            fetch(m, i).start()

    greet([over_y, across] + along_z)

    def keep_cot(i):
        at = pl.ds(i * chunk, chunk)
        return pltpu.make_async_copy(cotangent.at[t, at], cot.at[at], c_recv.at[i])

    def swap_cot(i):
        at = pl.ds(i * chunk, chunk)
        return remote(cotangent.at[t, at], cot.at[at], c_send.at[i], c_recv.at[i], across)

    def home_ref(i):
        if i < items:
            return held.at[t, pl.ds(i * ITEM, ITEM)]
        return out_b.at[pl.ds((i - items) * ITEM, ITEM)]

    def keep_home(i):
        return pltpu.make_async_copy(ready.at[pl.ds(i * ITEM, ITEM)], home_ref(i), h_recv.at[i])

    def send_home(i):
        src = ready.at[pl.ds(i * ITEM, ITEM)]
        return remote(src, home_ref(i), h_send.at[i], h_recv.at[i], across)

    def if_home(at_home, away):
        @pl.when(core == c)
        def _():
            at_home()

        @pl.when(core != c)
        def _():
            away()

    if_home(lambda: keep_cot(0).start(), lambda: swap_cot(0).start())

    up, down_line = (up_send, up_recv), (dn_send, dn_recv)
    chain = Line(s, c, t, last, items, ITEM, held, out_a, up, down_line, copied)

    def own_ready(i):
        if_home(lambda: keep_home(i).wait(), lambda: send_home(i).wait_recv())

    events = {
        (1, 2): ([0], []),
        (2, 2): ([1], []),
        (2, 3): ([2], [0]),
        (3, 2): ([], [1]),
        (3, 3): ([3], []),
        (4, 0): ([], [2]),
    }
    sizes = [ITEM] + [chunk] * (chunks - 1) + [chunk - ITEM]
    start_row = 0
    for i, size in enumerate(sizes):
        rows = slice(start_row, start_row + size)
        top = slice(0, size)
        if i == 0:
            fetch_o.wait()
        pre1 = x_ref[rows, :].astype(f32) + matmul_nt(mixed_ref[rows, :], wo[...])
        pre1 = pre1 + vec_ref[4:5, :]
        h1[rows, :] = pre1
        unit, _scale = norm_parts(pre1)
        first = unit * vec_ref[0:1, :] + vec_ref[1:2, :]
        low[top, :] = first.astype(bf16)
        down[top, :] = first + vec_ref[5:6, :]

        @pl.loop(0, steps)
        def _(j):
            if i == 0:
                fetch(0, j).wait()
                fetch(1, j).wait()
            for (at_chunk, at_step), (own, passing) in events.items():
                if at_chunk != i:
                    continue

                @pl.when(j == at_step)
                def _():
                    for n in own:
                        own_ready(n)
                        chain.send_own(n)
                    for n in passing:
                        chain.tick(n)

            hidden = matmul(low[top, :], w[0, :, block(j)]) + hid_ref[:, block(j)]
            act_now, slope_now = gelu_and_slope(hidden)
            act_now = act_now.astype(bf16)
            act[rows, block(j)] = act_now
            slope[rows, block(j)] = slope_now.astype(bf16)
            down[top, :] += matmul_nt(act_now, w[1, :, block(j)])

        second = down[top, :]
        total[rows, :] = second
        unit, _scale = norm_parts(second)
        ready[rows, :] = (unit * vec_ref[2:3, :] + vec_ref[3:4, :]).astype(bf16)
        for n in range(start_row // ITEM, (start_row + size) // ITEM):
            if_home(lambda: keep_home(n).start(), lambda: send_home(n).start())
        if i + 1 < chunks:
            if_home(lambda: keep_cot(i + 1).start(), lambda: swap_cot(i + 1).start())
        start_row += size
    chain.tick(4)

    sums_out[...] = jnp.zeros_like(sums_out)

    @pl.loop(0, chunks)
    def _(i):
        rows = pl.ds(pl.multiple_of(i * chunk, chunk), chunk)
        if_home(lambda: keep_cot(i).wait(), lambda: swap_cot(i).wait())
        unit, scale = norm_parts(total[rows, :])
        grad_out = cot[rows, :].astype(f32)
        grad = norm_back(grad_out, unit, scale, vec_ref[2:3, :])
        sums_out[2:3, :] += column_total(grad_out * unit)
        sums_out[3:4, :] += column_total(grad_out)
        total[rows, :] = grad
        grad_low = grad.astype(bf16)
        gs_low[rows, :] = grad_low
        sums_out[5:6, :] += column_total(grad_low)
        turned[:, rows] = grad.T.astype(bf16)
        unit, _scale = norm_parts(h1[rows, :])
        first = unit * vec_ref[0:1, :] + vec_ref[1:2, :]
        low_t[:, rows] = first.T.astype(bf16)

    part = D // 4

    def dw_copy(slot, m, j):
        return pltpu.make_async_copy(
            dw_s.at[slot, m], (dw1, dw2)[m].at[:, block(j)], dw_sem.at[2 * slot + m]
        )

    ticks = {(0, 1): 5, (1, 0): 3, (1, 1): 6, (2, 0): 8, (2, 1): 9, (3, 0): 7, (3, 1): 10}

    def pass_on(j, when):
        for (at, place), n in ticks.items():
            if place == when:

                @pl.when(j == at)
                def _():
                    chain.tick(n)

    @pl.loop(0, steps)
    def _(j):
        slot = lax.rem(j, 2)
        pass_on(j, 0)
        for i in range(chunks):
            rows = slice(i * chunk, (i + 1) * chunk)
            grad_act = matmul(gs_low[rows, :], w[1, :, block(j)]).astype(bf16).astype(f32)
            grad_pre = (grad_act * slope[rows, block(j)].astype(f32)).astype(bf16)
            pre[rows, :] = grad_pre
            total[rows, :] += matmul_nt(grad_pre, w[0, :, block(j)])
        pass_on(j, 1)
        hid_out[:, block(j)] = column_total(pre[...])

        @pl.when(j >= 2)
        def _():
            for m in range(2):
                dw_copy(slot, m, j - 2).wait()

        for n in range(4):
            out = slice(n * part, (n + 1) * part)
            dw_s[slot, 0, out, :] = matmul(low_t[out, :], pre[...]).astype(bf16)
            dw_s[slot, 1, out, :] = matmul(turned[out, :], act[:, block(j)]).astype(bf16)
        for m in range(2):
            dw_copy(slot, m, j).start()

    gm_s = gs_low

    @pl.loop(0, chunks)
    def _(i):
        rows = pl.ds(pl.multiple_of(i * chunk, chunk), chunk)
        unit, scale = norm_parts(h1[rows, :])
        grad_first = total[rows, :]
        grad_h1 = norm_back(grad_first, unit, scale, vec_ref[0:1, :])
        total[rows, :] = grad_h1
        grad_low = grad_h1.astype(bf16)
        gm_s[rows, :] = matmul(grad_low, wo[...]).astype(bf16)
        turned[:, rows] = grad_h1.T.astype(bf16)
        sums_out[0:1, :] += column_total(grad_first * unit)
        sums_out[1:2, :] += column_total(grad_first)
        sums_out[4:5, :] += column_total(grad_low)

    local = [
        pltpu.make_async_copy(total, gh1, own_sem.at[0]),
        pltpu.make_async_copy(gm_s, gm, own_sem.at[1]),
    ]
    for copy in local:
        copy.start()
    for j in range(steps - 2, steps):
        for m in range(2):
            dw_copy(j % 2, m, j).wait()

    @pl.loop(0, 4)
    def _(n):
        out = pl.ds(pl.multiple_of(n * part, part), part)
        dw_s[0, 0, out, :] = matmul(turned[out, :], mixed_ref[...]).astype(bf16)

    local.append(pltpu.make_async_copy(dw_s.at[0, 0], dwo, own_sem.at[2]))
    local[-1].start()
    chain.tick(11)
    for i in range(items, all_items):
        own_ready(i)
    for i in range(all_items):

        @pl.when(core != c)
        def _():
            send_home(i).wait_send()

    chain.settle()
    for copy in local:
        copy.wait()


def middle(n_tensor, x, mixed, hid_all, vec_par, cotangent, attn_full, ffn_full):
    rows = x.shape[0]
    steps = FF // D
    items, all_items = LINE_ITEMS, rows // ITEM
    dma = pltpu.SemaphoreType.DMA
    vmem, anywhere = pl.BlockSpec(memory_space=pltpu.VMEM), pl.BlockSpec(memory_space=pl.ANY)
    low, wide = pltpu.VMEM((rows, D), bf16), pltpu.VMEM((rows, D), f32)
    return pl.pallas_call(
        partial(middle_kernel, n_tensor),
        out_shape=[
            jax.ShapeDtypeStruct((n_tensor, items * ITEM, D), bf16),
            jax.ShapeDtypeStruct((rows - items * ITEM, D), bf16),
            jax.ShapeDtypeStruct((D, FF), bf16),
            jax.ShapeDtypeStruct((D, FF), bf16),
            jax.ShapeDtypeStruct((D, D), bf16),
            jax.ShapeDtypeStruct((rows, D), f32),
            jax.ShapeDtypeStruct((rows, D), bf16),
            jax.ShapeDtypeStruct((1, FF), f32),
            jax.ShapeDtypeStruct((8, D), f32),
        ],
        in_specs=[vmem] * 4 + [anywhere] * 3,
        out_specs=[anywhere] * 7 + [vmem] * 2,
        scratch_shapes=[
            pltpu.VMEM((2, D, FF), bf16),
            pltpu.VMEM((D, D), bf16),
            pltpu.VMEM((rows, FF), bf16),
            pltpu.VMEM((rows, FF), bf16),
            wide,
            wide,
            low,
            pltpu.VMEM((D, rows), bf16),
            pltpu.VMEM((D, rows), bf16),
            low,
            pltpu.VMEM((2, 2, D, D), bf16),
            low,
            low,
            pltpu.VMEM((256, D), bf16),
            pltpu.VMEM((256, D), f32),
            pltpu.VMEM((n_tensor, items * ITEM, D), bf16),
            dma((2 * steps + 1,)),
            dma((rows // 256,)),
            dma((rows // 256,)),
            dma((all_items,)),
            dma((all_items,)),
            dma((items * n_tensor,)),
            dma((items * n_tensor,)),
            dma((items * n_tensor,)),
            dma((items * n_tensor,)),
            dma((4,)),
            dma((3,)),
            dma((2 * n_tensor - 1,)),
        ],
        compiler_params=pltpu.CompilerParams(
            collective_id=3, has_side_effects=True, vmem_limit_bytes=VMEM_LIMIT
        ),
        cost_estimate=pl.CostEstimate(
            flops=2 * rows * D * (3 * D + 6 * FF),
            bytes_accessed=60 * 2**20,
            transcendentals=2 * rows * FF,
        ),
        name="middle",
    )(x, mixed, hid_all, vec_par, cotangent, attn_full, ffn_full)


def finish_kernel(n_tensor, *refs):
    dq, dk_own, dk_far, dv_own, dv_far, gh1, x_ref, weights = refs[:8]
    dw1, dw2, dwo, vec_sums, hid_sums = refs[8:13]
    attn_out, ffn_out, vec_out, qv_out, hid_out, tokens_out = refs[13:19]
    (
        dk,
        dv,
        xs,
        held,
        x_t,
        partial_sum,
        ready,
        dws,
        acc,
        got0,
        got1a,
        got1b,
        got2,
        zf,
        zf_got,
        za,
        za_got,
        run,
        run_got,
        run_z,
        wts,
    ) = refs[19:40]
    (
        e_send,
        e_recv,
        own_sem,
        s0,
        r0,
        s1,
        r1,
        s2,
        r2,
        zf_send,
        zf_recv,
        za_send,
        za_recv,
        sm,
        rm,
        h_send,
        h_recv,
        up_send,
        up_recv,
        dn_send,
        dn_recv,
        w_sem,
        copied,
    ) = refs[40:]
    s, c, t, x, core, sibling, over_x, over_y, across, along_z = places(n_tensor)
    n_rows = dq.shape[0]
    rows_each = n_rows // PIECES
    last = n_tensor - 1

    def pieces(path, i):
        if i < 2:
            return [(dw1 if path == 0 else dw2, i * WIDE, WIDE, 0)]
        if path == 0:
            return [(dws.at[0], 0, D, 0), (dws.at[1], 0, D, D)]
        return [(dws.at[2], 0, D, 0), (dwo, 0, D, D)]

    def slot(path, i):
        return path * 3 + i

    order = [(path, i) for i in range(3) for path in range(2)]

    def rows_of(xx, cc):
        return pl.ds(pl.multiple_of((4 * xx + 2 * cc) * STRIP, 2 * STRIP), 2 * STRIP)

    own, first = {}, {}
    for path, i in order:
        k = slot(path, i)
        own[k], first[k] = [], []
        for xx in range(2):
            for j, (ref, col, width, at) in enumerate(pieces(path, i)):
                n = (k * 2 + xx) * 2 + j
                cols, to = pl.ds(col, width), pl.ds(at, width)
                own[k].append(
                    pltpu.make_async_copy(
                        ref.at[rows_of(xx, core), cols], acc.at[k, xx, :, to], own_sem.at[n]
                    )
                )
                first[k].append(
                    remote(
                        ref.at[rows_of(xx, 1 - core), cols],
                        got0.at[k, xx, :, to],
                        s0.at[n],
                        r0.at[n],
                        sibling,
                    )
                )

    def start_own(i):
        for path in range(2):
            for copy in own[slot(path, i)]:
                copy.start()

    def start_first(i):
        for path in range(2):
            for copy in first[slot(path, i)]:
                copy.start()

    fetches = [
        pltpu.make_async_copy(gh1, partial_sum, w_sem.at[1]),
        pltpu.make_async_copy(weights.at[pl.ds(0, 3)], wts, w_sem.at[0]),
        pltpu.make_async_copy(x_ref, xs, w_sem.at[2]),
    ]
    for copy in fetches:
        copy.start()
    start_own(0)
    start_own(1)
    greet([sibling, over_x, over_y, across] + along_z)

    chunk = 256
    chunks = n_rows // chunk

    def exchange(i, n):
        at = pl.ds(i * chunk, chunk)
        src, dst = ((dk_far, dk), (dv_far, dv))[n]
        k = 2 * i + n
        return remote(src.at[at], dst.at[at], e_send.at[k], e_recv.at[k], sibling)

    swaps = [exchange(i, n) for i in range(chunks) for n in range(2)]
    for copy in swaps:
        copy.start()
    start_first(0)
    fetches[0].wait()
    fetches[1].wait()

    run[0] = jnp.zeros(run.shape[1:], f32)
    run[0, 0:6, :] = vec_sums[0:6, :]
    for n in range(FF // D):
        run[0, 8 + n : 9 + n, :] = hid_sums[:, n * D : (n + 1) * D]

    def keep_home(i):
        at = pl.ds(i * rows_each, rows_each)
        return pltpu.make_async_copy(ready.at[at], held.at[t, at], h_recv.at[i])

    def send_home(i):
        at = pl.ds(i * rows_each, rows_each)
        return remote(ready.at[at], held.at[t, at], h_send.at[i], h_recv.at[i], across)

    chain = Line(
        s,
        c,
        t,
        last,
        PIECES,
        rows_each,
        held,
        tokens_out,
        (up_send, up_recv),
        (dn_send, dn_recv),
        copied,
    )
    tick = chain.tick

    def send_own(i):
        @pl.when(core == c)
        def _():
            keep_home(i).wait()

        @pl.when(core != c)
        def _():
            send_home(i).wait_recv()

        chain.send_own(i)

    for i in range(PIECES):
        at = slice(i * rows_each, (i + 1) * rows_each)
        if i * rows_each % chunk == 0:
            for n in range(2):
                exchange(i * rows_each // chunk, n).wait_recv()
        dk_piece = (dk_own[at, :].astype(f32) + dk[at, :].astype(f32)).astype(bf16)
        dv_piece = (dv_own[at, :].astype(f32) + dv[at, :].astype(f32)).astype(bf16)
        dk[at, :] = dk_piece
        dv[at, :] = dv_piece
        total = partial_sum[at, :] + matmul_nt(dq[at, :], wts[0])
        total = total + matmul_nt(dk_piece, wts[1]) + matmul_nt(dv_piece, wts[2])
        ready[at, :] = total.astype(bf16)

        @pl.when(core == c)
        def _():
            keep_home(i).start()

        @pl.when(core != c)
        def _():
            send_home(i).start()

        if i > 0:
            send_own(i - 1)

    def add_rows(target, source, count):
        @pl.loop(0, count // 16)
        def _(j):
            rows = pl.ds(pl.multiple_of(j * 16, 16), 16)
            total = target[rows, :].astype(f32) + source[rows, :].astype(f32)
            target[rows, :] = total.astype(bf16)

    def half(cc):
        return pl.ds(pl.multiple_of(cc * STRIP, STRIP), STRIP)

    second, third = {}, {}

    def stage1(path, i):
        k = slot(path, i)
        for copy in own[k]:
            copy.wait()
        for copy in first[k]:
            copy.wait_recv()
        for xx in range(2):
            add_rows(acc.at[k, xx], got0.at[k, xx], 2 * STRIP)
        if path == 0:
            second[k] = remote(acc.at[k, 1 - x], got1a.at[i], s1.at[k], r1.at[k], over_x)
        else:
            second[k] = remote(
                acc.at[k, :, half(1 - c), :], got1b.at[i], s1.at[k], r1.at[k], over_y
            )
        second[k].start()

    def stage2(path, i):
        k = slot(path, i)
        second[k].wait_recv()
        if path == 0:
            add_rows(acc.at[k, x], got1a.at[i], 2 * STRIP)
            third[k] = remote(
                acc.at[k, x, half(1 - c), :], got2.at[k], s2.at[k], r2.at[k], over_y
            )
        else:
            for xx in range(2):
                add_rows(acc.at[k, xx, half(c), :], got1b.at[i, xx], STRIP)
            third[k] = remote(
                acc.at[k, 1 - x, half(c), :], got2.at[k], s2.at[k], r2.at[k], over_x
            )
        third[k].start()

    own_cols = D // n_tensor
    own_ff = FF // n_tensor
    per = WIDE // own_ff

    def stage3(path, i):
        k = slot(path, i)
        third[k].wait_recv()

        @pl.loop(0, STRIP // 16)
        def _(j):
            rows = pl.ds(pl.multiple_of(j * 16, 16), 16)
            here = pl.ds(pl.multiple_of(c * STRIP + j * 16, 16), 16)
            total = acc[k, x, here, :].astype(f32) + got2[k, rows, :].astype(f32)
            if i < 2:
                for n in range(per):
                    piece = total[:, n * own_ff : (n + 1) * own_ff].astype(bf16)
                    zf[per * i + n, rows, path * own_ff : (path + 1) * own_ff] = piece
            else:
                for n in range(n_tensor):
                    for m in range(2):
                        at = m * D + n * own_cols
                        to = (2 * path + m) * own_cols
                        piece = total[:, at : at + own_cols].astype(bf16)
                        za[n, rows, to : to + own_cols] = piece

    z_sent = []

    def z_step(k, buf, got, send, recv):
        @pl.when(t == k)
        def _():
            for d in range(last, k, -1):
                if k > 0:
                    hop(buf, got, send, recv, d, 0, k - 1).wait_recv()
                    add_rows(buf.at[d], got.at[0, d], STRIP)
                hop(buf, got, send, recv, d, 0, k + 1).start()

        @pl.when(t == last - k)
        def _():
            for d in range(0, last - k):
                if k > 0:
                    hop(buf, got, send, recv, d, 1, last - k + 1).wait_recv()
                    add_rows(buf.at[d], got.at[1, d], STRIP)
                hop(buf, got, send, recv, d, 1, last - k - 1).start()

    def hop(buf, got, send, recv, d, way, to):
        n = way * n_tensor + d
        return remote(buf.at[d], got.at[way, d], send.at[n], recv.at[n], (s, c, to))

    def z_collect(buf, got, send, recv, emit):
        @pl.when(t > 0)
        def _():
            hop(buf, got, send, recv, t, 0, t - 1).wait_recv()
            add_rows(buf.at[t], got.at[0, t], STRIP)

        @pl.when(t < last)
        def _():
            hop(buf, got, send, recv, t, 1, t + 1).wait_recv()
            add_rows(buf.at[t], got.at[1, t], STRIP)

        @pl.loop(0, STRIP // 16)
        def _(j):
            rows = pl.ds(pl.multiple_of(j * 16, 16), 16)
            emit(rows, buf[t, rows, :].astype(f32))

    def z_settle(buf, got, send, recv):
        for d in range(n_tensor):

            @pl.when(t < d)
            def _():
                hop(buf, got, send, recv, d, 0, t + 1).wait_send()

            @pl.when(t > d)
            def _():
                hop(buf, got, send, recv, d, 1, t - 1).wait_send()

    ffn_z = (zf, zf_got, zf_send, zf_recv)
    attn_z = (za, za_got, za_send, za_recv)

    small = []

    def small_send(n, where):
        small.append(remote(run.at[n], run_got.at[n], sm.at[n], rm.at[n], where))
        small[n].start()

    def small_add(n):
        small[n].wait_recv()
        run[n + 1] = run[n] + run_got[n]

    start_first(1)
    fetches[2].wait()
    for i in range(chunks):
        at = slice(i * chunk, (i + 1) * chunk)
        x_t[:, at] = xs[at, :].T
    dws[0] = matmul(x_t[...], dq[...]).astype(bf16)
    send_own(7)
    dws[1] = matmul(x_t[...], dk[...]).astype(bf16)
    dws[2] = matmul(x_t[...], dv[...]).astype(bf16)
    start_own(2)
    start_first(2)
    run[0, 6:7, :] = column_total(dq[...])
    run[0, 7:8, :] = column_total(dv[...])
    small_send(0, sibling)
    stage1(0, 0)
    stage1(1, 0)
    stage1(0, 1)
    stage1(1, 1)
    tick(0)
    stage1(0, 2)
    stage1(1, 2)
    small_add(0)
    small_send(1, over_x)
    tick(1)
    tick(2)
    tick(3)
    stage2(0, 0)
    stage2(1, 0)
    tick(4)
    tick(5)
    small_add(1)
    small_send(2, over_y)
    tick(6)
    stage2(0, 1)
    stage2(1, 1)
    tick(7)
    tick(8)
    small_add(2)
    run_z[t] = run[3]
    for k, where in enumerate(along_z):
        copy = remote(run.at[3], run_z.at[t], sm.at[3 + k], rm.at[3 + t], where)
        copy.start()
        z_sent.append(copy)
    stage3(0, 0)
    stage3(1, 0)
    stage2(0, 2)
    stage2(1, 2)
    tick(9)
    tick(10)
    stage3(0, 1)
    stage3(1, 1)
    z_step(0, *ffn_z)
    tick(11)
    tick(12)
    z_step(1, *ffn_z)
    stage3(0, 2)
    stage3(1, 2)
    z_step(0, *attn_z)
    tick(13)
    tick(14)
    z_step(2, *ffn_z)
    z_step(1, *attn_z)
    tick(15)
    tick(16)
    z_step(2, *attn_z)
    for j in range(17, PIECES * last):
        tick(j)

    for k, where in enumerate(along_z):
        u = where[2]
        remote(run.at[3], run_z.at[u], sm.at[3 + k], rm.at[3 + u], where).wait_recv()
    total = run_z[0]
    for n in range(1, n_tensor):
        total = total + run_z[n]
    vec_out[...] = total[0:6, :]
    for n in range(n_tensor):

        @pl.when(t == n)
        def _():
            qv_out[...] = total[6:8, n * own_cols : (n + 1) * own_cols]
            hid_out[...] = total[8 + n : 9 + n, :]


    def emit_ffn(rows, total):
        for m in range(2):
            ffn_out[m, rows, :] = total[:, m * own_ff : (m + 1) * own_ff]

    def emit_attn(rows, total):
        for m in range(4):
            attn_out[m, rows, :] = total[:, m * own_cols : (m + 1) * own_cols]

    z_collect(*ffn_z, emit_ffn)
    z_collect(*attn_z, emit_attn)
    z_settle(*ffn_z)
    z_settle(*attn_z)

    for copy in swaps:
        copy.wait_send()
    for path, i in order:
        k = slot(path, i)
        for copy in first[k]:
            copy.wait_send()
        second[k].wait_send()
        third[k].wait_send()
    for copy in small + z_sent:
        copy.wait_send()

    @pl.when(core != c)
    def _():
        for i in range(PIECES):
            send_home(i).wait_send()

    chain.settle()


def finish_all(n_tensor, grads, gh1, x, attn_full, dws, sums):
    rows = x.shape[0]
    own_cols, own_ff = D // n_tensor, FF // n_tensor
    dma = pltpu.SemaphoreType.DMA
    vmem, anywhere = pl.BlockSpec(memory_space=pltpu.VMEM), pl.BlockSpec(memory_space=pl.ANY)
    dq, dk_own, dk_far, dv_own, dv_far = grads
    tall = pltpu.VMEM((rows, D), bf16)
    items = PIECES * (n_tensor - 1)
    return pl.pallas_call(
        partial(finish_kernel, n_tensor),
        out_shape=[
            jax.ShapeDtypeStruct((4, STRIP, own_cols), f32),
            jax.ShapeDtypeStruct((2, STRIP, own_ff), f32),
            jax.ShapeDtypeStruct((6, D), f32),
            jax.ShapeDtypeStruct((2, own_cols), f32),
            jax.ShapeDtypeStruct((1, own_ff), f32),
            jax.ShapeDtypeStruct((n_tensor, rows, D), bf16),
        ],
        in_specs=[vmem, vmem, anywhere, vmem, anywhere] + [anywhere] * 6
        + [vmem] * 2,
        out_specs=[vmem] * 5 + [anywhere],
        scratch_shapes=[
            tall,
            tall,
            tall,
            pltpu.VMEM((n_tensor, rows, D), bf16),
            pltpu.VMEM((D, rows), bf16),
            pltpu.VMEM((rows, D), f32),
            tall,
            pltpu.VMEM((3, D, D), bf16),
            pltpu.VMEM((6, 2, 2 * STRIP, WIDE), bf16),
            pltpu.VMEM((6, 2, 2 * STRIP, WIDE), bf16),
            pltpu.VMEM((3, 2 * STRIP, WIDE), bf16),
            pltpu.VMEM((3, 2, STRIP, WIDE), bf16),
            pltpu.VMEM((6, STRIP, WIDE), bf16),
            pltpu.VMEM((n_tensor, STRIP, 2 * own_ff), bf16),
            pltpu.VMEM((2, n_tensor, STRIP, 2 * own_ff), bf16),
            pltpu.VMEM((n_tensor, STRIP, 4 * own_cols), bf16),
            pltpu.VMEM((2, n_tensor, STRIP, 4 * own_cols), bf16),
            pltpu.VMEM((4, 16, D), f32),
            pltpu.VMEM((3, 16, D), f32),
            pltpu.VMEM((n_tensor, 16, D), f32),
            pltpu.VMEM((3, D, D), bf16),
            dma((2 * rows // 256,)),
            dma((2 * rows // 256,)),
            dma((24,)),
            dma((24,)),
            dma((24,)),
            dma((6,)),
            dma((6,)),
            dma((6,)),
            dma((6,)),
            dma((2 * n_tensor,)),
            dma((2 * n_tensor,)),
            dma((2 * n_tensor,)),
            dma((2 * n_tensor,)),
            dma((3 + n_tensor,)),
            dma((3 + n_tensor,)),
            dma((PIECES,)),
            dma((PIECES,)),
            dma((items + PIECES,)),
            dma((items + PIECES,)),
            dma((items + PIECES,)),
            dma((items + PIECES,)),
            dma((3,)),
            dma((2 * n_tensor - 1,)),
        ],
        compiler_params=pltpu.CompilerParams(
            collective_id=1, has_side_effects=True, vmem_limit_bytes=VMEM_LIMIT
        ),
        cost_estimate=pl.CostEstimate(
            flops=12 * rows * D * D, bytes_accessed=400 * 2**20, transcendentals=0
        ),
        name="finish",
    )(dq, dk_own, dk_far, dv_own, dv_far, gh1, x, attn_full, *dws, *sums)


GROUP_RATES = (
    [2.0 / D**0.5] * 3 + [2.0 / (D // (4 * BLOCK)) ** 0.5],
    [2.0 / D**0.5, 2.0 / FF**0.5],
)


def last_kernel(tokens_ref, out_b, _output_a, *refs):
    attn_g, attn_w, attn_m, attn_v, ffn_g, ffn_w, ffn_m, ffn_v = refs[:8]
    plain = [refs[8 + 4 * n : 12 + 4 * n] for n in range(3)]
    tokens_out, output = refs[20:22]
    attn_moment, attn_square, out_states, attn_new, attn_copy = refs[22:27]
    ffn_moment, ffn_square, ffn_new, ffn_copy = refs[27:31]
    plain_out = [refs[31 + 3 * n : 34 + 3 * n] for n in range(3)]
    step = pl.program_id(0)

    @pl.when(step == 0)
    def _():
        for m in range(4):
            moment, square, new = adam_update(
                attn_w[m], attn_m[m], attn_v[m], attn_g[m], GROUP_RATES[0][m], decay_rate
            )
            if m < 3:
                attn_moment[m], attn_square[m] = moment, square
            else:
                out_states[0], out_states[1] = moment, square
            attn_new[m], attn_copy[m] = new, new.astype(bf16)
        for m in range(2):
            moment, square, new = adam_update(
                ffn_w[m], ffn_m[m], ffn_v[m], ffn_g[m], GROUP_RATES[1][m], decay_rate
            )
            ffn_moment[m], ffn_square[m] = moment, square
            ffn_new[m], ffn_copy[m] = new, new.astype(bf16)
        for (g, w, m, v), outs in zip(plain, plain_out):
            for ref, value in zip(outs, adam_update(w[...], m[...], v[...], g[...], 0.5, 0.0)):
                ref[...] = value

    tokens_out[...] = tokens_ref[...].astype(f32)

    output[...] = out_b[...]


def last(tokens_low, output, out_b, attn, ffn, plain):
    count, rows, _ = tokens_low.shape
    tile = lambda size, index: pl.BlockSpec((1, size, D), index)
    whole = lambda shape: pl.BlockSpec(
        shape, lambda i: (0,) * len(shape), pipeline_mode=pl.Buffered(1)
    )
    a, f = attn[0].shape, ffn[0].shape
    shapes = [
        ((3,) + a[1:], f32),
        ((3,) + a[1:], f32),
        ((2,) + a[1:], f32),
        (a, f32),
        (a, bf16),
        (f, f32),
        (f, f32),
        (f, f32),
        (f, bf16),
    ]
    for group in plain:
        shapes += [(group[0].shape, f32)] * 3
    inputs = list(attn) + list(ffn) + [array for group in plain for array in group]
    by_half = lambda i: (i // 2, i % 2, 0)
    by_one = lambda i: (i // 2, i % 2, 0)
    second = lambda i: (i // 2, 2 + i % 2, 0)
    quarter = rows // 4
    return pl.pallas_call(
        last_kernel,
        out_shape=[
            jax.ShapeDtypeStruct(tokens_low.shape, f32),
            jax.ShapeDtypeStruct(tokens_low.shape, bf16),
        ]
        + [jax.ShapeDtypeStruct(*entry) for entry in shapes],
        grid=(count * 2,),
        in_specs=[
            tile(rows // 2, by_half),
            tile(quarter, by_one),
            pl.BlockSpec(memory_space=pl.ANY),
        ]
        + [whole(array.shape) for array in inputs],
        out_specs=[tile(rows // 2, by_half), tile(quarter, second)]
        + [whole(shape) for shape, _ in shapes],
        input_output_aliases={2: 1},
        compiler_params=pltpu.CompilerParams(vmem_limit_bytes=VMEM_LIMIT),
        name="last",
    )(tokens_low, out_b, output, *inputs)


def make_body(mesh):
    n_shard, n_ctx, n_tensor = mesh.shape["shard"], mesh.shape["ctx"], mesh.shape["tensor"]
    rows_axes = ("shard", "ctx")
    all_axes = ("shard", "ctx", "tensor")
    paired = n_ctx == 2 and n_shard == 4 and n_tensor == 4

    def swapped(s, c):
        return (s - s % 2 + c, s % 2)

    def swap(array):
        if not paired:
            return array
        pairs = []
        for s in range(n_shard):
            for c in range(n_ctx):
                s_to, c_to = swapped(s, c)
                pairs.append((s * n_ctx + c, s_to * n_ctx + c_to))
        return lax.ppermute(array, rows_axes, pairs)

    def spread(array):
        return lax.all_gather(swap(array), "tensor", axis=0, tiled=True)

    def body(
        tokens,
        cotangent,
        segments,
        rand_blocks,
        attn_w,
        attn_m,
        attn_v,
        ffn_w,
        ffn_m,
        ffn_v,
        qv_bias,
        qv_m,
        qv_v,
        hid_bias,
        hid_m,
        hid_v,
        vec_par,
        vec_m,
        vec_v,
    ):
        t_index = lax.axis_index("tensor")
        nseq = tokens.shape[0] // n_tensor
        piece_len = tokens.shape[1]
        nb = piece_len // BLOCK
        own_rows, own_cols = attn_w.shape[1], attn_w.shape[2]
        own_ff = ffn_w.shape[2]

        def mine(array):
            return lax.dynamic_slice_in_dim(array, t_index * nseq, nseq, 0)

        ints = jnp.concatenate(
            [mine(segments), mine(rand_blocks).reshape(nseq, -1)], axis=1
        )
        ints = swap(ints)
        length = segments.shape[1]
        segs, rand = ints[:, :length], ints[:, length:].reshape(nseq, length // BLOCK, -1)
        piece = lax.axis_index("shard") % 2 if paired else lax.axis_index("ctx")
        tables = attention_tables(segs, rand, piece, nb, paired)

        if paired:
            rand_own, _meta, table = tables
            attn_full, ffn_full, hid_all, x, queries, keys, values, mixed, lse = start(
                n_tensor, attn_w, ffn_w, qv_bias, hid_bias, table[0], rand_own, tokens
            )
            flat = x
            x, queries = x[None], queries[None]
            keys, values = keys.reshape(1, length, D), values.reshape(1, length, D)
            pieces = [piece_len, piece_len]
        else:
            x, cot = mine(tokens), mine(cotangent)
            pieces = [length]
            ffn_z = lax.all_gather(ffn_w.astype(bf16), "tensor", axis=0, tiled=False)
            ffn_z = ffn_z.transpose(1, 2, 0, 3).reshape(2, own_rows, FF)
            ffn_full = lax.all_gather(ffn_z, rows_axes, axis=1, tiled=True)
            flat = x.reshape(-1, D)
            attn_low = attn_w.astype(bf16)
            attn_low = jnp.concatenate([attn_low[i] for i in range(4)], axis=1)
            attn_z = lax.all_gather(attn_low, "tensor", axis=0, tiled=False)
            attn_z = attn_z.reshape(n_tensor, own_rows, 4, own_cols).transpose(2, 1, 0, 3)
            attn_full = lax.all_gather(
                attn_z.reshape(4, own_rows, D), rows_axes, axis=1, tiled=True
            )
            bias_own = jnp.concatenate([qv_bias.reshape(-1), hid_bias])
            bias_all = lax.all_gather(bias_own, "tensor", axis=0, tiled=False)
            qv_all = bias_all[:, : 2 * own_cols].reshape(n_tensor, 2, own_cols)
            qv_all = qv_all.transpose(1, 0, 2).reshape(2, D)
            hid_all = bias_all[:, 2 * own_cols :].reshape(FF)
            keys = matmul(flat, attn_full[1]).astype(bf16).reshape(x.shape)
            values = (matmul(flat, attn_full[2]) + qv_all[1]).astype(bf16).reshape(x.shape)
            keys = lax.all_gather(keys, "ctx", axis=1, tiled=True)
            values = lax.all_gather(values, "ctx", axis=1, tiled=True)
            queries = (matmul(flat, attn_full[0]) + qv_all[0]).astype(bf16) * 0.125
            queries = queries.reshape(x.shape)
            mixed, lse = attend(tables, queries, keys, values)
        mixed_low = mixed.reshape(-1, D)
        if paired:
            out_a, out_b, dw1, dw2, dwo, grad_first_in, grad_mixed, hid_sum, vec_sums = middle(
                n_tensor, flat, mixed_low, hid_all, vec_par, cotangent, attn_full, ffn_full
            )
            out_b = lax.all_gather(out_b, "tensor", axis=0, tiled=False)
        else:
            act, slope, h1, result, grad_second, second_sums = feed_forward(
                flat, mixed_low, cot.reshape(-1, D), attn_full, ffn_full, hid_all, vec_par
            )
            output = spread(result.reshape(x.shape))
            out_a, out_b = output[:, : piece_len // 2], output[:, piece_len // 2 :]
            dw1, dw2, dwo, grad_first_in, grad_mixed, hid_sum, first_sums = feed_back(
                grad_second, h1, mixed_low, attn_full, ffn_full, act, slope, vec_par
            )

        grad_mixed = grad_mixed.reshape(x.shape)
        grad_query, output, dk_parts, dv_parts = attend_back(
            tables,
            queries,
            grad_mixed,
            mixed.reshape(x.shape),
            lse.reshape(nseq, nb, 8, ROWS),
            out_a,
            keys,
            values,
            pieces,
        )

        grad_query_low = grad_query.reshape(-1, D)
        if paired:
            attn_grad, ffn_grad, vec_grad, qv_grad, hid_grad, grad_tokens = finish_all(
                n_tensor,
                [grad_query_low] + [part[0] for part in list(dk_parts) + list(dv_parts)],
                grad_first_in,
                flat,
                attn_full,
                (dw1, dw2, dwo),
                (vec_sums, hid_sum),
            )
        else:
            grad_keys = lax.psum_scatter(dk_parts[0], "ctx", scatter_dimension=1, tiled=True)
            grad_values = lax.psum_scatter(dv_parts[0], "ctx", scatter_dimension=1, tiled=True)
            grad_keys_low = grad_keys.reshape(-1, D)
            grad_values_low = grad_values.reshape(-1, D)
            into_tokens = (
                matmul_nt(grad_query_low, attn_full[0])
                + matmul_nt(grad_keys_low, attn_full[1])
                + matmul_nt(grad_values_low, attn_full[2])
            )
            grad_tokens = spread((grad_first_in + into_tokens).astype(bf16).reshape(x.shape))
            dwq = matmul_tn(flat, grad_query_low).astype(bf16)
            dwk = matmul_tn(flat, grad_keys_low).astype(bf16)
            dwv = matmul_tn(flat, grad_values_low).astype(bf16)
            small = jnp.concatenate(
                [
                    first_sums[0],
                    first_sums[1],
                    second_sums[0],
                    second_sums[1],
                    first_sums[2],
                    second_sums[2],
                    column_sum(grad_query_low),
                    column_sum(grad_values_low),
                    hid_sum[0],
                ]
            )
            ffn_grad = lax.psum_scatter(
                jnp.stack([dw1, dw2]), rows_axes, scatter_dimension=1, tiled=True
            )
            ffn_grad = ffn_grad.reshape(2, own_rows, n_tensor, own_ff).transpose(2, 0, 1, 3)
            ffn_grad = lax.psum_scatter(ffn_grad, "tensor", scatter_dimension=0, tiled=False)
            ffn_grad = ffn_grad.astype(f32)
            attn_grad = lax.psum_scatter(
                jnp.stack([dwq, dwk, dwv, dwo]), rows_axes, scatter_dimension=1, tiled=True
            )
            attn_grad = attn_grad.reshape(4, own_rows, n_tensor, own_cols).transpose(2, 1, 0, 3)
            attn_grad = lax.psum_scatter(
                attn_grad.reshape(n_tensor, own_rows, D), "tensor", scatter_dimension=0
            )
            attn_grad = attn_grad.reshape(own_rows, 4, own_cols).transpose(1, 0, 2).astype(f32)
            small = lax.psum(small, all_axes)
            vec_grad = small[: 6 * D].reshape(6, D)
            qv_grad = lax.dynamic_slice_in_dim(
                small[6 * D : 8 * D].reshape(2, D), t_index * own_cols, own_cols, 1
            )
            hid_grad = lax.dynamic_slice_in_dim(
                small[8 * D : 8 * D + FF], t_index * own_ff, own_ff, 0
            )

        grad_tokens, output, *updated = last(
            grad_tokens,
            output,
            out_b,
            (attn_grad, attn_w, attn_m, attn_v),
            (ffn_grad, ffn_w, ffn_m, ffn_v),
            [
                (qv_grad, qv_bias, qv_m, qv_v),
                (hid_grad.reshape(own_ff), hid_bias, hid_m, hid_v),
                (vec_grad, vec_par, vec_m, vec_v),
            ],
        )
        return (output, grad_tokens, *updated)

    return body


def solution(mesh):
    rows = P("shard", "ctx", None)
    weight = P(None, ("shard", "ctx"), "tensor")
    in_specs = (
        (rows, rows, P("shard", None), P("shard", None, None))
        + (weight,) * 6
        + (P(None, "tensor"),) * 3
        + (P("tensor"),) * 3
        + (P(),) * 3
    )
    out_specs = (
        (rows, rows)
        + (weight,) * 9
        + (P(None, "tensor"),) * 3
        + (P("tensor"),) * 3
        + (P(),) * 3
    )
    return jax.shard_map(
        make_body(mesh), mesh=mesh, in_specs=in_specs, out_specs=out_specs, check_vma=False
    )
```

```python
from functools import partial

import jax
import jax.numpy as jnp
from jax import lax
from jax.experimental import pallas as pl
from jax.experimental.pallas import tpu as pltpu
from jax.sharding import PartitionSpec as P

D = 768
HEAD_DIM = 64
FF = 3072
BLOCK = 64
STEP = 5
GROUP = 4 * HEAD_DIM
GROUPS = D // GROUP
ROWS = 4 * BLOCK
LISTED = 8
KEYS = LISTED * BLOCK
VMEM_LIMIT = 60 * 2**20

beta_first = 0.9
beta_second = 0.999
adam_eps = 1e-08
decay_rate = 0.01
norm_eps = 1e-06
neg_large = -1e30

f32 = jnp.float32
bf16 = jnp.bfloat16


def matmul(left, right):
    return jnp.dot(left, right, preferred_element_type=f32)


def matmul_tn(left, right):
    return lax.dot_general(left, right, (((0,), (0,)), ((), ())), preferred_element_type=f32)


def matmul_nt(left, right):
    return lax.dot_general(left, right, (((1,), (1,)), ((), ())), preferred_element_type=f32)


def column_sum(array_in):
    return jnp.sum(array_in.astype(f32), axis=0)


def adam_update(weight, moment, square, gradient, step_rates, decay_on):
    moment_new = beta_first * moment + (1.0 - beta_first) * gradient
    square_new = beta_second * square + (1.0 - beta_second) * gradient * gradient
    step_ratio = (
        moment_new
        / (1.0 - beta_first**STEP)
        / (jnp.sqrt(square_new / (1.0 - beta_second**STEP)) + adam_eps)
    )
    weight_new = weight - step_rates * (step_ratio + decay_on * weight)
    return (moment_new, square_new, weight_new)


def same_head():
    row_head = lax.broadcasted_iota(jnp.int32, (ROWS, GROUP), 0) // BLOCK
    col_head = lax.broadcasted_iota(jnp.int32, (ROWS, GROUP), 1) // HEAD_DIM
    return row_head == col_head


def spread_heads(block, keep):
    stacked = jnp.concatenate([block] * 4, axis=0)
    return jnp.where(keep, stacked, jnp.zeros_like(stacked))


def fold_heads(full, keep):
    kept = jnp.where(keep, full, 0.0)
    return sum(kept[h * BLOCK : (h + 1) * BLOCK] for h in range(4))


def load_keys(k_all, v_all, seq, k_buf, v_buf, sems):
    return [
        pltpu.make_async_copy(k_all.at[seq], k_buf, sems.at[0]),
        pltpu.make_async_copy(v_all.at[seq], v_buf, sems.at[1]),
    ]


def picked_rows(buf, spots, cols):
    return jnp.concatenate([buf[at, :, cols] for at in spots], axis=0)


def chunk_rows(buf, i, cols):
    blocks = buf[pl.ds(i * LISTED, LISTED), :, cols]
    return blocks.reshape(KEYS, GROUP)


def listed_blocks(rand, base, blk, first, own, total):
    one = lambda condition: condition.astype(jnp.int32)
    me = first + blk
    ids = [me - 1, me, me + 1, me * 0, me * 0 + 1] + [rand[base + n] for n in range(LISTED - 5)]
    spots, unused, common = [], [], []
    for n, block in enumerate(ids):
        out = one(block < 0) + one(block >= total)
        for earlier in ids[:n]:
            out = out + one(block == earlier)
        out = lax.min(out, jnp.int32(1))
        at = lax.max(jnp.int32(0), lax.min(block, jnp.int32(total - 1))) - first + own
        spots.append(at + total * one(at < 0))
        unused.append(out)
        common.append(one(block < 2) * (1 - out))
    return spots, unused, common


def code_rows(tab_ref, spots, unused, common):
    low_half = lax.broadcasted_iota(jnp.int32, (1, 2 * BLOCK), 1) < BLOCK

    def one(n):
        plain = (1 - unused[n] - common[n]).astype(f32)
        return tab_ref[spots[n]] * plain - (unused[n] + 2 * common[n]).astype(f32)

    return [jnp.where(low_half, one(n), one(n + 1)) for n in range(0, LISTED, 2)]


def column_of(row):
    return jnp.broadcast_to(row, (2 * BLOCK, 2 * BLOCK)).T


def mask_bias(document, code):
    return jnp.where((document == code) | (code == -2.0), 0.0, neg_large)


def row_of(column):
    return jnp.broadcast_to(column, (ROWS, 2 * BLOCK)).T[0:1, :]


def forward_block(q_ref, out_ref, lse_ref, k_buf, v_buf, s_buf, tab_ref, rand, base, blk, first, own):
    keep = same_head()
    total_blocks = k_buf.shape[0]
    chunks = total_blocks // LISTED
    is_global = first + blk < 2

    @pl.when(jnp.logical_not(is_global))
    def _():
        spots, unused, common = listed_blocks(rand, base, blk, first, own, total_blocks)
        mine = column_of(tab_ref[own + blk])[:BLOCK]
        mine = jnp.concatenate([mine] * 4, axis=0)
        codes = code_rows(tab_ref, spots, unused, common)
        bias = jnp.concatenate([mask_bias(mine, code) for code in codes], axis=1)
        for g in range(GROUPS):
            cols = slice(g * GROUP, (g + 1) * GROUP)
            q_full = spread_heads(q_ref[:, cols], keep)
            scores = matmul_nt(q_full, picked_rows(k_buf, spots, cols)) + bias
            largest = jnp.max(scores, axis=-1, keepdims=True)
            weights = jnp.exp(scores - largest)
            total = jnp.sum(weights, axis=-1, keepdims=True)
            full = matmul(weights.astype(bf16), picked_rows(v_buf, spots, cols))
            out_ref[:, cols] = fold_heads(full * (1.0 / total), keep).astype(bf16)
            lse_ref[g : g + 1, :] = row_of(largest + jnp.log(total))

    @pl.when(is_global)
    def _():
        for g in range(GROUPS):
            cols = slice(g * GROUP, (g + 1) * GROUP)
            q_full = spread_heads(q_ref[:, cols], keep)

            def score_chunk(i, largest):
                scores = matmul_nt(q_full, chunk_rows(k_buf, i, cols))
                s_buf[i] = scores
                return jnp.maximum(largest, jnp.max(scores, axis=-1, keepdims=True))

            largest = lax.fori_loop(0, chunks, score_chunk, jnp.full((ROWS, 1), neg_large, f32))

            def mix_chunk(i, carry):
                total, full = carry
                weights = jnp.exp(s_buf[i] - largest)
                total = total + jnp.sum(weights, axis=-1, keepdims=True)
                return total, full + matmul(weights.astype(bf16), chunk_rows(v_buf, i, cols))

            total, full = lax.fori_loop(
                0, chunks, mix_chunk, (jnp.zeros((ROWS, 1), f32), jnp.zeros((ROWS, GROUP), f32))
            )
            out_ref[:, cols] = fold_heads(full * (1.0 / total), keep).astype(bf16)
            lse_ref[g : g + 1, :] = row_of(largest + jnp.log(total))


def forward_kernel(
    rand, meta, q_ref, tab_ref, k_all, v_all, out_ref, lse_ref, k_buf, v_buf, s_buf, sems
):
    seq, blk = pl.program_id(0), pl.program_id(1)
    nb = pl.num_programs(1)

    @pl.when(blk == 0)
    def _():
        copies = load_keys(k_all, v_all, seq, k_buf, v_buf, sems)
        for c in copies:
            c.start()
        for c in copies:
            c.wait()

    base = (seq * nb + blk) * (LISTED - 5)
    forward_block(
        q_ref, out_ref, lse_ref, k_buf, v_buf, s_buf, tab_ref, rand, base, blk, meta[0], meta[1]
    )


def back_tile(k_rows, v_rows, q_full, go_full, bias, lse, centre):
    scores = matmul_nt(k_rows, q_full)
    if bias is not None:
        scores = scores + bias
    probs = jnp.exp(scores - lse)
    grad_probs = matmul_nt(v_rows, go_full)
    grad_scores = (probs * (grad_probs - centre)).astype(bf16)
    dv_rows = matmul(probs.astype(bf16), go_full)
    dk_rows = matmul(grad_scores, q_full)
    return matmul_tn(grad_scores, k_rows), dk_rows, dv_rows


def backward_kernel(
    n_out, rand, meta, q_ref, go_ref, mixed_ref, lse_ref, tab_ref, out_a, k_all, v_all, *rest
):
    dq_ref, out_ref, *rest = rest
    dk_refs, dv_refs = rest[:n_out], rest[n_out : 2 * n_out]
    k_buf, v_buf, dk_acc, dv_acc, sems = rest[2 * n_out :]
    seq, blk = pl.program_id(0), pl.program_id(1)
    nb = pl.num_programs(1)
    total_blocks = k_buf.shape[0]
    chunks = total_blocks // LISTED

    out_ref[...] = out_a[...]

    @pl.when(blk == 0)
    def _():
        copies = load_keys(k_all, v_all, seq, k_buf, v_buf, sems)
        for c in copies:
            c.start()
        dk_acc[...] = jnp.zeros_like(dk_acc)
        dv_acc[...] = jnp.zeros_like(dv_acc)
        for c in copies:
            c.wait()

    keep = same_head()
    is_global = meta[0] + blk < 2
    base = (seq * nb + blk) * (LISTED - 5)

    def operands(g):
        cols = slice(g * GROUP, (g + 1) * GROUP)
        q_full = spread_heads(q_ref[:, cols], keep)
        go_full = spread_heads(go_ref[:, cols], keep)
        mixed = jnp.concatenate([mixed_ref[:, cols]] * 4, axis=0)
        product = go_full.astype(f32) * mixed.astype(f32)
        centre = row_of(jnp.sum(product, axis=-1, keepdims=True))
        return cols, q_full, go_full, lse_ref[g : g + 1, :], centre

    @pl.when(jnp.logical_not(is_global))
    def _():
        spots, unused, common = listed_blocks(rand, base, blk, meta[0], meta[1], total_blocks)
        stores = [at + (total_blocks - at) * out for at, out in zip(spots, unused)]
        own = tab_ref[meta[1] + blk]
        codes = code_rows(tab_ref, spots, unused, common)
        bias = jnp.concatenate([mask_bias(own, column_of(code)) for code in codes], axis=0)
        bias = jnp.concatenate([bias, bias], axis=1)
        for g in range(GROUPS):
            cols, q_full, go_full, lse, centre = operands(g)
            k_rows, v_rows = picked_rows(k_buf, spots, cols), picked_rows(v_buf, spots, cols)
            dq_full, dk_rows, dv_rows = back_tile(
                k_rows, v_rows, q_full, go_full, bias, lse, centre
            )
            dq_ref[:, cols] = (fold_heads(dq_full, keep) * 0.125).astype(bf16)
            places = [pl.ds(pl.multiple_of(at * BLOCK, BLOCK), BLOCK) for at in stores]
            dk_old = [dk_acc[at, cols] for at in places]
            dv_old = [dv_acc[at, cols] for at in places]
            for n, at in enumerate(places):
                own_rows = slice(n * BLOCK, (n + 1) * BLOCK)
                dk_acc[at, cols] = dk_old[n] + dk_rows[own_rows]
                dv_acc[at, cols] = dv_old[n] + dv_rows[own_rows]

    @pl.when(is_global)
    def _():
        for g in range(GROUPS):
            cols, q_full, go_full, lse, centre = operands(g)

            def chunk_back(i, dq_full):
                rows = pl.ds(pl.multiple_of(i * KEYS, KEYS), KEYS)
                dq_now, dk_rows, dv_rows = back_tile(
                    chunk_rows(k_buf, i, cols),
                    chunk_rows(v_buf, i, cols),
                    q_full,
                    go_full,
                    None,
                    lse,
                    centre,
                )
                dk_acc[rows, cols] += dk_rows
                dv_acc[rows, cols] += dv_rows
                return dq_full + dq_now

            dq_full = lax.fori_loop(0, chunks, chunk_back, jnp.zeros((ROWS, GROUP), f32))
            dq_ref[:, cols] = (fold_heads(dq_full, keep) * 0.125).astype(bf16)

    @pl.when(blk == nb - 1)
    def _():
        row = 0
        for dk_ref, dv_ref in zip(dk_refs, dv_refs):
            rows = dk_ref.shape[0]
            dk_ref[...] = dk_acc[row : row + rows].astype(bf16)
            dv_ref[...] = dv_acc[row : row + rows].astype(bf16)
            row += rows


def attention_tables(segments, random, piece, nb, own_first):
    seq_count, length = segments.shape
    total = length // BLOCK
    first = piece * nb
    rand = lax.dynamic_slice_in_dim(random, first, nb, 1).reshape(-1)
    table = segments.reshape(seq_count, total, BLOCK).astype(f32)
    table = jnp.concatenate([table, table], axis=2)[:, :, None, :]
    if own_first:
        table = lax.dynamic_slice_in_dim(jnp.concatenate([table, table], axis=1), first, total, 1)
    meta = jnp.stack([first, jnp.zeros_like(first) if own_first else first]).astype(jnp.int32)
    return rand, meta, table


def as_blocks(rows):
    return rows.reshape(rows.shape[0], -1, BLOCK, D)


def attend(tables, q, keys, values):
    rand, meta, table = tables
    seq_count, piece_len, _ = q.shape
    nb = piece_len // BLOCK
    length = keys.shape[1]
    any_spec = pl.BlockSpec(memory_space=pl.ANY)
    row_spec = pl.BlockSpec((None, BLOCK, D), lambda s, b, *_: (s, b, 0))
    return pl.pallas_call(
        forward_kernel,
        out_shape=[
            jax.ShapeDtypeStruct(q.shape, bf16),
            jax.ShapeDtypeStruct((seq_count, nb, 8, ROWS), f32),
        ],
        grid_spec=pltpu.PrefetchScalarGridSpec(
            num_scalar_prefetch=2,
            grid=(seq_count, nb),
            in_specs=[
                row_spec,
                pl.BlockSpec((None,) + table.shape[1:], lambda s, b, *_: (s, 0, 0, 0)),
                any_spec,
                any_spec,
            ],
            out_specs=[
                row_spec,
                pl.BlockSpec((None, None, 8, ROWS), lambda s, b, *_: (s, b, 0, 0)),
            ],
            scratch_shapes=[
                pltpu.VMEM((length // BLOCK, BLOCK, D), bf16),
                pltpu.VMEM((length // BLOCK, BLOCK, D), bf16),
                pltpu.VMEM((length // KEYS, ROWS, KEYS), f32),
                pltpu.SemaphoreType.DMA((2,)),
            ],
        ),
        compiler_params=pltpu.CompilerParams(vmem_limit_bytes=VMEM_LIMIT),
        name="attend",
    )(rand, meta, q, table, as_blocks(keys), as_blocks(values))


def attend_back(tables, q, grad_mixed, mixed, lse, out_a, keys, values, pieces):
    rand, meta, table = tables
    seq_count, piece_len, _ = q.shape
    nb = piece_len // BLOCK
    length = keys.shape[1]
    any_spec = pl.BlockSpec(memory_space=pl.ANY)
    row_spec = pl.BlockSpec((None, BLOCK, D), lambda s, b, *_: (s, b, 0))
    count, half, _ = out_a.shape
    share = count * half // (seq_count * nb)
    if share <= half:
        per = half // share
        tile = pl.BlockSpec(
            (None, share, D), lambda s, b, *_: ((s * nb + b) // per, (s * nb + b) % per, 0)
        )
    else:
        tile = pl.BlockSpec((share // half, half, D), lambda s, b, *_: (s * nb + b, 0, 0))
    part_specs = [pl.BlockSpec((None, rows, D), lambda s, b, *_: (s, 0, 0)) for rows in pieces]
    part_shapes = [jax.ShapeDtypeStruct((seq_count, rows, D), bf16) for rows in pieces]
    out = pl.pallas_call(
        partial(backward_kernel, len(pieces)),
        out_shape=[
            jax.ShapeDtypeStruct(q.shape, bf16),
            jax.ShapeDtypeStruct((count, 2 * half, D), bf16),
        ]
        + part_shapes * 2,
        grid_spec=pltpu.PrefetchScalarGridSpec(
            num_scalar_prefetch=2,
            grid=(seq_count, nb),
            in_specs=[
                row_spec,
                row_spec,
                row_spec,
                pl.BlockSpec((None, None, 8, ROWS), lambda s, b, *_: (s, b, 0, 0)),
                pl.BlockSpec((None,) + table.shape[1:], lambda s, b, *_: (s, 0, 0, 0)),
                tile,
                any_spec,
                any_spec,
            ],
            out_specs=[row_spec, tile] + part_specs * 2,
            scratch_shapes=[
                pltpu.VMEM((length // BLOCK, BLOCK, D), bf16),
                pltpu.VMEM((length // BLOCK, BLOCK, D), bf16),
                pltpu.VMEM((length + BLOCK, D), f32),
                pltpu.VMEM((length + BLOCK, D), f32),
                pltpu.SemaphoreType.DMA((2,)),
            ],
        ),
        compiler_params=pltpu.CompilerParams(vmem_limit_bytes=VMEM_LIMIT),
        cost_estimate=pl.CostEstimate(
            flops=seq_count * nb * GROUPS * 10 * ROWS * KEYS * GROUP,
            bytes_accessed=seq_count * (3 * piece_len + 4 * length) * D * 2,
            transcendentals=seq_count * nb * GROUPS * ROWS * KEYS,
        ),
        name="attend_back",
    )(rand, meta, q, grad_mixed, mixed, lse, table, out_a, as_blocks(keys), as_blocks(values))
    return out[0], out[1], out[2 : 2 + len(pieces)], out[2 + len(pieces) :]


def norm_parts(hidden):
    centred = hidden - jnp.mean(hidden, axis=-1, keepdims=True)
    scale = lax.rsqrt(jnp.mean(centred * centred, axis=-1, keepdims=True) + norm_eps)
    return centred * scale, scale


def norm_back(grad, unit, scale, gain):
    inner = grad * gain
    return scale * (
        inner
        - jnp.mean(inner, axis=-1, keepdims=True)
        - unit * jnp.mean(inner * unit, axis=-1, keepdims=True)
    )


def gelu_and_slope(pre):
    bell = jnp.exp(-0.5 * pre * pre)
    t = 1.0 / (1.0 + (0.3275911 * 0.5**0.5) * jnp.abs(pre))
    poly = 0.5 * 1.061405429
    for coefficient in (-1.453152027, 1.421413741, -0.284496736, 0.254829592):
        poly = poly * t + 0.5 * coefficient
    tail = poly * t * bell
    phi = jnp.where(pre >= 0.0, 1.0 - tail, tail)
    return pre * phi, phi + pre * bell * 0.3989422804014327


def column_total(array):
    return jnp.sum(array.astype(f32), axis=0, keepdims=True)


def up_kernel(
    chunk,
    x_ref,
    mixed_ref,
    cot_ref,
    wo_ref,
    w1_ref,
    w2_ref,
    hid_ref,
    vec_ref,
    act_ref,
    slope_ref,
    h1_ref,
    res_ref,
    gs_ref,
    sums_ref,
    low,
    down,
):
    step = pl.program_id(0)
    chunks = x_ref.shape[0] // chunk

    @pl.when(step == 0)
    def _():
        @pl.loop(0, chunks)
        def _(i):
            rows = pl.ds(pl.multiple_of(i * chunk, chunk), chunk)
            h1 = x_ref[rows, :].astype(f32) + matmul_nt(mixed_ref[rows, :], wo_ref[...])
            h1 = h1 + vec_ref[4:5, :]
            h1_ref[rows, :] = h1
            unit, _scale = norm_parts(h1)
            low[rows, :] = (unit * vec_ref[0:1, :] + vec_ref[1:2, :]).astype(bf16)
            down[rows, :] = jnp.zeros((chunk, D), f32)

    for i in range(chunks):
        rows = slice(i * chunk, (i + 1) * chunk)
        pre = matmul(low[rows, :], w1_ref[...]) + hid_ref[...]
        act, slope = gelu_and_slope(pre)
        act = act.astype(bf16)
        act_ref[rows, :] = act
        slope_ref[rows, :] = slope.astype(bf16)
        down[rows, :] += matmul_nt(act, w2_ref[...])

    @pl.when(step == pl.num_programs(0) - 1)
    def _():
        sums_ref[...] = jnp.zeros_like(sums_ref)

        @pl.loop(0, chunks)
        def _(i):
            rows = pl.ds(pl.multiple_of(i * chunk, chunk), chunk)
            unit, _scale = norm_parts(h1_ref[rows, :])
            first = unit * vec_ref[0:1, :] + vec_ref[1:2, :]
            unit, scale = norm_parts(first + down[rows, :] + vec_ref[5:6, :])
            res_ref[rows, :] = (unit * vec_ref[2:3, :] + vec_ref[3:4, :]).astype(bf16)
            cot = cot_ref[rows, :].astype(f32)
            grad = norm_back(cot, unit, scale, vec_ref[2:3, :])
            gs_ref[rows, :] = grad
            sums_ref[0:1, :] += column_total(cot * unit)
            sums_ref[1:2, :] += column_total(cot)
            sums_ref[2:3, :] += column_total(grad.astype(bf16))


def feed_forward(x, mixed, cot, attn_full, ffn_full, hid_all, vec_par):
    rows = x.shape[0]
    chunk = min(256, rows)
    steps = FF // D
    whole = lambda shape: pl.BlockSpec(shape, lambda t: (0,) * len(shape))
    once = lambda shape: pl.BlockSpec(
        shape, lambda t: (0,) * len(shape), pipeline_mode=pl.Buffered(1)
    )
    hidden = pl.BlockSpec((rows, D), lambda t: (0, t))
    return pl.pallas_call(
        partial(up_kernel, chunk),
        out_shape=[
            jax.ShapeDtypeStruct((rows, FF), bf16),
            jax.ShapeDtypeStruct((rows, FF), bf16),
            jax.ShapeDtypeStruct((rows, D), f32),
            jax.ShapeDtypeStruct((rows, D), bf16),
            jax.ShapeDtypeStruct((rows, D), f32),
            jax.ShapeDtypeStruct((8, D), f32),
        ],
        grid=(steps,),
        in_specs=[
            once((rows, D)),
            once((rows, D)),
            once((rows, D)),
            pl.BlockSpec((None, D, D), lambda t: (3, 0, 0), pipeline_mode=pl.Buffered(1)),
            pl.BlockSpec((None, D, D), lambda t: (0, 0, t)),
            pl.BlockSpec((None, D, D), lambda t: (1, 0, t)),
            pl.BlockSpec((1, D), lambda t: (0, t)),
            whole((6, D)),
        ],
        out_specs=[
            hidden,
            hidden,
            whole((rows, D)),
            whole((rows, D)),
            whole((rows, D)),
            whole((8, D)),
        ],
        scratch_shapes=[pltpu.VMEM((rows, D), bf16), pltpu.VMEM((rows, D), f32)],
        compiler_params=pltpu.CompilerParams(vmem_limit_bytes=VMEM_LIMIT),
        cost_estimate=pl.CostEstimate(
            flops=2 * rows * D * (D + 2 * FF),
            bytes_accessed=rows * D * 30 + 2 * D * FF * 2,
            transcendentals=2 * rows * FF,
        ),
        name="feed_forward",
    )(x, mixed, cot, attn_full, ffn_full, ffn_full, hid_all.reshape(1, FF), vec_par)


def down_kernel(
    chunk,
    gs_ref,
    h1_ref,
    mixed_ref,
    wo_ref,
    w1_ref,
    w2_ref,
    act_ref,
    slope_ref,
    vec_ref,
    dw1_ref,
    dw2_ref,
    dwo_ref,
    gh1_ref,
    gm_ref,
    hid_ref,
    sums_ref,
    turned,
    low_t,
    pre,
    total,
):
    step = pl.program_id(0)
    n_rows = gs_ref.shape[0]
    chunks = n_rows // chunk

    @pl.when(step == 0)
    def _():
        @pl.loop(0, chunks)
        def _(i):
            rows = pl.ds(pl.multiple_of(i * chunk, chunk), chunk)
            unit, _scale = norm_parts(h1_ref[rows, :])
            low = unit * vec_ref[0:1, :] + vec_ref[1:2, :]
            low_t[:, rows] = low.T.astype(bf16)
            turned[:, rows] = gs_ref[rows, :].T.astype(bf16)
            total[rows, :] = gs_ref[rows, :]

    for i in range(chunks):
        rows = slice(i * chunk, (i + 1) * chunk)
        grad_act = matmul(gs_ref[rows, :].astype(bf16), w2_ref[...]).astype(bf16).astype(f32)
        grad_pre = (grad_act * slope_ref[rows, :].astype(f32)).astype(bf16)
        pre[rows, :] = grad_pre
        total[rows, :] += matmul_nt(grad_pre, w1_ref[...])
    hid_ref[...] = column_total(pre[...])
    part = D // 4
    for j in range(4):
        out = slice(j * part, (j + 1) * part)
        dw1_ref[out, :] = matmul(low_t[out, :], pre[...]).astype(bf16)
        dw2_ref[out, :] = matmul(turned[out, :], act_ref[...]).astype(bf16)

    @pl.when(step == pl.num_programs(0) - 1)
    def _():
        sums_ref[...] = jnp.zeros_like(sums_ref)

        @pl.loop(0, chunks)
        def _(i):
            rows = pl.ds(pl.multiple_of(i * chunk, chunk), chunk)
            unit, scale = norm_parts(h1_ref[rows, :])
            grad_first = total[rows, :]
            grad_h1 = norm_back(grad_first, unit, scale, vec_ref[0:1, :])
            gh1_ref[rows, :] = grad_h1
            low = grad_h1.astype(bf16)
            gm_ref[rows, :] = matmul(low, wo_ref[...]).astype(bf16)
            turned[:, rows] = grad_h1.T.astype(bf16)
            sums_ref[0:1, :] += column_total(grad_first * unit)
            sums_ref[1:2, :] += column_total(grad_first)
            sums_ref[2:3, :] += column_total(low)

        @pl.loop(0, 4)
        def _(j):
            out = pl.ds(pl.multiple_of(j * part, part), part)
            dwo_ref[out, :] = matmul(turned[out, :], mixed_ref[...]).astype(bf16)


def feed_back(gs, h1, mixed, attn_full, ffn_full, act, slope, vec_par):
    rows = gs.shape[0]
    chunk = min(256, rows)
    steps = FF // D
    whole = lambda shape: pl.BlockSpec(shape, lambda t: (0,) * len(shape))
    once = lambda shape: pl.BlockSpec(
        shape, lambda t: (0,) * len(shape), pipeline_mode=pl.Buffered(1)
    )
    hidden = pl.BlockSpec((rows, D), lambda t: (0, t))
    slab = pl.BlockSpec((D, D), lambda t: (0, t))
    return pl.pallas_call(
        partial(down_kernel, chunk),
        out_shape=[
            jax.ShapeDtypeStruct((D, FF), bf16),
            jax.ShapeDtypeStruct((D, FF), bf16),
            jax.ShapeDtypeStruct((D, D), bf16),
            jax.ShapeDtypeStruct((rows, D), f32),
            jax.ShapeDtypeStruct((rows, D), bf16),
            jax.ShapeDtypeStruct((1, FF), f32),
            jax.ShapeDtypeStruct((8, D), f32),
        ],
        grid=(steps,),
        in_specs=[
            once((rows, D)),
            once((rows, D)),
            once((rows, D)),
            pl.BlockSpec((None, D, D), lambda t: (3, 0, 0), pipeline_mode=pl.Buffered(1)),
            pl.BlockSpec((None, D, D), lambda t: (0, 0, t)),
            pl.BlockSpec((None, D, D), lambda t: (1, 0, t)),
            hidden,
            hidden,
            whole((6, D)),
        ],
        out_specs=[
            slab,
            slab,
            whole((D, D)),
            whole((rows, D)),
            whole((rows, D)),
            pl.BlockSpec((1, D), lambda t: (0, t)),
            whole((8, D)),
        ],
        scratch_shapes=[
            pltpu.VMEM((D, rows), bf16),
            pltpu.VMEM((D, rows), bf16),
            pltpu.VMEM((rows, D), bf16),
            pltpu.VMEM((rows, D), f32),
        ],
        compiler_params=pltpu.CompilerParams(vmem_limit_bytes=VMEM_LIMIT),
        cost_estimate=pl.CostEstimate(
            flops=2 * rows * D * (2 * D + 4 * FF),
            bytes_accessed=rows * D * 30 + 4 * D * FF * 2,
            transcendentals=0,
        ),
        name="feed_back",
    )(gs, h1, mixed, attn_full, ffn_full, ffn_full, act, slope, vec_par)


WIDE = 1536
STRIP = 96
PIECES = 8
ITEM = 128
LINE_ITEMS = 4
MESH = pl.DeviceIdType.MESH


def remote(src, dst, send, recv, where):
    return pltpu.make_async_remote_copy(
        src_ref=src,
        dst_ref=dst,
        send_sem=send,
        recv_sem=recv,
        device_id=where,
        device_id_type=MESH,
    )


def greet(partners):
    barrier = pltpu.get_barrier_semaphore()
    for where in partners:
        pl.semaphore_signal(barrier, inc=1, device_id=where, device_id_type=MESH)
    pl.semaphore_wait(barrier, len(partners))


def places(n_tensor):
    s, c, t = lax.axis_index("shard"), lax.axis_index("ctx"), lax.axis_index("tensor")
    x, core = s // 2, s % 2
    sibling = (x * 2 + 1 - core, c, t)
    over_x = ((1 - x) * 2 + core, c, t)
    over_y = (s, 1 - c, t)
    across = (x * 2 + 1 - core, 1 - c, t)
    along_z = [(s, c, lax.rem(t + k, n_tensor)) for k in range(1, n_tensor)]
    return s, c, t, x, core, sibling, over_x, over_y, across, along_z


class Line:
    def __init__(self, s, c, t, last, items, rows, array, out, up, down, copied):
        self.s, self.c, self.t, self.last, self.items = s, c, t, last, items
        self.rows, self.array, self.out, self.up, self.down = rows, array, out, up, down
        self.copied = copied

    def hop(self, i, src_t, sems, n, to):
        ref = self.array.at[src_t, pl.ds(i * self.rows, self.rows)]
        return remote(ref, ref, sems[0].at[n], sems[1].at[n], (self.s, self.c, to))

    def keep(self, src_t, n):
        return pltpu.make_async_copy(self.array.at[src_t], self.out.at[src_t], self.copied.at[n])

    def send_own(self, i):
        t = self.t

        @pl.when(t < self.last)
        def _():
            self.hop(i, t, self.up, i, t + 1).start()

        @pl.when(t > 0)
        def _():
            self.hop(i, t, self.down, i, t - 1).start()

        if i == self.items - 1:
            self.keep(t, 2 * self.last).start()

    def tick(self, j):
        t, last = self.t, self.last
        i, hops, n = j % self.items, j // self.items + 1, j + self.items

        @pl.when(t >= hops)
        def _():
            self.hop(i, t - hops, self.up, j, t - 1).wait_recv()

            @pl.when(t < last)
            def _():
                self.hop(i, t - hops, self.up, n, t + 1).start()

            if i == self.items - 1:
                self.keep(t - hops, hops - 1).start()

        @pl.when(t + hops <= last)
        def _():
            self.hop(i, t + hops, self.down, j, t + 1).wait_recv()

            @pl.when(t > 0)
            def _():
                self.hop(i, t + hops, self.down, n, t - 1).start()

            if i == self.items - 1:
                self.keep(t + hops, last + hops - 1).start()

    def settle(self):
        t, last = self.t, self.last
        for j in range(self.items * last):
            i, hops = j % self.items, j // self.items

            @pl.when((t < last) & (t >= hops))
            def _():
                self.hop(i, t - hops, self.up, j, t + 1).wait_send()

            @pl.when((t > 0) & (t + hops <= last))
            def _():
                self.hop(i, t + hops, self.down, j, t - 1).wait_send()

        self.keep(t, 2 * last).wait()
        for hops in range(1, last + 1):

            @pl.when(t >= hops)
            def _():
                self.keep(t - hops, hops - 1).wait()

            @pl.when(t + hops <= last)
            def _():
                self.keep(t + hops, last + hops - 1).wait()


class Relay:
    def __init__(self, s, c, t, items, rows, array, out, send, recv, passed, copied):
        self.s, self.c, self.t, self.items, self.rows = s, c, t, items, rows
        self.array, self.out, self.send, self.recv = array, out, send, recv
        self.passed, self.copied = passed, copied

    def copy(self, i, source, send, to):
        ref = self.array.at[source, pl.ds(i * self.rows, self.rows)]
        return remote(ref, ref, send, self.recv.at[source * self.items + i], (self.s, self.c, to))

    def keep(self, u):
        return pltpu.make_async_copy(self.array.at[u], self.out.at[u], self.copied.at[u])

    def own(self, i, act):
        t = self.t
        for n, step in enumerate((2, -2, 1, -1)):

            @pl.when((t + step >= 0) & (t + step < 4))
            def _():
                act(self.copy(i, t, self.send.at[4 * i + n], t + step))

    def send_own(self, i):
        self.own(i, lambda copy: copy.start())

    def through(self, i, act):
        for t, source, to in ((2, 0, 3), (1, 3, 0)):

            @pl.when(self.t == t)
            def _():
                act(self.copy(i, source, self.passed.at[i], to))

    def relay(self, i):
        def act(copy):
            copy.wait_recv()
            copy.start()

        self.through(i, act)

    def settle(self):
        t = self.t
        for u, relayed_by in ((1, 1), (2, 2), (0, 2), (3, 1)):

            @pl.when((t != u) & (t != relayed_by))
            def _():
                for i in range(self.items):
                    self.copy(i, u, self.send.at[0], lax.rem(t + 1, 4)).wait_recv()

            self.keep(u).start()
        for i in range(self.items):
            self.own(i, lambda copy: copy.wait_send())
            self.through(i, lambda copy: copy.wait_send())
        for u in range(4):
            self.keep(u).wait()


def start_kernel(n_tensor, *refs):
    attn_ref, ffn_ref, qv_ref, hid_ref, tab_ref, rand, tokens = refs[:7]
    attn_out, ffn_out, hid_out, x_out, q_out, k_out, v_out, mixed_out, lse_out = refs[7:16]
    low, low_z, bias, bias_z, bias_qv, ffn_low, full, xs, qs, ms, k_buf, v_buf, s_buf = refs[16:29]
    (
        z_send,
        z_recv,
        b_send,
        b_recv,
        fz_send,
        fz_recv,
        x_send,
        x_recv,
        g_send,
        g_recv,
        p_send,
        p_recv,
        fg_send,
        fg_recv,
        fp_send,
        fp_recv,
        kv_send,
        kv_recv,
        own_sem,
    ) = refs[29:]
    s, c, t, x, core, sibling, over_x, over_y, across, along_z = places(n_tensor)
    own_cols, own_ff = D // n_tensor, FF // n_tensor
    n_rows = xs.shape[0]

    for m in range(4):
        low[:, m * own_cols : (m + 1) * own_cols] = attn_ref[m].astype(bf16)
    for m in range(2):
        ffn_low[m] = ffn_ref[m].astype(bf16)
    bias[0:2, 0:own_cols] = qv_ref[...]
    bias[2:3, 0:own_ff] = hid_ref[...]

    greet([sibling, over_x, over_y, across] + along_z)

    sent = []

    def put(copy):
        copy.start()
        sent.append(copy)

    half = 2 * own_cols

    def z_hop(path, k, u):
        cols = pl.ds(path * half, half)
        n = path * n_tensor
        return remote(
            low.at[:, cols], low_z.at[u, :, cols], z_send.at[n + k], z_recv.at[n + u], along_z[k]
        )

    for path in range(2):
        for k in range(n_tensor - 1):
            put(z_hop(path, k, t))

    def keep_rows(src, dst, n):
        return pltpu.make_async_copy(src.at[t], dst, x_recv.at[n])

    def swap_rows(src, dst, n):
        return remote(src.at[t], dst, x_send.at[n], x_recv.at[n], across)

    @pl.when(core == c)
    def _():
        keep_rows(tokens, xs, 0).start()

    @pl.when(core != c)
    def _():
        swap_rows(tokens, xs, 0).start()

    low_z[t] = low[...]
    bias_z[t] = bias[...]

    def strip(shard, ctx):
        return pl.ds(pl.multiple_of((2 * shard + ctx) * STRIP, STRIP), STRIP)

    here = strip(s, c)

    def lay_out(path):
        for k, where in enumerate(along_z):
            z_hop(path, k, where[2]).wait_recv()
        for n in range(n_tensor):
            for m in range(2 * path, 2 * path + 2):
                piece = low_z[n, :, m * own_cols : (m + 1) * own_cols]
                full[m, here, n * own_cols : (n + 1) * own_cols] = piece

    far_x, far_y = over_x[0], 1 - c
    labels = ["own", "x", "y", "xy"]
    rows = {
        "own": here,
        "x": strip(far_x, c),
        "y": strip(s, far_y),
        "xy": strip(far_x, far_y),
    }
    far_rows = {
        "own": strip(sibling[0], c),
        "x": strip(2 * (1 - x) + 1 - core, c),
        "y": strip(sibling[0], far_y),
        "xy": strip(2 * (1 - x) + 1 - core, far_y),
    }

    def attn_block(path, at):
        return full.at[pl.ds(2 * path, 2), at, :]

    def ffn_block(path, at):
        return ffn_out.at[path, at, :]

    class Gather:
        def __init__(self, block, ways, gs, gr, ps, pr):
            self.block, self.gs, self.gr, self.ps, self.pr = block, gs, gr, ps, pr
            x_first = (("x", over_x), ("y", over_y))
            self.ways = [x_first if way == 0 else x_first[::-1] for way in ways]

        def hop(self, path, name, label, where):
            n = path * 3 + labels.index(label) - 1
            ref = self.block(path, rows[name])
            return remote(ref, ref, self.gs.at[n], self.gr.at[n], where)

        def give(self, path, name, label, where):
            put(self.hop(path, name, label, where))

        def take(self, path, label):
            self.hop(path, label, label, over_x).wait_recv()

        def share(self, path, name):
            put(self.shared(path, name))

        def take_shared(self, path):
            for n, name in enumerate(labels):
                ref = self.block(path, far_rows[name])
                n = path * 4 + n
                remote(ref, ref, self.ps.at[n], self.pr.at[n], sibling).wait_recv()

        def shared(self, path, name):
            n = path * 4 + labels.index(name)
            ref = self.block(path, rows[name])
            return remote(ref, ref, self.ps.at[n], self.pr.at[n], sibling)

        def again(self, path, number):
            near, far = self.ways[path]
            if number == 1:
                sent.append(self.hop(path, near[0], "xy", far[1]))
            sent.append(self.shared(path, {1: near[0], 2: far[0], 3: "xy"}[number]))

        def step(self, path, number):
            near, far = self.ways[path]
            if number == 0:
                self.give(path, "own", near[0], near[1])
                self.give(path, "own", far[0], far[1])
                self.share(path, "own")
            elif number == 1:
                self.take(path, near[0])
                self.give(path, near[0], "xy", far[1])
                self.share(path, near[0])
            elif number == 2:
                self.take(path, far[0])
                self.share(path, far[0])
            else:
                self.take(path, "xy")
                self.share(path, "xy")

    attn = Gather(attn_block, (1, 1), g_send, g_recv, p_send, p_recv)
    ffn = Gather(ffn_block, (0, 1), fg_send, fg_recv, fp_send, fp_recv)

    def ffn_cols(path, u):
        return ffn_out.at[path, here, pl.ds(pl.multiple_of(u * own_ff, own_ff), own_ff)]

    def ffn_hop(path, k, u):
        n = path * n_tensor
        return remote(
            ffn_low.at[path],
            ffn_cols(path, u),
            fz_send.at[n + k],
            fz_recv.at[n + u],
            along_z[k],
        )

    local = []

    def write(src, dst, n):
        copy = pltpu.make_async_copy(src, dst, own_sem.at[n])
        copy.start()
        local.append(copy)

    def ffn_along_z(path):
        for k in range(n_tensor - 1):
            put(ffn_hop(path, k, t))
        write(ffn_low.at[path], ffn_cols(path, t), 5 + path)

    def ffn_ready(path):
        for k, where in enumerate(along_z):
            ffn_hop(path, k, where[2]).wait_recv()
        local[path].wait()
        ffn.step(path, 0)

    lay_out(0)
    attn.step(0, 0)
    lay_out(1)
    attn.step(1, 0)
    ffn_along_z(0)
    ffn_along_z(1)
    for k, where in enumerate(along_z):
        put(remote(bias, bias_z.at[t], b_send.at[k], b_recv.at[t], where))
    attn.step(0, 1)
    attn.step(1, 1)
    ffn_ready(0)
    attn.step(0, 2)
    attn.step(1, 2)
    attn.step(0, 3)
    attn.step(1, 3)
    for k, where in enumerate(along_z):
        u = where[2]
        remote(bias, bias_z.at[u], b_send.at[k], b_recv.at[u], where).wait_recv()
    for n in range(n_tensor):
        cols = slice(n * own_cols, (n + 1) * own_cols)
        bias_qv[0:2, cols] = bias_z[n, 0:2, 0:own_cols]
        hid_out[:, n * own_ff : (n + 1) * own_ff] = bias_z[n, 2:3, 0:own_ff]

    @pl.when(core == c)
    def _():
        keep_rows(tokens, xs, 0).wait()

    @pl.when(core != c)
    def _():
        swap_rows(tokens, xs, 0).wait()

    chunk = 256
    chunks = n_rows // chunk
    per = chunk // BLOCK

    def kv_hop(buf, i, n):
        at, to = pl.ds(i * per, per), pl.ds(n_rows // BLOCK + i * per, per)
        return remote(buf.at[at], buf.at[to], kv_send.at[n], kv_recv.at[n], sibling)

    attn.take_shared(0)
    for i in range(chunks):
        at = pl.ds(i * chunk, chunk)
        k = matmul(xs[at, :], full[1]).astype(bf16)
        k_buf[pl.ds(i * per, per)] = k.reshape(per, BLOCK, D)
        put(kv_hop(k_buf, i, i))
    ffn_ready(1)
    for i in range(chunks):
        at = pl.ds(i * chunk, chunk)
        q = matmul(xs[at, :], full[0]) + bias_qv[0:1, :]
        qs[at, :] = (q.astype(bf16).astype(f32) * 0.125).astype(bf16)
    attn.take_shared(1)
    for i in range(chunks):
        at = pl.ds(i * chunk, chunk)
        v = (matmul(xs[at, :], full[2]) + bias_qv[1:2, :]).astype(bf16)
        v_buf[pl.ds(i * per, per)] = v.reshape(per, BLOCK, D)
        put(kv_hop(v_buf, i, chunks + i))
    ffn.step(0, 1)
    write(xs, x_out, 0)
    write(qs, q_out, 1)
    write(full, attn_out, 2)
    for i in range(chunks):
        kv_hop(k_buf, i, i).wait_recv()
        kv_hop(v_buf, i, chunks + i).wait_recv()
    write(k_buf, k_out, 3)
    write(v_buf, v_out, 4)

    nb = n_rows // BLOCK
    first = core * nb
    stops = {0: [(1, 1)], 1: [(0, 2), (1, 2)], 9: [(0, 3), (1, 3)]}

    @pl.loop(0, nb)
    def _(blk):
        at = pl.ds(pl.multiple_of(blk * BLOCK, BLOCK), BLOCK)
        forward_block(
            qs.at[at],
            ms.at[at],
            lse_out.at[blk],
            k_buf,
            v_buf,
            s_buf,
            tab_ref,
            rand,
            blk * (LISTED - 5),
            blk,
            first,
            0,
        )

        for at_block, moves in stops.items():

            @pl.when(blk == at_block)
            def _():
                mark = len(sent)
                for path, number in moves:
                    ffn.step(path, number)
                del sent[mark:]

    write(ms, mixed_out, 7)
    for path, number in [move for moves in stops.values() for move in moves]:
        ffn.again(path, number)
    ffn.take_shared(0)
    ffn.take_shared(1)

    for copy in sent:
        copy.wait_send()
    for copy in local[2:]:
        copy.wait()


def start(n_tensor, attn_w, ffn_w, qv_bias, hid_bias, table, rand, tokens):
    rows = tokens.shape[1]
    own_ff = FF // n_tensor
    dma = pltpu.SemaphoreType.DMA
    vmem, anywhere = pl.BlockSpec(memory_space=pltpu.VMEM), pl.BlockSpec(memory_space=pl.ANY)
    smem = pl.BlockSpec(memory_space=pltpu.SMEM)
    tall = jax.ShapeDtypeStruct((rows, D), bf16)
    both = jax.ShapeDtypeStruct((2 * rows // BLOCK, BLOCK, D), bf16)
    items = 2 * (rows // 256)
    return pl.pallas_call(
        partial(start_kernel, n_tensor),
        out_shape=[
            jax.ShapeDtypeStruct((4, D, D), bf16),
            jax.ShapeDtypeStruct((2, D, FF), bf16),
            jax.ShapeDtypeStruct((1, FF), f32),
            tall,
            tall,
            both,
            both,
            tall,
            jax.ShapeDtypeStruct((rows // BLOCK, 8, ROWS), f32),
        ],
        in_specs=[vmem] * 5 + [smem, anywhere],
        out_specs=[anywhere, anywhere, vmem] + [anywhere] * 5 + [vmem],
        scratch_shapes=[
            pltpu.VMEM((STRIP, D), bf16),
            pltpu.VMEM((n_tensor, STRIP, D), bf16),
            pltpu.VMEM((8, D), f32),
            pltpu.VMEM((n_tensor, 8, D), f32),
            pltpu.VMEM((8, D), f32),
            pltpu.VMEM((2, STRIP, own_ff), bf16),
            pltpu.VMEM((4, D, D), bf16),
            pltpu.VMEM((rows, D), bf16),
            pltpu.VMEM((rows, D), bf16),
            pltpu.VMEM((rows, D), bf16),
            pltpu.VMEM((2 * rows // BLOCK, BLOCK, D), bf16),
            pltpu.VMEM((2 * rows // BLOCK, BLOCK, D), bf16),
            pltpu.VMEM((2 * rows // KEYS, ROWS, KEYS), f32),
            dma((2 * n_tensor,)),
            dma((2 * n_tensor,)),
            dma((n_tensor,)),
            dma((n_tensor,)),
            dma((2 * n_tensor,)),
            dma((2 * n_tensor,)),
            dma((2,)),
            dma((2,)),
            dma((6,)),
            dma((6,)),
            dma((8,)),
            dma((8,)),
            dma((6,)),
            dma((6,)),
            dma((8,)),
            dma((8,)),
            dma((items,)),
            dma((items,)),
            dma((8,)),
        ],
        compiler_params=pltpu.CompilerParams(
            collective_id=2, has_side_effects=True, vmem_limit_bytes=VMEM_LIMIT
        ),
        cost_estimate=pl.CostEstimate(
            flops=6 * rows * D * D, bytes_accessed=100 * 2**20, transcendentals=0
        ),
        name="start",
    )(attn_w, ffn_w, qv_bias, hid_bias.reshape(1, own_ff), table, rand, tokens)


def middle_kernel(n_tensor, *refs):
    x_ref, mixed_ref, hid_ref, vec_ref, cotangent, attn_full, ffn_full = refs[:7]
    out_a, out_b, dw1, dw2, dwo, gh1, gm, hid_out, sums_out = refs[7:16]
    w, wo, act, slope, h1, total, gs_low, low_t, turned, pre, dw_s, cot, ready, low, down, held = refs[16:32]
    (
        w_sem,
        c_send,
        c_recv,
        h_send,
        h_recv,
        z_send,
        z_recv,
        z_passed,
        dw_sem,
        own_sem,
        copied,
    ) = refs[32:]
    s, c, t, x, core, sibling, over_x, over_y, across, along_z = places(n_tensor)
    n_rows = x_ref.shape[0]
    chunk = 256
    chunks = n_rows // chunk
    steps = FF // D
    items, all_items = LINE_ITEMS, n_rows // ITEM

    def block(i):
        return pl.ds(pl.multiple_of(i * D, D), D)

    fetch_o = pltpu.make_async_copy(attn_full.at[3], wo, w_sem.at[2 * steps])
    fetch_o.start()

    def fetch(m, i):
        at = w.at[m, :, block(i)]
        return pltpu.make_async_copy(ffn_full.at[m, :, block(i)], at, w_sem.at[m * steps + i])

    for i in range(steps):
        for m in range(2):
            fetch(m, i).start()

    greet([over_y, across] + along_z)

    def keep_cot(i):
        at = pl.ds(i * chunk, chunk)
        return pltpu.make_async_copy(cotangent.at[t, at], cot.at[at], c_recv.at[i])

    def swap_cot(i):
        at = pl.ds(i * chunk, chunk)
        return remote(cotangent.at[t, at], cot.at[at], c_send.at[i], c_recv.at[i], across)

    def home_ref(i):
        if i < items:
            return held.at[t, pl.ds(i * ITEM, ITEM)]
        return out_b.at[pl.ds((i - items) * ITEM, ITEM)]

    def keep_home(i):
        return pltpu.make_async_copy(ready.at[pl.ds(i * ITEM, ITEM)], home_ref(i), h_recv.at[i])

    def send_home(i):
        src = ready.at[pl.ds(i * ITEM, ITEM)]
        return remote(src, home_ref(i), h_send.at[i], h_recv.at[i], across)

    def if_home(at_home, away):
        @pl.when(core == c)
        def _():
            at_home()

        @pl.when(core != c)
        def _():
            away()

    if_home(lambda: keep_cot(0).start(), lambda: swap_cot(0).start())

    chain = Relay(s, c, t, items, ITEM, held, out_a, z_send, z_recv, z_passed, copied)

    def own_ready(i):
        if_home(lambda: keep_home(i).wait(), lambda: send_home(i).wait_recv())

    events = {
        (1, 2): ([0], []),
        (2, 2): ([1], []),
        (2, 3): ([2], []),
        (3, 2): ([], [0]),
        (3, 3): ([3], []),
    }
    sizes = [ITEM] + [chunk] * (chunks - 1) + [chunk - ITEM]
    start_row = 0
    for i, size in enumerate(sizes):
        rows = slice(start_row, start_row + size)
        top = slice(0, size)
        if i == 0:
            fetch_o.wait()
        pre1 = x_ref[rows, :].astype(f32) + matmul_nt(mixed_ref[rows, :], wo[...])
        pre1 = pre1 + vec_ref[4:5, :]
        h1[rows, :] = pre1
        unit, _scale = norm_parts(pre1)
        first = unit * vec_ref[0:1, :] + vec_ref[1:2, :]
        low[top, :] = first.astype(bf16)
        down[top, :] = first + vec_ref[5:6, :]

        @pl.loop(0, steps)
        def _(j):
            if i == 0:
                fetch(0, j).wait()
                fetch(1, j).wait()
            for (at_chunk, at_step), (own, passing) in events.items():
                if at_chunk != i:
                    continue

                @pl.when(j == at_step)
                def _():
                    for n in own:
                        own_ready(n)
                        chain.send_own(n)
                    for n in passing:
                        chain.relay(n)

            hidden = matmul(low[top, :], w[0, :, block(j)]) + hid_ref[:, block(j)]
            act_now, slope_now = gelu_and_slope(hidden)
            act_now = act_now.astype(bf16)
            act[rows, block(j)] = act_now
            slope[rows, block(j)] = slope_now.astype(bf16)
            down[top, :] += matmul_nt(act_now, w[1, :, block(j)])

        second = down[top, :]
        total[rows, :] = second
        unit, _scale = norm_parts(second)
        ready[rows, :] = (unit * vec_ref[2:3, :] + vec_ref[3:4, :]).astype(bf16)
        for n in range(start_row // ITEM, (start_row + size) // ITEM):
            if_home(lambda: keep_home(n).start(), lambda: send_home(n).start())
        if i + 1 < chunks:
            if_home(lambda: keep_cot(i + 1).start(), lambda: swap_cot(i + 1).start())
        start_row += size

    sums_out[...] = jnp.zeros_like(sums_out)

    @pl.loop(0, chunks)
    def _(i):
        rows = pl.ds(pl.multiple_of(i * chunk, chunk), chunk)
        if_home(lambda: keep_cot(i).wait(), lambda: swap_cot(i).wait())
        unit, scale = norm_parts(total[rows, :])
        grad_out = cot[rows, :].astype(f32)
        grad = norm_back(grad_out, unit, scale, vec_ref[2:3, :])
        sums_out[2:3, :] += column_total(grad_out * unit)
        sums_out[3:4, :] += column_total(grad_out)
        total[rows, :] = grad
        grad_low = grad.astype(bf16)
        gs_low[rows, :] = grad_low
        sums_out[5:6, :] += column_total(grad_low)
        turned[:, rows] = grad.T.astype(bf16)
        unit, _scale = norm_parts(h1[rows, :])
        first = unit * vec_ref[0:1, :] + vec_ref[1:2, :]
        low_t[:, rows] = first.T.astype(bf16)

    part = D // 4

    def dw_copy(slot, m, j):
        return pltpu.make_async_copy(
            dw_s.at[slot, m], (dw1, dw2)[m].at[:, block(j)], dw_sem.at[2 * slot + m]
        )

    passing_on = {(0, 1): 1, (2, 0): 2, (3, 1): 3}

    def pass_on(j, when):
        for (at, place), n in passing_on.items():
            if place == when:

                @pl.when(j == at)
                def _():
                    chain.relay(n)

    @pl.loop(0, steps)
    def _(j):
        slot = lax.rem(j, 2)
        pass_on(j, 0)
        for i in range(chunks):
            rows = slice(i * chunk, (i + 1) * chunk)
            grad_act = matmul(gs_low[rows, :], w[1, :, block(j)]).astype(bf16).astype(f32)
            grad_pre = (grad_act * slope[rows, block(j)].astype(f32)).astype(bf16)
            pre[rows, :] = grad_pre
            total[rows, :] += matmul_nt(grad_pre, w[0, :, block(j)])
        pass_on(j, 1)
        hid_out[:, block(j)] = column_total(pre[...])

        @pl.when(j >= 2)
        def _():
            for m in range(2):
                dw_copy(slot, m, j - 2).wait()

        for n in range(4):
            out = slice(n * part, (n + 1) * part)
            dw_s[slot, 0, out, :] = matmul(low_t[out, :], pre[...]).astype(bf16)
            dw_s[slot, 1, out, :] = matmul(turned[out, :], act[:, block(j)]).astype(bf16)
        for m in range(2):
            dw_copy(slot, m, j).start()

    gm_s = gs_low

    @pl.loop(0, chunks)
    def _(i):
        rows = pl.ds(pl.multiple_of(i * chunk, chunk), chunk)
        unit, scale = norm_parts(h1[rows, :])
        grad_first = total[rows, :]
        grad_h1 = norm_back(grad_first, unit, scale, vec_ref[0:1, :])
        total[rows, :] = grad_h1
        grad_low = grad_h1.astype(bf16)
        gm_s[rows, :] = matmul(grad_low, wo[...]).astype(bf16)
        turned[:, rows] = grad_h1.T.astype(bf16)
        sums_out[0:1, :] += column_total(grad_first * unit)
        sums_out[1:2, :] += column_total(grad_first)
        sums_out[4:5, :] += column_total(grad_low)

    local = [
        pltpu.make_async_copy(total, gh1, own_sem.at[0]),
        pltpu.make_async_copy(gm_s, gm, own_sem.at[1]),
    ]
    for copy in local:
        copy.start()
    for j in range(steps - 2, steps):
        for m in range(2):
            dw_copy(j % 2, m, j).wait()

    @pl.loop(0, 4)
    def _(n):
        out = pl.ds(pl.multiple_of(n * part, part), part)
        dw_s[0, 0, out, :] = matmul(turned[out, :], mixed_ref[...]).astype(bf16)

    local.append(pltpu.make_async_copy(dw_s.at[0, 0], dwo, own_sem.at[2]))
    local[-1].start()
    for i in range(items, all_items):
        own_ready(i)
    for i in range(all_items):

        @pl.when(core != c)
        def _():
            send_home(i).wait_send()

    chain.settle()
    for copy in local:
        copy.wait()


def middle(n_tensor, x, mixed, hid_all, vec_par, cotangent, attn_full, ffn_full):
    rows = x.shape[0]
    steps = FF // D
    items, all_items = LINE_ITEMS, rows // ITEM
    dma = pltpu.SemaphoreType.DMA
    vmem, anywhere = pl.BlockSpec(memory_space=pltpu.VMEM), pl.BlockSpec(memory_space=pl.ANY)
    low, wide = pltpu.VMEM((rows, D), bf16), pltpu.VMEM((rows, D), f32)
    return pl.pallas_call(
        partial(middle_kernel, n_tensor),
        out_shape=[
            jax.ShapeDtypeStruct((n_tensor, items * ITEM, D), bf16),
            jax.ShapeDtypeStruct((rows - items * ITEM, D), bf16),
            jax.ShapeDtypeStruct((D, FF), bf16),
            jax.ShapeDtypeStruct((D, FF), bf16),
            jax.ShapeDtypeStruct((D, D), bf16),
            jax.ShapeDtypeStruct((rows, D), f32),
            jax.ShapeDtypeStruct((rows, D), bf16),
            jax.ShapeDtypeStruct((1, FF), f32),
            jax.ShapeDtypeStruct((8, D), f32),
        ],
        in_specs=[vmem] * 4 + [anywhere] * 3,
        out_specs=[anywhere] * 7 + [vmem] * 2,
        scratch_shapes=[
            pltpu.VMEM((2, D, FF), bf16),
            pltpu.VMEM((D, D), bf16),
            pltpu.VMEM((rows, FF), bf16),
            pltpu.VMEM((rows, FF), bf16),
            wide,
            wide,
            low,
            pltpu.VMEM((D, rows), bf16),
            pltpu.VMEM((D, rows), bf16),
            low,
            pltpu.VMEM((2, 2, D, D), bf16),
            low,
            low,
            pltpu.VMEM((256, D), bf16),
            pltpu.VMEM((256, D), f32),
            pltpu.VMEM((n_tensor, items * ITEM, D), bf16),
            dma((2 * steps + 1,)),
            dma((rows // 256,)),
            dma((rows // 256,)),
            dma((all_items,)),
            dma((all_items,)),
            dma((items * n_tensor,)),
            dma((items * n_tensor,)),
            dma((items,)),
            dma((4,)),
            dma((3,)),
            dma((n_tensor,)),
        ],
        compiler_params=pltpu.CompilerParams(
            collective_id=3, has_side_effects=True, vmem_limit_bytes=VMEM_LIMIT
        ),
        cost_estimate=pl.CostEstimate(
            flops=2 * rows * D * (3 * D + 6 * FF),
            bytes_accessed=60 * 2**20,
            transcendentals=2 * rows * FF,
        ),
        name="middle",
    )(x, mixed, hid_all, vec_par, cotangent, attn_full, ffn_full)


def finish_kernel(n_tensor, *refs):
    dq, dk_own, dk_far, dv_own, dv_far, gh1, x_ref, weights = refs[:8]
    dw1, dw2, dwo, vec_sums, hid_sums = refs[8:13]
    attn_out, ffn_out, vec_out, qv_out, hid_out, tokens_out = refs[13:19]
    (
        dk,
        dv,
        xs,
        held,
        x_t,
        partial_sum,
        ready,
        dws,
        acc,
        got0,
        got1a,
        got1b,
        got2,
        zf,
        zf_got,
        za,
        za_got,
        run,
        run_got,
        run_z,
        wts,
    ) = refs[19:40]
    (
        e_send,
        e_recv,
        own_sem,
        s0,
        r0,
        s1,
        r1,
        s2,
        r2,
        zf_send,
        zf_recv,
        za_send,
        za_recv,
        sm,
        rm,
        h_send,
        h_recv,
        up_send,
        up_recv,
        dn_send,
        dn_recv,
        w_sem,
        copied,
    ) = refs[40:]
    s, c, t, x, core, sibling, over_x, over_y, across, along_z = places(n_tensor)
    n_rows = dq.shape[0]
    rows_each = n_rows // PIECES
    last = n_tensor - 1

    def pieces(path, i):
        if i < 2:
            return [(dw1 if path == 0 else dw2, i * WIDE, WIDE, 0)]
        if path == 0:
            return [(dws.at[0], 0, D, 0), (dws.at[1], 0, D, D)]
        return [(dws.at[2], 0, D, 0), (dwo, 0, D, D)]

    def slot(path, i):
        return path * 3 + i

    order = [(path, i) for i in range(3) for path in range(2)]

    def rows_of(xx, cc):
        return pl.ds(pl.multiple_of((4 * xx + 2 * cc) * STRIP, 2 * STRIP), 2 * STRIP)

    own, first = {}, {}
    for path, i in order:
        k = slot(path, i)
        own[k], first[k] = [], []
        for xx in range(2):
            for j, (ref, col, width, at) in enumerate(pieces(path, i)):
                n = (k * 2 + xx) * 2 + j
                cols, to = pl.ds(col, width), pl.ds(at, width)
                own[k].append(
                    pltpu.make_async_copy(
                        ref.at[rows_of(xx, core), cols], acc.at[k, xx, :, to], own_sem.at[n]
                    )
                )
                first[k].append(
                    remote(
                        ref.at[rows_of(xx, 1 - core), cols],
                        got0.at[k, xx, :, to],
                        s0.at[n],
                        r0.at[n],
                        sibling,
                    )
                )

    def start_own(i):
        for path in range(2):
            for copy in own[slot(path, i)]:
                copy.start()

    def start_first(i):
        for path in range(2):
            for copy in first[slot(path, i)]:
                copy.start()

    fetches = [
        pltpu.make_async_copy(gh1, partial_sum, w_sem.at[1]),
        pltpu.make_async_copy(weights.at[pl.ds(0, 3)], wts, w_sem.at[0]),
        pltpu.make_async_copy(x_ref, xs, w_sem.at[2]),
    ]
    for copy in fetches:
        copy.start()
    start_own(0)
    start_own(1)
    greet([sibling, over_x, over_y, across] + along_z)

    chunk = 256
    chunks = n_rows // chunk

    def exchange(i, n):
        at = pl.ds(i * chunk, chunk)
        src, dst = ((dk_far, dk), (dv_far, dv))[n]
        k = 2 * i + n
        return remote(src.at[at], dst.at[at], e_send.at[k], e_recv.at[k], sibling)

    swaps = [exchange(i, n) for i in range(chunks) for n in range(2)]
    for copy in swaps:
        copy.start()
    start_first(0)
    fetches[0].wait()
    fetches[1].wait()

    run[0] = jnp.zeros(run.shape[1:], f32)
    run[0, 0:6, :] = vec_sums[0:6, :]
    for n in range(FF // D):
        run[0, 8 + n : 9 + n, :] = hid_sums[:, n * D : (n + 1) * D]

    def keep_home(i):
        at = pl.ds(i * rows_each, rows_each)
        return pltpu.make_async_copy(ready.at[at], held.at[t, at], h_recv.at[i])

    def send_home(i):
        at = pl.ds(i * rows_each, rows_each)
        return remote(ready.at[at], held.at[t, at], h_send.at[i], h_recv.at[i], across)

    chain = Line(
        s,
        c,
        t,
        last,
        PIECES,
        rows_each,
        held,
        tokens_out,
        (up_send, up_recv),
        (dn_send, dn_recv),
        copied,
    )
    tick = chain.tick

    def send_own(i):
        @pl.when(core == c)
        def _():
            keep_home(i).wait()

        @pl.when(core != c)
        def _():
            send_home(i).wait_recv()

        chain.send_own(i)

    for i in range(PIECES):
        at = slice(i * rows_each, (i + 1) * rows_each)
        if i * rows_each % chunk == 0:
            for n in range(2):
                exchange(i * rows_each // chunk, n).wait_recv()
        dk_piece = (dk_own[at, :].astype(f32) + dk[at, :].astype(f32)).astype(bf16)
        dv_piece = (dv_own[at, :].astype(f32) + dv[at, :].astype(f32)).astype(bf16)
        dk[at, :] = dk_piece
        dv[at, :] = dv_piece
        total = partial_sum[at, :] + matmul_nt(dq[at, :], wts[0])
        total = total + matmul_nt(dk_piece, wts[1]) + matmul_nt(dv_piece, wts[2])
        ready[at, :] = total.astype(bf16)

        @pl.when(core == c)
        def _():
            keep_home(i).start()

        @pl.when(core != c)
        def _():
            send_home(i).start()

        if i > 0:
            send_own(i - 1)

    def add_rows(target, source, count):
        @pl.loop(0, count // 16)
        def _(j):
            rows = pl.ds(pl.multiple_of(j * 16, 16), 16)
            total = target[rows, :].astype(f32) + source[rows, :].astype(f32)
            target[rows, :] = total.astype(bf16)

    def half(cc):
        return pl.ds(pl.multiple_of(cc * STRIP, STRIP), STRIP)

    second, third = {}, {}

    def stage1(path, i):
        k = slot(path, i)
        for copy in own[k]:
            copy.wait()
        for copy in first[k]:
            copy.wait_recv()
        for xx in range(2):
            add_rows(acc.at[k, xx], got0.at[k, xx], 2 * STRIP)
        if path == 0:
            second[k] = remote(acc.at[k, 1 - x], got1a.at[i], s1.at[k], r1.at[k], over_x)
        else:
            second[k] = remote(
                acc.at[k, :, half(1 - c), :], got1b.at[i], s1.at[k], r1.at[k], over_y
            )
        second[k].start()

    def stage2(path, i):
        k = slot(path, i)
        second[k].wait_recv()
        if path == 0:
            add_rows(acc.at[k, x], got1a.at[i], 2 * STRIP)
            third[k] = remote(
                acc.at[k, x, half(1 - c), :], got2.at[k], s2.at[k], r2.at[k], over_y
            )
        else:
            for xx in range(2):
                add_rows(acc.at[k, xx, half(c), :], got1b.at[i, xx], STRIP)
            third[k] = remote(
                acc.at[k, 1 - x, half(c), :], got2.at[k], s2.at[k], r2.at[k], over_x
            )
        third[k].start()

    own_cols = D // n_tensor
    own_ff = FF // n_tensor
    per = WIDE // own_ff

    def stage3(path, i):
        k = slot(path, i)
        third[k].wait_recv()

        @pl.loop(0, STRIP // 16)
        def _(j):
            rows = pl.ds(pl.multiple_of(j * 16, 16), 16)
            here = pl.ds(pl.multiple_of(c * STRIP + j * 16, 16), 16)
            total = acc[k, x, here, :].astype(f32) + got2[k, rows, :].astype(f32)
            if i < 2:
                for n in range(per):
                    piece = total[:, n * own_ff : (n + 1) * own_ff].astype(bf16)
                    zf[per * i + n, rows, path * own_ff : (path + 1) * own_ff] = piece
            else:
                for n in range(n_tensor):
                    for m in range(2):
                        at = m * D + n * own_cols
                        to = (2 * path + m) * own_cols
                        piece = total[:, at : at + own_cols].astype(bf16)
                        za[n, rows, to : to + own_cols] = piece

    z_sent = []

    def z_step(k, buf, got, send, recv):
        @pl.when(t == k)
        def _():
            for d in range(last, k, -1):
                if k > 0:
                    hop(buf, got, send, recv, d, 0, k - 1).wait_recv()
                    add_rows(buf.at[d], got.at[0, d], STRIP)
                hop(buf, got, send, recv, d, 0, k + 1).start()

        @pl.when(t == last - k)
        def _():
            for d in range(0, last - k):
                if k > 0:
                    hop(buf, got, send, recv, d, 1, last - k + 1).wait_recv()
                    add_rows(buf.at[d], got.at[1, d], STRIP)
                hop(buf, got, send, recv, d, 1, last - k - 1).start()

    def hop(buf, got, send, recv, d, way, to):
        n = way * n_tensor + d
        return remote(buf.at[d], got.at[way, d], send.at[n], recv.at[n], (s, c, to))

    def z_collect(buf, got, send, recv, emit):
        @pl.when(t > 0)
        def _():
            hop(buf, got, send, recv, t, 0, t - 1).wait_recv()
            add_rows(buf.at[t], got.at[0, t], STRIP)

        @pl.when(t < last)
        def _():
            hop(buf, got, send, recv, t, 1, t + 1).wait_recv()
            add_rows(buf.at[t], got.at[1, t], STRIP)

        @pl.loop(0, STRIP // 16)
        def _(j):
            rows = pl.ds(pl.multiple_of(j * 16, 16), 16)
            emit(rows, buf[t, rows, :].astype(f32))

    def z_settle(buf, got, send, recv):
        for d in range(n_tensor):

            @pl.when(t < d)
            def _():
                hop(buf, got, send, recv, d, 0, t + 1).wait_send()

            @pl.when(t > d)
            def _():
                hop(buf, got, send, recv, d, 1, t - 1).wait_send()

    ffn_z = (zf, zf_got, zf_send, zf_recv)
    attn_z = (za, za_got, za_send, za_recv)

    small = []

    def small_send(n, where):
        small.append(remote(run.at[n], run_got.at[n], sm.at[n], rm.at[n], where))
        small[n].start()

    def small_add(n):
        small[n].wait_recv()
        run[n + 1] = run[n] + run_got[n]

    start_first(1)
    fetches[2].wait()
    for i in range(chunks):
        at = slice(i * chunk, (i + 1) * chunk)
        x_t[:, at] = xs[at, :].T
    dws[0] = matmul(x_t[...], dq[...]).astype(bf16)
    send_own(7)
    dws[1] = matmul(x_t[...], dk[...]).astype(bf16)
    dws[2] = matmul(x_t[...], dv[...]).astype(bf16)
    start_own(2)
    start_first(2)
    run[0, 6:7, :] = column_total(dq[...])
    run[0, 7:8, :] = column_total(dv[...])
    small_send(0, sibling)
    stage1(0, 0)
    stage1(1, 0)
    stage1(0, 1)
    stage1(1, 1)
    tick(0)
    stage1(0, 2)
    stage1(1, 2)
    small_add(0)
    small_send(1, over_x)
    tick(1)
    tick(2)
    tick(3)
    stage2(0, 0)
    stage2(1, 0)
    tick(4)
    tick(5)
    small_add(1)
    small_send(2, over_y)
    tick(6)
    stage2(0, 1)
    stage2(1, 1)
    tick(7)
    tick(8)
    small_add(2)
    run_z[t] = run[3]
    for k, where in enumerate(along_z):
        copy = remote(run.at[3], run_z.at[t], sm.at[3 + k], rm.at[3 + t], where)
        copy.start()
        z_sent.append(copy)
    stage3(0, 0)
    stage3(1, 0)
    stage2(0, 2)
    stage2(1, 2)
    tick(9)
    tick(10)
    stage3(0, 1)
    stage3(1, 1)
    z_step(0, *ffn_z)
    tick(11)
    tick(12)
    z_step(1, *ffn_z)
    stage3(0, 2)
    stage3(1, 2)
    z_step(0, *attn_z)
    tick(13)
    tick(14)
    z_step(2, *ffn_z)
    z_step(1, *attn_z)
    tick(15)
    tick(16)
    z_step(2, *attn_z)
    for j in range(17, PIECES * last):
        tick(j)

    for k, where in enumerate(along_z):
        u = where[2]
        remote(run.at[3], run_z.at[u], sm.at[3 + k], rm.at[3 + u], where).wait_recv()
    total = run_z[0]
    for n in range(1, n_tensor):
        total = total + run_z[n]
    vec_out[...] = total[0:6, :]
    for n in range(n_tensor):

        @pl.when(t == n)
        def _():
            qv_out[...] = total[6:8, n * own_cols : (n + 1) * own_cols]
            hid_out[...] = total[8 + n : 9 + n, :]


    def emit_ffn(rows, total):
        for m in range(2):
            ffn_out[m, rows, :] = total[:, m * own_ff : (m + 1) * own_ff]

    def emit_attn(rows, total):
        for m in range(4):
            attn_out[m, rows, :] = total[:, m * own_cols : (m + 1) * own_cols]

    z_collect(*ffn_z, emit_ffn)
    z_collect(*attn_z, emit_attn)
    z_settle(*ffn_z)
    z_settle(*attn_z)

    for copy in swaps:
        copy.wait_send()
    for path, i in order:
        k = slot(path, i)
        for copy in first[k]:
            copy.wait_send()
        second[k].wait_send()
        third[k].wait_send()
    for copy in small + z_sent:
        copy.wait_send()

    @pl.when(core != c)
    def _():
        for i in range(PIECES):
            send_home(i).wait_send()

    chain.settle()


def finish_all(n_tensor, grads, gh1, x, attn_full, dws, sums):
    rows = x.shape[0]
    own_cols, own_ff = D // n_tensor, FF // n_tensor
    dma = pltpu.SemaphoreType.DMA
    vmem, anywhere = pl.BlockSpec(memory_space=pltpu.VMEM), pl.BlockSpec(memory_space=pl.ANY)
    dq, dk_own, dk_far, dv_own, dv_far = grads
    tall = pltpu.VMEM((rows, D), bf16)
    items = PIECES * (n_tensor - 1)
    return pl.pallas_call(
        partial(finish_kernel, n_tensor),
        out_shape=[
            jax.ShapeDtypeStruct((4, STRIP, own_cols), f32),
            jax.ShapeDtypeStruct((2, STRIP, own_ff), f32),
            jax.ShapeDtypeStruct((6, D), f32),
            jax.ShapeDtypeStruct((2, own_cols), f32),
            jax.ShapeDtypeStruct((1, own_ff), f32),
            jax.ShapeDtypeStruct((n_tensor, rows, D), bf16),
        ],
        in_specs=[vmem, vmem, anywhere, vmem, anywhere] + [anywhere] * 6
        + [vmem] * 2,
        out_specs=[vmem] * 5 + [anywhere],
        scratch_shapes=[
            tall,
            tall,
            tall,
            pltpu.VMEM((n_tensor, rows, D), bf16),
            pltpu.VMEM((D, rows), bf16),
            pltpu.VMEM((rows, D), f32),
            tall,
            pltpu.VMEM((3, D, D), bf16),
            pltpu.VMEM((6, 2, 2 * STRIP, WIDE), bf16),
            pltpu.VMEM((6, 2, 2 * STRIP, WIDE), bf16),
            pltpu.VMEM((3, 2 * STRIP, WIDE), bf16),
            pltpu.VMEM((3, 2, STRIP, WIDE), bf16),
            pltpu.VMEM((6, STRIP, WIDE), bf16),
            pltpu.VMEM((n_tensor, STRIP, 2 * own_ff), bf16),
            pltpu.VMEM((2, n_tensor, STRIP, 2 * own_ff), bf16),
            pltpu.VMEM((n_tensor, STRIP, 4 * own_cols), bf16),
            pltpu.VMEM((2, n_tensor, STRIP, 4 * own_cols), bf16),
            pltpu.VMEM((4, 16, D), f32),
            pltpu.VMEM((3, 16, D), f32),
            pltpu.VMEM((n_tensor, 16, D), f32),
            pltpu.VMEM((3, D, D), bf16),
            dma((2 * rows // 256,)),
            dma((2 * rows // 256,)),
            dma((24,)),
            dma((24,)),
            dma((24,)),
            dma((6,)),
            dma((6,)),
            dma((6,)),
            dma((6,)),
            dma((2 * n_tensor,)),
            dma((2 * n_tensor,)),
            dma((2 * n_tensor,)),
            dma((2 * n_tensor,)),
            dma((3 + n_tensor,)),
            dma((3 + n_tensor,)),
            dma((PIECES,)),
            dma((PIECES,)),
            dma((items + PIECES,)),
            dma((items + PIECES,)),
            dma((items + PIECES,)),
            dma((items + PIECES,)),
            dma((3,)),
            dma((2 * n_tensor - 1,)),
        ],
        compiler_params=pltpu.CompilerParams(
            collective_id=1, has_side_effects=True, vmem_limit_bytes=VMEM_LIMIT
        ),
        cost_estimate=pl.CostEstimate(
            flops=12 * rows * D * D, bytes_accessed=400 * 2**20, transcendentals=0
        ),
        name="finish",
    )(dq, dk_own, dk_far, dv_own, dv_far, gh1, x, attn_full, *dws, *sums)


GROUP_RATES = (
    [2.0 / D**0.5] * 3 + [2.0 / (D // (4 * BLOCK)) ** 0.5],
    [2.0 / D**0.5, 2.0 / FF**0.5],
)


def last_kernel(tokens_ref, out_b, _output_a, *refs):
    attn_g, attn_w, attn_m, attn_v, ffn_g, ffn_w, ffn_m, ffn_v = refs[:8]
    plain = [refs[8 + 4 * n : 12 + 4 * n] for n in range(3)]
    tokens_out, output = refs[20:22]
    attn_moment, attn_square, out_states, attn_new, attn_copy = refs[22:27]
    ffn_moment, ffn_square, ffn_new, ffn_copy = refs[27:31]
    plain_out = [refs[31 + 3 * n : 34 + 3 * n] for n in range(3)]
    step = pl.program_id(0)

    @pl.when(step == 0)
    def _():
        for m in range(4):
            moment, square, new = adam_update(
                attn_w[m], attn_m[m], attn_v[m], attn_g[m], GROUP_RATES[0][m], decay_rate
            )
            if m < 3:
                attn_moment[m], attn_square[m] = moment, square
            else:
                out_states[0], out_states[1] = moment, square
            attn_new[m], attn_copy[m] = new, new.astype(bf16)
        for m in range(2):
            moment, square, new = adam_update(
                ffn_w[m], ffn_m[m], ffn_v[m], ffn_g[m], GROUP_RATES[1][m], decay_rate
            )
            ffn_moment[m], ffn_square[m] = moment, square
            ffn_new[m], ffn_copy[m] = new, new.astype(bf16)
        for (g, w, m, v), outs in zip(plain, plain_out):
            gradient = g[...] if len(g.shape) == len(w.shape) else g[0, :]
            for ref, value in zip(outs, adam_update(w[...], m[...], v[...], gradient, 0.5, 0.0)):
                ref[...] = value

    tokens_out[...] = tokens_ref[...].astype(f32)

    output[...] = out_b[...]


def last(tokens_low, output, out_b, attn, ffn, plain):
    count, rows, _ = tokens_low.shape
    tile = lambda size, index: pl.BlockSpec((1, size, D), index)
    whole = lambda shape: pl.BlockSpec(
        shape, lambda i: (0,) * len(shape), pipeline_mode=pl.Buffered(1)
    )
    a, f = attn[0].shape, ffn[0].shape
    shapes = [
        ((3,) + a[1:], f32),
        ((3,) + a[1:], f32),
        ((2,) + a[1:], f32),
        (a, f32),
        (a, bf16),
        (f, f32),
        (f, f32),
        (f, f32),
        (f, bf16),
    ]
    for group in plain:
        shapes += [(group[1].shape, f32)] * 3
    inputs = list(attn) + list(ffn) + [array for group in plain for array in group]
    by_half = lambda i: (i // 2, i % 2, 0)
    by_one = lambda i: (i // 2, i % 2, 0)
    second = lambda i: (i // 2, 2 + i % 2, 0)
    quarter = rows // 4
    return pl.pallas_call(
        last_kernel,
        out_shape=[
            jax.ShapeDtypeStruct(tokens_low.shape, f32),
            jax.ShapeDtypeStruct(tokens_low.shape, bf16),
        ]
        + [jax.ShapeDtypeStruct(*entry) for entry in shapes],
        grid=(count * 2,),
        in_specs=[
            tile(rows // 2, by_half),
            tile(quarter, by_one),
            pl.BlockSpec(memory_space=pl.ANY),
        ]
        + [whole(array.shape) for array in inputs],
        out_specs=[tile(rows // 2, by_half), tile(quarter, second)]
        + [whole(shape) for shape, _ in shapes],
        input_output_aliases={2: 1},
        compiler_params=pltpu.CompilerParams(vmem_limit_bytes=VMEM_LIMIT),
        name="last",
    )(tokens_low, out_b, output, *inputs)


def make_body(mesh):
    n_shard, n_ctx, n_tensor = mesh.shape["shard"], mesh.shape["ctx"], mesh.shape["tensor"]
    rows_axes = ("shard", "ctx")
    all_axes = ("shard", "ctx", "tensor")
    paired = n_ctx == 2 and n_shard == 4 and n_tensor == 4

    def swapped(s, c):
        return (s - s % 2 + c, s % 2)

    def swap(array):
        if not paired:
            return array
        pairs = []
        for s in range(n_shard):
            for c in range(n_ctx):
                s_to, c_to = swapped(s, c)
                pairs.append((s * n_ctx + c, s_to * n_ctx + c_to))
        return lax.ppermute(array, rows_axes, pairs)

    def spread(array):
        return lax.all_gather(swap(array), "tensor", axis=0, tiled=True)

    def body(
        tokens,
        cotangent,
        segments,
        rand_blocks,
        attn_w,
        attn_m,
        attn_v,
        ffn_w,
        ffn_m,
        ffn_v,
        qv_bias,
        qv_m,
        qv_v,
        hid_bias,
        hid_m,
        hid_v,
        vec_par,
        vec_m,
        vec_v,
    ):
        t_index = lax.axis_index("tensor")
        nseq = tokens.shape[0] // n_tensor
        piece_len = tokens.shape[1]
        nb = piece_len // BLOCK
        own_rows, own_cols = attn_w.shape[1], attn_w.shape[2]
        own_ff = ffn_w.shape[2]

        def mine(array):
            return lax.dynamic_slice_in_dim(array, t_index * nseq, nseq, 0)

        ints = jnp.concatenate(
            [mine(segments), mine(rand_blocks).reshape(nseq, -1)], axis=1
        )
        ints = swap(ints)
        length = segments.shape[1]
        segs, rand = ints[:, :length], ints[:, length:].reshape(nseq, length // BLOCK, -1)
        piece = lax.axis_index("shard") % 2 if paired else lax.axis_index("ctx")
        tables = attention_tables(segs, rand, piece, nb, paired)

        if paired:
            rand_own, _meta, table = tables
            attn_full, ffn_full, hid_all, x, queries, keys, values, mixed, lse = start(
                n_tensor, attn_w, ffn_w, qv_bias, hid_bias, table[0], rand_own, tokens
            )
            flat = x
            x, queries = x[None], queries[None]
            keys, values = keys.reshape(1, length, D), values.reshape(1, length, D)
            pieces = [piece_len, piece_len]
        else:
            x, cot = mine(tokens), mine(cotangent)
            pieces = [length]
            ffn_z = lax.all_gather(ffn_w.astype(bf16), "tensor", axis=0, tiled=False)
            ffn_z = ffn_z.transpose(1, 2, 0, 3).reshape(2, own_rows, FF)
            ffn_full = lax.all_gather(ffn_z, rows_axes, axis=1, tiled=True)
            flat = x.reshape(-1, D)
            attn_low = attn_w.astype(bf16)
            attn_low = jnp.concatenate([attn_low[i] for i in range(4)], axis=1)
            attn_z = lax.all_gather(attn_low, "tensor", axis=0, tiled=False)
            attn_z = attn_z.reshape(n_tensor, own_rows, 4, own_cols).transpose(2, 1, 0, 3)
            attn_full = lax.all_gather(
                attn_z.reshape(4, own_rows, D), rows_axes, axis=1, tiled=True
            )
            bias_own = jnp.concatenate([qv_bias.reshape(-1), hid_bias])
            bias_all = lax.all_gather(bias_own, "tensor", axis=0, tiled=False)
            qv_all = bias_all[:, : 2 * own_cols].reshape(n_tensor, 2, own_cols)
            qv_all = qv_all.transpose(1, 0, 2).reshape(2, D)
            hid_all = bias_all[:, 2 * own_cols :].reshape(FF)
            keys = matmul(flat, attn_full[1]).astype(bf16).reshape(x.shape)
            values = (matmul(flat, attn_full[2]) + qv_all[1]).astype(bf16).reshape(x.shape)
            keys = lax.all_gather(keys, "ctx", axis=1, tiled=True)
            values = lax.all_gather(values, "ctx", axis=1, tiled=True)
            queries = (matmul(flat, attn_full[0]) + qv_all[0]).astype(bf16) * 0.125
            queries = queries.reshape(x.shape)
            mixed, lse = attend(tables, queries, keys, values)
        mixed_low = mixed.reshape(-1, D)
        if paired:
            out_a, out_b, dw1, dw2, dwo, grad_first_in, grad_mixed, hid_sum, vec_sums = middle(
                n_tensor, flat, mixed_low, hid_all, vec_par, cotangent, attn_full, ffn_full
            )
            out_b = lax.all_gather(out_b, "tensor", axis=0, tiled=False)
        else:
            act, slope, h1, result, grad_second, second_sums = feed_forward(
                flat, mixed_low, cot.reshape(-1, D), attn_full, ffn_full, hid_all, vec_par
            )
            output = spread(result.reshape(x.shape))
            out_a, out_b = output[:, : piece_len // 2], output[:, piece_len // 2 :]
            dw1, dw2, dwo, grad_first_in, grad_mixed, hid_sum, first_sums = feed_back(
                grad_second, h1, mixed_low, attn_full, ffn_full, act, slope, vec_par
            )

        grad_mixed = grad_mixed.reshape(x.shape)
        grad_query, output, dk_parts, dv_parts = attend_back(
            tables,
            queries,
            grad_mixed,
            mixed.reshape(x.shape),
            lse.reshape(nseq, nb, 8, ROWS),
            out_a,
            keys,
            values,
            pieces,
        )

        grad_query_low = grad_query.reshape(-1, D)
        if paired:
            attn_grad, ffn_grad, vec_grad, qv_grad, hid_grad, grad_tokens = finish_all(
                n_tensor,
                [grad_query_low] + [part[0] for part in list(dk_parts) + list(dv_parts)],
                grad_first_in,
                flat,
                attn_full,
                (dw1, dw2, dwo),
                (vec_sums, hid_sum),
            )
        else:
            grad_keys = lax.psum_scatter(dk_parts[0], "ctx", scatter_dimension=1, tiled=True)
            grad_values = lax.psum_scatter(dv_parts[0], "ctx", scatter_dimension=1, tiled=True)
            grad_keys_low = grad_keys.reshape(-1, D)
            grad_values_low = grad_values.reshape(-1, D)
            into_tokens = (
                matmul_nt(grad_query_low, attn_full[0])
                + matmul_nt(grad_keys_low, attn_full[1])
                + matmul_nt(grad_values_low, attn_full[2])
            )
            grad_tokens = spread((grad_first_in + into_tokens).astype(bf16).reshape(x.shape))
            dwq = matmul_tn(flat, grad_query_low).astype(bf16)
            dwk = matmul_tn(flat, grad_keys_low).astype(bf16)
            dwv = matmul_tn(flat, grad_values_low).astype(bf16)
            small = jnp.concatenate(
                [
                    first_sums[0],
                    first_sums[1],
                    second_sums[0],
                    second_sums[1],
                    first_sums[2],
                    second_sums[2],
                    column_sum(grad_query_low),
                    column_sum(grad_values_low),
                    hid_sum[0],
                ]
            )
            ffn_grad = lax.psum_scatter(
                jnp.stack([dw1, dw2]), rows_axes, scatter_dimension=1, tiled=True
            )
            ffn_grad = ffn_grad.reshape(2, own_rows, n_tensor, own_ff).transpose(2, 0, 1, 3)
            ffn_grad = lax.psum_scatter(ffn_grad, "tensor", scatter_dimension=0, tiled=False)
            ffn_grad = ffn_grad.astype(f32)
            attn_grad = lax.psum_scatter(
                jnp.stack([dwq, dwk, dwv, dwo]), rows_axes, scatter_dimension=1, tiled=True
            )
            attn_grad = attn_grad.reshape(4, own_rows, n_tensor, own_cols).transpose(2, 1, 0, 3)
            attn_grad = lax.psum_scatter(
                attn_grad.reshape(n_tensor, own_rows, D), "tensor", scatter_dimension=0
            )
            attn_grad = attn_grad.reshape(own_rows, 4, own_cols).transpose(1, 0, 2).astype(f32)
            small = lax.psum(small, all_axes)
            vec_grad = small[: 6 * D].reshape(6, D)
            qv_grad = lax.dynamic_slice_in_dim(
                small[6 * D : 8 * D].reshape(2, D), t_index * own_cols, own_cols, 1
            )
            hid_grad = lax.dynamic_slice_in_dim(
                small[8 * D : 8 * D + FF], t_index * own_ff, own_ff, 0
            )

        grad_tokens, output, *updated = last(
            grad_tokens,
            output,
            out_b,
            (attn_grad, attn_w, attn_m, attn_v),
            (ffn_grad, ffn_w, ffn_m, ffn_v),
            [
                (qv_grad, qv_bias, qv_m, qv_v),
                (hid_grad.reshape(1, own_ff), hid_bias, hid_m, hid_v),
                (vec_grad, vec_par, vec_m, vec_v),
            ],
        )
        return (output, grad_tokens, *updated)

    return body


def solution(mesh):
    rows = P("shard", "ctx", None)
    weight = P(None, ("shard", "ctx"), "tensor")
    in_specs = (
        (rows, rows, P("shard", None), P("shard", None, None))
        + (weight,) * 6
        + (P(None, "tensor"),) * 3
        + (P("tensor"),) * 3
        + (P(),) * 3
    )
    out_specs = (
        (rows, rows)
        + (weight,) * 9
        + (P(None, "tensor"),) * 3
        + (P("tensor"),) * 3
        + (P(),) * 3
    )
    return jax.shard_map(
        make_body(mesh), mesh=mesh, in_specs=in_specs, out_specs=out_specs, check_vma=False
    )
```

```python
from functools import partial

import jax
import jax.numpy as jnp
from jax import lax
from jax.experimental import pallas as pl
from jax.experimental.pallas import tpu as pltpu
from jax.sharding import PartitionSpec as P

D = 768
HEAD_DIM = 64
FF = 3072
BLOCK = 64
STEP = 5
GROUP = 4 * HEAD_DIM
GROUPS = D // GROUP
ROWS = 4 * BLOCK
LISTED = 8
KEYS = LISTED * BLOCK
VMEM_LIMIT = 60 * 2**20

beta_first = 0.9
beta_second = 0.999
adam_eps = 1e-08
decay_rate = 0.01
norm_eps = 1e-06
neg_large = -1e30

f32 = jnp.float32
bf16 = jnp.bfloat16


def matmul(left, right):
    return jnp.dot(left, right, preferred_element_type=f32)


def matmul_tn(left, right):
    return lax.dot_general(left, right, (((0,), (0,)), ((), ())), preferred_element_type=f32)


def matmul_nt(left, right):
    return lax.dot_general(left, right, (((1,), (1,)), ((), ())), preferred_element_type=f32)


def column_sum(array_in):
    return jnp.sum(array_in.astype(f32), axis=0)


def adam_update(weight, moment, square, gradient, step_rates, decay_on):
    moment_new = beta_first * moment + (1.0 - beta_first) * gradient
    square_new = beta_second * square + (1.0 - beta_second) * gradient * gradient
    step_ratio = (
        moment_new
        / (1.0 - beta_first**STEP)
        / (jnp.sqrt(square_new / (1.0 - beta_second**STEP)) + adam_eps)
    )
    weight_new = weight - step_rates * (step_ratio + decay_on * weight)
    return (moment_new, square_new, weight_new)


def same_head():
    row_head = lax.broadcasted_iota(jnp.int32, (ROWS, GROUP), 0) // BLOCK
    col_head = lax.broadcasted_iota(jnp.int32, (ROWS, GROUP), 1) // HEAD_DIM
    return row_head == col_head


def spread_heads(block, keep):
    stacked = jnp.concatenate([block] * 4, axis=0)
    return jnp.where(keep, stacked, jnp.zeros_like(stacked))


def fold_heads(full, keep):
    kept = jnp.where(keep, full, 0.0)
    return sum(kept[h * BLOCK : (h + 1) * BLOCK] for h in range(4))


def load_keys(k_all, v_all, seq, k_buf, v_buf, sems):
    return [
        pltpu.make_async_copy(k_all.at[seq], k_buf, sems.at[0]),
        pltpu.make_async_copy(v_all.at[seq], v_buf, sems.at[1]),
    ]


def picked_rows(buf, spots, cols):
    return jnp.concatenate([buf[at, :, cols] for at in spots], axis=0)


def chunk_rows(buf, i, cols):
    blocks = buf[pl.ds(i * LISTED, LISTED), :, cols]
    return blocks.reshape(KEYS, GROUP)


def listed_blocks(rand, base, blk, first, own, total):
    one = lambda condition: condition.astype(jnp.int32)
    me = first + blk
    ids = [me - 1, me, me + 1, me * 0, me * 0 + 1] + [rand[base + n] for n in range(LISTED - 5)]
    spots, unused, common = [], [], []
    for n, block in enumerate(ids):
        out = one(block < 0) + one(block >= total)
        for earlier in ids[:n]:
            out = out + one(block == earlier)
        out = lax.min(out, jnp.int32(1))
        at = lax.max(jnp.int32(0), lax.min(block, jnp.int32(total - 1))) - first + own
        spots.append(at + total * one(at < 0))
        unused.append(out)
        common.append(one(block < 2) * (1 - out))
    return spots, unused, common


def code_rows(tab_ref, spots, unused, common):
    low_half = lax.broadcasted_iota(jnp.int32, (1, 2 * BLOCK), 1) < BLOCK

    def one(n):
        plain = (1 - unused[n] - common[n]).astype(f32)
        return tab_ref[spots[n]] * plain - (unused[n] + 2 * common[n]).astype(f32)

    return [jnp.where(low_half, one(n), one(n + 1)) for n in range(0, LISTED, 2)]


def column_of(row):
    return jnp.broadcast_to(row, (2 * BLOCK, 2 * BLOCK)).T


def mask_bias(document, code):
    return jnp.where((document == code) | (code == -2.0), 0.0, neg_large)


def row_of(column):
    return jnp.broadcast_to(column, (ROWS, 2 * BLOCK)).T[0:1, :]


def forward_block(q_ref, out_ref, lse_ref, k_buf, v_buf, s_buf, tab_ref, rand, base, blk, first, own):
    keep = same_head()
    total_blocks = k_buf.shape[0]
    chunks = total_blocks // LISTED
    is_global = first + blk < 2

    @pl.when(jnp.logical_not(is_global))
    def _():
        spots, unused, common = listed_blocks(rand, base, blk, first, own, total_blocks)
        mine = column_of(tab_ref[own + blk])[:BLOCK]
        mine = jnp.concatenate([mine] * 4, axis=0)
        codes = code_rows(tab_ref, spots, unused, common)
        bias = jnp.concatenate([mask_bias(mine, code) for code in codes], axis=1)
        for g in range(GROUPS):
            cols = slice(g * GROUP, (g + 1) * GROUP)
            q_full = spread_heads(q_ref[:, cols], keep)
            scores = matmul_nt(q_full, picked_rows(k_buf, spots, cols)) + bias
            largest = jnp.max(scores, axis=-1, keepdims=True)
            weights = jnp.exp(scores - largest)
            total = jnp.sum(weights, axis=-1, keepdims=True)
            full = matmul(weights.astype(bf16), picked_rows(v_buf, spots, cols))
            out_ref[:, cols] = fold_heads(full * (1.0 / total), keep).astype(bf16)
            lse_ref[g : g + 1, :] = row_of(largest + jnp.log(total))

    @pl.when(is_global)
    def _():
        for g in range(GROUPS):
            cols = slice(g * GROUP, (g + 1) * GROUP)
            q_full = spread_heads(q_ref[:, cols], keep)

            def score_chunk(i, largest):
                scores = matmul_nt(q_full, chunk_rows(k_buf, i, cols))
                s_buf[i] = scores
                return jnp.maximum(largest, jnp.max(scores, axis=-1, keepdims=True))

            largest = lax.fori_loop(0, chunks, score_chunk, jnp.full((ROWS, 1), neg_large, f32))

            def mix_chunk(i, carry):
                total, full = carry
                weights = jnp.exp(s_buf[i] - largest)
                total = total + jnp.sum(weights, axis=-1, keepdims=True)
                return total, full + matmul(weights.astype(bf16), chunk_rows(v_buf, i, cols))

            total, full = lax.fori_loop(
                0, chunks, mix_chunk, (jnp.zeros((ROWS, 1), f32), jnp.zeros((ROWS, GROUP), f32))
            )
            out_ref[:, cols] = fold_heads(full * (1.0 / total), keep).astype(bf16)
            lse_ref[g : g + 1, :] = row_of(largest + jnp.log(total))


def forward_kernel(
    rand, meta, q_ref, tab_ref, k_all, v_all, out_ref, lse_ref, k_buf, v_buf, s_buf, sems
):
    seq, blk = pl.program_id(0), pl.program_id(1)
    nb = pl.num_programs(1)

    @pl.when(blk == 0)
    def _():
        copies = load_keys(k_all, v_all, seq, k_buf, v_buf, sems)
        for c in copies:
            c.start()
        for c in copies:
            c.wait()

    base = (seq * nb + blk) * (LISTED - 5)
    forward_block(
        q_ref, out_ref, lse_ref, k_buf, v_buf, s_buf, tab_ref, rand, base, blk, meta[0], meta[1]
    )


def back_tile(k_rows, v_rows, q_full, go_full, bias, lse, centre):
    scores = matmul_nt(k_rows, q_full)
    if bias is not None:
        scores = scores + bias
    probs = jnp.exp(scores - lse)
    grad_probs = matmul_nt(v_rows, go_full)
    grad_scores = (probs * (grad_probs - centre)).astype(bf16)
    dv_rows = matmul(probs.astype(bf16), go_full)
    dk_rows = matmul(grad_scores, q_full)
    return matmul_tn(grad_scores, k_rows), dk_rows, dv_rows


def backward_kernel(
    n_out, rand, meta, q_ref, go_ref, mixed_ref, lse_ref, tab_ref, out_a, k_all, v_all, *rest
):
    dq_ref, out_ref, *rest = rest
    dk_refs, dv_refs = rest[:n_out], rest[n_out : 2 * n_out]
    k_buf, v_buf, dk_acc, dv_acc, sems = rest[2 * n_out :]
    seq, blk = pl.program_id(0), pl.program_id(1)
    nb = pl.num_programs(1)
    total_blocks = k_buf.shape[0]
    chunks = total_blocks // LISTED

    out_ref[...] = out_a[...]

    @pl.when(blk == 0)
    def _():
        copies = load_keys(k_all, v_all, seq, k_buf, v_buf, sems)
        for c in copies:
            c.start()
        dk_acc[...] = jnp.zeros_like(dk_acc)
        dv_acc[...] = jnp.zeros_like(dv_acc)
        for c in copies:
            c.wait()

    keep = same_head()
    is_global = meta[0] + blk < 2
    base = (seq * nb + blk) * (LISTED - 5)

    def operands(g):
        cols = slice(g * GROUP, (g + 1) * GROUP)
        q_full = spread_heads(q_ref[:, cols], keep)
        go_full = spread_heads(go_ref[:, cols], keep)
        mixed = jnp.concatenate([mixed_ref[:, cols]] * 4, axis=0)
        product = go_full.astype(f32) * mixed.astype(f32)
        centre = row_of(jnp.sum(product, axis=-1, keepdims=True))
        return cols, q_full, go_full, lse_ref[g : g + 1, :], centre

    @pl.when(jnp.logical_not(is_global))
    def _():
        spots, unused, common = listed_blocks(rand, base, blk, meta[0], meta[1], total_blocks)
        stores = [at + (total_blocks - at) * out for at, out in zip(spots, unused)]
        own = tab_ref[meta[1] + blk]
        codes = code_rows(tab_ref, spots, unused, common)
        bias = jnp.concatenate([mask_bias(own, column_of(code)) for code in codes], axis=0)
        bias = jnp.concatenate([bias, bias], axis=1)
        for g in range(GROUPS):
            cols, q_full, go_full, lse, centre = operands(g)
            k_rows, v_rows = picked_rows(k_buf, spots, cols), picked_rows(v_buf, spots, cols)
            dq_full, dk_rows, dv_rows = back_tile(
                k_rows, v_rows, q_full, go_full, bias, lse, centre
            )
            dq_ref[:, cols] = (fold_heads(dq_full, keep) * 0.125).astype(bf16)
            places = [pl.ds(pl.multiple_of(at * BLOCK, BLOCK), BLOCK) for at in stores]
            dk_old = [dk_acc[at, cols] for at in places]
            dv_old = [dv_acc[at, cols] for at in places]
            for n, at in enumerate(places):
                own_rows = slice(n * BLOCK, (n + 1) * BLOCK)
                dk_acc[at, cols] = dk_old[n] + dk_rows[own_rows]
                dv_acc[at, cols] = dv_old[n] + dv_rows[own_rows]

    @pl.when(is_global)
    def _():
        for g in range(GROUPS):
            cols, q_full, go_full, lse, centre = operands(g)

            def chunk_back(i, dq_full):
                rows = pl.ds(pl.multiple_of(i * KEYS, KEYS), KEYS)
                dq_now, dk_rows, dv_rows = back_tile(
                    chunk_rows(k_buf, i, cols),
                    chunk_rows(v_buf, i, cols),
                    q_full,
                    go_full,
                    None,
                    lse,
                    centre,
                )
                dk_acc[rows, cols] += dk_rows
                dv_acc[rows, cols] += dv_rows
                return dq_full + dq_now

            dq_full = lax.fori_loop(0, chunks, chunk_back, jnp.zeros((ROWS, GROUP), f32))
            dq_ref[:, cols] = (fold_heads(dq_full, keep) * 0.125).astype(bf16)

    @pl.when(blk == nb - 1)
    def _():
        row = 0
        for dk_ref, dv_ref in zip(dk_refs, dv_refs):
            rows = dk_ref.shape[0]
            dk_ref[...] = dk_acc[row : row + rows].astype(bf16)
            dv_ref[...] = dv_acc[row : row + rows].astype(bf16)
            row += rows


def attention_tables(segments, random, piece, nb, own_first):
    seq_count, length = segments.shape
    total = length // BLOCK
    first = piece * nb
    rand = lax.dynamic_slice_in_dim(random, first, nb, 1).reshape(-1)
    table = segments.reshape(seq_count, total, BLOCK).astype(f32)
    table = jnp.concatenate([table, table], axis=2)[:, :, None, :]
    if own_first:
        table = lax.dynamic_slice_in_dim(jnp.concatenate([table, table], axis=1), first, total, 1)
    meta = jnp.stack([first, jnp.zeros_like(first) if own_first else first]).astype(jnp.int32)
    return rand, meta, table


def as_blocks(rows):
    return rows.reshape(rows.shape[0], -1, BLOCK, D)


def attend(tables, q, keys, values):
    rand, meta, table = tables
    seq_count, piece_len, _ = q.shape
    nb = piece_len // BLOCK
    length = keys.shape[1]
    any_spec = pl.BlockSpec(memory_space=pl.ANY)
    row_spec = pl.BlockSpec((None, BLOCK, D), lambda s, b, *_: (s, b, 0))
    return pl.pallas_call(
        forward_kernel,
        out_shape=[
            jax.ShapeDtypeStruct(q.shape, bf16),
            jax.ShapeDtypeStruct((seq_count, nb, 8, ROWS), f32),
        ],
        grid_spec=pltpu.PrefetchScalarGridSpec(
            num_scalar_prefetch=2,
            grid=(seq_count, nb),
            in_specs=[
                row_spec,
                pl.BlockSpec((None,) + table.shape[1:], lambda s, b, *_: (s, 0, 0, 0)),
                any_spec,
                any_spec,
            ],
            out_specs=[
                row_spec,
                pl.BlockSpec((None, None, 8, ROWS), lambda s, b, *_: (s, b, 0, 0)),
            ],
            scratch_shapes=[
                pltpu.VMEM((length // BLOCK, BLOCK, D), bf16),
                pltpu.VMEM((length // BLOCK, BLOCK, D), bf16),
                pltpu.VMEM((length // KEYS, ROWS, KEYS), f32),
                pltpu.SemaphoreType.DMA((2,)),
            ],
        ),
        compiler_params=pltpu.CompilerParams(vmem_limit_bytes=VMEM_LIMIT),
        name="attend",
    )(rand, meta, q, table, as_blocks(keys), as_blocks(values))


def attend_back(tables, q, grad_mixed, mixed, lse, out_a, keys, values, pieces):
    rand, meta, table = tables
    seq_count, piece_len, _ = q.shape
    nb = piece_len // BLOCK
    length = keys.shape[1]
    any_spec = pl.BlockSpec(memory_space=pl.ANY)
    row_spec = pl.BlockSpec((None, BLOCK, D), lambda s, b, *_: (s, b, 0))
    count, half, _ = out_a.shape
    share = count * half // (seq_count * nb)
    if share <= half:
        per = half // share
        tile = pl.BlockSpec(
            (None, share, D), lambda s, b, *_: ((s * nb + b) // per, (s * nb + b) % per, 0)
        )
    else:
        tile = pl.BlockSpec((share // half, half, D), lambda s, b, *_: (s * nb + b, 0, 0))
    part_specs = [pl.BlockSpec((None, rows, D), lambda s, b, *_: (s, 0, 0)) for rows in pieces]
    part_shapes = [jax.ShapeDtypeStruct((seq_count, rows, D), bf16) for rows in pieces]
    out = pl.pallas_call(
        partial(backward_kernel, len(pieces)),
        out_shape=[
            jax.ShapeDtypeStruct(q.shape, bf16),
            jax.ShapeDtypeStruct((count, 2 * half, D), bf16),
        ]
        + part_shapes * 2,
        grid_spec=pltpu.PrefetchScalarGridSpec(
            num_scalar_prefetch=2,
            grid=(seq_count, nb),
            in_specs=[
                row_spec,
                row_spec,
                row_spec,
                pl.BlockSpec((None, None, 8, ROWS), lambda s, b, *_: (s, b, 0, 0)),
                pl.BlockSpec((None,) + table.shape[1:], lambda s, b, *_: (s, 0, 0, 0)),
                tile,
                any_spec,
                any_spec,
            ],
            out_specs=[row_spec, tile] + part_specs * 2,
            scratch_shapes=[
                pltpu.VMEM((length // BLOCK, BLOCK, D), bf16),
                pltpu.VMEM((length // BLOCK, BLOCK, D), bf16),
                pltpu.VMEM((length + BLOCK, D), f32),
                pltpu.VMEM((length + BLOCK, D), f32),
                pltpu.SemaphoreType.DMA((2,)),
            ],
        ),
        compiler_params=pltpu.CompilerParams(vmem_limit_bytes=VMEM_LIMIT),
        cost_estimate=pl.CostEstimate(
            flops=seq_count * nb * GROUPS * 10 * ROWS * KEYS * GROUP,
            bytes_accessed=seq_count * (3 * piece_len + 4 * length) * D * 2,
            transcendentals=seq_count * nb * GROUPS * ROWS * KEYS,
        ),
        name="attend_back",
    )(rand, meta, q, grad_mixed, mixed, lse, table, out_a, as_blocks(keys), as_blocks(values))
    return out[0], out[1], out[2 : 2 + len(pieces)], out[2 + len(pieces) :]


def norm_parts(hidden):
    centred = hidden - jnp.mean(hidden, axis=-1, keepdims=True)
    scale = lax.rsqrt(jnp.mean(centred * centred, axis=-1, keepdims=True) + norm_eps)
    return centred * scale, scale


def norm_back(grad, unit, scale, gain):
    inner = grad * gain
    return scale * (
        inner
        - jnp.mean(inner, axis=-1, keepdims=True)
        - unit * jnp.mean(inner * unit, axis=-1, keepdims=True)
    )


def gelu_and_slope(pre):
    bell = jnp.exp(-0.5 * pre * pre)
    t = 1.0 / (1.0 + (0.3275911 * 0.5**0.5) * jnp.abs(pre))
    poly = 0.5 * 1.061405429
    for coefficient in (-1.453152027, 1.421413741, -0.284496736, 0.254829592):
        poly = poly * t + 0.5 * coefficient
    tail = poly * t * bell
    phi = jnp.where(pre >= 0.0, 1.0 - tail, tail)
    return pre * phi, phi + pre * bell * 0.3989422804014327


def column_total(array):
    return jnp.sum(array.astype(f32), axis=0, keepdims=True)


def up_kernel(
    chunk,
    x_ref,
    mixed_ref,
    cot_ref,
    wo_ref,
    w1_ref,
    w2_ref,
    hid_ref,
    vec_ref,
    act_ref,
    slope_ref,
    h1_ref,
    res_ref,
    gs_ref,
    sums_ref,
    low,
    down,
):
    step = pl.program_id(0)
    chunks = x_ref.shape[0] // chunk

    @pl.when(step == 0)
    def _():
        @pl.loop(0, chunks)
        def _(i):
            rows = pl.ds(pl.multiple_of(i * chunk, chunk), chunk)
            h1 = x_ref[rows, :].astype(f32) + matmul_nt(mixed_ref[rows, :], wo_ref[...])
            h1 = h1 + vec_ref[4:5, :]
            h1_ref[rows, :] = h1
            unit, _scale = norm_parts(h1)
            low[rows, :] = (unit * vec_ref[0:1, :] + vec_ref[1:2, :]).astype(bf16)
            down[rows, :] = jnp.zeros((chunk, D), f32)

    for i in range(chunks):
        rows = slice(i * chunk, (i + 1) * chunk)
        pre = matmul(low[rows, :], w1_ref[...]) + hid_ref[...]
        act, slope = gelu_and_slope(pre)
        act = act.astype(bf16)
        act_ref[rows, :] = act
        slope_ref[rows, :] = slope.astype(bf16)
        down[rows, :] += matmul_nt(act, w2_ref[...])

    @pl.when(step == pl.num_programs(0) - 1)
    def _():
        sums_ref[...] = jnp.zeros_like(sums_ref)

        @pl.loop(0, chunks)
        def _(i):
            rows = pl.ds(pl.multiple_of(i * chunk, chunk), chunk)
            unit, _scale = norm_parts(h1_ref[rows, :])
            first = unit * vec_ref[0:1, :] + vec_ref[1:2, :]
            unit, scale = norm_parts(first + down[rows, :] + vec_ref[5:6, :])
            res_ref[rows, :] = (unit * vec_ref[2:3, :] + vec_ref[3:4, :]).astype(bf16)
            cot = cot_ref[rows, :].astype(f32)
            grad = norm_back(cot, unit, scale, vec_ref[2:3, :])
            gs_ref[rows, :] = grad
            sums_ref[0:1, :] += column_total(cot * unit)
            sums_ref[1:2, :] += column_total(cot)
            sums_ref[2:3, :] += column_total(grad.astype(bf16))


def feed_forward(x, mixed, cot, attn_full, ffn_full, hid_all, vec_par):
    rows = x.shape[0]
    chunk = min(256, rows)
    steps = FF // D
    whole = lambda shape: pl.BlockSpec(shape, lambda t: (0,) * len(shape))
    once = lambda shape: pl.BlockSpec(
        shape, lambda t: (0,) * len(shape), pipeline_mode=pl.Buffered(1)
    )
    hidden = pl.BlockSpec((rows, D), lambda t: (0, t))
    return pl.pallas_call(
        partial(up_kernel, chunk),
        out_shape=[
            jax.ShapeDtypeStruct((rows, FF), bf16),
            jax.ShapeDtypeStruct((rows, FF), bf16),
            jax.ShapeDtypeStruct((rows, D), f32),
            jax.ShapeDtypeStruct((rows, D), bf16),
            jax.ShapeDtypeStruct((rows, D), f32),
            jax.ShapeDtypeStruct((8, D), f32),
        ],
        grid=(steps,),
        in_specs=[
            once((rows, D)),
            once((rows, D)),
            once((rows, D)),
            pl.BlockSpec((None, D, D), lambda t: (3, 0, 0), pipeline_mode=pl.Buffered(1)),
            pl.BlockSpec((None, D, D), lambda t: (0, 0, t)),
            pl.BlockSpec((None, D, D), lambda t: (1, 0, t)),
            pl.BlockSpec((1, D), lambda t: (0, t)),
            whole((6, D)),
        ],
        out_specs=[
            hidden,
            hidden,
            whole((rows, D)),
            whole((rows, D)),
            whole((rows, D)),
            whole((8, D)),
        ],
        scratch_shapes=[pltpu.VMEM((rows, D), bf16), pltpu.VMEM((rows, D), f32)],
        compiler_params=pltpu.CompilerParams(vmem_limit_bytes=VMEM_LIMIT),
        cost_estimate=pl.CostEstimate(
            flops=2 * rows * D * (D + 2 * FF),
            bytes_accessed=rows * D * 30 + 2 * D * FF * 2,
            transcendentals=2 * rows * FF,
        ),
        name="feed_forward",
    )(x, mixed, cot, attn_full, ffn_full, ffn_full, hid_all.reshape(1, FF), vec_par)


def down_kernel(
    chunk,
    gs_ref,
    h1_ref,
    mixed_ref,
    wo_ref,
    w1_ref,
    w2_ref,
    act_ref,
    slope_ref,
    vec_ref,
    dw1_ref,
    dw2_ref,
    dwo_ref,
    gh1_ref,
    gm_ref,
    hid_ref,
    sums_ref,
    turned,
    low_t,
    pre,
    total,
):
    step = pl.program_id(0)
    n_rows = gs_ref.shape[0]
    chunks = n_rows // chunk

    @pl.when(step == 0)
    def _():
        @pl.loop(0, chunks)
        def _(i):
            rows = pl.ds(pl.multiple_of(i * chunk, chunk), chunk)
            unit, _scale = norm_parts(h1_ref[rows, :])
            low = unit * vec_ref[0:1, :] + vec_ref[1:2, :]
            low_t[:, rows] = low.T.astype(bf16)
            turned[:, rows] = gs_ref[rows, :].T.astype(bf16)
            total[rows, :] = gs_ref[rows, :]

    for i in range(chunks):
        rows = slice(i * chunk, (i + 1) * chunk)
        grad_act = matmul(gs_ref[rows, :].astype(bf16), w2_ref[...]).astype(bf16).astype(f32)
        grad_pre = (grad_act * slope_ref[rows, :].astype(f32)).astype(bf16)
        pre[rows, :] = grad_pre
        total[rows, :] += matmul_nt(grad_pre, w1_ref[...])
    hid_ref[...] = column_total(pre[...])
    part = D // 4
    for j in range(4):
        out = slice(j * part, (j + 1) * part)
        dw1_ref[out, :] = matmul(low_t[out, :], pre[...]).astype(bf16)
        dw2_ref[out, :] = matmul(turned[out, :], act_ref[...]).astype(bf16)

    @pl.when(step == pl.num_programs(0) - 1)
    def _():
        sums_ref[...] = jnp.zeros_like(sums_ref)

        @pl.loop(0, chunks)
        def _(i):
            rows = pl.ds(pl.multiple_of(i * chunk, chunk), chunk)
            unit, scale = norm_parts(h1_ref[rows, :])
            grad_first = total[rows, :]
            grad_h1 = norm_back(grad_first, unit, scale, vec_ref[0:1, :])
            gh1_ref[rows, :] = grad_h1
            low = grad_h1.astype(bf16)
            gm_ref[rows, :] = matmul(low, wo_ref[...]).astype(bf16)
            turned[:, rows] = grad_h1.T.astype(bf16)
            sums_ref[0:1, :] += column_total(grad_first * unit)
            sums_ref[1:2, :] += column_total(grad_first)
            sums_ref[2:3, :] += column_total(low)

        @pl.loop(0, 4)
        def _(j):
            out = pl.ds(pl.multiple_of(j * part, part), part)
            dwo_ref[out, :] = matmul(turned[out, :], mixed_ref[...]).astype(bf16)


def feed_back(gs, h1, mixed, attn_full, ffn_full, act, slope, vec_par):
    rows = gs.shape[0]
    chunk = min(256, rows)
    steps = FF // D
    whole = lambda shape: pl.BlockSpec(shape, lambda t: (0,) * len(shape))
    once = lambda shape: pl.BlockSpec(
        shape, lambda t: (0,) * len(shape), pipeline_mode=pl.Buffered(1)
    )
    hidden = pl.BlockSpec((rows, D), lambda t: (0, t))
    slab = pl.BlockSpec((D, D), lambda t: (0, t))
    return pl.pallas_call(
        partial(down_kernel, chunk),
        out_shape=[
            jax.ShapeDtypeStruct((D, FF), bf16),
            jax.ShapeDtypeStruct((D, FF), bf16),
            jax.ShapeDtypeStruct((D, D), bf16),
            jax.ShapeDtypeStruct((rows, D), f32),
            jax.ShapeDtypeStruct((rows, D), bf16),
            jax.ShapeDtypeStruct((1, FF), f32),
            jax.ShapeDtypeStruct((8, D), f32),
        ],
        grid=(steps,),
        in_specs=[
            once((rows, D)),
            once((rows, D)),
            once((rows, D)),
            pl.BlockSpec((None, D, D), lambda t: (3, 0, 0), pipeline_mode=pl.Buffered(1)),
            pl.BlockSpec((None, D, D), lambda t: (0, 0, t)),
            pl.BlockSpec((None, D, D), lambda t: (1, 0, t)),
            hidden,
            hidden,
            whole((6, D)),
        ],
        out_specs=[
            slab,
            slab,
            whole((D, D)),
            whole((rows, D)),
            whole((rows, D)),
            pl.BlockSpec((1, D), lambda t: (0, t)),
            whole((8, D)),
        ],
        scratch_shapes=[
            pltpu.VMEM((D, rows), bf16),
            pltpu.VMEM((D, rows), bf16),
            pltpu.VMEM((rows, D), bf16),
            pltpu.VMEM((rows, D), f32),
        ],
        compiler_params=pltpu.CompilerParams(vmem_limit_bytes=VMEM_LIMIT),
        cost_estimate=pl.CostEstimate(
            flops=2 * rows * D * (2 * D + 4 * FF),
            bytes_accessed=rows * D * 30 + 4 * D * FF * 2,
            transcendentals=0,
        ),
        name="feed_back",
    )(gs, h1, mixed, attn_full, ffn_full, ffn_full, act, slope, vec_par)


WIDE = 1536
STRIP = 96
PIECES = 8
ITEM = 128
LINE_ITEMS = 4
MESH = pl.DeviceIdType.MESH


def remote(src, dst, send, recv, where):
    return pltpu.make_async_remote_copy(
        src_ref=src,
        dst_ref=dst,
        send_sem=send,
        recv_sem=recv,
        device_id=where,
        device_id_type=MESH,
    )


def greet(partners):
    barrier = pltpu.get_barrier_semaphore()
    for where in partners:
        pl.semaphore_signal(barrier, inc=1, device_id=where, device_id_type=MESH)
    pl.semaphore_wait(barrier, len(partners))


def places(n_tensor):
    s, c, t = lax.axis_index("shard"), lax.axis_index("ctx"), lax.axis_index("tensor")
    x, core = s // 2, s % 2
    sibling = (x * 2 + 1 - core, c, t)
    over_x = ((1 - x) * 2 + core, c, t)
    over_y = (s, 1 - c, t)
    across = (x * 2 + 1 - core, 1 - c, t)
    along_z = [(s, c, lax.rem(t + k, n_tensor)) for k in range(1, n_tensor)]
    return s, c, t, x, core, sibling, over_x, over_y, across, along_z


class Line:
    def __init__(self, s, c, t, last, items, rows, array, out, up, down, copied):
        self.s, self.c, self.t, self.last, self.items = s, c, t, last, items
        self.rows, self.array, self.out, self.up, self.down = rows, array, out, up, down
        self.copied = copied

    def hop(self, i, src_t, sems, n, to):
        ref = self.array.at[src_t, pl.ds(i * self.rows, self.rows)]
        return remote(ref, ref, sems[0].at[n], sems[1].at[n], (self.s, self.c, to))

    def keep(self, src_t, n):
        return pltpu.make_async_copy(self.array.at[src_t], self.out.at[src_t], self.copied.at[n])

    def send_own(self, i):
        t = self.t

        @pl.when(t < self.last)
        def _():
            self.hop(i, t, self.up, i, t + 1).start()

        @pl.when(t > 0)
        def _():
            self.hop(i, t, self.down, i, t - 1).start()

        if i == self.items - 1:
            self.keep(t, 2 * self.last).start()

    def tick(self, j):
        t, last = self.t, self.last
        i, hops, n = j % self.items, j // self.items + 1, j + self.items

        @pl.when(t >= hops)
        def _():
            self.hop(i, t - hops, self.up, j, t - 1).wait_recv()

            @pl.when(t < last)
            def _():
                self.hop(i, t - hops, self.up, n, t + 1).start()

            if i == self.items - 1:
                self.keep(t - hops, hops - 1).start()

        @pl.when(t + hops <= last)
        def _():
            self.hop(i, t + hops, self.down, j, t + 1).wait_recv()

            @pl.when(t > 0)
            def _():
                self.hop(i, t + hops, self.down, n, t - 1).start()

            if i == self.items - 1:
                self.keep(t + hops, last + hops - 1).start()

    def settle(self):
        t, last = self.t, self.last
        for j in range(self.items * last):
            i, hops = j % self.items, j // self.items

            @pl.when((t < last) & (t >= hops))
            def _():
                self.hop(i, t - hops, self.up, j, t + 1).wait_send()

            @pl.when((t > 0) & (t + hops <= last))
            def _():
                self.hop(i, t + hops, self.down, j, t - 1).wait_send()

        self.keep(t, 2 * last).wait()
        for hops in range(1, last + 1):

            @pl.when(t >= hops)
            def _():
                self.keep(t - hops, hops - 1).wait()

            @pl.when(t + hops <= last)
            def _():
                self.keep(t + hops, last + hops - 1).wait()


class Relay:
    def __init__(self, s, c, t, items, rows, array, out, send, recv, passed, copied):
        self.s, self.c, self.t, self.items, self.rows = s, c, t, items, rows
        self.array, self.out, self.send, self.recv = array, out, send, recv
        self.passed, self.copied = passed, copied

    def copy(self, i, source, send, to):
        ref = self.array.at[source, pl.ds(i * self.rows, self.rows)]
        return remote(ref, ref, send, self.recv.at[source * self.items + i], (self.s, self.c, to))

    def keep(self, u):
        return pltpu.make_async_copy(self.array.at[u], self.out.at[u], self.copied.at[u])

    def own(self, i, act):
        t = self.t
        for n, step in enumerate((2, -2, 1, -1)):

            @pl.when((t + step >= 0) & (t + step < 4))
            def _():
                act(self.copy(i, t, self.send.at[4 * i + n], t + step))

    def send_own(self, i):
        self.own(i, lambda copy: copy.start())

    def through(self, i, act):
        for t, source, to in ((2, 0, 3), (1, 3, 0)):

            @pl.when(self.t == t)
            def _():
                act(self.copy(i, source, self.passed.at[i], to))

    def relay(self, i):
        def act(copy):
            copy.wait_recv()
            copy.start()

        self.through(i, act)

    def settle(self):
        t = self.t
        for u, relayed_by in ((1, 1), (2, 2), (0, 2), (3, 1)):

            @pl.when((t != u) & (t != relayed_by))
            def _():
                for i in range(self.items):
                    self.copy(i, u, self.send.at[0], lax.rem(t + 1, 4)).wait_recv()

            self.keep(u).start()
        for i in range(self.items):
            self.own(i, lambda copy: copy.wait_send())
            self.through(i, lambda copy: copy.wait_send())
        for u in range(4):
            self.keep(u).wait()


def start_kernel(n_tensor, *refs):
    attn_ref, ffn_ref, qv_ref, hid_ref, tab_ref, rand, tokens = refs[:7]
    attn_out, ffn_out, hid_out, x_out, q_out, k_out, v_out, mixed_out, lse_out = refs[7:16]
    low, low_z, bias, bias_z, bias_qv, ffn_low, full, xs, qs, ms, k_buf, v_buf, s_buf = refs[16:29]
    (
        z_send,
        z_recv,
        b_send,
        b_recv,
        fz_send,
        fz_recv,
        x_send,
        x_recv,
        g_send,
        g_recv,
        p_send,
        p_recv,
        fg_send,
        fg_recv,
        fp_send,
        fp_recv,
        kv_send,
        kv_recv,
        own_sem,
    ) = refs[29:]
    s, c, t, x, core, sibling, over_x, over_y, across, along_z = places(n_tensor)
    own_cols, own_ff = D // n_tensor, FF // n_tensor
    n_rows = xs.shape[0]

    for m in range(4):
        low[:, m * own_cols : (m + 1) * own_cols] = attn_ref[m].astype(bf16)
    for m in range(2):
        ffn_low[m] = ffn_ref[m].astype(bf16)
    bias[0:2, 0:own_cols] = qv_ref[...]
    bias[2:3, 0:own_ff] = hid_ref[...]

    greet([sibling, over_x, over_y, across] + along_z)

    sent = []

    def put(copy):
        copy.start()
        sent.append(copy)

    half = 2 * own_cols

    def z_hop(path, k, u):
        cols = pl.ds(path * half, half)
        n = path * n_tensor
        return remote(
            low.at[:, cols], low_z.at[u, :, cols], z_send.at[n + k], z_recv.at[n + u], along_z[k]
        )

    for path in range(2):
        for k in range(n_tensor - 1):
            put(z_hop(path, k, t))

    def keep_rows(src, dst, n):
        return pltpu.make_async_copy(src.at[t], dst, x_recv.at[n])

    def swap_rows(src, dst, n):
        return remote(src.at[t], dst, x_send.at[n], x_recv.at[n], across)

    @pl.when(core == c)
    def _():
        keep_rows(tokens, xs, 0).start()

    @pl.when(core != c)
    def _():
        swap_rows(tokens, xs, 0).start()

    low_z[t] = low[...]
    bias_z[t] = bias[...]

    def strip(shard, ctx):
        return pl.ds(pl.multiple_of((2 * shard + ctx) * STRIP, STRIP), STRIP)

    here = strip(s, c)

    def lay_out(path):
        for k, where in enumerate(along_z):
            z_hop(path, k, where[2]).wait_recv()
        for n in range(n_tensor):
            for m in range(2 * path, 2 * path + 2):
                piece = low_z[n, :, m * own_cols : (m + 1) * own_cols]
                full[m, here, n * own_cols : (n + 1) * own_cols] = piece

    far_x, far_y = over_x[0], 1 - c
    labels = ["own", "x", "y", "xy"]
    rows = {
        "own": here,
        "x": strip(far_x, c),
        "y": strip(s, far_y),
        "xy": strip(far_x, far_y),
    }
    far_rows = {
        "own": strip(sibling[0], c),
        "x": strip(2 * (1 - x) + 1 - core, c),
        "y": strip(sibling[0], far_y),
        "xy": strip(2 * (1 - x) + 1 - core, far_y),
    }

    def attn_block(path, at):
        return full.at[pl.ds(2 * path, 2), at, :]

    def ffn_block(path, at):
        return ffn_out.at[path, at, :]

    class Gather:
        def __init__(self, block, ways, gs, gr, ps, pr):
            self.block, self.gs, self.gr, self.ps, self.pr = block, gs, gr, ps, pr
            x_first = (("x", over_x), ("y", over_y))
            self.ways = [x_first if way == 0 else x_first[::-1] for way in ways]

        def hop(self, path, name, label, where):
            n = path * 3 + labels.index(label) - 1
            ref = self.block(path, rows[name])
            return remote(ref, ref, self.gs.at[n], self.gr.at[n], where)

        def give(self, path, name, label, where):
            put(self.hop(path, name, label, where))

        def take(self, path, label):
            self.hop(path, label, label, over_x).wait_recv()

        def share(self, path, name):
            put(self.shared(path, name))

        def take_shared(self, path):
            for n, name in enumerate(labels):
                ref = self.block(path, far_rows[name])
                n = path * 4 + n
                remote(ref, ref, self.ps.at[n], self.pr.at[n], sibling).wait_recv()

        def shared(self, path, name):
            n = path * 4 + labels.index(name)
            ref = self.block(path, rows[name])
            return remote(ref, ref, self.ps.at[n], self.pr.at[n], sibling)

        def again(self, path, number):
            near, far = self.ways[path]
            if number == 1:
                sent.append(self.hop(path, near[0], "xy", far[1]))
            sent.append(self.shared(path, {1: near[0], 2: far[0], 3: "xy"}[number]))

        def step(self, path, number):
            near, far = self.ways[path]
            if number == 0:
                self.give(path, "own", near[0], near[1])
                self.give(path, "own", far[0], far[1])
                self.share(path, "own")
            elif number == 1:
                self.take(path, near[0])
                self.give(path, near[0], "xy", far[1])
                self.share(path, near[0])
            elif number == 2:
                self.take(path, far[0])
                self.share(path, far[0])
            else:
                self.take(path, "xy")
                self.share(path, "xy")

    attn = Gather(attn_block, (1, 1), g_send, g_recv, p_send, p_recv)
    ffn = Gather(ffn_block, (0, 1), fg_send, fg_recv, fp_send, fp_recv)

    def ffn_cols(path, u):
        return ffn_out.at[path, here, pl.ds(pl.multiple_of(u * own_ff, own_ff), own_ff)]

    def ffn_hop(path, k, u):
        n = path * n_tensor
        return remote(
            ffn_low.at[path],
            ffn_cols(path, u),
            fz_send.at[n + k],
            fz_recv.at[n + u],
            along_z[k],
        )

    local = []

    def write(src, dst, n):
        copy = pltpu.make_async_copy(src, dst, own_sem.at[n])
        copy.start()
        local.append(copy)

    def ffn_along_z(path):
        for k in range(n_tensor - 1):
            put(ffn_hop(path, k, t))
        write(ffn_low.at[path], ffn_cols(path, t), 5 + path)

    def ffn_ready(path):
        for k, where in enumerate(along_z):
            ffn_hop(path, k, where[2]).wait_recv()
        local[path].wait()
        ffn.step(path, 0)

    lay_out(0)
    attn.step(0, 0)
    lay_out(1)
    attn.step(1, 0)
    ffn_along_z(0)
    ffn_along_z(1)
    for k, where in enumerate(along_z):
        put(remote(bias, bias_z.at[t], b_send.at[k], b_recv.at[t], where))
    attn.step(0, 1)
    attn.step(1, 1)
    ffn_ready(0)
    attn.step(0, 2)
    attn.step(1, 2)
    attn.step(0, 3)
    attn.step(1, 3)
    for k, where in enumerate(along_z):
        u = where[2]
        remote(bias, bias_z.at[u], b_send.at[k], b_recv.at[u], where).wait_recv()
    for n in range(n_tensor):
        cols = slice(n * own_cols, (n + 1) * own_cols)
        bias_qv[0:2, cols] = bias_z[n, 0:2, 0:own_cols]
        hid_out[:, n * own_ff : (n + 1) * own_ff] = bias_z[n, 2:3, 0:own_ff]

    @pl.when(core == c)
    def _():
        keep_rows(tokens, xs, 0).wait()

    @pl.when(core != c)
    def _():
        swap_rows(tokens, xs, 0).wait()

    chunk = 256
    chunks = n_rows // chunk
    per = chunk // BLOCK

    def kv_hop(buf, i, n):
        at, to = pl.ds(i * per, per), pl.ds(n_rows // BLOCK + i * per, per)
        return remote(buf.at[at], buf.at[to], kv_send.at[n], kv_recv.at[n], sibling)

    attn.take_shared(0)
    for i in range(chunks):
        at = pl.ds(i * chunk, chunk)
        k = matmul(xs[at, :], full[1]).astype(bf16)
        k_buf[pl.ds(i * per, per)] = k.reshape(per, BLOCK, D)
        put(kv_hop(k_buf, i, i))
    ffn_ready(1)
    for i in range(chunks):
        at = pl.ds(i * chunk, chunk)
        q = matmul(xs[at, :], full[0]) + bias_qv[0:1, :]
        qs[at, :] = (q.astype(bf16).astype(f32) * 0.125).astype(bf16)
    attn.take_shared(1)
    for i in range(chunks):
        at = pl.ds(i * chunk, chunk)
        v = (matmul(xs[at, :], full[2]) + bias_qv[1:2, :]).astype(bf16)
        v_buf[pl.ds(i * per, per)] = v.reshape(per, BLOCK, D)
        put(kv_hop(v_buf, i, chunks + i))
    ffn.step(0, 1)
    write(xs, x_out, 0)
    write(qs, q_out, 1)
    write(full, attn_out, 2)
    for i in range(chunks):
        kv_hop(k_buf, i, i).wait_recv()
        kv_hop(v_buf, i, chunks + i).wait_recv()
    write(k_buf, k_out, 3)
    write(v_buf, v_out, 4)

    nb = n_rows // BLOCK
    first = core * nb
    stops = {0: [(1, 1)], 1: [(0, 2), (1, 2)], 9: [(0, 3), (1, 3)]}

    @pl.loop(0, nb)
    def _(blk):
        at = pl.ds(pl.multiple_of(blk * BLOCK, BLOCK), BLOCK)
        forward_block(
            qs.at[at],
            ms.at[at],
            lse_out.at[blk],
            k_buf,
            v_buf,
            s_buf,
            tab_ref,
            rand,
            blk * (LISTED - 5),
            blk,
            first,
            0,
        )

        for at_block, moves in stops.items():

            @pl.when(blk == at_block)
            def _():
                mark = len(sent)
                for path, number in moves:
                    ffn.step(path, number)
                del sent[mark:]

    write(ms, mixed_out, 7)
    for path, number in [move for moves in stops.values() for move in moves]:
        ffn.again(path, number)
    ffn.take_shared(0)
    ffn.take_shared(1)

    for copy in sent:
        copy.wait_send()
    for copy in local[2:]:
        copy.wait()


def start(n_tensor, attn_w, ffn_w, qv_bias, hid_bias, table, rand, tokens):
    rows = tokens.shape[1]
    own_ff = FF // n_tensor
    dma = pltpu.SemaphoreType.DMA
    vmem, anywhere = pl.BlockSpec(memory_space=pltpu.VMEM), pl.BlockSpec(memory_space=pl.ANY)
    smem = pl.BlockSpec(memory_space=pltpu.SMEM)
    tall = jax.ShapeDtypeStruct((rows, D), bf16)
    both = jax.ShapeDtypeStruct((2 * rows // BLOCK, BLOCK, D), bf16)
    items = 2 * (rows // 256)
    return pl.pallas_call(
        partial(start_kernel, n_tensor),
        out_shape=[
            jax.ShapeDtypeStruct((4, D, D), bf16),
            jax.ShapeDtypeStruct((2, D, FF), bf16),
            jax.ShapeDtypeStruct((1, FF), f32),
            tall,
            tall,
            both,
            both,
            tall,
            jax.ShapeDtypeStruct((rows // BLOCK, 8, ROWS), f32),
        ],
        in_specs=[vmem] * 5 + [smem, anywhere],
        out_specs=[anywhere, anywhere, vmem] + [anywhere] * 5 + [vmem],
        scratch_shapes=[
            pltpu.VMEM((STRIP, D), bf16),
            pltpu.VMEM((n_tensor, STRIP, D), bf16),
            pltpu.VMEM((8, D), f32),
            pltpu.VMEM((n_tensor, 8, D), f32),
            pltpu.VMEM((8, D), f32),
            pltpu.VMEM((2, STRIP, own_ff), bf16),
            pltpu.VMEM((4, D, D), bf16),
            pltpu.VMEM((rows, D), bf16),
            pltpu.VMEM((rows, D), bf16),
            pltpu.VMEM((rows, D), bf16),
            pltpu.VMEM((2 * rows // BLOCK, BLOCK, D), bf16),
            pltpu.VMEM((2 * rows // BLOCK, BLOCK, D), bf16),
            pltpu.VMEM((2 * rows // KEYS, ROWS, KEYS), f32),
            dma((2 * n_tensor,)),
            dma((2 * n_tensor,)),
            dma((n_tensor,)),
            dma((n_tensor,)),
            dma((2 * n_tensor,)),
            dma((2 * n_tensor,)),
            dma((2,)),
            dma((2,)),
            dma((6,)),
            dma((6,)),
            dma((8,)),
            dma((8,)),
            dma((6,)),
            dma((6,)),
            dma((8,)),
            dma((8,)),
            dma((items,)),
            dma((items,)),
            dma((8,)),
        ],
        compiler_params=pltpu.CompilerParams(
            collective_id=2, has_side_effects=True, vmem_limit_bytes=VMEM_LIMIT
        ),
        cost_estimate=pl.CostEstimate(
            flops=6 * rows * D * D, bytes_accessed=100 * 2**20, transcendentals=0
        ),
        name="start",
    )(attn_w, ffn_w, qv_bias, hid_bias.reshape(1, own_ff), table, rand, tokens)


def middle_kernel(n_tensor, *refs):
    x_ref, mixed_ref, hid_ref, vec_ref, cotangent, attn_full, ffn_full = refs[:7]
    out_a, out_b, dw1, dw2, dwo, gh1, gm, hid_out, sums_out = refs[7:16]
    w, wo, act, slope, h1, total, gs_low, low_t, turned, pre, dw_s, cot, ready, low, down, held = refs[16:32]
    (
        w_sem,
        c_send,
        c_recv,
        h_send,
        h_recv,
        z_send,
        z_recv,
        z_passed,
        dw_sem,
        own_sem,
        copied,
    ) = refs[32:]
    s, c, t, x, core, sibling, over_x, over_y, across, along_z = places(n_tensor)
    n_rows = x_ref.shape[0]
    chunk = 256
    chunks = n_rows // chunk
    steps = FF // D
    items, all_items = LINE_ITEMS, n_rows // ITEM

    def block(i):
        return pl.ds(pl.multiple_of(i * D, D), D)

    fetch_o = pltpu.make_async_copy(attn_full.at[3], wo, w_sem.at[2 * steps])
    fetch_o.start()

    def fetch(m, i):
        at = w.at[m, :, block(i)]
        return pltpu.make_async_copy(ffn_full.at[m, :, block(i)], at, w_sem.at[m * steps + i])

    for i in range(steps):
        for m in range(2):
            fetch(m, i).start()

    greet([over_y, across] + along_z)

    def keep_cot(i):
        at = pl.ds(i * chunk, chunk)
        return pltpu.make_async_copy(cotangent.at[t, at], cot.at[at], c_recv.at[i])

    def swap_cot(i):
        at = pl.ds(i * chunk, chunk)
        return remote(cotangent.at[t, at], cot.at[at], c_send.at[i], c_recv.at[i], across)

    def home_ref(i):
        if i < items:
            return held.at[t, pl.ds(i * ITEM, ITEM)]
        return out_b.at[pl.ds((i - items) * ITEM, ITEM)]

    def keep_home(i):
        return pltpu.make_async_copy(ready.at[pl.ds(i * ITEM, ITEM)], home_ref(i), h_recv.at[i])

    def send_home(i):
        src = ready.at[pl.ds(i * ITEM, ITEM)]
        return remote(src, home_ref(i), h_send.at[i], h_recv.at[i], across)

    def if_home(at_home, away):
        @pl.when(core == c)
        def _():
            at_home()

        @pl.when(core != c)
        def _():
            away()

    if_home(lambda: keep_cot(0).start(), lambda: swap_cot(0).start())

    chain = Relay(s, c, t, items, ITEM, held, out_a, z_send, z_recv, z_passed, copied)

    def own_ready(i):
        if_home(lambda: keep_home(i).wait(), lambda: send_home(i).wait_recv())

    events = {
        (2, 0): ([0], []),
        (3, 0): ([1], []),
        (4, 0): ([2], []),
        (4, 2): ([3], []),
        (5, 1): ([], [0]),
    }
    sizes = [ITEM] * items + [chunk] * ((n_rows - items * ITEM) // chunk)
    cot_after = {items - 1: (1, 2), items: (3,)}
    start_row = 0
    for i, size in enumerate(sizes):
        rows = slice(start_row, start_row + size)
        top = slice(0, size)
        if i == 0:
            fetch_o.wait()
        pre1 = x_ref[rows, :].astype(f32) + matmul_nt(mixed_ref[rows, :], wo[...])
        pre1 = pre1 + vec_ref[4:5, :]
        h1[rows, :] = pre1
        unit, _scale = norm_parts(pre1)
        first = unit * vec_ref[0:1, :] + vec_ref[1:2, :]
        low[top, :] = first.astype(bf16)
        down[top, :] = first + vec_ref[5:6, :]

        @pl.loop(0, steps)
        def _(j):
            if i == 0:
                fetch(0, j).wait()
                fetch(1, j).wait()
            for (at_chunk, at_step), (own, passing) in events.items():
                if at_chunk != i:
                    continue

                @pl.when(j == at_step)
                def _():
                    for n in own:
                        own_ready(n)
                        chain.send_own(n)
                    for n in passing:
                        chain.relay(n)

            hidden = matmul(low[top, :], w[0, :, block(j)]) + hid_ref[:, block(j)]
            act_now, slope_now = gelu_and_slope(hidden)
            act_now = act_now.astype(bf16)
            act[rows, block(j)] = act_now
            slope[rows, block(j)] = slope_now.astype(bf16)
            down[top, :] += matmul_nt(act_now, w[1, :, block(j)])

        second = down[top, :]
        total[rows, :] = second
        unit, _scale = norm_parts(second)
        ready[rows, :] = (unit * vec_ref[2:3, :] + vec_ref[3:4, :]).astype(bf16)
        for n in range(start_row // ITEM, (start_row + size) // ITEM):
            if_home(lambda: keep_home(n).start(), lambda: send_home(n).start())
        for n in cot_after.get(i, ()):
            if_home(lambda: keep_cot(n).start(), lambda: swap_cot(n).start())
        start_row += size

    sums_out[...] = jnp.zeros_like(sums_out)

    @pl.loop(0, chunks)
    def _(i):
        rows = pl.ds(pl.multiple_of(i * chunk, chunk), chunk)
        if_home(lambda: keep_cot(i).wait(), lambda: swap_cot(i).wait())
        unit, scale = norm_parts(total[rows, :])
        grad_out = cot[rows, :].astype(f32)
        grad = norm_back(grad_out, unit, scale, vec_ref[2:3, :])
        sums_out[2:3, :] += column_total(grad_out * unit)
        sums_out[3:4, :] += column_total(grad_out)
        total[rows, :] = grad
        grad_low = grad.astype(bf16)
        gs_low[rows, :] = grad_low
        sums_out[5:6, :] += column_total(grad_low)
        turned[:, rows] = grad.T.astype(bf16)
        unit, _scale = norm_parts(h1[rows, :])
        first = unit * vec_ref[0:1, :] + vec_ref[1:2, :]
        low_t[:, rows] = first.T.astype(bf16)

    part = D // 4

    def dw_copy(slot, m, j):
        return pltpu.make_async_copy(
            dw_s.at[slot, m], (dw1, dw2)[m].at[:, block(j)], dw_sem.at[2 * slot + m]
        )

    passing_on = {(0, 1): 1, (2, 0): 2, (3, 1): 3}

    def pass_on(j, when):
        for (at, place), n in passing_on.items():
            if place == when:

                @pl.when(j == at)
                def _():
                    chain.relay(n)

    @pl.loop(0, steps)
    def _(j):
        slot = lax.rem(j, 2)
        pass_on(j, 0)
        for i in range(chunks):
            rows = slice(i * chunk, (i + 1) * chunk)
            grad_act = matmul(gs_low[rows, :], w[1, :, block(j)]).astype(bf16).astype(f32)
            grad_pre = (grad_act * slope[rows, block(j)].astype(f32)).astype(bf16)
            pre[rows, :] = grad_pre
            total[rows, :] += matmul_nt(grad_pre, w[0, :, block(j)])
        pass_on(j, 1)
        hid_out[:, block(j)] = column_total(pre[...])

        @pl.when(j >= 2)
        def _():
            for m in range(2):
                dw_copy(slot, m, j - 2).wait()

        for n in range(4):
            out = slice(n * part, (n + 1) * part)
            dw_s[slot, 0, out, :] = matmul(low_t[out, :], pre[...]).astype(bf16)
            dw_s[slot, 1, out, :] = matmul(turned[out, :], act[:, block(j)]).astype(bf16)
        for m in range(2):
            dw_copy(slot, m, j).start()

    gm_s = gs_low

    @pl.loop(0, chunks)
    def _(i):
        rows = pl.ds(pl.multiple_of(i * chunk, chunk), chunk)
        unit, scale = norm_parts(h1[rows, :])
        grad_first = total[rows, :]
        grad_h1 = norm_back(grad_first, unit, scale, vec_ref[0:1, :])
        total[rows, :] = grad_h1
        grad_low = grad_h1.astype(bf16)
        gm_s[rows, :] = matmul(grad_low, wo[...]).astype(bf16)
        turned[:, rows] = grad_h1.T.astype(bf16)
        sums_out[0:1, :] += column_total(grad_first * unit)
        sums_out[1:2, :] += column_total(grad_first)
        sums_out[4:5, :] += column_total(grad_low)

    local = [
        pltpu.make_async_copy(total, gh1, own_sem.at[0]),
        pltpu.make_async_copy(gm_s, gm, own_sem.at[1]),
    ]
    for copy in local:
        copy.start()
    for j in range(steps - 2, steps):
        for m in range(2):
            dw_copy(j % 2, m, j).wait()

    @pl.loop(0, 4)
    def _(n):
        out = pl.ds(pl.multiple_of(n * part, part), part)
        dw_s[0, 0, out, :] = matmul(turned[out, :], mixed_ref[...]).astype(bf16)

    local.append(pltpu.make_async_copy(dw_s.at[0, 0], dwo, own_sem.at[2]))
    local[-1].start()
    for i in range(items, all_items):
        own_ready(i)
    for i in range(all_items):

        @pl.when(core != c)
        def _():
            send_home(i).wait_send()

    chain.settle()
    for copy in local:
        copy.wait()


def middle(n_tensor, x, mixed, hid_all, vec_par, cotangent, attn_full, ffn_full):
    rows = x.shape[0]
    steps = FF // D
    items, all_items = LINE_ITEMS, rows // ITEM
    dma = pltpu.SemaphoreType.DMA
    vmem, anywhere = pl.BlockSpec(memory_space=pltpu.VMEM), pl.BlockSpec(memory_space=pl.ANY)
    low, wide = pltpu.VMEM((rows, D), bf16), pltpu.VMEM((rows, D), f32)
    return pl.pallas_call(
        partial(middle_kernel, n_tensor),
        out_shape=[
            jax.ShapeDtypeStruct((n_tensor, items * ITEM, D), bf16),
            jax.ShapeDtypeStruct((rows - items * ITEM, D), bf16),
            jax.ShapeDtypeStruct((D, FF), bf16),
            jax.ShapeDtypeStruct((D, FF), bf16),
            jax.ShapeDtypeStruct((D, D), bf16),
            jax.ShapeDtypeStruct((rows, D), f32),
            jax.ShapeDtypeStruct((rows, D), bf16),
            jax.ShapeDtypeStruct((1, FF), f32),
            jax.ShapeDtypeStruct((8, D), f32),
        ],
        in_specs=[vmem] * 4 + [anywhere] * 3,
        out_specs=[anywhere] * 7 + [vmem] * 2,
        scratch_shapes=[
            pltpu.VMEM((2, D, FF), bf16),
            pltpu.VMEM((D, D), bf16),
            pltpu.VMEM((rows, FF), bf16),
            pltpu.VMEM((rows, FF), bf16),
            wide,
            wide,
            low,
            pltpu.VMEM((D, rows), bf16),
            pltpu.VMEM((D, rows), bf16),
            low,
            pltpu.VMEM((2, 2, D, D), bf16),
            low,
            low,
            pltpu.VMEM((256, D), bf16),
            pltpu.VMEM((256, D), f32),
            pltpu.VMEM((n_tensor, items * ITEM, D), bf16),
            dma((2 * steps + 1,)),
            dma((rows // 256,)),
            dma((rows // 256,)),
            dma((all_items,)),
            dma((all_items,)),
            dma((items * n_tensor,)),
            dma((items * n_tensor,)),
            dma((items,)),
            dma((4,)),
            dma((3,)),
            dma((n_tensor,)),
        ],
        compiler_params=pltpu.CompilerParams(
            collective_id=3, has_side_effects=True, vmem_limit_bytes=VMEM_LIMIT
        ),
        cost_estimate=pl.CostEstimate(
            flops=2 * rows * D * (3 * D + 6 * FF),
            bytes_accessed=60 * 2**20,
            transcendentals=2 * rows * FF,
        ),
        name="middle",
    )(x, mixed, hid_all, vec_par, cotangent, attn_full, ffn_full)


def finish_kernel(n_tensor, *refs):
    dq, dk_own, dk_far, dv_own, dv_far, gh1, x_ref, weights = refs[:8]
    dw1, dw2, dwo, vec_sums, hid_sums = refs[8:13]
    attn_out, ffn_out, vec_out, qv_out, hid_out, tokens_out = refs[13:19]
    (
        dk,
        dv,
        xs,
        held,
        x_t,
        partial_sum,
        ready,
        dws,
        acc,
        got0,
        got1a,
        got1b,
        got2,
        zf,
        zf_got,
        za,
        za_got,
        run,
        run_got,
        run_z,
        wts,
    ) = refs[19:40]
    (
        e_send,
        e_recv,
        own_sem,
        s0,
        r0,
        s1,
        r1,
        s2,
        r2,
        zf_send,
        zf_recv,
        za_send,
        za_recv,
        sm,
        rm,
        h_send,
        h_recv,
        up_send,
        up_recv,
        dn_send,
        dn_recv,
        w_sem,
        copied,
    ) = refs[40:]
    s, c, t, x, core, sibling, over_x, over_y, across, along_z = places(n_tensor)
    n_rows = dq.shape[0]
    rows_each = n_rows // PIECES
    last = n_tensor - 1

    def pieces(path, i):
        if i < 2:
            return [(dw1 if path == 0 else dw2, i * WIDE, WIDE, 0)]
        if path == 0:
            return [(dws.at[0], 0, D, 0), (dws.at[1], 0, D, D)]
        return [(dws.at[2], 0, D, 0), (dwo, 0, D, D)]

    def slot(path, i):
        return path * 3 + i

    order = [(path, i) for i in range(3) for path in range(2)]

    def rows_of(xx, cc):
        return pl.ds(pl.multiple_of((4 * xx + 2 * cc) * STRIP, 2 * STRIP), 2 * STRIP)

    own, first = {}, {}
    for path, i in order:
        k = slot(path, i)
        own[k], first[k] = [], []
        for xx in range(2):
            for j, (ref, col, width, at) in enumerate(pieces(path, i)):
                n = (k * 2 + xx) * 2 + j
                cols, to = pl.ds(col, width), pl.ds(at, width)
                own[k].append(
                    pltpu.make_async_copy(
                        ref.at[rows_of(xx, core), cols], acc.at[k, xx, :, to], own_sem.at[n]
                    )
                )
                first[k].append(
                    remote(
                        ref.at[rows_of(xx, 1 - core), cols],
                        got0.at[k, xx, :, to],
                        s0.at[n],
                        r0.at[n],
                        sibling,
                    )
                )

    def start_own(i):
        for path in range(2):
            for copy in own[slot(path, i)]:
                copy.start()

    def start_first(i):
        for path in range(2):
            for copy in first[slot(path, i)]:
                copy.start()

    fetches = [
        pltpu.make_async_copy(gh1, partial_sum, w_sem.at[1]),
        pltpu.make_async_copy(weights.at[pl.ds(0, 3)], wts, w_sem.at[0]),
        pltpu.make_async_copy(x_ref, xs, w_sem.at[2]),
    ]
    for copy in fetches:
        copy.start()
    start_own(0)
    start_own(1)
    greet([sibling, over_x, over_y, across] + along_z)

    chunk = 256
    chunks = n_rows // chunk

    def exchange(i, n):
        at = pl.ds(i * chunk, chunk)
        src, dst = ((dk_far, dk), (dv_far, dv))[n]
        k = 2 * i + n
        return remote(src.at[at], dst.at[at], e_send.at[k], e_recv.at[k], sibling)

    swaps = [exchange(i, n) for i in range(chunks) for n in range(2)]
    for copy in swaps:
        copy.start()
    start_first(0)
    fetches[0].wait()
    fetches[1].wait()

    run[0] = jnp.zeros(run.shape[1:], f32)
    run[0, 0:6, :] = vec_sums[0:6, :]
    for n in range(FF // D):
        run[0, 8 + n : 9 + n, :] = hid_sums[:, n * D : (n + 1) * D]

    def keep_home(i):
        at = pl.ds(i * rows_each, rows_each)
        return pltpu.make_async_copy(ready.at[at], held.at[t, at], h_recv.at[i])

    def send_home(i):
        at = pl.ds(i * rows_each, rows_each)
        return remote(ready.at[at], held.at[t, at], h_send.at[i], h_recv.at[i], across)

    chain = Line(
        s,
        c,
        t,
        last,
        PIECES,
        rows_each,
        held,
        tokens_out,
        (up_send, up_recv),
        (dn_send, dn_recv),
        copied,
    )
    tick = chain.tick

    def send_own(i):
        @pl.when(core == c)
        def _():
            keep_home(i).wait()

        @pl.when(core != c)
        def _():
            send_home(i).wait_recv()

        chain.send_own(i)

    for i in range(PIECES):
        at = slice(i * rows_each, (i + 1) * rows_each)
        if i * rows_each % chunk == 0:
            for n in range(2):
                exchange(i * rows_each // chunk, n).wait_recv()
        dk_piece = (dk_own[at, :].astype(f32) + dk[at, :].astype(f32)).astype(bf16)
        dv_piece = (dv_own[at, :].astype(f32) + dv[at, :].astype(f32)).astype(bf16)
        dk[at, :] = dk_piece
        dv[at, :] = dv_piece
        total = partial_sum[at, :] + matmul_nt(dq[at, :], wts[0])
        total = total + matmul_nt(dk_piece, wts[1]) + matmul_nt(dv_piece, wts[2])
        ready[at, :] = total.astype(bf16)

        @pl.when(core == c)
        def _():
            keep_home(i).start()

        @pl.when(core != c)
        def _():
            send_home(i).start()

        if i > 0:
            send_own(i - 1)

    def add_rows(target, source, count):
        @pl.loop(0, count // 16)
        def _(j):
            rows = pl.ds(pl.multiple_of(j * 16, 16), 16)
            total = target[rows, :].astype(f32) + source[rows, :].astype(f32)
            target[rows, :] = total.astype(bf16)

    def half(cc):
        return pl.ds(pl.multiple_of(cc * STRIP, STRIP), STRIP)

    second, third = {}, {}

    def stage1(path, i):
        k = slot(path, i)
        for copy in own[k]:
            copy.wait()
        for copy in first[k]:
            copy.wait_recv()
        for xx in range(2):
            add_rows(acc.at[k, xx], got0.at[k, xx], 2 * STRIP)
        if path == 0:
            second[k] = remote(acc.at[k, 1 - x], got1a.at[i], s1.at[k], r1.at[k], over_x)
        else:
            second[k] = remote(
                acc.at[k, :, half(1 - c), :], got1b.at[i], s1.at[k], r1.at[k], over_y
            )
        second[k].start()

    def stage2(path, i):
        k = slot(path, i)
        second[k].wait_recv()
        if path == 0:
            add_rows(acc.at[k, x], got1a.at[i], 2 * STRIP)
            third[k] = remote(
                acc.at[k, x, half(1 - c), :], got2.at[k], s2.at[k], r2.at[k], over_y
            )
        else:
            for xx in range(2):
                add_rows(acc.at[k, xx, half(c), :], got1b.at[i, xx], STRIP)
            third[k] = remote(
                acc.at[k, 1 - x, half(c), :], got2.at[k], s2.at[k], r2.at[k], over_x
            )
        third[k].start()

    own_cols = D // n_tensor
    own_ff = FF // n_tensor
    per = WIDE // own_ff

    def stage3(path, i):
        k = slot(path, i)
        third[k].wait_recv()

        @pl.loop(0, STRIP // 16)
        def _(j):
            rows = pl.ds(pl.multiple_of(j * 16, 16), 16)
            here = pl.ds(pl.multiple_of(c * STRIP + j * 16, 16), 16)
            total = acc[k, x, here, :].astype(f32) + got2[k, rows, :].astype(f32)
            if i < 2:
                for n in range(per):
                    piece = total[:, n * own_ff : (n + 1) * own_ff].astype(bf16)
                    zf[per * i + n, rows, path * own_ff : (path + 1) * own_ff] = piece
            else:
                for n in range(n_tensor):
                    for m in range(2):
                        at = m * D + n * own_cols
                        to = (2 * path + m) * own_cols
                        piece = total[:, at : at + own_cols].astype(bf16)
                        za[n, rows, to : to + own_cols] = piece

    z_sent = []

    def z_step(k, buf, got, send, recv):
        @pl.when(t == k)
        def _():
            for d in range(last, k, -1):
                if k > 0:
                    hop(buf, got, send, recv, d, 0, k - 1).wait_recv()
                    add_rows(buf.at[d], got.at[0, d], STRIP)
                hop(buf, got, send, recv, d, 0, k + 1).start()

        @pl.when(t == last - k)
        def _():
            for d in range(0, last - k):
                if k > 0:
                    hop(buf, got, send, recv, d, 1, last - k + 1).wait_recv()
                    add_rows(buf.at[d], got.at[1, d], STRIP)
                hop(buf, got, send, recv, d, 1, last - k - 1).start()

    def hop(buf, got, send, recv, d, way, to):
        n = way * n_tensor + d
        return remote(buf.at[d], got.at[way, d], send.at[n], recv.at[n], (s, c, to))

    def z_collect(buf, got, send, recv, emit):
        @pl.when(t > 0)
        def _():
            hop(buf, got, send, recv, t, 0, t - 1).wait_recv()
            add_rows(buf.at[t], got.at[0, t], STRIP)

        @pl.when(t < last)
        def _():
            hop(buf, got, send, recv, t, 1, t + 1).wait_recv()
            add_rows(buf.at[t], got.at[1, t], STRIP)

        @pl.loop(0, STRIP // 16)
        def _(j):
            rows = pl.ds(pl.multiple_of(j * 16, 16), 16)
            emit(rows, buf[t, rows, :].astype(f32))

    def z_settle(buf, got, send, recv):
        for d in range(n_tensor):

            @pl.when(t < d)
            def _():
                hop(buf, got, send, recv, d, 0, t + 1).wait_send()

            @pl.when(t > d)
            def _():
                hop(buf, got, send, recv, d, 1, t - 1).wait_send()

    ffn_z = (zf, zf_got, zf_send, zf_recv)
    attn_z = (za, za_got, za_send, za_recv)

    small = []

    def small_send(n, where):
        small.append(remote(run.at[n], run_got.at[n], sm.at[n], rm.at[n], where))
        small[n].start()

    def small_add(n):
        small[n].wait_recv()
        run[n + 1] = run[n] + run_got[n]

    start_first(1)
    fetches[2].wait()
    for i in range(chunks):
        at = slice(i * chunk, (i + 1) * chunk)
        x_t[:, at] = xs[at, :].T
    dws[0] = matmul(x_t[...], dq[...]).astype(bf16)
    send_own(7)
    dws[1] = matmul(x_t[...], dk[...]).astype(bf16)
    dws[2] = matmul(x_t[...], dv[...]).astype(bf16)
    start_own(2)
    start_first(2)
    run[0, 6:7, :] = column_total(dq[...])
    run[0, 7:8, :] = column_total(dv[...])
    small_send(0, sibling)
    stage1(0, 0)
    stage1(1, 0)
    stage1(0, 1)
    stage1(1, 1)
    tick(0)
    stage1(0, 2)
    stage1(1, 2)
    small_add(0)
    small_send(1, over_x)
    tick(1)
    tick(2)
    tick(3)
    stage2(0, 0)
    stage2(1, 0)
    tick(4)
    tick(5)
    small_add(1)
    small_send(2, over_y)
    tick(6)
    stage2(0, 1)
    stage2(1, 1)
    tick(7)
    tick(8)
    small_add(2)
    run_z[t] = run[3]
    for k, where in enumerate(along_z):
        copy = remote(run.at[3], run_z.at[t], sm.at[3 + k], rm.at[3 + t], where)
        copy.start()
        z_sent.append(copy)
    stage3(0, 0)
    stage3(1, 0)
    stage2(0, 2)
    stage2(1, 2)
    tick(9)
    tick(10)
    stage3(0, 1)
    stage3(1, 1)
    z_step(0, *ffn_z)
    tick(11)
    tick(12)
    z_step(1, *ffn_z)
    stage3(0, 2)
    stage3(1, 2)
    z_step(0, *attn_z)
    tick(13)
    tick(14)
    z_step(2, *ffn_z)
    z_step(1, *attn_z)
    tick(15)
    tick(16)
    z_step(2, *attn_z)
    for j in range(17, PIECES * last):
        tick(j)

    for k, where in enumerate(along_z):
        u = where[2]
        remote(run.at[3], run_z.at[u], sm.at[3 + k], rm.at[3 + u], where).wait_recv()
    total = run_z[0]
    for n in range(1, n_tensor):
        total = total + run_z[n]
    vec_out[...] = total[0:6, :]
    for n in range(n_tensor):

        @pl.when(t == n)
        def _():
            qv_out[...] = total[6:8, n * own_cols : (n + 1) * own_cols]
            hid_out[...] = total[8 + n : 9 + n, :]


    def emit_ffn(rows, total):
        for m in range(2):
            ffn_out[m, rows, :] = total[:, m * own_ff : (m + 1) * own_ff]

    def emit_attn(rows, total):
        for m in range(4):
            attn_out[m, rows, :] = total[:, m * own_cols : (m + 1) * own_cols]

    z_collect(*ffn_z, emit_ffn)
    z_collect(*attn_z, emit_attn)
    z_settle(*ffn_z)
    z_settle(*attn_z)

    for copy in swaps:
        copy.wait_send()
    for path, i in order:
        k = slot(path, i)
        for copy in first[k]:
            copy.wait_send()
        second[k].wait_send()
        third[k].wait_send()
    for copy in small + z_sent:
        copy.wait_send()

    @pl.when(core != c)
    def _():
        for i in range(PIECES):
            send_home(i).wait_send()

    chain.settle()


def finish_all(n_tensor, grads, gh1, x, attn_full, dws, sums):
    rows = x.shape[0]
    own_cols, own_ff = D // n_tensor, FF // n_tensor
    dma = pltpu.SemaphoreType.DMA
    vmem, anywhere = pl.BlockSpec(memory_space=pltpu.VMEM), pl.BlockSpec(memory_space=pl.ANY)
    dq, dk_own, dk_far, dv_own, dv_far = grads
    tall = pltpu.VMEM((rows, D), bf16)
    items = PIECES * (n_tensor - 1)
    return pl.pallas_call(
        partial(finish_kernel, n_tensor),
        out_shape=[
            jax.ShapeDtypeStruct((4, STRIP, own_cols), f32),
            jax.ShapeDtypeStruct((2, STRIP, own_ff), f32),
            jax.ShapeDtypeStruct((6, D), f32),
            jax.ShapeDtypeStruct((2, own_cols), f32),
            jax.ShapeDtypeStruct((1, own_ff), f32),
            jax.ShapeDtypeStruct((n_tensor, rows, D), bf16),
        ],
        in_specs=[vmem, vmem, anywhere, vmem, anywhere] + [anywhere] * 6
        + [vmem] * 2,
        out_specs=[vmem] * 5 + [anywhere],
        scratch_shapes=[
            tall,
            tall,
            tall,
            pltpu.VMEM((n_tensor, rows, D), bf16),
            pltpu.VMEM((D, rows), bf16),
            pltpu.VMEM((rows, D), f32),
            tall,
            pltpu.VMEM((3, D, D), bf16),
            pltpu.VMEM((6, 2, 2 * STRIP, WIDE), bf16),
            pltpu.VMEM((6, 2, 2 * STRIP, WIDE), bf16),
            pltpu.VMEM((3, 2 * STRIP, WIDE), bf16),
            pltpu.VMEM((3, 2, STRIP, WIDE), bf16),
            pltpu.VMEM((6, STRIP, WIDE), bf16),
            pltpu.VMEM((n_tensor, STRIP, 2 * own_ff), bf16),
            pltpu.VMEM((2, n_tensor, STRIP, 2 * own_ff), bf16),
            pltpu.VMEM((n_tensor, STRIP, 4 * own_cols), bf16),
            pltpu.VMEM((2, n_tensor, STRIP, 4 * own_cols), bf16),
            pltpu.VMEM((4, 16, D), f32),
            pltpu.VMEM((3, 16, D), f32),
            pltpu.VMEM((n_tensor, 16, D), f32),
            pltpu.VMEM((3, D, D), bf16),
            dma((2 * rows // 256,)),
            dma((2 * rows // 256,)),
            dma((24,)),
            dma((24,)),
            dma((24,)),
            dma((6,)),
            dma((6,)),
            dma((6,)),
            dma((6,)),
            dma((2 * n_tensor,)),
            dma((2 * n_tensor,)),
            dma((2 * n_tensor,)),
            dma((2 * n_tensor,)),
            dma((3 + n_tensor,)),
            dma((3 + n_tensor,)),
            dma((PIECES,)),
            dma((PIECES,)),
            dma((items + PIECES,)),
            dma((items + PIECES,)),
            dma((items + PIECES,)),
            dma((items + PIECES,)),
            dma((3,)),
            dma((2 * n_tensor - 1,)),
        ],
        compiler_params=pltpu.CompilerParams(
            collective_id=1, has_side_effects=True, vmem_limit_bytes=VMEM_LIMIT
        ),
        cost_estimate=pl.CostEstimate(
            flops=12 * rows * D * D, bytes_accessed=400 * 2**20, transcendentals=0
        ),
        name="finish",
    )(dq, dk_own, dk_far, dv_own, dv_far, gh1, x, attn_full, *dws, *sums)


GROUP_RATES = (
    [2.0 / D**0.5] * 3 + [2.0 / (D // (4 * BLOCK)) ** 0.5],
    [2.0 / D**0.5, 2.0 / FF**0.5],
)


def last_kernel(tokens_ref, out_b, _output_a, *refs):
    attn_g, attn_w, attn_m, attn_v, ffn_g, ffn_w, ffn_m, ffn_v = refs[:8]
    plain = [refs[8 + 4 * n : 12 + 4 * n] for n in range(3)]
    tokens_out, output = refs[20:22]
    attn_moment, attn_square, out_states, attn_new, attn_copy = refs[22:27]
    ffn_moment, ffn_square, ffn_new, ffn_copy = refs[27:31]
    plain_out = [refs[31 + 3 * n : 34 + 3 * n] for n in range(3)]
    step = pl.program_id(0)

    @pl.when(step == 0)
    def _():
        for m in range(4):
            moment, square, new = adam_update(
                attn_w[m], attn_m[m], attn_v[m], attn_g[m], GROUP_RATES[0][m], decay_rate
            )
            if m < 3:
                attn_moment[m], attn_square[m] = moment, square
            else:
                out_states[0], out_states[1] = moment, square
            attn_new[m], attn_copy[m] = new, new.astype(bf16)
        for m in range(2):
            moment, square, new = adam_update(
                ffn_w[m], ffn_m[m], ffn_v[m], ffn_g[m], GROUP_RATES[1][m], decay_rate
            )
            ffn_moment[m], ffn_square[m] = moment, square
            ffn_new[m], ffn_copy[m] = new, new.astype(bf16)
        for (g, w, m, v), outs in zip(plain, plain_out):
            gradient = g[...] if len(g.shape) == len(w.shape) else g[0, :]
            for ref, value in zip(outs, adam_update(w[...], m[...], v[...], gradient, 0.5, 0.0)):
                ref[...] = value

    tokens_out[...] = tokens_ref[...].astype(f32)

    output[...] = out_b[...]


def last(tokens_low, output, out_b, attn, ffn, plain):
    count, rows, _ = tokens_low.shape
    tile = lambda size, index: pl.BlockSpec((1, size, D), index)
    whole = lambda shape: pl.BlockSpec(
        shape, lambda i: (0,) * len(shape), pipeline_mode=pl.Buffered(1)
    )
    a, f = attn[0].shape, ffn[0].shape
    shapes = [
        ((3,) + a[1:], f32),
        ((3,) + a[1:], f32),
        ((2,) + a[1:], f32),
        (a, f32),
        (a, bf16),
        (f, f32),
        (f, f32),
        (f, f32),
        (f, bf16),
    ]
    for group in plain:
        shapes += [(group[1].shape, f32)] * 3
    inputs = list(attn) + list(ffn) + [array for group in plain for array in group]
    by_half = lambda i: (i // 2, i % 2, 0)
    by_one = lambda i: (i // 2, i % 2, 0)
    second = lambda i: (i // 2, 2 + i % 2, 0)
    quarter = rows // 4
    return pl.pallas_call(
        last_kernel,
        out_shape=[
            jax.ShapeDtypeStruct(tokens_low.shape, f32),
            jax.ShapeDtypeStruct(tokens_low.shape, bf16),
        ]
        + [jax.ShapeDtypeStruct(*entry) for entry in shapes],
        grid=(count * 2,),
        in_specs=[
            tile(rows // 2, by_half),
            tile(quarter, by_one),
            pl.BlockSpec(memory_space=pl.ANY),
        ]
        + [whole(array.shape) for array in inputs],
        out_specs=[tile(rows // 2, by_half), tile(quarter, second)]
        + [whole(shape) for shape, _ in shapes],
        input_output_aliases={2: 1},
        compiler_params=pltpu.CompilerParams(vmem_limit_bytes=VMEM_LIMIT),
        name="last",
    )(tokens_low, out_b, output, *inputs)


def make_body(mesh):
    n_shard, n_ctx, n_tensor = mesh.shape["shard"], mesh.shape["ctx"], mesh.shape["tensor"]
    rows_axes = ("shard", "ctx")
    all_axes = ("shard", "ctx", "tensor")
    paired = n_ctx == 2 and n_shard == 4 and n_tensor == 4

    def swapped(s, c):
        return (s - s % 2 + c, s % 2)

    def swap(array):
        if not paired:
            return array
        pairs = []
        for s in range(n_shard):
            for c in range(n_ctx):
                s_to, c_to = swapped(s, c)
                pairs.append((s * n_ctx + c, s_to * n_ctx + c_to))
        return lax.ppermute(array, rows_axes, pairs)

    def spread(array):
        return lax.all_gather(swap(array), "tensor", axis=0, tiled=True)

    def body(
        tokens,
        cotangent,
        segments,
        rand_blocks,
        attn_w,
        attn_m,
        attn_v,
        ffn_w,
        ffn_m,
        ffn_v,
        qv_bias,
        qv_m,
        qv_v,
        hid_bias,
        hid_m,
        hid_v,
        vec_par,
        vec_m,
        vec_v,
    ):
        t_index = lax.axis_index("tensor")
        nseq = tokens.shape[0] // n_tensor
        piece_len = tokens.shape[1]
        nb = piece_len // BLOCK
        own_rows, own_cols = attn_w.shape[1], attn_w.shape[2]
        own_ff = ffn_w.shape[2]

        def mine(array):
            return lax.dynamic_slice_in_dim(array, t_index * nseq, nseq, 0)

        ints = jnp.concatenate(
            [mine(segments), mine(rand_blocks).reshape(nseq, -1)], axis=1
        )
        ints = swap(ints)
        length = segments.shape[1]
        segs, rand = ints[:, :length], ints[:, length:].reshape(nseq, length // BLOCK, -1)
        piece = lax.axis_index("shard") % 2 if paired else lax.axis_index("ctx")
        tables = attention_tables(segs, rand, piece, nb, paired)

        if paired:
            rand_own, _meta, table = tables
            attn_full, ffn_full, hid_all, x, queries, keys, values, mixed, lse = start(
                n_tensor, attn_w, ffn_w, qv_bias, hid_bias, table[0], rand_own, tokens
            )
            flat = x
            x, queries = x[None], queries[None]
            keys, values = keys.reshape(1, length, D), values.reshape(1, length, D)
            pieces = [piece_len, piece_len]
        else:
            x, cot = mine(tokens), mine(cotangent)
            pieces = [length]
            ffn_z = lax.all_gather(ffn_w.astype(bf16), "tensor", axis=0, tiled=False)
            ffn_z = ffn_z.transpose(1, 2, 0, 3).reshape(2, own_rows, FF)
            ffn_full = lax.all_gather(ffn_z, rows_axes, axis=1, tiled=True)
            flat = x.reshape(-1, D)
            attn_low = attn_w.astype(bf16)
            attn_low = jnp.concatenate([attn_low[i] for i in range(4)], axis=1)
            attn_z = lax.all_gather(attn_low, "tensor", axis=0, tiled=False)
            attn_z = attn_z.reshape(n_tensor, own_rows, 4, own_cols).transpose(2, 1, 0, 3)
            attn_full = lax.all_gather(
                attn_z.reshape(4, own_rows, D), rows_axes, axis=1, tiled=True
            )
            bias_own = jnp.concatenate([qv_bias.reshape(-1), hid_bias])
            bias_all = lax.all_gather(bias_own, "tensor", axis=0, tiled=False)
            qv_all = bias_all[:, : 2 * own_cols].reshape(n_tensor, 2, own_cols)
            qv_all = qv_all.transpose(1, 0, 2).reshape(2, D)
            hid_all = bias_all[:, 2 * own_cols :].reshape(FF)
            keys = matmul(flat, attn_full[1]).astype(bf16).reshape(x.shape)
            values = (matmul(flat, attn_full[2]) + qv_all[1]).astype(bf16).reshape(x.shape)
            keys = lax.all_gather(keys, "ctx", axis=1, tiled=True)
            values = lax.all_gather(values, "ctx", axis=1, tiled=True)
            queries = (matmul(flat, attn_full[0]) + qv_all[0]).astype(bf16) * 0.125
            queries = queries.reshape(x.shape)
            mixed, lse = attend(tables, queries, keys, values)
        mixed_low = mixed.reshape(-1, D)
        if paired:
            out_a, out_b, dw1, dw2, dwo, grad_first_in, grad_mixed, hid_sum, vec_sums = middle(
                n_tensor, flat, mixed_low, hid_all, vec_par, cotangent, attn_full, ffn_full
            )
            out_b = lax.all_gather(out_b, "tensor", axis=0, tiled=False)
        else:
            act, slope, h1, result, grad_second, second_sums = feed_forward(
                flat, mixed_low, cot.reshape(-1, D), attn_full, ffn_full, hid_all, vec_par
            )
            output = spread(result.reshape(x.shape))
            out_a, out_b = output[:, : piece_len // 2], output[:, piece_len // 2 :]
            dw1, dw2, dwo, grad_first_in, grad_mixed, hid_sum, first_sums = feed_back(
                grad_second, h1, mixed_low, attn_full, ffn_full, act, slope, vec_par
            )

        grad_mixed = grad_mixed.reshape(x.shape)
        grad_query, output, dk_parts, dv_parts = attend_back(
            tables,
            queries,
            grad_mixed,
            mixed.reshape(x.shape),
            lse.reshape(nseq, nb, 8, ROWS),
            out_a,
            keys,
            values,
            pieces,
        )

        grad_query_low = grad_query.reshape(-1, D)
        if paired:
            attn_grad, ffn_grad, vec_grad, qv_grad, hid_grad, grad_tokens = finish_all(
                n_tensor,
                [grad_query_low] + [part[0] for part in list(dk_parts) + list(dv_parts)],
                grad_first_in,
                flat,
                attn_full,
                (dw1, dw2, dwo),
                (vec_sums, hid_sum),
            )
        else:
            grad_keys = lax.psum_scatter(dk_parts[0], "ctx", scatter_dimension=1, tiled=True)
            grad_values = lax.psum_scatter(dv_parts[0], "ctx", scatter_dimension=1, tiled=True)
            grad_keys_low = grad_keys.reshape(-1, D)
            grad_values_low = grad_values.reshape(-1, D)
            into_tokens = (
                matmul_nt(grad_query_low, attn_full[0])
                + matmul_nt(grad_keys_low, attn_full[1])
                + matmul_nt(grad_values_low, attn_full[2])
            )
            grad_tokens = spread((grad_first_in + into_tokens).astype(bf16).reshape(x.shape))
            dwq = matmul_tn(flat, grad_query_low).astype(bf16)
            dwk = matmul_tn(flat, grad_keys_low).astype(bf16)
            dwv = matmul_tn(flat, grad_values_low).astype(bf16)
            small = jnp.concatenate(
                [
                    first_sums[0],
                    first_sums[1],
                    second_sums[0],
                    second_sums[1],
                    first_sums[2],
                    second_sums[2],
                    column_sum(grad_query_low),
                    column_sum(grad_values_low),
                    hid_sum[0],
                ]
            )
            ffn_grad = lax.psum_scatter(
                jnp.stack([dw1, dw2]), rows_axes, scatter_dimension=1, tiled=True
            )
            ffn_grad = ffn_grad.reshape(2, own_rows, n_tensor, own_ff).transpose(2, 0, 1, 3)
            ffn_grad = lax.psum_scatter(ffn_grad, "tensor", scatter_dimension=0, tiled=False)
            ffn_grad = ffn_grad.astype(f32)
            attn_grad = lax.psum_scatter(
                jnp.stack([dwq, dwk, dwv, dwo]), rows_axes, scatter_dimension=1, tiled=True
            )
            attn_grad = attn_grad.reshape(4, own_rows, n_tensor, own_cols).transpose(2, 1, 0, 3)
            attn_grad = lax.psum_scatter(
                attn_grad.reshape(n_tensor, own_rows, D), "tensor", scatter_dimension=0
            )
            attn_grad = attn_grad.reshape(own_rows, 4, own_cols).transpose(1, 0, 2).astype(f32)
            small = lax.psum(small, all_axes)
            vec_grad = small[: 6 * D].reshape(6, D)
            qv_grad = lax.dynamic_slice_in_dim(
                small[6 * D : 8 * D].reshape(2, D), t_index * own_cols, own_cols, 1
            )
            hid_grad = lax.dynamic_slice_in_dim(
                small[8 * D : 8 * D + FF], t_index * own_ff, own_ff, 0
            )

        grad_tokens, output, *updated = last(
            grad_tokens,
            output,
            out_b,
            (attn_grad, attn_w, attn_m, attn_v),
            (ffn_grad, ffn_w, ffn_m, ffn_v),
            [
                (qv_grad, qv_bias, qv_m, qv_v),
                (hid_grad.reshape(1, own_ff), hid_bias, hid_m, hid_v),
                (vec_grad, vec_par, vec_m, vec_v),
            ],
        )
        return (output, grad_tokens, *updated)

    return body


def solution(mesh):
    rows = P("shard", "ctx", None)
    weight = P(None, ("shard", "ctx"), "tensor")
    in_specs = (
        (rows, rows, P("shard", None), P("shard", None, None))
        + (weight,) * 6
        + (P(None, "tensor"),) * 3
        + (P("tensor"),) * 3
        + (P(),) * 3
    )
    out_specs = (
        (rows, rows)
        + (weight,) * 9
        + (P(None, "tensor"),) * 3
        + (P("tensor"),) * 3
        + (P(),) * 3
    )
    return jax.shard_map(
        make_body(mesh), mesh=mesh, in_specs=in_specs, out_specs=out_specs, check_vma=False
    )
```
